32 devices in a mesh: tile: 8 (over z, y), layer: 4 (over x, core).
Axes of the slice: x: 2, y: 2, z: 4, core: 2. Of those that a mesh axis runs over, the one named last changes fastest.
Arguments:
- newton_rhs: float32 [3, 12, 128, 2048], P(None, 'layer', 'tile'), may hold values from -6 to 6
- weights: float32 [3, 12, 128, 2048], P(None, 'layer', 'tile'), may hold values from 0.2 to 1
- block_diag: float32 [3, 3, 12, 128, 2048], P(None, None, 'layer', 'tile'), as said below
- block_inv: float32 [3, 3, 12, 128, 2048], P(None, None, 'layer', 'tile'), as said below
- trans_x: float32 [12, 128, 2048], P('layer', 'tile'), may hold values from 0.2 to 1
- trans_y: float32 [12, 128, 2048], P('layer', 'tile'), may hold values from 0.2 to 1
- trans_z: float32 [12, 128, 2048], P('layer', 'tile'), may hold values from 0.2 to 1
- storage: float32 [12, 128, 2048], P('layer', 'tile'), may hold values from 0.05 to 0.5
- perf_cell: int32 [8192], P(('tile', 'layer')), may hold values from 0 to 98303
- perf_front: int32 [8192], P(('tile', 'layer')), may hold values from 0 to 8191
- productivity: float32 [8192], P(('tile', 'layer')), may hold values from 0.5 to 2
- front_inverse: float32 [8192, 8192], P(('tile', 'layer')), may hold values from -0.0625 to 0.0625
Outputs:
- update: float32 [3, 12, 128, 2048], P(None, 'layer', 'tile')
- lin_res: float32 [3, 12, 128, 2048], P(None, 'layer', 'tile')
- ratio: float32 [], replicated
The draws below stay inside these ranges and needn't reach their ends.
Inputs may be any that keep to these rules, and one draw needn't show every extreme that they name: perf_cell indexes the [3, 16, 2048] block of the device that holds the perforation; cells may hold several perforations. `perf_front`: front unknowns may receive several perforations from many devices. Diagonal entries of block_diag lie between 6 and 9. Diagonal entries of block_inv lie between 0.1 and 0.2.
All inputs are finite; a program needn't handle non-finite values.
Results may differ from the reference program's by a relative error of at most 0.000098.
Values sent between devices are 32-bit elements; how exact they have to be, the bound alone decides.
No kernel may reach another device: no remote copies, remote signals or barrier semaphores. Data moves between devices by JAX's collectives and lax.ppermute only.
A program may use at most 128 MiB of HBM per device.

```python
import math
import jax
import jax.numpy as jnp
from jax import lax

LZ = 3
CX = 16
NY = 2048
NF = 8192
PERF_DEV = 256
NZ = 12
NX = 128
NPERF = 8192
N_LAYER = 4


def draw_block_diag(key, part):
    first, second = jax.random.split(jax.random.fold_in(key, 11))
    shape = (3, 3, NZ, NX, NY)
    eye = jnp.eye(3, dtype=jnp.float32)[:, :, None, None, None]
    off = 0.5 * jax.random.normal(first, shape, jnp.float32)
    diag = 6.0 + 3.0 * jax.random.uniform(second, shape, jnp.float32)
    return eye * diag + (1.0 - eye) * off


def draw_block_inv(key, part):
    first, second = jax.random.split(jax.random.fold_in(key, 23))
    shape = (3, 3, NZ, NX, NY)
    eye = jnp.eye(3, dtype=jnp.float32)[:, :, None, None, None]
    off = 0.02 * jax.random.normal(first, shape, jnp.float32)
    diag = 0.1 + 0.1 * jax.random.uniform(second, shape, jnp.float32)
    return eye * diag + (1.0 - eye) * off


def touch_ends(values, key, smallest, top_value):
    longest = values.shape.index(max(values.shape))
    spots = []
    for shift in (0, 1):
        where = [jax.random.randint(jax.random.fold_in(key, axis), (), 0, length) for axis, length in enumerate(values.shape)]
        where[longest] = (where[longest] + shift) % values.shape[longest]
        spots.append(tuple(where))
    return values.at[spots[0]].set(smallest).at[spots[1]].set(top_value)


def block_scale(own_key, extent, shards, least, top_value):
    def one(position, blocks):
        steps = jax.random.uniform(jax.random.fold_in(jax.random.fold_in(own_key, 6), position), (blocks,), jnp.float32, least / len(shards), top_value / len(shards))
        return jnp.repeat(jnp.exp(steps), extent[position] // blocks).reshape((-1,) + (1,) * (len(extent) - position - 1))

    level = one(*shards[0])
    for cut in shards[1:]:
        level = level * one(*cut)
    return level


def noise(stream_key, extent, scale, most, pieces=(), held_as=jnp.bfloat16):
    drawn = scale * jax.random.normal(stream_key, extent, jnp.float32)
    if pieces:
        drawn = drawn * block_scale(stream_key, extent, pieces, -0.22, 0.18)
    return jnp.clip(drawn, -most, most).astype(held_as)


def setup_inputs(seed: int = 0) -> dict:
    splits = jax.random.split(jax.random.key(seed), 13)
    newton_rhs = noise(splits[0], (3, NZ, NX, NY), 1.0, 6.0, ((1, 4), (2, 8)), jnp.float32)
    weights = jnp.clip(0.2 + 0.8 * jax.random.uniform(splits[1], (3, NZ, NX, NY), jnp.float32) ** block_scale(splits[1], (3, NZ, NX, NY), ((1, 4), (2, 8)), -0.2, 0.2), 0.2, 1.0)
    block_diag = draw_block_diag(jax.random.fold_in(splits[12], 71), 0)
    block_inv = draw_block_inv(jax.random.fold_in(splits[12], 71), 0)
    trans_x = jnp.clip(jnp.exp(math.log(1.0) - 1.609438 * jax.random.uniform(splits[4], (NZ, NX, NY), jnp.float32) ** block_scale(splits[4], (NZ, NX, NY), ((0, 4), (1, 8)), -0.2, 0.2)), 0.2, 1.0)
    trans_y = jnp.clip(jnp.exp(math.log(1.0) - 1.609438 * jax.random.uniform(splits[5], (NZ, NX, NY), jnp.float32) ** block_scale(splits[5], (NZ, NX, NY), ((0, 4), (1, 8)), -0.2, 0.2)), 0.2, 1.0)
    trans_z = jnp.clip(jnp.exp(math.log(1.0) - 1.609438 * jax.random.uniform(splits[6], (NZ, NX, NY), jnp.float32) ** block_scale(splits[6], (NZ, NX, NY), ((0, 4), (1, 8)), -0.2, 0.2)), 0.2, 1.0)
    storage = jnp.clip(jnp.exp(math.log(0.5) - 2.3025851 * jax.random.uniform(splits[7], (NZ, NX, NY), jnp.float32) ** block_scale(splits[7], (NZ, NX, NY), ((0, 4), (1, 8)), -0.2, 0.2)), 0.05, 0.5)
    perf_cell = touch_ends(jax.random.randint(splits[8], (NPERF,), 0, LZ * CX * NY), jax.random.fold_in(splits[8], 1), 0, (LZ * CX * NY) - 1).astype(jnp.int32)
    perf_front = touch_ends(jax.random.randint(splits[9], (NPERF,), 0, NF), jax.random.fold_in(splits[9], 1), 0, NF - 1).astype(jnp.int32)
    productivity = jnp.clip(jnp.exp(math.log(2.0) - 1.3862944 * jax.random.uniform(splits[10], (NPERF,), jnp.float32) ** block_scale(splits[10], (NPERF,), ((0, 32),), -0.2, 0.2)), 0.5, 2.0)
    front_inverse = noise(splits[11], (NF, NF), NF ** -0.5, 0.0625, ((0, 32),), jnp.float32)
    return {"newton_rhs": newton_rhs, "weights": weights, "block_diag": block_diag, "block_inv": block_inv, "trans_x": trans_x, "trans_y": trans_y, "trans_z": trans_z, "storage": storage, "perf_cell": perf_cell, "perf_front": perf_front, "productivity": productivity, "front_inverse": front_inverse}


def couple(field, trans_x, trans_y, trans_z):
    lead = field.ndim - 3
    pads = [(0, 0)] * lead + [(1, 1), (1, 1), (1, 1)]
    padded = jnp.pad(field, pads)
    tpad = [(1, 1), (1, 1), (1, 1)]
    txp = jnp.pad(trans_x, tpad)
    typ = jnp.pad(trans_y, tpad)
    tzp = jnp.pad(trans_z, tpad)
    total = trans_x * padded[..., 1:-1, 2:, 1:-1] + txp[1:-1, :-2, 1:-1] * padded[..., 1:-1, :-2, 1:-1]
    total = total + trans_y * padded[..., 1:-1, 1:-1, 2:] + typ[1:-1, 1:-1, :-2] * padded[..., 1:-1, 1:-1, :-2]
    total = total + trans_z * padded[..., 2:, 1:-1, 1:-1] + tzp[:-2, 1:-1, 1:-1] * padded[..., :-2, 1:-1, 1:-1]
    return total

def block_apply(matrix, vector):
    return matrix[:, 0] * vector[0][None] + matrix[:, 1] * vector[1][None] + matrix[:, 2] * vector[2][None]

def jacobian(field, block_diag, trans_x, trans_y, trans_z):
    return block_apply(block_diag, field) - couple(field, trans_x, trans_y, trans_z)

def line_solve(rhs, upper_raw, store):
    depth = rhs.shape[0]
    live = (lax.iota(jnp.int32, depth) < depth - 1).astype(jnp.float32)[:, None, None]
    upper = upper_raw * live
    lower = jnp.concatenate([jnp.zeros_like(upper[:1]), upper[:-1]], 0)
    diag = lower + upper + store

    def forward(carry, item):
        gprev, dprev = carry
        low, up, dia, rh = item
        pivot = dia - low * gprev
        gnow = up / pivot
        dnow = (rh + low * dprev) / pivot
        return ((gnow, dnow), (gnow, dnow))
    zero = jnp.zeros_like(rhs[0])
    _, (gall, dall) = lax.scan(forward, (zero, zero), (lower, upper, diag, rhs))

    def backward(carry, item):
        gnow, dnow = item
        value = dnow + gnow * carry
        return (value, value)
    _, sol = lax.scan(backward, zero, (gall, dall), reverse=True)
    return sol

def reference(newton_rhs, weights, block_diag, block_inv, trans_x, trans_y, trans_z, storage, perf_cell, perf_front, productivity, front_inverse):
    pres_rhs = lax.optimization_barrier(jnp.sum(weights * newton_rhs, axis=0))
    slot = lax.iota(jnp.int32, NPERF)
    device = slot // PERF_DEV
    tile_idx = device // N_LAYER
    layer_idx = device % N_LAYER
    local_z = perf_cell // (CX * NY)
    local_x = perf_cell // NY % CX
    local_y = perf_cell % NY
    glob = ((layer_idx * LZ + local_z) * NX + tile_idx * CX + local_x) * NY + local_y
    glob = glob.astype(jnp.int32)
    flat = pres_rhs.reshape(-1)
    front_rhs = jnp.zeros((NF,), jnp.float32).at[perf_front].add(productivity * flat[glob])
    front_sol = jnp.dot(front_inverse, front_rhs, precision=lax.Precision.HIGHEST)
    adjusted = flat.at[glob].add(-productivity * front_sol[perf_front]).reshape(pres_rhs.shape)
    pressure = line_solve(adjusted, trans_z, storage)
    zeros_two = jnp.zeros((2,) + pressure.shape, jnp.float32)
    pe0 = jnp.concatenate([pressure[None], zeros_two], 0)
    remain = newton_rhs - jacobian(pe0, block_diag, trans_x, trans_y, trans_z)
    search = pe0 + block_apply(block_inv, remain)
    image = jacobian(search, block_diag, trans_x, trans_y, trans_z)
    along = jnp.sum(image * newton_rhs)
    power = jnp.sum(image * image)
    start_sq = jnp.sum(newton_rhs * newton_rhs)
    omega = along / power
    update = omega * search
    lin_res = newton_rhs - omega * image
    ratio = jnp.sqrt(jnp.sum(lin_res * lin_res) / start_sq)
    return (update, lin_res, ratio)
```

```python
import functools
import jax
import jax.numpy as jnp
from jax import lax
from jax.experimental import pallas as pl
from jax.experimental.pallas import tpu as pltpu
from jax.sharding import PartitionSpec as P

F32 = jnp.float32
BF16 = jnp.bfloat16
I32 = jnp.int32
BOTH = ("tile", "layer")
VM = pl.BlockSpec(memory_space=pltpu.VMEM)
LIMIT = 16 << 20


def hbm(shape):
    return jax.ShapeDtypeStruct(shape, F32)


def vmem(shape, dtype=F32):
    return pltpu.VMEM(shape, dtype)


def call(kernel, outs, args, flops=0, limit=LIMIT):
    args = [pltpu.with_memory_space_constraint(a, pltpu.VMEM) for a in args]
    size = 4 * sum(a.size for a in args)
    return pl.pallas_call(
        kernel,
        out_shape=outs,
        in_specs=[VM] * len(args),
        out_specs=jax.tree.map(lambda _: VM, outs),
        compiler_params=pltpu.CompilerParams(vmem_limit_bytes=limit),
        cost_estimate=pl.CostEstimate(flops=flops, bytes_accessed=size, transcendentals=0),
    )(*args)


def iota(shape, dim):
    return lax.broadcasted_iota(I32, shape, dim)


def split(x):
    one = x.astype(BF16)
    rest = x - one.astype(F32)
    two = rest.astype(BF16)
    three = (rest - two.astype(F32)).astype(BF16)
    return [one, two, three]


def fold(x):
    n = x.shape[0] // 3
    return x[:n] + (x[n : 2 * n] + x[2 * n :])


def onehot(index, size):
    return jnp.where(iota((size, index.shape[1]), 0) == index, 1.0, 0.0)


def dot(a, b):
    return lax.dot_general(a, b, (((1,), (0,)), ((), ())), preferred_element_type=F32)


def dot_nt(a, b):
    return lax.dot_general(a, b, (((1,), (1,)), ((), ())), preferred_element_type=F32)


def pick(table, hi, lo):
    rows, cols = table.shape
    parts = jnp.concatenate(split(table), 0)
    got = fold(dot(parts, onehot(lo, cols).astype(BF16)))
    return jnp.sum(got * onehot(hi, rows), axis=0, keepdims=True)


def spread(value, hi, lo, rows, cols):
    parts = [jnp.where(iota((rows, hi.shape[1]), 0) == hi, v.astype(F32), 0.0).astype(BF16) for v in split(value)]
    return fold(dot_nt(jnp.concatenate(parts, 0), onehot(lo, cols).astype(BF16)))


def pres_kernel(rhs, wts, cell, front, prod, pres, send):
    depth, width, long = pres.shape
    for z in range(depth):
        pres[z] = wts[0, z] * rhs[0, z] + wts[1, z] * rhs[1, z] + wts[2, z] * rhs[2, z]
    where = cell[...]
    table = pres[...].reshape(depth * width, long)
    value = prod[...] * pick(table, lax.div(where, long), lax.rem(where, long))
    both = jnp.concatenate([value, front[...].astype(F32)], 1)
    send[...] = jnp.broadcast_to(both, send.shape)


def front_kernel(recv, inverse, send):
    devices = recv.shape[0]
    count = recv.shape[1] // 2
    rows, length = inverse.shape
    lanes = 128
    total = jnp.zeros((length // lanes, lanes), F32)
    group = 8
    for first in range(0, devices, group):
        lefts, rights = ([], [])
        for d in range(first, first + group):
            value = recv[d : d + 1, :count]
            index = recv[d : d + 1, count:].astype(I32)
            hi, lo = lax.div(index, lanes), lax.rem(index, lanes)
            hit = iota((length // lanes, count), 0) == hi
            lefts.append(jnp.concatenate([jnp.where(hit, v.astype(F32), 0.0).astype(BF16) for v in split(value)], 0))
            rights.append(onehot(lo, lanes).astype(BF16))
        total = total + fold(dot_nt(jnp.concatenate(lefts, 1), jnp.concatenate(rights, 1)))
    acc = jnp.zeros((rows, lanes), F32)
    for r in range(length // lanes):
        acc = acc + inverse[:, r * lanes : (r + 1) * lanes] * total[r : r + 1]
    parts = jnp.concatenate(split(acc), 1)
    out = dot_nt(jnp.ones((8, parts.shape[1]), BF16), parts)
    send[...] = jnp.broadcast_to(out[0:1], send.shape)


def coef_kernel(last, tz, store, tz_prev, upper, inv, sides, ends):
    depth = tz.shape[0]
    is_last = lax.axis_index("layer") == last
    low = tz_prev[0]
    gs, invs, lows = ([], [], [])
    g = jnp.zeros_like(low)
    before = low
    for z in range(depth):
        up = tz[z]
        if z == depth - 1:
            up = jnp.where(is_last, 0.0, up)
        pivot = before + up + store[z]
        if z:
            pivot = pivot - before * g
        ipv = 1.0 / pivot
        g = up * ipv
        inv[z] = ipv
        upper[z] = g
        gs.append(g)
        invs.append(ipv)
        lows.append(before)
        before = up
    a = [low * invs[0]]
    for z in range(1, depth):
        a.append(lows[z] * a[-1] * invs[z])
    b = [None] * depth
    b[-1] = gs[-1]
    for z in range(depth - 2, -1, -1):
        a[z] = a[z] + gs[z] * a[z + 1]
        b[z] = gs[z] * b[z + 1]
    for z in range(depth):
        sides[0, z] = a[z]
        sides[1, z] = b[z]
    ends[0], ends[1], ends[2], ends[3] = (a[0], a[-1], b[0], b[-1])


def is_right(level):
    return (lax.axis_index("layer") >> level) % 2 == 1


def choose(level, mine, other):
    right = is_right(level)
    return (jnp.where(right, other, mine), jnp.where(right, mine, other))


def join_coef_kernel(level, own, sib, out):
    af, af_ = choose(level, own[0], sib[0])
    al, al_ = choose(level, own[1], sib[1])
    bf, bf_ = choose(level, own[2], sib[2])
    bl, bl_ = choose(level, own[3], sib[3])
    den = 1.0 / (1.0 - bl * af_)
    out[0] = af + bf * af_ * al * den
    out[1] = al_ * al * den
    out[2] = bf * bf_ * den
    out[3] = bl_ + al_ * bl * bf_ * den


def local_solve(rhs, upper, inv, tz):
    depth = len(rhs)
    y = [rhs[0] * inv[0]]
    for z in range(1, depth):
        y.append((rhs[z] + tz[z - 1] * y[-1]) * inv[z])
    for z in range(depth - 2, -1, -1):
        y[z] = y[z] + upper[z] * y[z + 1]
    return y


def adjust_kernel(sol, cell, front, prod, pres, upper, inv, tz, y_out, ends):
    depth, width, long = pres.shape
    where, index = (cell[...], front[...])
    rows = sol.shape[1]
    value = prod[...] * pick(sol[...], lax.div(index, rows), lax.rem(index, rows))
    change = spread(value, lax.div(where, long), lax.rem(where, long), depth * width, long)
    change = change.reshape(depth, width, long)
    y = local_solve([pres[z] - change[z] for z in range(depth)], upper, inv, tz)
    for z in range(depth):
        y_out[z] = y[z]
    ends[0] = y[0]
    ends[1] = y[-1]


def join_kernel(level, own, sib, ocoef, scoef, out):
    yf, yf_ = choose(level, own[0], sib[0])
    yl, yl_ = choose(level, own[1], sib[1])
    af, af_ = choose(level, ocoef[0], scoef[0])
    al, al_ = choose(level, ocoef[1], scoef[1])
    bf, bf_ = choose(level, ocoef[2], scoef[2])
    bl, bl_ = choose(level, ocoef[3], scoef[3])
    den = 1.0 / (1.0 - bl * af_)
    out[0] = yf + bf * (yf_ + af_ * yl) * den
    out[1] = yl_ + al_ * (yl + bl * yf_) * den


def pressure_kernel(levels, *refs):
    groups = [refs[4 * i : 4 * i + 4] for i in range(levels)]
    y, sides, p, outer, row_first, row_last = refs[4 * levels :]
    zero = jnp.zeros(y.shape[1:], F32)
    above, below = (zero, zero)
    for level in range(levels - 1, -1, -1):
        own, sib, ocoef, scoef = groups[level]
        if level == levels - 1:
            yl, yf_ = choose(level, own[1], sib[0])[0], choose(level, own[0], sib[0])[1]
            bl, af_ = choose(level, ocoef[3], scoef[0])[0], choose(level, ocoef[0], scoef[0])[1]
            den = 1.0 / (1.0 - bl * af_)
            ml = (yl + bl * yf_) * den
            mr = (yf_ + af_ * yl) * den
        else:
            yl, _ = choose(level, own[1], sib[1])
            _, yf_ = choose(level, own[0], sib[0])
            _, af_ = choose(level, ocoef[0], scoef[0])
            al, _ = choose(level, ocoef[1], scoef[1])
            _, bf_ = choose(level, ocoef[2], scoef[2])
            bl, _ = choose(level, ocoef[3], scoef[3])
            den = 1.0 / (1.0 - bl * af_)
            one = yl + al * above
            two = yf_ + bf_ * below
            ml = (one + bl * two) * den
            mr = (two + af_ * one) * den
        right = is_right(level)
        above, below = (jnp.where(right, ml, above), jnp.where(right, below, mr))
    outer[0] = above
    outer[1] = below
    width = y.shape[1]
    for z in range(y.shape[0]):
        value = y[z] + sides[0, z] * above + sides[1, z] * below
        p[z] = value
        row_first[z] = value[0:1]
        row_last[z] = value[width - 1 : width]


def near(centre, above, below, row_before, row_after, tx, tx_row, ty, tz, tz_above):
    width, long = centre.shape
    row, col = (iota(centre.shape, 0), iota(centre.shape, 1))
    total = tz * below + tz_above * above
    after = jnp.where(row == width - 1, row_after, pltpu.roll(centre, width - 1, 0))
    total = total + tx * after
    total = total + jnp.where(row == 0, tx_row * row_before, pltpu.roll(tx * centre, 1, 0))
    total = total + ty * jnp.where(col == long - 1, 0.0, pltpu.roll(centre, long - 1, 1))
    total = total + jnp.where(col == 0, 0.0, pltpu.roll(ty * centre, 1, 1))
    return total


def search_kernel(p, outer, before, after, rhs, dcol, binv, tx, tx_row, ty, tz, tz_prev, s, s_first, s_last, s_top, s_bottom):
    depth, width, _ = p.shape
    for z in range(depth):
        above = outer[0] if z == 0 else p[z - 1]
        below = outer[1] if z == depth - 1 else p[z + 1]
        tza = tz_prev[0] if z == 0 else tz[z - 1]
        centre = p[z]
        coupled = near(centre, above, below, before[z], after[z], tx[z], tx_row[z], ty[z], tz[z], tza)
        remain = [rhs[c, z] - dcol[c, z] * centre for c in range(3)]
        remain[0] = remain[0] + coupled
        for c in range(3):
            value = binv[c, 0, z] * remain[0] + binv[c, 1, z] * remain[1] + binv[c, 2, z] * remain[2]
            if c == 0:
                value = centre + value
            s[c, z] = value
            s_first[c, z] = value[0:1]
            s_last[c, z] = value[width - 1 : width]
            if z == 0:
                s_top[c] = value
            if z == depth - 1:
                s_bottom[c] = value


def image_kernel(s, before, after, above_s, below_s, rhs, diag, tx, tx_row, ty, tz, tz_prev, image, send):
    depth = s.shape[1]
    along = power = start = 0.0
    for z in range(depth):
        tza = tz_prev[0] if z == 0 else tz[z - 1]
        for c in range(3):
            above = above_s[c] if z == 0 else s[c, z - 1]
            below = below_s[c] if z == depth - 1 else s[c, z + 1]
            coupled = near(s[c, z], above, below, before[c, z], after[c, z], tx[z], tx_row[z], ty[z], tz[z], tza)
            value = diag[c, 0, z] * s[0, z] + diag[c, 1, z] * s[1, z] + diag[c, 2, z] * s[2, z] - coupled
            image[c, z] = value
            right = rhs[c, z]
            along = along + value * right
            power = power + value * value
            start = start + right * right
    along, power, start = (jnp.sum(along), jnp.sum(power), jnp.sum(start))
    omega = along / jnp.where(power > 0.0, power, 1.0)
    square = cross = 0.0
    for z in range(depth):
        for c in range(3):
            value = image[c, z]
            left = rhs[c, z] - omega * value
            square = square + left * left
            cross = cross + left * value
    lane = iota((1, send.shape[1]), 1)
    out = jnp.zeros((1, send.shape[1]), F32)
    for i, value in enumerate((along, power, start, jnp.sum(square), jnp.sum(cross), omega)):
        out = jnp.where(lane == i, value, out)
    send[...] = jnp.broadcast_to(out, send.shape)


def finish_kernel(recv, s, image, rhs, update, lin_res, ratio):
    sums = recv[...]
    whole = jnp.sum(sums, axis=0, keepdims=True)
    omega = whole[:, 0:1] / whole[:, 1:2]
    shift = sums[:, 5:6] - omega
    square = sums[:, 3:4] + 2.0 * shift * sums[:, 4:5] + shift * shift * sums[:, 1:2]
    ratio[...] = jnp.sqrt(jnp.sum(square, axis=0, keepdims=True) / whole[:, 2:3])
    for c in range(3):
        for z in range(s.shape[1]):
            update[c, z] = omega * s[c, z]
            lin_res[c, z] = rhs[c, z] - omega * image[c, z]


def up(x, axis):
    return lax.ppermute(x, axis, [(i, i + 1) for i in range(lax.axis_size(axis) - 1)])


def down(x, axis):
    return lax.ppermute(x, axis, [(i + 1, i) for i in range(lax.axis_size(axis) - 1)])


def flip(x, level):
    return lax.ppermute(x, "layer", [(i, i ^ (1 << level)) for i in range(lax.axis_size("layer"))])


def everywhere(x):
    return lax.all_to_all(x, BOTH, split_axis=0, concat_axis=0, tiled=True)


def shards(rhs, weights, block_diag, block_inv, tx, ty, tz, store, cell, front, prod, inverse):
    devices = lax.axis_size("tile") * lax.axis_size("layer")
    layers = lax.axis_size("layer")
    levels = layers.bit_length() - 1
    depth, width, long = tx.shape
    plane = (width, long)
    count = cell.shape[0]
    rows = inverse.shape[0]
    cell, front, prod = (cell.reshape(1, -1), front.reshape(1, -1), prod.reshape(1, -1))

    tz_prev = up(tz[-1:], "layer")
    tx_row = up(tx[:, -1:], "tile")
    pres, send = call(
        pres_kernel, (vmem(tx.shape), vmem((devices, 2 * count))), (rhs, weights, cell, front, prod)
    )
    terms = everywhere(send)

    field = vmem(tx.shape)
    upper, inv, sides, ends = call(
        functools.partial(coef_kernel, layers - 1),
        (field, field, vmem((2,) + tx.shape), vmem((4,) + plane)),
        (tz, store, tz_prev),
    )
    coefs = []
    right = lambda level: (lax.axis_index("layer") >> level) % 2 == 1
    for level in range(levels):
        if level == levels - 1:
            face = jnp.where(right(level), ends[0], ends[3])[None]
            coefs.append((ends, flip(face, level)))
        else:
            sib = flip(ends, level)
            coefs.append((ends, sib))
            ends = call(functools.partial(join_coef_kernel, level), vmem((4,) + plane), (ends, sib))

    rows_sol = call(front_kernel, vmem((devices, rows)), (terms, inverse))
    sol = everywhere(rows_sol)

    y, yends = call(
        adjust_kernel, (field, vmem((2,) + plane)), (sol, cell, front, prod, pres, upper, inv, tz)
    )
    args = []
    for level in range(levels):
        own, scoef = coefs[level]
        if level == levels - 1:
            face = jnp.where(right(level), yends[0], yends[1])[None]
            args += [yends, flip(face, level), own, scoef]
        else:
            sib = flip(yends, level)
            args += [yends, sib, own, scoef]
            yends = call(functools.partial(join_kernel, level), vmem((2,) + plane), (yends, sib, own, scoef))
    row3 = vmem((depth, 1, long))
    p, outer, p_first, p_last = call(
        functools.partial(pressure_kernel, levels), (field, vmem((2,) + plane), row3, row3), (*args, y, sides)
    )
    before, after = (up(p_last, "tile"), down(p_first, "tile"))
    row9 = vmem((3, depth, 1, long))
    plane3 = vmem((3,) + plane)
    s, s_first, s_last, s_top, s_bottom = call(
        search_kernel,
        (vmem(rhs.shape), row9, row9, plane3, plane3),
        (p, outer, before, after, rhs, block_diag[:, 0], block_inv, tx, tx_row, ty, tz, tz_prev),
    )
    above, below = (up(s_bottom, "layer"), down(s_top, "layer"))
    before, after = (up(s_last, "tile"), down(s_first, "tile"))
    image, send = call(
        image_kernel,
        (vmem(rhs.shape), vmem((devices, 128))),
        (s, before, after, above, below, rhs, block_diag, tx, tx_row, ty, tz, tz_prev),
    )
    sums = everywhere(send)
    update, lin_res, ratio = call(
        finish_kernel, (hbm(rhs.shape), hbm(rhs.shape), hbm((1, 1))), (sums, s, image, rhs)
    )
    return (update, lin_res, ratio.reshape(()))


def solution(mesh):
    return jax.shard_map(
        shards,
        mesh=mesh,
        in_specs=(
            P(None, "layer", "tile", None),
            P(None, "layer", "tile", None),
            P(None, None, "layer", "tile", None),
            P(None, None, "layer", "tile", None),
            P("layer", "tile", None),
            P("layer", "tile", None),
            P("layer", "tile", None),
            P("layer", "tile", None),
            P(("tile", "layer")),
            P(("tile", "layer")),
            P(("tile", "layer")),
            P(("tile", "layer"), None),
        ),
        out_specs=(P(None, "layer", "tile", None), P(None, "layer", "tile", None), P()),
        check_vma=False,
    )
```

```python
import functools
import jax
import jax.numpy as jnp
from jax import lax
from jax.experimental import pallas as pl
from jax.experimental.pallas import tpu as pltpu
from jax.sharding import PartitionSpec as P

F32 = jnp.float32
BF16 = jnp.bfloat16
I32 = jnp.int32
BOTH = ("tile", "layer")
VM = pl.BlockSpec(memory_space=pltpu.VMEM)
LIMIT = 16 << 20


def hbm(shape):
    return jax.ShapeDtypeStruct(shape, F32)


def vmem(shape, dtype=F32):
    return pltpu.VMEM(shape, dtype)


def staged(kernel, where, outs, *refs):
    count, sems = len(where), refs[-1]
    held = list(refs[count + outs : -1])
    operands, copies = ([], [])
    for i, far in enumerate(where):
        if far:
            copies.append(pltpu.make_async_copy(refs[i], held[len(copies)], sems.at[len(copies)]))
            operands.append(held[len(copies) - 1])
        else:
            operands.append(refs[i])
    for copy in copies:
        copy.start()
    for copy in copies:
        copy.wait()
    kernel(*operands, *refs[count : count + outs])


def call(kernel, outs, args, far=(), limit=LIMIT):
    where = [i in far for i in range(len(args))]
    spaces = [pltpu.HBM if w else pltpu.VMEM for w in where]
    count = len(jax.tree.leaves(outs, is_leaf=lambda x: hasattr(x, "shape")))
    return pl.pallas_call(
        functools.partial(staged, kernel, where, count),
        out_shape=outs,
        in_specs=[pl.BlockSpec(memory_space=s) for s in spaces],
        out_specs=VM if not isinstance(outs, tuple) else (VM,) * count,
        scratch_shapes=[vmem(a.shape, a.dtype) for a, w in zip(args, where) if w]
        + [pltpu.SemaphoreType.DMA((max(1, sum(where)),))],
        compiler_params=pltpu.CompilerParams(vmem_limit_bytes=limit),
    )(*[pltpu.with_memory_space_constraint(a, s) for a, s in zip(args, spaces)])


def iota(shape, dim):
    return lax.broadcasted_iota(I32, shape, dim)


def split(x):
    one = x.astype(BF16)
    rest = x - one.astype(F32)
    two = rest.astype(BF16)
    three = (rest - two.astype(F32)).astype(BF16)
    return [one, two, three]


def fold(x):
    n = x.shape[0] // 3
    return x[:n] + (x[n : 2 * n] + x[2 * n :])


def onehot(index, size):
    return jnp.where(iota((size, index.shape[1]), 0) == index, 1.0, 0.0)


def dot(a, b):
    return lax.dot_general(a, b, (((1,), (0,)), ((), ())), preferred_element_type=F32)


def dot_nt(a, b):
    return lax.dot_general(a, b, (((1,), (1,)), ((), ())), preferred_element_type=F32)


def pick(table, hi, lo):
    rows, cols = table.shape
    parts = jnp.concatenate(split(table), 0)
    got = fold(dot(parts, onehot(lo, cols).astype(BF16)))
    return jnp.sum(got * onehot(hi, rows), axis=0, keepdims=True)


def spread(value, hi, lo, rows, cols):
    parts = [jnp.where(iota((rows, hi.shape[1]), 0) == hi, v.astype(F32), 0.0).astype(BF16) for v in split(value)]
    return fold(dot_nt(jnp.concatenate(parts, 0), onehot(lo, cols).astype(BF16)))


def load_kernel(count, *refs):
    sems = refs[-1]
    copies = [pltpu.make_async_copy(refs[i], refs[count + i], sems.at[i]) for i in range(count)]
    for copy in copies:
        copy.start()
    for copy in copies:
        copy.wait()


def load(*args):
    count = len(args)
    args = [pltpu.with_memory_space_constraint(a, pltpu.HBM) for a in args]
    return pl.pallas_call(
        functools.partial(load_kernel, count),
        out_shape=tuple(vmem(a.shape, a.dtype) for a in args),
        in_specs=[pl.BlockSpec(memory_space=pltpu.HBM)] * count,
        out_specs=tuple(VM for _ in args),
        scratch_shapes=[pltpu.SemaphoreType.DMA((count,))],
        compiler_params=pltpu.CompilerParams(vmem_limit_bytes=1 << 20),
    )(*args)


def pres_kernel(rhs, wts, cell, front, prod, pres, send):
    depth, width, long = pres.shape
    for z in range(depth):
        pres[z] = wts[0, z] * rhs[0, z] + wts[1, z] * rhs[1, z] + wts[2, z] * rhs[2, z]
    where = cell[...]
    table = pres[...].reshape(depth * width, long)
    value = prod[...] * pick(table, lax.div(where, long), lax.rem(where, long))
    both = jnp.concatenate([value, front[...].astype(F32)], 1)
    send[...] = jnp.broadcast_to(both[:, None], send.shape)


def front_kernel(recv, inverse, send, held, sems):
    devices = recv.shape[0]
    count = recv.shape[2] // 2
    rows, length = inverse.shape
    lanes = 128
    chunks = sems.shape[0]
    wide = length // chunks
    copies = [
        pltpu.make_async_copy(inverse.at[:, pl.ds(i * wide, wide)], held.at[:, pl.ds(i * wide, wide)], sems.at[i])
        for i in range(chunks)
    ]
    for copy in copies:
        copy.start()
    total = jnp.zeros((length // lanes, lanes), F32)
    group = 8
    for first in range(0, devices, group):
        lefts, rights = ([], [])
        for d in range(first, first + group):
            value = recv[d, :, :count]
            index = recv[d, :, count:].astype(I32)
            hi, lo = lax.div(index, lanes), lax.rem(index, lanes)
            hit = iota((length // lanes, count), 0) == hi
            lefts.append(jnp.concatenate([jnp.where(hit, v.astype(F32), 0.0).astype(BF16) for v in split(value)], 0))
            rights.append(onehot(lo, lanes).astype(BF16))
        total = total + fold(dot_nt(jnp.concatenate(lefts, 1), jnp.concatenate(rights, 1)))
    acc = jnp.zeros((rows, lanes), F32)
    for i in range(chunks):
        copies[i].wait()
        for r in range(i * wide // lanes, (i + 1) * wide // lanes):
            acc = acc + held[:, r * lanes : (r + 1) * lanes] * total[r : r + 1]
    parts = jnp.concatenate(split(acc), 1)
    out = dot_nt(jnp.ones((8, parts.shape[1]), BF16), parts)
    send[...] = jnp.broadcast_to(out[0:1][:, None], send.shape)


def coef_kernel(last, tz, store, tz_prev, upper, inv, sides, ends, face):
    depth = tz.shape[0]
    is_last = lax.axis_index("layer") == last
    low = tz_prev[0]
    gs, invs, lows = ([], [], [])
    g = jnp.zeros_like(low)
    before = low
    for z in range(depth):
        up = tz[z]
        if z == depth - 1:
            up = jnp.where(is_last, 0.0, up)
        pivot = before + up + store[z]
        if z:
            pivot = pivot - before * g
        ipv = 1.0 / pivot
        g = up * ipv
        inv[z] = ipv
        upper[z] = g
        gs.append(g)
        invs.append(ipv)
        lows.append(before)
        before = up
    a = [low * invs[0]]
    for z in range(1, depth):
        a.append(lows[z] * a[-1] * invs[z])
    b = [None] * depth
    b[-1] = gs[-1]
    for z in range(depth - 2, -1, -1):
        a[z] = a[z] + gs[z] * a[z + 1]
        b[z] = gs[z] * b[z + 1]
    for z in range(depth):
        sides[0, z] = a[z]
        sides[1, z] = b[z]
    ends[0], ends[1], ends[2], ends[3] = (a[0], a[-1], b[0], b[-1])
    face[0] = jnp.where(is_right(0), a[0], b[-1])


def is_right(level):
    return (lax.axis_index("layer") >> level) % 2 == 1


def choose(level, mine, other):
    right = is_right(level)
    return (jnp.where(right, other, mine), jnp.where(right, mine, other))


def join_coef_kernel(level, own, sib, out, face):
    af, af_ = choose(level, own[0], sib[0])
    al, al_ = choose(level, own[1], sib[1])
    bf, bf_ = choose(level, own[2], sib[2])
    bl, bl_ = choose(level, own[3], sib[3])
    den = 1.0 / (1.0 - bl * af_)
    first = af + bf * af_ * al * den
    last = bl_ + al_ * bl * bf_ * den
    out[0] = first
    out[1] = al_ * al * den
    out[2] = bf * bf_ * den
    out[3] = last
    face[0] = jnp.where(is_right(level + 1), first, last)


def local_solve(rhs, upper, inv, tz):
    depth = len(rhs)
    y = [rhs[0] * inv[0]]
    for z in range(1, depth):
        y.append((rhs[z] + tz[z - 1] * y[-1]) * inv[z])
    for z in range(depth - 2, -1, -1):
        y[z] = y[z] + upper[z] * y[z + 1]
    return y


def adjust_kernel(sol, cell, front, prod, pres, upper, inv, tz, y_out, ends, face):
    depth, width, long = pres.shape
    where, index = (cell[...], front[...])
    rows = sol.shape[2]
    value = prod[...] * pick(sol[...].reshape(sol.shape[0], rows), lax.div(index, rows), lax.rem(index, rows))
    change = spread(value, lax.div(where, long), lax.rem(where, long), depth * width, long)
    change = change.reshape(depth, width, long)
    y = local_solve([pres[z] - change[z] for z in range(depth)], upper, inv, tz)
    for z in range(depth):
        y_out[z] = y[z]
    ends[0] = y[0]
    ends[1] = y[-1]
    face[0] = jnp.where(is_right(0), y[0], y[-1])


def join_kernel(level, own, sib, ocoef, scoef, out, face):
    yf, yf_ = choose(level, own[0], sib[0])
    yl, yl_ = choose(level, own[1], sib[1])
    af, af_ = choose(level, ocoef[0], scoef[0])
    al, al_ = choose(level, ocoef[1], scoef[1])
    bf, bf_ = choose(level, ocoef[2], scoef[2])
    bl, bl_ = choose(level, ocoef[3], scoef[3])
    den = 1.0 / (1.0 - bl * af_)
    first = yf + bf * (yf_ + af_ * yl) * den
    last = yl_ + al_ * (yl + bl * yf_) * den
    out[0] = first
    out[1] = last
    face[0] = jnp.where(is_right(level + 1), first, last)


def pressure_kernel(levels, *refs):
    groups = [refs[4 * i : 4 * i + 4] for i in range(levels)]
    y, sides, p, outer, row_first, row_last = refs[4 * levels :]
    zero = jnp.zeros(y.shape[1:], F32)
    above, below = (zero, zero)
    for level in range(levels - 1, -1, -1):
        own, sib, ocoef, scoef = groups[level]
        if level == levels - 1:
            yl, yf_ = choose(level, own[1], sib[0])[0], choose(level, own[0], sib[0])[1]
            bl, af_ = choose(level, ocoef[3], scoef[0])[0], choose(level, ocoef[0], scoef[0])[1]
            den = 1.0 / (1.0 - bl * af_)
            ml = (yl + bl * yf_) * den
            mr = (yf_ + af_ * yl) * den
        else:
            yl, _ = choose(level, own[1], sib[1])
            _, yf_ = choose(level, own[0], sib[0])
            _, af_ = choose(level, ocoef[0], scoef[0])
            al, _ = choose(level, ocoef[1], scoef[1])
            _, bf_ = choose(level, ocoef[2], scoef[2])
            bl, _ = choose(level, ocoef[3], scoef[3])
            den = 1.0 / (1.0 - bl * af_)
            one = yl + al * above
            two = yf_ + bf_ * below
            ml = (one + bl * two) * den
            mr = (two + af_ * one) * den
        right = is_right(level)
        above, below = (jnp.where(right, ml, above), jnp.where(right, below, mr))
    outer[0] = above
    outer[1] = below
    width = y.shape[1]
    for z in range(y.shape[0]):
        value = y[z] + sides[0, z] * above + sides[1, z] * below
        p[z] = value
        row_first[z] = value[0:1]
        row_last[z] = value[width - 1 : width]


def near(centre, above, below, row_before, row_after, tx, tx_row, ty, tz, tz_above):
    width, long = centre.shape
    row, col = (iota(centre.shape, 0), iota(centre.shape, 1))
    total = tz * below + tz_above * above
    after = jnp.where(row == width - 1, row_after, pltpu.roll(centre, width - 1, 0))
    total = total + tx * after
    total = total + jnp.where(row == 0, tx_row * row_before, pltpu.roll(tx * centre, 1, 0))
    total = total + ty * jnp.where(col == long - 1, 0.0, pltpu.roll(centre, long - 1, 1))
    total = total + jnp.where(col == 0, 0.0, pltpu.roll(ty * centre, 1, 1))
    return total


def search_kernel(p, outer, before, after, rhs, diag, binv, tx, tx_row, ty, tz, tz_prev, s, s_first, s_last, s_top, s_bottom):
    depth, width, _ = p.shape
    for z in range(depth):
        above = outer[0] if z == 0 else p[z - 1]
        below = outer[1] if z == depth - 1 else p[z + 1]
        tza = tz_prev[0] if z == 0 else tz[z - 1]
        centre = p[z]
        coupled = near(centre, above, below, before[z], after[z], tx[z], tx_row[z], ty[z], tz[z], tza)
        remain = [rhs[c, z] - diag[c, 0, z] * centre for c in range(3)]
        remain[0] = remain[0] + coupled
        for c in range(3):
            value = binv[c, 0, z] * remain[0] + binv[c, 1, z] * remain[1] + binv[c, 2, z] * remain[2]
            if c == 0:
                value = centre + value
            s[c, z] = value
            s_first[c, z] = value[0:1]
            s_last[c, z] = value[width - 1 : width]
            if z == 0:
                s_top[c] = value
            if z == depth - 1:
                s_bottom[c] = value


def inner_kernel(s, before, after, diag, tx, tx_row, ty, tz, image):
    depth = s.shape[1]
    zero = jnp.zeros(s.shape[2:], F32)
    for z in range(depth):
        tza = zero if z == 0 else tz[z - 1]
        for c in range(3):
            above = zero if z == 0 else s[c, z - 1]
            below = zero if z == depth - 1 else s[c, z + 1]
            coupled = near(s[c, z], above, below, before[c, z], after[c, z], tx[z], tx_row[z], ty[z], tz[z], tza)
            image[c, z] = diag[c, 0, z] * s[0, z] + diag[c, 1, z] * s[1, z] + diag[c, 2, z] * s[2, z] - coupled


def image_kernel(part, above_s, below_s, rhs, tz, tz_prev, image, send):
    depth = part.shape[1]
    along = power = start = 0.0
    for z in range(depth):
        for c in range(3):
            value = part[c, z]
            if z == 0:
                value = value - tz_prev[0] * above_s[c]
            if z == depth - 1:
                value = value - tz[z] * below_s[c]
            image[c, z] = value
            right = rhs[c, z]
            along = along + value * right
            power = power + value * value
            start = start + right * right
    along, power, start = (jnp.sum(along), jnp.sum(power), jnp.sum(start))
    omega = along / jnp.where(power > 0.0, power, 1.0)
    square = cross = 0.0
    for z in range(depth):
        for c in range(3):
            value = image[c, z]
            left = rhs[c, z] - omega * value
            square = square + left * left
            cross = cross + left * value
    lane = iota((1, send.shape[2]), 1)
    out = jnp.zeros((1, send.shape[2]), F32)
    for i, value in enumerate((along, power, start, jnp.sum(square), jnp.sum(cross), omega)):
        out = jnp.where(lane == i, value, out)
    send[...] = jnp.broadcast_to(out[:, None], send.shape)


def finish_kernel(recv, s, image, rhs, update, lin_res, ratio):
    sums = recv[...].reshape(recv.shape[0], recv.shape[2])
    whole = jnp.sum(sums, axis=0, keepdims=True)
    omega = whole[:, 0:1] / whole[:, 1:2]
    shift = sums[:, 5:6] - omega
    square = sums[:, 3:4] + 2.0 * shift * sums[:, 4:5] + shift * shift * sums[:, 1:2]
    ratio[...] = jnp.sqrt(jnp.sum(square, axis=0, keepdims=True) / whole[:, 2:3])
    for c in range(3):
        for z in range(s.shape[1]):
            update[c, z] = omega * s[c, z]
            lin_res[c, z] = rhs[c, z] - omega * image[c, z]


def up(x, axis):
    return lax.ppermute(x, axis, [(i, i + 1) for i in range(lax.axis_size(axis) - 1)])


def down(x, axis):
    return lax.ppermute(x, axis, [(i + 1, i) for i in range(lax.axis_size(axis) - 1)])


def flip(x, level):
    return lax.ppermute(x, "layer", [(i, i ^ (1 << level)) for i in range(lax.axis_size("layer"))])


def everywhere(x):
    return lax.all_to_all(x, BOTH, split_axis=0, concat_axis=0, tiled=True)


def shards(rhs, weights, block_diag, block_inv, tx, ty, tz, store, cell, front, prod, inverse):
    devices = lax.axis_size("tile") * lax.axis_size("layer")
    layers = lax.axis_size("layer")
    levels = layers.bit_length() - 1
    depth, width, long = tx.shape
    plane = (width, long)
    count = cell.shape[0]
    rows = inverse.shape[0]
    cell, front, prod = (cell.reshape(1, -1), front.reshape(1, -1), prod.reshape(1, -1))

    pres, send = call(
        pres_kernel,
        (vmem(tx.shape), vmem((devices, 1, 2 * count))),
        (rhs, weights, cell, front, prod),
        far=range(5),
    )
    send, tz, store, tx = lax.optimization_barrier((send, tz, store, tx))
    tz_prev = up(tz[-1:], "layer")
    tx_row = up(tx[:, -1:], "tile")
    terms = everywhere(send)
    terms, store, tz_prev = lax.optimization_barrier((terms, store, tz_prev))

    field = vmem(tx.shape)
    one, two, four = (vmem((k,) + plane) for k in (1, 2, 4))
    upper, inv, sides, ends, face = call(
        functools.partial(coef_kernel, layers - 1),
        (field, field, vmem((2,) + tx.shape), four, one),
        (tz, store, tz_prev),
        far=(0, 1),
    )
    coefs = []
    for level in range(levels):
        if level == levels - 1:
            coefs.append((ends, flip(face, level)))
        else:
            sib = flip(ends, level)
            coefs.append((ends, sib))
            ends, face = call(functools.partial(join_coef_kernel, level), (four, one), (ends, sib))

    chunks = 8
    solved = pl.pallas_call(
        front_kernel,
        out_shape=vmem((devices, 1, rows)),
        in_specs=[VM, pl.BlockSpec(memory_space=pltpu.HBM)],
        out_specs=VM,
        scratch_shapes=[vmem(inverse.shape), pltpu.SemaphoreType.DMA((chunks,))],
        compiler_params=pltpu.CompilerParams(vmem_limit_bytes=LIMIT),
    )(terms, pltpu.with_memory_space_constraint(inverse, pltpu.HBM))
    solved, coefs = lax.optimization_barrier((solved, coefs))
    sol = everywhere(solved)

    y, yends, yface = call(
        adjust_kernel,
        (field, two, one),
        (sol, cell, front, prod, pres, upper, inv, tz),
        far=(1, 2, 3, 7),
    )
    tz_prev_v = tz_prev
    diag, binv, rhs_v, tx_v, ty_v, tz_v = load(block_diag, block_inv, rhs, tx, ty, tz)
    args = []
    for level in range(levels):
        own, scoef = coefs[level]
        if level == levels - 1:
            args += [yends, flip(yface, level), own, scoef]
        else:
            sib = flip(yends, level)
            args += [yends, sib, own, scoef]
            yends, yface = call(
                functools.partial(join_kernel, level), (two, one), (yends, sib, own, scoef)
            )
    row3 = vmem((depth, 1, long))
    p, outer, p_first, p_last = call(
        functools.partial(pressure_kernel, levels),
        (field, two, row3, row3),
        (*args, y, sides),
    )
    before, after = (up(p_last, "tile"), down(p_first, "tile"))
    row9 = vmem((3, depth, 1, long))
    plane3 = vmem((3,) + plane)
    s, s_first, s_last, s_top, s_bottom = call(
        search_kernel,
        (vmem(rhs.shape), row9, row9, plane3, plane3),
        (p, outer, before, after, rhs_v, diag, binv, tx_v, tx_row, ty_v, tz_v, tz_prev_v),
    )
    above, below = (up(s_bottom, "layer"), down(s_top, "layer"))
    before, after = (up(s_last, "tile"), down(s_first, "tile"))
    part = call(inner_kernel, vmem(rhs.shape), (s, before, after, diag, tx_v, tx_row, ty_v, tz_v))
    image, send = call(
        image_kernel,
        (vmem(rhs.shape), vmem((devices, 1, 128))),
        (part, above, below, rhs_v, tz_v, tz_prev_v),
    )
    sums = everywhere(send)
    update, lin_res, ratio = call(
        finish_kernel, (hbm(rhs.shape), hbm(rhs.shape), hbm((1, 1))), (sums, s, image, rhs_v)
    )
    return (update, lin_res, ratio.reshape(()))


def solution(mesh):
    return jax.shard_map(
        shards,
        mesh=mesh,
        in_specs=(
            P(None, "layer", "tile", None),
            P(None, "layer", "tile", None),
            P(None, None, "layer", "tile", None),
            P(None, None, "layer", "tile", None),
            P("layer", "tile", None),
            P("layer", "tile", None),
            P("layer", "tile", None),
            P("layer", "tile", None),
            P(("tile", "layer")),
            P(("tile", "layer")),
            P(("tile", "layer")),
            P(("tile", "layer"), None),
        ),
        out_specs=(P(None, "layer", "tile", None), P(None, "layer", "tile", None), P()),
        check_vma=False,
    )
```

```python
import functools
import jax
import jax.numpy as jnp
from jax import lax
from jax.experimental import pallas as pl
from jax.experimental.pallas import tpu as pltpu
from jax.sharding import PartitionSpec as P

F32 = jnp.float32
BF16 = jnp.bfloat16
I32 = jnp.int32
BOTH = ("tile", "layer")
VM = pl.BlockSpec(memory_space=pltpu.VMEM)
LIMIT = 16 << 20


def hbm(shape):
    return jax.ShapeDtypeStruct(shape, F32)


def vmem(shape, dtype=F32):
    return pltpu.VMEM(shape, dtype)


def staged(kernel, where, outs, kept, *refs):
    count, sems = (len(where), refs[-1])
    held = list(refs[count + outs + len(kept) : -1])
    target = dict(zip(kept, refs[count + outs : count + outs + len(kept)]))
    operands, copies = ([], [])
    for i, far in enumerate(where):
        if far:
            to = target[i] if i in target else held.pop(0)
            copies.append(pltpu.make_async_copy(refs[i], to, sems.at[len(copies)]))
            operands.append(to)
        else:
            operands.append(refs[i])
    for copy in copies:
        copy.start()
    for copy in copies:
        copy.wait()
    kernel(*operands, *refs[count : count + outs])


def call(kernel, outs, args, far=(), keep=(), limit=LIMIT):
    where = [i in far for i in range(len(args))]
    spaces = [pltpu.HBM if w else pltpu.VMEM for w in where]
    every = (*outs, *(vmem(args[i].shape, args[i].dtype) for i in keep))
    return pl.pallas_call(
        functools.partial(staged, kernel, where, len(outs), tuple(keep)),
        out_shape=every,
        in_specs=[pl.BlockSpec(memory_space=s) for s in spaces],
        out_specs=(VM,) * len(every),
        scratch_shapes=[vmem(a.shape, a.dtype) for i, a in enumerate(args) if where[i] and i not in keep]
        + [pltpu.SemaphoreType.DMA((max(1, sum(where)),))],
        compiler_params=pltpu.CompilerParams(vmem_limit_bytes=limit),
    )(*[pltpu.with_memory_space_constraint(a, s) for a, s in zip(args, spaces)])


def iota(shape, dim):
    return lax.broadcasted_iota(I32, shape, dim)


def split(x):
    one = x.astype(BF16)
    rest = x - one.astype(F32)
    two = rest.astype(BF16)
    three = (rest - two.astype(F32)).astype(BF16)
    return [one, two, three]


def fold(x):
    n = x.shape[0] // 3
    return x[:n] + (x[n : 2 * n] + x[2 * n :])


def onehot(index, size):
    return jnp.where(iota((size, index.shape[1]), 0) == index, 1.0, 0.0)


def dot(a, b):
    return lax.dot_general(a, b, (((1,), (0,)), ((), ())), preferred_element_type=F32)


def dot_nt(a, b):
    return lax.dot_general(a, b, (((1,), (1,)), ((), ())), preferred_element_type=F32)


def pick(table, hi, lo):
    rows, cols = table.shape
    parts = jnp.concatenate(split(table), 0)
    got = fold(dot(parts, onehot(lo, cols).astype(BF16)))
    return jnp.sum(got * onehot(hi, rows), axis=0, keepdims=True)


def spread(value, hi, lo, rows, cols):
    parts = [jnp.where(iota((rows, hi.shape[1]), 0) == hi, v.astype(F32), 0.0).astype(BF16) for v in split(value)]
    return fold(dot_nt(jnp.concatenate(parts, 0), onehot(lo, cols).astype(BF16)))


def pres_kernel(rhs, wts, cell, front, prod, tz, pres, send, tz_last):
    depth, width, long = pres.shape
    for z in range(depth):
        pres[z] = wts[0, z] * rhs[0, z] + wts[1, z] * rhs[1, z] + wts[2, z] * rhs[2, z]
    where = cell[...]
    table = pres[...].reshape(depth * width, long)
    value = prod[...] * pick(table, lax.div(where, long), lax.rem(where, long))
    both = jnp.concatenate([value, front[...].astype(F32), where.astype(F32)], 1)
    send[...] = jnp.broadcast_to(both[:, None], send.shape)
    tz_last[0] = tz[depth - 1]


def edge_kernel(rhs, diag, binv, tz, store, tx, ty, pres, tz_prev, low, high):
    depth, width, long = pres.shape
    planes = [ref[z] for ref in (tz, store, pres, tx, ty) for z in range(depth)] + [tz_prev[0]]
    single = 2 * len(planes)
    low[...] = jnp.zeros(low.shape, F32)
    high[...] = jnp.zeros(high.shape, F32)
    for i, plane in enumerate(planes):
        low[2 * i : 2 * i + 2] = plane[0:2]
        high[2 * i : 2 * i + 2] = plane[width - 2 : width]
    for out, rows, at in ((low, slice(0, 8), 0), (high, slice(width - 8, width), 7)):
        for z in range(depth):
            right = [rhs[d, z, rows] for d in range(3)]
            column = [diag[d, 0, z, rows] for d in range(3)]
            for c in range(3):
                m = [binv[c, d, z, rows] for d in range(3)]
                first = m[0] * right[0] + m[1] * right[1] + m[2] * right[2]
                slope = (1.0 if c == 0 else 0.0) - (m[0] * column[0] + m[1] * column[1] + m[2] * column[2])
                for k, value in enumerate((first, slope, m[0])):
                    i = single + (k * 3 + c) * depth + z
                    out[i : i + 1] = value[at : at + 1]


def is_right(level):
    return (lax.axis_index("layer") >> level) % 2 == 1


def choose(level, mine, other):
    right = is_right(level)
    return (jnp.where(right, other, mine), jnp.where(right, mine, other))


def local_solve(rhs, upper, inv, tz):
    depth = len(rhs)
    y = [rhs[0] * inv[0]]
    for z in range(1, depth):
        y.append((rhs[z] + tz[z - 1] * y[-1]) * inv[z])
    for z in range(depth - 2, -1, -1):
        y[z] = y[z] + upper[z] * y[z + 1]
    return y


def coef_kernel(last, tz, store, tx, ty, pres, tz_prev, after, before, fields, halo, upper, inv, answers, sides, ends):
    depth, width, long = pres.shape
    pieces = [(ref, z) for ref in (tz, store, pres, tx, ty) for z in range(depth)] + [(tz_prev, 0)]
    for i, (ref, z) in enumerate(pieces):
        fields[i, :width] = ref[z]
        fields[i, width:] = jnp.zeros((8, long), F32)
        fields[i, width : width + 2] = after[2 * i : 2 * i + 2]
        fields[i, width + 6 :] = before[2 * i : 2 * i + 2]
    single = 2 * len(pieces)
    halo[...] = jnp.zeros(halo.shape, F32)
    for i in range(9 * depth):
        halo[i, 0:1] = after[single + i : single + i + 1]
        halo[i, 7:8] = before[single + i : single + i + 1]
    is_last = lax.axis_index("layer") == last
    tzs = [fields[z] for z in range(depth)]
    low = fields[5 * depth]
    gs, invs = ([], [])
    g, up_last = (None, None)
    above = low
    for z in range(depth):
        up = tzs[z]
        if z == depth - 1:
            up = jnp.where(is_last, 0.0, up)
            up_last = up
        kept = fields[depth + z]
        pivot = above + up + jnp.where(kept == 0.0, 1.0, kept)
        if z:
            pivot = pivot - above * g
        ipv = 1.0 / pivot
        g = up * ipv
        inv[z] = ipv
        upper[z] = g
        gs.append(g)
        invs.append(ipv)
        above = up
    first = [invs[0]]
    for z in range(1, depth):
        first.append(tzs[z - 1] * first[-1] * invs[z])
    final = [None] * depth
    final[-1] = invs[-1]
    for z in range(depth - 2, -1, -1):
        first[z] = first[z] + gs[z] * first[z + 1]
        final[z] = gs[z] * final[z + 1]
    for z in range(depth):
        answers[z] = first[z][:width]
        answers[depth + z] = final[z][:width]
        sides[z] = low * first[z]
        sides[depth + z] = up_last * final[z]
    y = local_solve([fields[2 * depth + z] for z in range(depth)], gs, invs, tzs)
    ends[0], ends[1] = (low * first[0], low * first[-1])
    ends[2], ends[3] = (up_last * final[0], up_last * final[-1])
    ends[4], ends[5] = (y[0], y[-1])


def pair(level, own, sib):
    af, af_ = choose(level, own[0], sib[0])
    al, al_ = choose(level, own[1], sib[1])
    bf, bf_ = choose(level, own[2], sib[2])
    bl, bl_ = choose(level, own[3], sib[3])
    return af, al, bf, bl, af_, al_, bf_, bl_, 1.0 / (1.0 - bl * af_)


def join_ends(level, own, sib, mine, other):
    _, _, bf, bl, af_, al_, _, _, den = pair(level, own, sib)
    yf, yf_ = choose(level, mine[0], other[0])
    yl, yl_ = choose(level, mine[1], other[1])
    return (yf + bf * (yf_ + af_ * yl) * den, yl_ + al_ * (yl + bl * yf_) * den)


def join_kernel(level, own, sib, answers, out, face, more, one):
    depth, width, _ = more.shape
    depth = depth // 2
    af, al, bf, bl, af_, al_, bf_, bl_, den = pair(level, own, sib)
    first = af + bf * af_ * al * den
    last = bl_ + al_ * bl * bf_ * den
    yf, yl = join_ends(level, own, sib, (own[4], own[5]), (sib[4], sib[5]))
    out[0], out[1], out[2], out[3] = (first, al_ * al * den, bf * bf_ * den, last)
    out[4], out[5] = (yf, yl)
    right, later = (is_right(level), is_right(level + 1))
    face[0], face[1] = (jnp.where(later, first, last), jnp.where(later, yf, yl))
    bfd, ald, af_, bl = ((bf * den)[:width], (al_ * den)[:width], af_[:width], bl[:width])
    for z in range(depth):
        kf, kl = (answers[z], answers[depth + z])
        top = jnp.where(right, bfd * kf, kf + bfd * af_ * kl)
        bottom = jnp.where(right, kl + ald * bl * kf, ald * kl)
        more[z] = top
        more[depth + z] = bottom
        one[z] = jnp.where(later, top, bottom)


def groups_of(lists, levels):
    tiles = lax.axis_size("tile")
    layers = lax.axis_size("layer")
    t, l = (lax.axis_index("tile"), lax.axis_index("layer"))
    out = []
    for level in range(-1, levels):
        members = [l] if level < 0 else [(((l >> level) ^ 1) << level) + i for i in range(1 << level)]
        group = []
        for member in members:
            for step in (-1, 0, 1):
                there = jnp.clip(t + step, 0, tiles - 1)
                group.append((there * layers + member, step, there == t + step))
        out.append(group)
    return out


def front_kernel(levels, shape, ext, recv, inverse, solved, rows_hot, lanes_hot, sol_hot, sol_row, layer, held, sems):
    devices = recv.shape[0]
    count = recv.shape[2] // 3
    rows, length = inverse.shape
    depth, width, long = shape
    lanes = 128
    chunks = sems.shape[0]
    wide = length // chunks
    copies = [
        pltpu.make_async_copy(inverse.at[:, pl.ds(i * wide, wide)], held.at[:, pl.ds(i * wide, wide)], sems.at[i])
        for i in range(chunks)
    ]
    for copy in copies:
        copy.start()
    total = jnp.zeros((length // lanes, lanes), F32)
    group = 8
    for first in range(0, devices, group):
        lefts, rights = ([], [])
        for d in range(first, first + group):
            value = recv[d, :, :count]
            index = recv[d, :, count : 2 * count].astype(I32)
            hi, lo = lax.div(index, lanes), lax.rem(index, lanes)
            hit = iota((length // lanes, count), 0) == hi
            lefts.append(jnp.concatenate([jnp.where(hit, v.astype(F32), 0.0).astype(BF16) for v in split(value)], 0))
            rights.append(onehot(lo, lanes).astype(BF16))
        total = total + fold(dot_nt(jnp.concatenate(lefts, 1), jnp.concatenate(rights, 1)))
    at = 0
    for members in groups_of(recv, levels):
        for device, step, valid in members:
            entry = recv[device]
            index = entry[:, count : 2 * count].astype(I32)
            cell = entry[:, 2 * count :].astype(I32)
            y, x = lax.rem(cell, long), lax.rem(lax.div(cell, long), width)
            if step == 1:
                x = jnp.where(x < 2, x + width, -1)
            if step == -1:
                x = jnp.where(x >= width - 2, x - width + ext, -1)
            row = jnp.where(jnp.logical_and(valid, x >= 0), lax.div(y, lanes) * ext + x, -1)
            here = pl.ds(at, count)
            rows_hot[:, here] = onehot(row, rows_hot.shape[0]).astype(BF16)
            lanes_hot[:, here] = onehot(lax.rem(y, lanes), lanes).astype(BF16)
            sol_hot[:, here] = onehot(lax.rem(index, rows), rows).astype(BF16)
            sol_row[:, here] = lax.div(index, rows)
            if at < layer.shape[1]:
                layer[:, here] = lax.div(cell, long * width)
            at += count
    acc = jnp.zeros((rows, lanes), F32)
    for i in range(chunks):
        copies[i].wait()
        for r in range(i * wide // lanes, (i + 1) * wide // lanes):
            acc = acc + held[:, r * lanes : (r + 1) * lanes] * total[r : r + 1]
    parts = jnp.concatenate(split(acc), 1)
    out = dot_nt(jnp.ones((8, parts.shape[1]), BF16), parts)
    solved[...] = out[0:1]


def list_kernel(solved, cell, prod, *refs):
    tables, send = (refs[:-1], refs[-1])
    where, value = (cell[...], prod[...])
    hi, lo = None, None
    depth, width, long = tables[-1].shape
    hi, lo = lax.div(where, long), lax.rem(where, long)
    stack = [t[k * depth : (k + 1) * depth].reshape(depth * width, long) for t in tables for k in range(t.shape[0] // depth)]
    parts = jnp.concatenate([p for table in stack for p in split(table)], 0)
    got = dot(parts, onehot(lo, long).astype(BF16))
    mask = onehot(hi, depth * width)
    n = 3 * depth * width
    found = [value * jnp.sum(fold(got[i * n : (i + 1) * n]) * mask, axis=0, keepdims=True) for i in range(len(stack))]
    send[...] = jnp.broadcast_to(jnp.concatenate([solved[...], value, *found], 1)[:, None], send.shape)


def gathered(values, rows_hot, lanes_hot, start, size, ext, parts):
    hot = lanes_hot[:, start : start + size]
    pieces = [hot * p for v in values for p in split(v)[:parts]]
    got = dot_nt(rows_hot[:, start : start + size], jnp.concatenate(pieces, 0))
    planes = []
    lanes = hot.shape[0]
    for i in range(len(values)):
        plane = got[:, i * parts * lanes : (i * parts + 1) * lanes]
        for k in range(1, parts):
            j = i * parts + k
            plane = plane + got[:, j * lanes : (j + 1) * lanes]
        planes.append(jnp.concatenate([plane[r : r + ext] for r in range(0, plane.shape[0], ext)], 1))
    return planes


def near(centre, above, below, tx, ty, tz, tza):
    high, long = centre.shape
    col = iota(centre.shape, 1)
    total = tz * below + tza * above
    total = total + tx * pltpu.roll(centre, high - 1, 0) + pltpu.roll(tx * centre, 1, 0)
    total = total + ty * jnp.where(col == long - 1, 0.0, pltpu.roll(centre, long - 1, 1))
    return total + jnp.where(col == 0, 0.0, pltpu.roll(ty * centre, 1, 1))


def search_kernel(levels, recv, rows_hot, lanes_hot, sol_hot, sol_row, layer, fields, halo, upper, inv, sides, rhs, diag, binv, *refs):
    own, sib = (refs[:levels], refs[levels : 2 * levels])
    s, inner, outer, p = refs[2 * levels :]
    depth, ext, long = (upper.shape[0], upper.shape[1], upper.shape[2])
    width = ext - 8
    rows, count = (sol_hot.shape[0], layer.shape[1] // 3)
    table = jnp.concatenate(split(recv[...].reshape(recv.shape[0], recv.shape[2])[:, :rows]), 0)
    sol = fold(dot(table, sol_hot[...]))
    sol = jnp.sum(jnp.where(iota(sol.shape, 0) == sol_row[...], sol, 0.0), axis=0, keepdims=True)
    groups = groups_of(recv, levels)

    def listed(group, column):
        at = rows + column * count
        return jnp.concatenate([recv[device][:, at : at + count] for device, _, _ in group], 1)

    start = layer.shape[1]
    value = listed(groups[0], 0) * sol[:, :start]
    which = layer[...]
    change = gathered([jnp.where(which == z, value, 0.0) for z in range(depth)], rows_hot, lanes_hot, 0, start, ext, 3)
    tzs = [fields[z] for z in range(depth)]
    y = local_solve([fields[2 * depth + z] - change[z] for z in range(depth)], upper, inv, tzs)
    mine = (y[0], y[-1])
    steps = []
    for level in range(levels):
        group = groups[level + 1]
        size = len(group) * count
        top = level == levels - 1
        columns = [1 + 2 * level] if top else [1 + 2 * level, 2 + 2 * level]
        values = [listed(group, c) * sol[:, start : start + size] for c in columns]
        change = gathered(values, rows_hot, lanes_hot, start, size, ext, 3)
        start += size
        if top:
            other = sib[level][1] - change[0]
            steps.append((mine, (other, other)))
        else:
            other = (sib[level][4] - change[0], sib[level][5] - change[1])
            steps.append((mine, other))
            mine = join_ends(level, own[level], sib[level], mine, other)
    zero = jnp.zeros((ext, long), F32)
    above, below = (zero, zero)
    for level in range(levels - 1, -1, -1):
        mine, other = steps[level]
        yl, _ = choose(level, mine[1], other[1])
        _, yf_ = choose(level, mine[0], other[0])
        if level == levels - 1:
            bl, _ = choose(level, own[level][3], sib[level][0])
            _, af_ = choose(level, own[level][0], sib[level][0])
            den = 1.0 / (1.0 - bl * af_)
            ml = (yl + bl * yf_) * den
            mr = (yf_ + af_ * yl) * den
        else:
            _, al, _, bl, af_, _, bf_, _, den = pair(level, own[level], sib[level])
            one = yl + al * above
            two = yf_ + bf_ * below
            ml = (one + bl * two) * den
            mr = (two + af_ * one) * den
        right = is_right(level)
        above, below = (jnp.where(right, ml, above), jnp.where(right, below, mr))
    for z in range(depth):
        p[z] = y[z] + sides[z] * above + sides[depth + z] * below
    odd = is_right(0)
    for z in range(depth):
        up = above if z == 0 else p[z - 1]
        down = below if z == depth - 1 else p[z + 1]
        tza = fields[5 * depth] if z == 0 else fields[z - 1]
        centre = p[z]
        coupled = near(centre, up, down, fields[3 * depth + z], fields[4 * depth + z], fields[z], tza)
        c16, n16, c8, n8 = (centre[:width], coupled[:width], centre[width:], coupled[width:])
        remain = [rhs[c, z] - diag[c, 0, z] * c16 for c in range(3)]
        remain[0] = remain[0] + n16
        for c in range(3):
            value = binv[c, 0, z] * remain[0] + binv[c, 1, z] * remain[1] + binv[c, 2, z] * remain[2]
            if c == 0:
                value = c16 + value
            s[c, z, :width] = value
            i = c * depth + z
            s[c, z, width:] = halo[i] + halo[3 * depth + i] * c8 + halo[6 * depth + i] * n8
    for c in range(3):
        top, bottom = (s[c, 0, :width], s[c, depth - 1, :width])
        inner[c] = jnp.where(odd, top, bottom)
        outer[c] = jnp.where(odd, bottom, top)


def inner_kernel(s, diag, fields, image):
    depth, ext, long = s.shape[1:]
    width = ext - 8
    zero = jnp.zeros((ext, long), F32)
    for z in range(depth):
        tza = zero if z == 0 else fields[z - 1]
        for c in range(3):
            above = zero if z == 0 else s[c, z - 1]
            below = zero if z == depth - 1 else s[c, z + 1]
            coupled = near(s[c, z], above, below, fields[3 * depth + z], fields[4 * depth + z], fields[z], tza)
            total = diag[c, 0, z] * s[0, z, :width] + diag[c, 1, z] * s[1, z, :width] + diag[c, 2, z] * s[2, z, :width]
            image[c, z] = total - coupled[:width]


def image_kernel(part, inner, outer, rhs, fields, image, send):
    depth, width = part.shape[1:3]
    odd = is_right(0)
    along = power = start = 0.0
    for z in range(depth):
        for c in range(3):
            value = part[c, z]
            if z == 0:
                value = value - fields[5 * depth, :width] * jnp.where(odd, inner[c], outer[c])
            if z == depth - 1:
                value = value - fields[z, :width] * jnp.where(odd, outer[c], inner[c])
            image[c, z] = value
            right = rhs[c, z]
            along = along + value * right
            power = power + value * value
            start = start + right * right
    along, power, start = (jnp.sum(along), jnp.sum(power), jnp.sum(start))
    omega = along / jnp.where(power > 0.0, power, 1.0)
    square = cross = 0.0
    for z in range(depth):
        for c in range(3):
            value = image[c, z]
            left = rhs[c, z] - omega * value
            square = square + left * left
            cross = cross + left * value
    lane = iota((1, send.shape[2]), 1)
    out = jnp.zeros((1, send.shape[2]), F32)
    for i, value in enumerate((along, power, start, jnp.sum(square), jnp.sum(cross), omega)):
        out = jnp.where(lane == i, value, out)
    send[...] = jnp.broadcast_to(out[:, None], send.shape)


def finish_kernel(recv, s, image, rhs, update, lin_res, ratio):
    sums = recv[...].reshape(recv.shape[0], recv.shape[2])
    whole = jnp.sum(sums, axis=0, keepdims=True)
    omega = whole[:, 0:1] / whole[:, 1:2]
    shift = sums[:, 5:6] - omega
    square = sums[:, 3:4] + 2.0 * shift * sums[:, 4:5] + shift * shift * sums[:, 1:2]
    ratio[...] = jnp.sqrt(jnp.sum(square, axis=0, keepdims=True) / whole[:, 2:3])
    for c in range(3):
        for z in range(s.shape[1]):
            update[c, z] = omega * s[c, z, : rhs.shape[2]]
            lin_res[c, z] = rhs[c, z] - omega * image[c, z]


def up(x, axis):
    return lax.ppermute(x, axis, [(i, i + 1) for i in range(lax.axis_size(axis) - 1)])


def down(x, axis):
    return lax.ppermute(x, axis, [(i + 1, i) for i in range(lax.axis_size(axis) - 1)])


def flip(x, level):
    return lax.ppermute(x, "layer", [(i, i ^ (1 << level)) for i in range(lax.axis_size("layer"))])


def neighbour(x):
    size = lax.axis_size("layer")
    pairs = [(i, i + 1) for i in range(1, size - 1, 2)]
    return lax.ppermute(x, "layer", pairs + [(j, i) for i, j in pairs])


def everywhere(x):
    return lax.all_to_all(x, BOTH, split_axis=0, concat_axis=0, tiled=True)


def shards(rhs, weights, block_diag, block_inv, tx, ty, tz, store, cell, front, prod, inverse):
    layers = lax.axis_size("layer")
    devices = lax.axis_size("tile") * layers
    levels = layers.bit_length() - 1
    depth, width, long = tx.shape
    ext = width + 8
    count = cell.shape[0]
    rows = inverse.shape[0]
    lists = 3 * layers * count
    cell, front, prod = (cell.reshape(1, -1), front.reshape(1, -1), prod.reshape(1, -1))
    field = vmem(tx.shape)

    def planes(n, high=ext):
        return vmem((n, high, long))

    pres, send, tz_last = call(
        pres_kernel,
        (field, vmem((devices, 1, 3 * count)), vmem((1, width, long))),
        (rhs, weights, cell, front, prod, tz),
        far=range(6),
    )
    tz_prev = up(tz_last, "layer")
    terms = everywhere(send)
    terms, tz_prev, rhs, block_diag = lax.optimization_barrier((terms, tz_prev, rhs, block_diag))

    edge = vmem((8 * (-(-(10 * depth + 2 + 9 * depth) // 8)), long))
    low, high, rhs, diag, binv, tz, store, tx, ty = call(
        edge_kernel,
        (edge, edge),
        (rhs, block_diag, block_inv, tz, store, tx, ty, pres, tz_prev),
        far=range(7),
        keep=range(7),
    )
    after, before = (down(low, "tile"), up(high, "tile"))
    six = planes(6)
    fields, halo, upper, inv, answers, sides, ends = call(
        functools.partial(coef_kernel, layers - 1),
        (planes(5 * depth + 1), planes(9 * depth, 8), planes(depth), planes(depth), planes(2 * depth, width), planes(2 * depth), six),
        (tz, store, tx, ty, pres, tz_prev, after, before),
    )
    chunks = 8
    solved, rows_hot, lanes_hot, sol_hot, sol_row, layer = pl.pallas_call(
        functools.partial(front_kernel, levels, (depth, width, long), ext),
        out_shape=(
            vmem((1, rows)),
            vmem((ext * long // 128, lists), BF16),
            vmem((128, lists), BF16),
            vmem((rows, lists), BF16),
            vmem((1, lists), I32),
            vmem((1, 3 * count), I32),
        ),
        in_specs=[VM, pl.BlockSpec(memory_space=pltpu.HBM)],
        out_specs=(VM,) * 6,
        scratch_shapes=[vmem(inverse.shape), pltpu.SemaphoreType.DMA((chunks,))],
        compiler_params=pltpu.CompilerParams(vmem_limit_bytes=LIMIT),
    )(terms, pltpu.with_memory_space_constraint(inverse, pltpu.HBM))
    own, sib, tables = ([ends], [], [])
    face, last = (None, answers)
    for level in range(levels - 1):
        tables.append(answers)
        sib.append(flip(ends, level))
        ends, face, answers, last = call(
            functools.partial(join_kernel, level),
            (six, planes(2), planes(2 * depth, width), planes(depth, width)),
            (ends, sib[-1], answers),
        )
        own.append(ends)
    tables.append(last)
    sib.append(flip(face, levels - 1))
    (send,) = call(
        list_kernel,
        (vmem((devices, 1, rows + 2 * levels * count)),),
        (solved, cell, prod, *tables),
        far=(1, 2),
    )
    send, sib = lax.optimization_barrier((send, sib))
    sol = everywhere(send)
    plane3 = vmem((3, width, long))
    s, inner, outer, _ = call(
        functools.partial(search_kernel, levels),
        (vmem((3, depth, ext, long)), plane3, plane3, planes(depth)),
        (sol, rows_hot, lanes_hot, sol_hot, sol_row, layer, fields, halo, upper, inv, sides, rhs, diag, binv, *own, *sib),
    )
    inner, outer = (flip(inner, 0), neighbour(outer))
    (part,) = call(inner_kernel, (vmem(rhs.shape),), (s, diag, fields))
    image, send = call(
        image_kernel,
        (vmem(rhs.shape), vmem((devices, 1, 128))),
        (part, inner, outer, rhs, fields),
    )
    sums = everywhere(send)
    update, lin_res, ratio = call(
        finish_kernel, (hbm(rhs.shape), hbm(rhs.shape), hbm((1, 1))), (sums, s, image, rhs)
    )
    return (update, lin_res, ratio.reshape(()))


def solution(mesh):
    return jax.shard_map(
        shards,
        mesh=mesh,
        in_specs=(
            P(None, "layer", "tile", None),
            P(None, "layer", "tile", None),
            P(None, None, "layer", "tile", None),
            P(None, None, "layer", "tile", None),
            P("layer", "tile", None),
            P("layer", "tile", None),
            P("layer", "tile", None),
            P("layer", "tile", None),
            P(("tile", "layer")),
            P(("tile", "layer")),
            P(("tile", "layer")),
            P(("tile", "layer"), None),
        ),
        out_specs=(P(None, "layer", "tile", None), P(None, "layer", "tile", None), P()),
        check_vma=False,
    )
```

```python
import functools
import jax
import jax.numpy as jnp
from jax import lax
from jax.experimental import pallas as pl
from jax.experimental.pallas import tpu as pltpu
from jax.sharding import PartitionSpec as P

F32 = jnp.float32
BF16 = jnp.bfloat16
I32 = jnp.int32
BOTH = ("tile", "layer")
VM = pl.BlockSpec(memory_space=pltpu.VMEM)
LIMIT = 16 << 20


def hbm(shape):
    return jax.ShapeDtypeStruct(shape, F32)


def vmem(shape, dtype=F32):
    return pltpu.VMEM(shape, dtype)


def staged(kernel, where, outs, kept, column, *refs):
    count, sems = (len(where), refs[-1])
    held = list(refs[count + outs + len(kept) : -1])
    target = dict(zip(kept, refs[count + outs : count + outs + len(kept)]))
    operands, copies = ([], [])
    for i, far in enumerate(where):
        if far:
            to = target[i] if i in target else held.pop(0)
            part = refs[i].at[:, 0] if i in column else refs[i]
            copies.append(pltpu.make_async_copy(part, to, sems.at[len(copies)]))
            operands.append(to)
        else:
            operands.append(refs[i])
    for copy in copies:
        copy.start()
    for copy in copies:
        copy.wait()
    kernel(*operands, *refs[count : count + outs])


def call(kernel, outs, args, far=(), keep=(), column=(), limit=LIMIT):
    where = [i in far for i in range(len(args))]
    spaces = [pltpu.HBM if w else pltpu.VMEM for w in where]
    every = (*outs, *(vmem(args[i].shape, args[i].dtype) for i in keep))
    return pl.pallas_call(
        functools.partial(staged, kernel, where, len(outs), tuple(keep), tuple(column)),
        out_shape=every,
        in_specs=[pl.BlockSpec(memory_space=s) for s in spaces],
        out_specs=(VM,) * len(every),
        scratch_shapes=[
            vmem(a.shape[:1] + a.shape[2:] if i in column else a.shape, a.dtype)
            for i, a in enumerate(args)
            if where[i] and i not in keep
        ]
        + [pltpu.SemaphoreType.DMA((max(1, sum(where)),))],
        compiler_params=pltpu.CompilerParams(vmem_limit_bytes=limit),
    )(*[pltpu.with_memory_space_constraint(a, s) for a, s in zip(args, spaces)])


def iota(shape, dim):
    return lax.broadcasted_iota(I32, shape, dim)


def split(x):
    one = x.astype(BF16)
    rest = x - one.astype(F32)
    two = rest.astype(BF16)
    three = (rest - two.astype(F32)).astype(BF16)
    return [one, two, three]


def fold(x):
    n = x.shape[0] // 3
    return x[:n] + (x[n : 2 * n] + x[2 * n :])


def onehot(index, size):
    return jnp.where(iota((size, index.shape[1]), 0) == index, 1.0, 0.0)


def dot(a, b):
    return lax.dot_general(a, b, (((1,), (0,)), ((), ())), preferred_element_type=F32)


def dot_nt(a, b):
    return lax.dot_general(a, b, (((1,), (1,)), ((), ())), preferred_element_type=F32)


def pick(table, hi, lo):
    rows, cols = table.shape
    parts = jnp.concatenate(split(table), 0)
    got = fold(dot(parts, onehot(lo, cols).astype(BF16)))
    return jnp.sum(got * onehot(hi, rows), axis=0, keepdims=True)


def spread(value, hi, lo, rows, cols):
    parts = [jnp.where(iota((rows, hi.shape[1]), 0) == hi, v.astype(F32), 0.0).astype(BF16) for v in split(value)]
    return fold(dot_nt(jnp.concatenate(parts, 0), onehot(lo, cols).astype(BF16)))


def pres_kernel(rhs, wts, cell, front, prod, tz, store, pres, send, tz_last, low, high):
    depth, width, long = pres.shape
    for z in range(depth):
        pres[z] = wts[0, z] * rhs[0, z] + wts[1, z] * rhs[1, z] + wts[2, z] * rhs[2, z]
    where = cell[...]
    table = pres[...].reshape(depth * width, long)
    value = prod[...] * pick(table, lax.div(where, long), lax.rem(where, long))
    both = jnp.concatenate([value, front[...].astype(F32), where.astype(F32)], 1)
    send[...] = jnp.broadcast_to(both[:, None], send.shape)
    tz_last[0] = tz[depth - 1]
    planes = [(ref, z) for ref in (tz, store, pres) for z in range(depth)]
    for i, (ref, z) in enumerate(planes):
        low[2 * i : 2 * i + 2] = ref[z, 0:2]
        high[2 * i : 2 * i + 2] = ref[z, width - 2 : width]
    for out in (low, high):
        out[2 * len(planes) :] = jnp.zeros((out.shape[0] - 2 * len(planes), long), F32)


def edge_kernel(rhs, column, binv, tx, ty, tz_prev, low, high):
    depth, width, long = tx.shape
    for out, rows, at, two in ((low, slice(0, 8), 0, 0), (high, slice(width - 8, width), 7, 6)):
        out[...] = jnp.zeros(out.shape, F32)
        out[0:1] = tz_prev[0, rows][at : at + 1]
        for z in range(depth):
            out[1 + z : 2 + z] = ty[z, rows][at : at + 1]
            i = 1 + depth + 2 * z
            out[i : i + 2] = tx[z, rows][two : two + 2]
            right = [rhs[d, z, rows] for d in range(3)]
            slope_of = [column[d, z, rows] for d in range(3)]
            for c in range(3):
                m = [binv[c, d, z, rows] for d in range(3)]
                first = m[0] * right[0] + m[1] * right[1] + m[2] * right[2]
                slope = (1.0 if c == 0 else 0.0) - (m[0] * slope_of[0] + m[1] * slope_of[1] + m[2] * slope_of[2])
                for k, value in enumerate((first, slope, m[0])):
                    i = 1 + 3 * depth + (k * 3 + c) * depth + z
                    out[i : i + 1] = value[at : at + 1]


def is_right(level):
    return (lax.axis_index("layer") >> level) % 2 == 1


def choose(level, mine, other):
    right = is_right(level)
    return (jnp.where(right, other, mine), jnp.where(right, mine, other))


def local_solve(rhs, upper, inv, tz):
    depth = len(rhs)
    y = [rhs[0] * inv[0]]
    for z in range(1, depth):
        y.append((rhs[z] + tz[z - 1] * y[-1]) * inv[z])
    for z in range(depth - 2, -1, -1):
        y[z] = y[z] + upper[z] * y[z + 1]
    return y


def factors(tz, store):
    depth = len(tz)
    gs, invs = ([], [])
    own = None
    for z in range(depth):
        own = store[z] if z == 0 else store[z] + gs[-1] * own
        invs.append(1.0 / (own + tz[z] if z < depth - 1 else own))
        gs.append(tz[z] * invs[-1])
    first = [invs[0]]
    for z in range(1, depth):
        first.append(tz[z - 1] * first[-1] * invs[z])
    final = [None] * depth
    final[-1] = invs[-1]
    for z in range(depth - 2, -1, -1):
        first[z] = first[z] + gs[z] * first[z + 1]
        final[z] = gs[z] * final[z + 1]
    return gs, invs, first, final, (first[0], first[-1], final[-1] + 1.0 / jnp.maximum(tz[-1], 1e-30))


def coef_kernel(tz, store, pres, after, before, base, answers, ends):
    depth, width, long = pres.shape
    for k, ref in enumerate((tz, store, pres)):
        for z in range(depth):
            i = k * depth + z
            base[i, :width] = ref[z]
            base[i, width:] = jnp.full((8, long), 1.0 if k == 1 else 0.0, F32)
            for side, at in ((after, width), (before, width + 6)):
                rows = side[2 * i : 2 * i + 2]
                base[i, at : at + 2] = jnp.where(rows == 0.0, 1.0, rows) if k == 1 else rows
    tzs = [base[z] for z in range(depth)]
    gs, invs, first, final, coefs = factors(tzs, [base[depth + z] for z in range(depth)])
    for z in range(depth):
        answers[z] = first[z][:width]
        answers[depth + z] = final[z][:width]
    y = local_solve([base[2 * depth + z] for z in range(depth)], gs, invs, tzs)
    for i, value in enumerate((*coefs, y[0], y[-1])):
        ends[i] = value


def pair(level, own, sib):
    af, af_ = choose(level, own[0], sib[0])
    c, c_ = choose(level, own[1], sib[1])
    b, b_ = choose(level, own[2], sib[2])
    return af, c, b, af_, c_, b_, 1.0 / (b + af_)


def join_coefs(level, own, sib):
    af, c, _, _, c_, b_, g = pair(level, own, sib)
    return (af - c * c * g, c * c_ * g, b_ - c_ * c_ * g)


def join_ends(level, own, sib, mine, other):
    _, c, _, _, c_, _, g = pair(level, own, sib)
    yf, yf_ = choose(level, mine[0], other[0])
    yl, yl_ = choose(level, mine[1], other[1])
    flux = g * (yl - yf_)
    return (yf - c * flux, yl_ + c_ * flux)


def join_kernel(level, own, sib, answers, out, face, more, one):
    depth, width, _ = more.shape
    depth = depth // 2
    _, c, _, _, c_, _, g = pair(level, own, sib)
    first, both, last = join_coefs(level, own, sib)
    yf, yl = join_ends(level, own, sib, (own[3], own[4]), (sib[3], sib[4]))
    out[0], out[1], out[2] = (first, both, last)
    out[3], out[4] = (yf, yl)
    right, later = (is_right(level), is_right(level + 1))
    face[0], face[1] = (jnp.where(later, first, last), jnp.where(later, yf, yl))
    cg, cg_ = ((c * g)[:width], (c_ * g)[:width])
    for z in range(depth):
        kf, kl = (answers[z], answers[depth + z])
        top = jnp.where(right, cg * kf, kf - cg * kl)
        bottom = jnp.where(right, kl - cg_ * kf, cg_ * kl)
        more[z] = top
        more[depth + z] = bottom
        one[z] = jnp.where(later, top, bottom)


def groups_of(lists, levels):
    tiles = lax.axis_size("tile")
    layers = lax.axis_size("layer")
    t, l = (lax.axis_index("tile"), lax.axis_index("layer"))
    out = []
    for level in range(-1, levels):
        members = [l] if level < 0 else [(((l >> level) ^ 1) << level) + i for i in range(1 << level)]
        group = []
        for member in members:
            for step in (-1, 0, 1):
                there = jnp.clip(t + step, 0, tiles - 1)
                group.append((there * layers + member, step, there == t + step))
        out.append(group)
    return out


def front_kernel(recv, inverse, solved, held, sems):
    devices = recv.shape[0]
    count = recv.shape[2] // 3
    rows, length = inverse.shape
    lanes = 128
    chunks = sems.shape[0]
    wide = length // chunks
    copies = [
        pltpu.make_async_copy(inverse.at[:, pl.ds(i * wide, wide)], held.at[:, pl.ds(i * wide, wide)], sems.at[i])
        for i in range(chunks)
    ]
    for copy in copies:
        copy.start()
    total = jnp.zeros((length // lanes, lanes), F32)
    group = 8
    for first in range(0, devices, group):
        lefts, rights = ([], [])
        for d in range(first, first + group):
            value = recv[d, :, :count]
            index = recv[d, :, count : 2 * count].astype(I32)
            hi, lo = lax.div(index, lanes), lax.rem(index, lanes)
            hit = iota((length // lanes, count), 0) == hi
            lefts.append(jnp.concatenate([jnp.where(hit, v.astype(F32), 0.0).astype(BF16) for v in split(value)], 0))
            rights.append(onehot(lo, lanes).astype(BF16))
        total = total + fold(dot_nt(jnp.concatenate(lefts, 1), jnp.concatenate(rights, 1)))
    acc = jnp.zeros((rows, lanes), F32)
    for i in range(chunks):
        copies[i].wait()
        for r in range(i * wide // lanes, (i + 1) * wide // lanes):
            acc = acc + held[:, r * lanes : (r + 1) * lanes] * total[r : r + 1]
    parts = jnp.concatenate(split(acc), 1)
    out = dot_nt(jnp.ones((8, parts.shape[1]), BF16), parts)
    solved[...] = out[0:1]


def list_kernel(solved, cell, prod, *refs):
    tables, send = (refs[:-1], refs[-1])
    where, value = (cell[...], prod[...])
    hi, lo = None, None
    depth, width, long = tables[-1].shape
    hi, lo = lax.div(where, long), lax.rem(where, long)
    stack = [t[k * depth : (k + 1) * depth].reshape(depth * width, long) for t in tables for k in range(t.shape[0] // depth)]
    parts = jnp.concatenate([p for table in stack for p in split(table)], 0)
    got = dot(parts, onehot(lo, long).astype(BF16))
    mask = onehot(hi, depth * width)
    n = 3 * depth * width
    found = [value * jnp.sum(fold(got[i * n : (i + 1) * n]) * mask, axis=0, keepdims=True) for i in range(len(stack))]
    send[...] = jnp.broadcast_to(jnp.concatenate([solved[...], value, *found], 1)[:, None], send.shape)


def gathered(values, rows_hot, lanes_hot, start, size, ext, parts):
    hot = lanes_hot[:, start : start + size]
    pieces = [hot * p for v in values for p in split(v)[:parts]]
    got = dot_nt(rows_hot[:, start : start + size], jnp.concatenate(pieces, 0))
    planes = []
    lanes = hot.shape[0]
    for i in range(len(values)):
        plane = got[:, i * parts * lanes : (i * parts + 1) * lanes]
        for k in range(1, parts):
            j = i * parts + k
            plane = plane + got[:, j * lanes : (j + 1) * lanes]
        planes.append(jnp.concatenate([plane[r : r + ext] for r in range(0, plane.shape[0], ext)], 1))
    return planes


def beside(centre, tx, ty):
    high, long = centre.shape
    col = iota(centre.shape, 1)
    total = tx * pltpu.roll(centre, high - 1, 0) + pltpu.roll(tx * centre, 1, 0)
    total = total + ty * jnp.where(col == long - 1, 0.0, pltpu.roll(centre, long - 1, 1))
    return total + jnp.where(col == 0, 0.0, pltpu.roll(ty * centre, 1, 1))


def search_kernel(levels, *refs):
    (recv, terms, base), refs = (refs[:3], refs[3:])
    far, refs = (refs[: levels + 8], refs[levels + 8 :])
    (s, inner, outer, tx_wide, ty_wide, tzp), near_by, refs = (refs[:6], refs[6:11], refs[11:])
    near_by = [*near_by, *refs[: levels + 3]]
    p, rows_hot, lanes_hot, sol_hot, sol_row, layer, sems = refs[levels + 3 :]
    copies = [pltpu.make_async_copy(a, b, sems.at[i]) for i, (a, b) in enumerate(zip(far, near_by))]
    for copy in copies[5:] + copies[:5]:
        copy.start()
    tx, ty, rhs, diag, binv = near_by[:5]
    sib, (after, before, tz_prev) = (near_by[5 : levels + 5], near_by[levels + 5 :])
    depth = base.shape[0] // 3
    ext, long = base.shape[1:]
    width = ext - 8
    rows = sol_hot.shape[0]
    count = terms.shape[2] // 3
    lanes = 128
    groups = groups_of(recv, levels)
    at = 0
    for members in groups:
        for device, step, valid in members:
            entry = terms[device]
            index = entry[:, count : 2 * count].astype(I32)
            cell = entry[:, 2 * count :].astype(I32)
            y, x = lax.rem(cell, long), lax.rem(lax.div(cell, long), width)
            if step == 1:
                x = jnp.where(x < 2, x + width, -1)
            if step == -1:
                x = jnp.where(x >= width - 2, x - width + ext, -1)
            row = jnp.where(jnp.logical_and(valid, x >= 0), lax.div(y, lanes) * ext + x, -1)
            here = pl.ds(at, count)
            rows_hot[:, here] = onehot(row, rows_hot.shape[0]).astype(BF16)
            lanes_hot[:, here] = onehot(lax.rem(y, lanes), lanes).astype(BF16)
            sol_hot[:, here] = onehot(lax.rem(index, rows), rows).astype(BF16)
            sol_row[:, here] = lax.div(index, rows)
            if at < layer.shape[1]:
                layer[:, here] = lax.div(cell, long * width)
            at += count
    table = jnp.concatenate(split(recv[...].reshape(recv.shape[0], recv.shape[2])[:, :rows]), 0)
    sol = fold(dot(table, sol_hot[...]))
    sol = jnp.sum(jnp.where(iota(sol.shape, 0) == sol_row[...], sol, 0.0), axis=0, keepdims=True)

    def listed(group, column):
        at = rows + column * count
        return jnp.concatenate([recv[device][:, at : at + count] for device, _, _ in group], 1)

    tzs = [base[z] for z in range(depth)]
    gs, invs, first, final, coefs = factors(tzs, [base[depth + z] for z in range(depth)])
    own = [coefs]
    start = layer.shape[1]
    value = listed(groups[0], 0) * sol[:, :start]
    which = layer[...]
    change = gathered([jnp.where(which == z, value, 0.0) for z in range(depth)], rows_hot, lanes_hot, 0, start, ext, 3)
    y = local_solve([base[2 * depth + z] - change[z] for z in range(depth)], gs, invs, tzs)
    for copy in copies[5:]:
        copy.wait()
    mine = (y[0], y[-1])
    steps = []
    for level in range(levels):
        size = len(groups[level + 1]) * count
        top = level == levels - 1
        columns = [1 + 2 * level] if top else [1 + 2 * level, 2 + 2 * level]
        values = [listed(groups[level + 1], c) * sol[:, start : start + size] for c in columns]
        change = gathered(values, rows_hot, lanes_hot, start, size, ext, 3)
        start += size
        if top:
            other = sib[level][1] - change[0]
            steps.append((mine, (other, other)))
        else:
            other = (sib[level][3] - change[0], sib[level][4] - change[1])
            steps.append((mine, other))
            mine = join_ends(level, own[level], sib[level], mine, other)
            own.append(join_coefs(level, own[level], sib[level]))
    zero = jnp.zeros((8, long), F32)
    for z in range(depth):
        tx_wide[z, width:] = zero
        ty_wide[z, width:] = zero
        at = 1 + depth + 2 * z
        tx_wide[z, width : width + 2] = after[at : at + 2]
        tx_wide[z, width + 6 :] = before[at : at + 2]
        ty_wide[z, width : width + 1] = after[1 + z : 2 + z]
        ty_wide[z, width + 7 :] = before[1 + z : 2 + z]
    tzp[0, :width] = tz_prev[0]
    tzp[0, width:] = zero
    tzp[0, width : width + 1] = after[0:1]
    tzp[0, width + 7 :] = before[0:1]
    above = below = None
    for level in range(levels - 1, -1, -1):
        mine, other = steps[level]
        yl, _ = choose(level, mine[1], other[1])
        _, yf_ = choose(level, mine[0], other[0])
        flux = yl - yf_
        if level == levels - 1:
            b, _ = choose(level, own[level][2], sib[level][0])
            _, af_ = choose(level, own[level][0], sib[level][0])
            g = 1.0 / (b + af_)
        else:
            _, c, _, _, c_, _, g = pair(level, own[level], sib[level])
            flux = flux + c * above - c_ * below
        flux = g * flux
        right = is_right(level)
        if above is None:
            above = below = jnp.zeros((ext, long), F32)
        above, below = (jnp.where(right, flux, above), jnp.where(right, below, -flux))
    for z in range(depth):
        p[z] = y[z] + first[z] * above + final[z] * below
    is_last = lax.axis_index("layer") == (1 << levels) - 1
    for copy in copies[:5]:
        copy.wait()
    odd = is_right(0)
    for z in range(depth):
        tx_wide[z, :width] = tx[z]
        ty_wide[z, :width] = ty[z]
        centre = p[z]
        coupled = beside(centre, tx_wide[z], ty_wide[z])
        coupled = coupled + (above + tzp[0] * centre if z == 0 else tzs[z - 1] * p[z - 1])
        if z == depth - 1:
            coupled = coupled + jnp.where(is_last, 0.0, below + tzs[z] * centre)
        else:
            coupled = coupled + tzs[z] * p[z + 1]
        c16, n16, c8, n8 = (centre[:width], coupled[:width], centre[width:], coupled[width:])
        remain = [rhs[c, z] - diag[c, 0, z] * c16 for c in range(3)]
        remain[0] = remain[0] + n16
        for c in range(3):
            value = binv[c, 0, z] * remain[0] + binv[c, 1, z] * remain[1] + binv[c, 2, z] * remain[2]
            if c == 0:
                value = c16 + value
            s[c, z, :width] = value
            s[c, z, width:] = jnp.zeros((8, long), F32)
            for side, at in ((after, 0), (before, 7)):
                i = 1 + 3 * depth + c * depth + z
                j, k = (i + 3 * depth, i + 6 * depth)
                row = side[i : i + 1] + side[j : j + 1] * c8[at : at + 1] + side[k : k + 1] * n8[at : at + 1]
                s[c, z, width + at : width + at + 1] = row
    for c in range(3):
        top, bottom = (s[c, 0, :width], s[c, depth - 1, :width])
        inner[c] = jnp.where(odd, top, bottom)
        outer[c] = jnp.where(odd, bottom, top)


def inner_kernel(s, diag, tzs, tx, ty, image):
    depth, ext, long = s.shape[1:]
    width = ext - 8
    for z in range(depth):
        for c in range(3):
            total = diag[c, 0, z] * s[0, z, :width] + diag[c, 1, z] * s[1, z, :width] + diag[c, 2, z] * s[2, z, :width]
            total = total - beside(s[c, z], tx[z], ty[z])[:width]
            if z:
                total = total - tzs[z - 1, :width] * s[c, z - 1, :width]
            if z < depth - 1:
                total = total - tzs[z, :width] * s[c, z + 1, :width]
            image[c, z] = total


def image_kernel(part, inner, outer, rhs, tzs, tzp, image, send):
    depth, width = part.shape[1:3]
    odd = is_right(0)
    along = power = start = 0.0
    for z in range(depth):
        for c in range(3):
            value = part[c, z]
            if z == 0:
                value = value - tzp[0, :width] * jnp.where(odd, inner[c], outer[c])
            if z == depth - 1:
                value = value - tzs[z, :width] * jnp.where(odd, outer[c], inner[c])
            image[c, z] = value
            right = rhs[c, z]
            along = along + value * right
            power = power + value * value
            start = start + right * right
    along, power, start = (jnp.sum(along), jnp.sum(power), jnp.sum(start))
    omega = along / jnp.where(power > 0.0, power, 1.0)
    square = cross = 0.0
    for z in range(depth):
        for c in range(3):
            value = image[c, z]
            left = rhs[c, z] - omega * value
            square = square + left * left
            cross = cross + left * value
    lane = iota((1, send.shape[2]), 1)
    out = jnp.zeros((1, send.shape[2]), F32)
    for i, value in enumerate((along, power, start, jnp.sum(square), jnp.sum(cross), omega)):
        out = jnp.where(lane == i, value, out)
    send[...] = jnp.broadcast_to(out[:, None], send.shape)


def finish_kernel(recv, s, image, rhs, update, lin_res, ratio):
    sums = recv[...].reshape(recv.shape[0], recv.shape[2])
    whole = jnp.sum(sums, axis=0, keepdims=True)
    omega = whole[:, 0:1] / whole[:, 1:2]
    shift = sums[:, 5:6] - omega
    square = sums[:, 3:4] + 2.0 * shift * sums[:, 4:5] + shift * shift * sums[:, 1:2]
    ratio[...] = jnp.sqrt(jnp.sum(square, axis=0, keepdims=True) / whole[:, 2:3])
    for c in range(3):
        for z in range(s.shape[1]):
            update[c, z] = omega * s[c, z, : rhs.shape[2]]
            lin_res[c, z] = rhs[c, z] - omega * image[c, z]


def up(x, axis):
    return lax.ppermute(x, axis, [(i, i + 1) for i in range(lax.axis_size(axis) - 1)])


def down(x, axis):
    return lax.ppermute(x, axis, [(i + 1, i) for i in range(lax.axis_size(axis) - 1)])


def flip(x, level):
    return lax.ppermute(x, "layer", [(i, i ^ (1 << level)) for i in range(lax.axis_size("layer"))])


def neighbour(x):
    size = lax.axis_size("layer")
    pairs = [(i, i + 1) for i in range(1, size - 1, 2)]
    return lax.ppermute(x, "layer", pairs + [(j, i) for i, j in pairs])


def everywhere(x):
    return lax.all_to_all(x, BOTH, split_axis=0, concat_axis=0, tiled=True)


def shards(rhs, weights, block_diag, block_inv, tx, ty, tz, store, cell, front, prod, inverse):
    layers = lax.axis_size("layer")
    devices = lax.axis_size("tile") * layers
    levels = layers.bit_length() - 1
    depth, width, long = tx.shape
    ext = width + 8
    count = cell.shape[0]
    rows = inverse.shape[0]
    lists = 3 * layers * count
    cell, front, prod = (cell.reshape(1, -1), front.reshape(1, -1), prod.reshape(1, -1))
    field = vmem(tx.shape)

    def planes(n, high=ext):
        return vmem((n, high, long))

    rim = vmem((8 * (-(-6 * depth // 8)), long))
    pres, send, tz_last, low, high, tz, store = call(
        pres_kernel,
        (field, vmem((devices, 1, 3 * count)), vmem((1, width, long)), rim, rim),
        (rhs, weights, cell, front, prod, tz, store),
        far=range(7),
        keep=(5, 6),
    )
    terms = everywhere(send)
    tz_prev = up(tz_last, "layer")
    after, before = (down(low, "tile"), up(high, "tile"))
    terms, after, before = lax.optimization_barrier((terms, after, before))
    five = planes(5)
    base, answers, ends = call(
        coef_kernel, (planes(3 * depth), planes(2 * depth, width), five), (tz, store, pres, after, before)
    )
    rim = vmem((8 * (-(-(1 + 12 * depth) // 8)), long))
    low, high = call(
        edge_kernel, (rim, rim), (rhs, block_diag, block_inv, tx, ty, tz_prev), far=range(5), column=(1,)
    )
    after, before = (down(low, "tile"), up(high, "tile"))
    terms, low, high, ends = lax.optimization_barrier((terms, low, high, ends))
    chunks = 8
    solved = pl.pallas_call(
        front_kernel,
        out_shape=vmem((1, rows)),
        in_specs=[VM, pl.BlockSpec(memory_space=pltpu.HBM)],
        out_specs=VM,
        scratch_shapes=[vmem(inverse.shape), pltpu.SemaphoreType.DMA((chunks,))],
        compiler_params=pltpu.CompilerParams(vmem_limit_bytes=LIMIT),
    )(terms, pltpu.with_memory_space_constraint(inverse, pltpu.HBM))
    sib, tables = ([], [])
    last = answers
    for level in range(levels - 1):
        tables.append(answers)
        got = flip(ends, level)
        solved, got = lax.optimization_barrier((solved, got))
        sib.append(got)
        ends, face, answers, last = call(
            functools.partial(join_kernel, level),
            (five, planes(2), planes(2 * depth, width), planes(depth, width)),
            (ends, sib[-1], answers),
        )
    tables.append(last)
    sib.append(flip(face, levels - 1))
    (send,) = call(
        list_kernel,
        (vmem((devices, 1, rows + 2 * levels * count)),),
        (solved, cell, prod, *tables),
        far=(1, 2),
    )
    sol = everywhere(send)
    plane3 = vmem((3, width, long))
    far = (tx, ty, rhs, block_diag, block_inv, *sib, after, before, tz_prev)
    args = (sol, terms, base)
    s, inner, outer, tx, ty, tzp, _, _, rhs, diag, _ = pl.pallas_call(
        functools.partial(search_kernel, levels),
        out_shape=(vmem((3, depth, ext, long)), plane3, plane3, planes(depth), planes(depth), planes(1))
        + tuple(vmem(a.shape) for a in far[:5]),
        in_specs=[VM] * len(args) + [pl.BlockSpec(memory_space=pltpu.HBM)] * len(far),
        out_specs=(VM,) * 11,
        scratch_shapes=[vmem(a.shape) for a in far[5:]]
        + [
            planes(depth),
            vmem((ext * long // 128, lists), BF16),
            vmem((128, lists), BF16),
            vmem((rows, lists), BF16),
            vmem((1, lists), I32),
            vmem((1, 3 * count), I32),
            pltpu.SemaphoreType.DMA((len(far),)),
        ],
        compiler_params=pltpu.CompilerParams(vmem_limit_bytes=2 * LIMIT),
    )(
        *[pltpu.with_memory_space_constraint(a, pltpu.VMEM) for a in args],
        *[pltpu.with_memory_space_constraint(a, pltpu.HBM) for a in far],
    )
    inner, outer = (flip(inner, 0), neighbour(outer))
    (part,) = call(inner_kernel, (vmem(rhs.shape),), (s, diag, base, tx, ty))
    image, send = call(
        image_kernel,
        (vmem(rhs.shape), vmem((devices, 1, 128))),
        (part, inner, outer, rhs, base, tzp),
    )
    sums = everywhere(send)
    update, lin_res, ratio = call(
        finish_kernel, (hbm(rhs.shape), hbm(rhs.shape), hbm((1, 1))), (sums, s, image, rhs)
    )
    return (update, lin_res, ratio.reshape(()))


def solution(mesh):
    return jax.shard_map(
        shards,
        mesh=mesh,
        in_specs=(
            P(None, "layer", "tile", None),
            P(None, "layer", "tile", None),
            P(None, None, "layer", "tile", None),
            P(None, None, "layer", "tile", None),
            P("layer", "tile", None),
            P("layer", "tile", None),
            P("layer", "tile", None),
            P("layer", "tile", None),
            P(("tile", "layer")),
            P(("tile", "layer")),
            P(("tile", "layer")),
            P(("tile", "layer"), None),
        ),
        out_specs=(P(None, "layer", "tile", None), P(None, "layer", "tile", None), P()),
        check_vma=False,
    )
```

```python
import functools
import jax
import jax.numpy as jnp
from jax import lax
from jax.experimental import pallas as pl
from jax.experimental.pallas import tpu as pltpu
from jax.sharding import PartitionSpec as P

F32 = jnp.float32
BF16 = jnp.bfloat16
I32 = jnp.int32
BOTH = ("tile", "layer")
VM = pl.BlockSpec(memory_space=pltpu.VMEM)
LIMIT = 16 << 20


def hbm(shape):
    return jax.ShapeDtypeStruct(shape, F32)


def vmem(shape, dtype=F32):
    return pltpu.VMEM(shape, dtype)


def staged(kernel, where, outs, kept, column, *refs):
    count, sems = (len(where), refs[-1])
    held = list(refs[count + outs + len(kept) : -1])
    target = dict(zip(kept, refs[count + outs : count + outs + len(kept)]))
    operands, copies = ([], [])
    for i, far in enumerate(where):
        if far:
            to = target[i] if i in target else held.pop(0)
            part = refs[i].at[:, 0] if i in column else refs[i]
            copies.append(pltpu.make_async_copy(part, to, sems.at[len(copies)]))
            operands.append(to)
        else:
            operands.append(refs[i])
    for copy in copies:
        copy.start()
    for copy in copies:
        copy.wait()
    kernel(*operands, *refs[count : count + outs])


def call(kernel, outs, args, far=(), keep=(), column=(), limit=LIMIT):
    where = [i in far for i in range(len(args))]
    spaces = [pltpu.HBM if w else pltpu.VMEM for w in where]
    every = (*outs, *(vmem(args[i].shape, args[i].dtype) for i in keep))
    return pl.pallas_call(
        functools.partial(staged, kernel, where, len(outs), tuple(keep), tuple(column)),
        out_shape=every,
        in_specs=[pl.BlockSpec(memory_space=s) for s in spaces],
        out_specs=(VM,) * len(every),
        scratch_shapes=[
            vmem(a.shape[:1] + a.shape[2:] if i in column else a.shape, a.dtype)
            for i, a in enumerate(args)
            if where[i] and i not in keep
        ]
        + [pltpu.SemaphoreType.DMA((max(1, sum(where)),))],
        compiler_params=pltpu.CompilerParams(vmem_limit_bytes=limit),
    )(*[pltpu.with_memory_space_constraint(a, s) for a, s in zip(args, spaces)])


def iota(shape, dim):
    return lax.broadcasted_iota(I32, shape, dim)


def split(x):
    one = x.astype(BF16)
    rest = x - one.astype(F32)
    two = rest.astype(BF16)
    three = (rest - two.astype(F32)).astype(BF16)
    return [one, two, three]


def fold(x):
    n = x.shape[0] // 3
    return x[:n] + (x[n : 2 * n] + x[2 * n :])


def onehot(index, size):
    return jnp.where(iota((size, index.shape[1]), 0) == index, 1.0, 0.0)


def dot(a, b):
    return lax.dot_general(a, b, (((1,), (0,)), ((), ())), preferred_element_type=F32)


def dot_nt(a, b):
    return lax.dot_general(a, b, (((1,), (1,)), ((), ())), preferred_element_type=F32)


def pick(table, hi, lo):
    rows, cols = table.shape
    parts = jnp.concatenate(split(table), 0)
    got = fold(dot(parts, onehot(lo, cols).astype(BF16)))
    return jnp.sum(got * onehot(hi, rows), axis=0, keepdims=True)


def spread(value, hi, lo, rows, cols):
    parts = [jnp.where(iota((rows, hi.shape[1]), 0) == hi, v.astype(F32), 0.0).astype(BF16) for v in split(value)]
    return fold(dot_nt(jnp.concatenate(parts, 0), onehot(lo, cols).astype(BF16)))


def pres_kernel(rhs, wts, cell, front, prod, pres, send):
    depth, width, long = pres.shape
    for z in range(depth):
        pres[z] = wts[0, z] * rhs[0, z] + wts[1, z] * rhs[1, z] + wts[2, z] * rhs[2, z]
    where = cell[...]
    table = pres[...].reshape(depth * width, long)
    value = prod[...] * pick(table, lax.div(where, long), lax.rem(where, long))
    both = jnp.concatenate([value, front[...].astype(F32), where.astype(F32)], 1)
    send[...] = jnp.broadcast_to(both[:, None], send.shape)


def is_right(level, axis="layer"):
    return (lax.axis_index(axis) >> level) % 2 == 1


def choose(level, mine, other, axis="layer"):
    right = is_right(level, axis)
    return (jnp.where(right, other, mine), jnp.where(right, mine, other))


def local_solve(rhs, upper, inv, tz):
    depth = len(rhs)
    y = [rhs[0] * inv[0]]
    for z in range(1, depth):
        y.append((rhs[z] + tz[z - 1] * y[-1]) * inv[z])
    for z in range(depth - 2, -1, -1):
        y[z] = y[z] + upper[z] * y[z + 1]
    return y


def factors(tz, store):
    depth = len(tz)
    gs, invs = ([], [])
    own = None
    for z in range(depth):
        own = store[z] if z == 0 else store[z] + gs[-1] * own
        invs.append(1.0 / (own + tz[z] if z < depth - 1 else own))
        gs.append(tz[z] * invs[-1])
    first = [invs[0]]
    for z in range(1, depth):
        first.append(tz[z - 1] * first[-1] * invs[z])
    final = [None] * depth
    final[-1] = invs[-1]
    for z in range(depth - 2, -1, -1):
        first[z] = first[z] + gs[z] * first[z + 1]
        final[z] = gs[z] * final[z + 1]
    return gs, invs, first, final, (first[0], first[-1], final[-1] + 1.0 / jnp.maximum(tz[-1], 1e-30))


def coef_kernel(tz, store, pres, answers, ends):
    depth = pres.shape[0]
    tzs = [tz[z] for z in range(depth)]
    gs, invs, first, final, coefs = factors(tzs, [store[z] for z in range(depth)])
    for z in range(depth):
        answers[z] = first[z]
        answers[depth + z] = final[z]
    y = local_solve([pres[z] for z in range(depth)], gs, invs, tzs)
    for i, value in enumerate((*coefs, y[0], y[-1], tzs[-1])):
        ends[i] = value


def pair(level, own, sib):
    af, af_ = choose(level, own[0], sib[0])
    c, c_ = choose(level, own[1], sib[1])
    b, b_ = choose(level, own[2], sib[2])
    return af, c, b, af_, c_, b_, 1.0 / (b + af_)


def join_coefs(level, own, sib):
    af, c, _, _, c_, b_, g = pair(level, own, sib)
    return (af - c * c * g, c * c_ * g, b_ - c_ * c_ * g)


def join_ends(level, own, sib, mine, other):
    _, c, _, _, c_, _, g = pair(level, own, sib)
    yf, yf_ = choose(level, mine[0], other[0])
    yl, yl_ = choose(level, mine[1], other[1])
    flux = g * (yl - yf_)
    return (yf - c * flux, yl_ + c_ * flux)


def join_kernel(level, own, sib, answers, out, face, more, one):
    depth, width, _ = more.shape
    depth = depth // 2
    _, c, _, _, c_, _, g = pair(level, own, sib)
    first, both, last = join_coefs(level, own, sib)
    yf, yl = join_ends(level, own, sib, (own[3], own[4]), (sib[3], sib[4]))
    out[0], out[1], out[2] = (first, both, last)
    out[3], out[4] = (yf, yl)
    lower = choose(level, own[5], sib[5])[1]
    out[5] = lower
    face[2] = lower
    right, later = (is_right(level), is_right(level + 1))
    face[0], face[1] = (jnp.where(later, first, last), jnp.where(later, yf, yl))
    cg, cg_ = (c * g, c_ * g)
    for z in range(depth):
        kf, kl = (answers[z], answers[depth + z])
        top = jnp.where(right, cg * kf, kf - cg * kl)
        bottom = jnp.where(right, kl - cg_ * kf, cg_ * kl)
        more[z] = top
        more[depth + z] = bottom
        one[z] = jnp.where(later, top, bottom)


def groups_of(levels):
    layers = lax.axis_size("layer")
    l = lax.axis_index("layer")
    base = lax.axis_index("tile") * layers
    out = [[base + l]]
    for level in range(levels):
        out.append([base + (((l >> level) ^ 1) << level) + i for i in range(1 << level)])
    return out


def front_kernel(recv, cell, prod, tables, inverse, send, held, sems):
    devices = recv.shape[0]
    count = recv.shape[2] // 3
    rows, length = inverse.shape
    lanes = 128
    chunks = sems.shape[0]
    wide = length // chunks
    cell, prod = (cell[...], prod[...])
    copies = [
        pltpu.make_async_copy(inverse.at[:, pl.ds(i * wide, wide)], held.at[:, pl.ds(i * wide, wide)], sems.at[i])
        for i in range(chunks)
    ]
    for copy in copies:
        copy.start()
    where, value = (cell, prod)
    depth, width, long = tables[-1].shape
    hi, lo = lax.div(where, long), lax.rem(where, long)
    stack = [t[k * depth : (k + 1) * depth].reshape(depth * width, long) for t in tables for k in range(t.shape[0] // depth)]
    parts = jnp.concatenate([p for table in stack for p in split(table)], 0)
    got = dot(parts, onehot(lo, long).astype(BF16))
    mask = onehot(hi, depth * width)
    n = 3 * depth * width
    found = [value * jnp.sum(fold(got[i * n : (i + 1) * n]) * mask, axis=0, keepdims=True) for i in range(len(stack))]
    total = jnp.zeros((length // lanes, lanes), F32)
    group = 8
    for first in range(0, devices, group):
        lefts, rights = ([], [])
        for d in range(first, first + group):
            term = recv[d, :, :count]
            index = recv[d, :, count : 2 * count].astype(I32)
            hi, lo = lax.div(index, lanes), lax.rem(index, lanes)
            hit = iota((length // lanes, count), 0) == hi
            lefts.append(jnp.concatenate([jnp.where(hit, v.astype(F32), 0.0).astype(BF16) for v in split(term)], 0))
            rights.append(onehot(lo, lanes).astype(BF16))
        total = total + fold(dot_nt(jnp.concatenate(lefts, 1), jnp.concatenate(rights, 1)))
    acc = jnp.zeros((rows, lanes), F32)
    for i in range(chunks):
        copies[i].wait()
        for r in range(i * wide // lanes, (i + 1) * wide // lanes):
            acc = acc + held[:, r * lanes : (r + 1) * lanes] * total[r : r + 1]
    parts = jnp.concatenate(split(acc), 1)
    out = dot_nt(jnp.ones((8, parts.shape[1]), BF16), parts)
    send[...] = jnp.broadcast_to(jnp.concatenate([out[0:1], value, *found], 1)[:, None], send.shape)


def gathered(values, rows_hot, lanes_hot, start, size, ext, parts):
    hot = lanes_hot[:, start : start + size]
    pieces = [hot * p for v in values for p in split(v)[:parts]]
    got = dot_nt(rows_hot[:, start : start + size], jnp.concatenate(pieces, 0))
    planes = []
    lanes = hot.shape[0]
    for i in range(len(values)):
        plane = got[:, i * parts * lanes : (i * parts + 1) * lanes]
        for k in range(1, parts):
            j = i * parts + k
            plane = plane + got[:, j * lanes : (j + 1) * lanes]
        planes.append(jnp.concatenate([plane[r : r + ext] for r in range(0, plane.shape[0], ext)], 1))
    return planes


def beside(centre, tx, ty):
    width, long = centre.shape
    row, col = (iota(centre.shape, 0), iota(centre.shape, 1))
    total = tx * jnp.where(row == width - 1, 0.0, pltpu.roll(centre, width - 1, 0))
    total = total + jnp.where(row == 0, 0.0, pltpu.roll(tx * centre, 1, 0))
    total = total + ty * jnp.where(col == long - 1, 0.0, pltpu.roll(centre, long - 1, 1))
    return total + jnp.where(col == 0, 0.0, pltpu.roll(ty * centre, 1, 1))


def tile_rows(first, last, one, two):
    odd = is_right(0, "tile")
    one[...] = jnp.where(odd, first, last)
    two[...] = jnp.where(odd, last, first)


def pressure_kernel(levels, *refs):
    (recv, terms, tz, store, pres), refs = (refs[:5], refs[5:])
    sib, refs = (refs[:levels], refs[levels:])
    far, refs = (refs[:5], refs[5:])
    (p, coupled_z, one, two), near_by, refs = (refs[:4], refs[4:9], refs[9:])
    rows_hot, lanes_hot, sol_hot, sol_row, sems = refs
    copies = [pltpu.make_async_copy(a, b, sems.at[i]) for i, (a, b) in enumerate(zip(far, near_by))]
    for copy in copies:
        copy.start()
    tx = near_by[0]
    depth, width, long = pres.shape
    rows = sol_hot.shape[0]
    count = terms.shape[2] // 3
    lanes = 128
    groups = groups_of(levels)
    at = 0
    layer = None
    for members in groups:
        for device in members:
            entry = terms[device]
            index = entry[:, count : 2 * count].astype(I32)
            cell = entry[:, 2 * count :].astype(I32)
            y, x = lax.rem(cell, long), lax.rem(lax.div(cell, long), width)
            here = pl.ds(at, count)
            rows_hot[:, here] = onehot(lax.div(y, lanes) * width + x, rows_hot.shape[0]).astype(BF16)
            lanes_hot[:, here] = onehot(lax.rem(y, lanes), lanes).astype(BF16)
            sol_hot[:, here] = onehot(lax.rem(index, rows), rows).astype(BF16)
            sol_row[:, here] = lax.div(index, rows)
            if layer is None:
                layer = lax.div(cell, long * width)
            at += count
    table = jnp.concatenate(split(recv[...].reshape(recv.shape[0], recv.shape[2])[:, :rows]), 0)
    sol = fold(dot(table, sol_hot[...]))
    sol = jnp.sum(jnp.where(iota(sol.shape, 0) == sol_row[...], sol, 0.0), axis=0, keepdims=True)

    def listed(group, column):
        at = rows + column * count
        return jnp.concatenate([recv[device][:, at : at + count] for device in group], 1)

    tzs = [tz[z] for z in range(depth)]
    gs, invs, first, final, coefs = factors(tzs, [store[z] for z in range(depth)])
    own = [coefs]
    value = listed(groups[0], 0) * sol[:, :count]
    values = [jnp.where(layer == z, value, 0.0) for z in range(depth)]
    change = gathered(values, rows_hot, lanes_hot, 0, count, width, 3)
    y = local_solve([pres[z] - change[z] for z in range(depth)], gs, invs, tzs)
    mine = (y[0], y[-1])
    steps = []
    start = count
    for level in range(levels):
        size = len(groups[level + 1]) * count
        top = level == levels - 1
        columns = [1 + 2 * level] if top else [1 + 2 * level, 2 + 2 * level]
        values = [listed(groups[level + 1], c) * sol[:, start : start + size] for c in columns]
        change = gathered(values, rows_hot, lanes_hot, start, size, width, 3)
        start += size
        if top:
            other = sib[level][1] - change[0]
            steps.append((mine, (other, other)))
        else:
            other = (sib[level][3] - change[0], sib[level][4] - change[1])
            steps.append((mine, other))
            mine = join_ends(level, own[level], sib[level], mine, other)
            own.append(join_coefs(level, own[level], sib[level]))
    above = below = jnp.zeros((width, long), F32)
    tzp = jnp.zeros((width, long), F32)
    place = lax.axis_index("layer")
    for level in range(levels - 1, -1, -1):
        mine, other = steps[level]
        yl, _ = choose(level, mine[1], other[1])
        _, yf_ = choose(level, mine[0], other[0])
        flux = yl - yf_
        if level == levels - 1:
            b, _ = choose(level, own[level][2], sib[level][0])
            _, af_ = choose(level, own[level][0], sib[level][0])
            g = 1.0 / (b + af_)
            before = sib[level][2]
        else:
            _, c, _, _, c_, _, g = pair(level, own[level], sib[level])
            flux = flux + c * above - c_ * below
            before = sib[level][5]
        tzp = jnp.where(place % (2 << level) == 1 << level, before, tzp)
        flux = g * flux
        right = is_right(level)
        above, below = (jnp.where(right, flux, above), jnp.where(right, below, -flux))
    values = [y[z] + first[z] * above + final[z] * below for z in range(depth)]
    is_last = place == (1 << levels) - 1
    for z in range(depth):
        p[z] = values[z]
        total = above + tzp * values[z] if z == 0 else tzs[z - 1] * values[z - 1]
        if z == depth - 1:
            coupled_z[z] = total + jnp.where(is_last, 0.0, below + tzs[z] * values[z])
        else:
            coupled_z[z] = total + tzs[z] * values[z + 1]
    for copy in copies:
        copy.wait()
    for z in range(depth):
        tile_rows(values[z][0:1], (tx[z] * values[z])[width - 1 :], one.at[z], two.at[z])


def search_kernel(p, coupled_z, one, two, tx, ty, tz, rhs, diag, binv, s, row_one, row_two, inner, outer):
    depth, width, _ = p.shape
    odd = is_right(0, "tile")
    right = is_right(0)
    row = iota(p.shape[1:], 0)
    for z in range(depth):
        centre = p[z]
        after = jnp.where(odd, two[z], one[z])
        before = jnp.where(odd, one[z], two[z])
        coupled = coupled_z[z] + beside(centre, tx[z], ty[z])
        coupled = coupled + jnp.where(row == 0, before, 0.0) + jnp.where(row == width - 1, tx[z] * after, 0.0)
        remain = [rhs[c, z] - diag[c, 0, z] * centre for c in range(3)]
        remain[0] = remain[0] + coupled
        for c in range(3):
            value = binv[c, 0, z] * remain[0] + binv[c, 1, z] * remain[1] + binv[c, 2, z] * remain[2]
            if c == 0:
                value = centre + value
            s[c, z] = value
            tile_rows(value[0:1], (tx[z] * value)[width - 1 :], row_one.at[c, z], row_two.at[c, z])
    for c in range(3):
        top, bottom = (s[c, 0], tz[depth - 1] * s[c, depth - 1])
        inner[c] = jnp.where(right, top, bottom)
        outer[c] = jnp.where(right, bottom, top)


def inner_kernel(s, diag, tz, tx, ty, image):
    depth = s.shape[1]
    for z in range(depth):
        for c in range(3):
            total = diag[c, 0, z] * s[0, z] + diag[c, 1, z] * s[1, z] + diag[c, 2, z] * s[2, z]
            total = total - beside(s[c, z], tx[z], ty[z])
            if z:
                total = total - tz[z - 1] * s[c, z - 1]
            if z < depth - 1:
                total = total - tz[z] * s[c, z + 1]
            image[c, z] = total


def image_kernel(part, row_one, row_two, inner, outer, rhs, tz, tx, image, send):
    depth, width = part.shape[1:3]
    right, odd = (is_right(0), is_right(0, "tile"))
    row = iota(part.shape[2:], 0)
    along = power = start = 0.0
    for z in range(depth):
        for c in range(3):
            value = part[c, z]
            if z == 0:
                value = value - jnp.where(right, inner[c], outer[c])
            if z == depth - 1:
                value = value - tz[z] * jnp.where(right, outer[c], inner[c])
            after = jnp.where(odd, row_two[c, z], row_one[c, z])
            before = jnp.where(odd, row_one[c, z], row_two[c, z])
            value = value - jnp.where(row == 0, before, 0.0) - jnp.where(row == width - 1, tx[z] * after, 0.0)
            image[c, z] = value
            given = rhs[c, z]
            along = along + value * given
            power = power + value * value
            start = start + given * given
    along, power, start = (jnp.sum(along), jnp.sum(power), jnp.sum(start))
    omega = along / jnp.where(power > 0.0, power, 1.0)
    square = cross = 0.0
    for z in range(depth):
        for c in range(3):
            value = image[c, z]
            left = rhs[c, z] - omega * value
            square = square + left * left
            cross = cross + left * value
    lane = iota((1, send.shape[2]), 1)
    out = jnp.zeros((1, send.shape[2]), F32)
    for i, value in enumerate((along, power, start, jnp.sum(square), jnp.sum(cross), omega)):
        out = jnp.where(lane == i, value, out)
    send[...] = jnp.broadcast_to(out[:, None], send.shape)


def finish_kernel(recv, s, image, rhs, update, lin_res, ratio):
    sums = recv[...].reshape(recv.shape[0], recv.shape[2])
    whole = jnp.sum(sums, axis=0, keepdims=True)
    omega = whole[:, 0:1] / whole[:, 1:2]
    shift = sums[:, 5:6] - omega
    square = sums[:, 3:4] + 2.0 * shift * sums[:, 4:5] + shift * shift * sums[:, 1:2]
    ratio[...] = jnp.sqrt(jnp.sum(square, axis=0, keepdims=True) / whole[:, 2:3])
    for c in range(3):
        for z in range(s.shape[1]):
            update[c, z] = omega * s[c, z]
            lin_res[c, z] = rhs[c, z] - omega * image[c, z]


def flip(x, level, axis="layer"):
    return lax.ppermute(x, axis, [(i, i ^ (1 << level)) for i in range(lax.axis_size(axis))])


def neighbour(x, axis="layer"):
    pairs = [(i, i + 1) for i in range(1, lax.axis_size(axis) - 1, 2)]
    return lax.ppermute(x, axis, pairs + [(j, i) for i, j in pairs])


def everywhere(x):
    return lax.all_to_all(x, BOTH, split_axis=0, concat_axis=0, tiled=True)


def shards(rhs, weights, block_diag, block_inv, tx, ty, tz, store, cell, front, prod, inverse):
    layers = lax.axis_size("layer")
    devices = lax.axis_size("tile") * layers
    levels = layers.bit_length() - 1
    depth, width, long = tx.shape
    count = cell.shape[0]
    rows = inverse.shape[0]
    lists = layers * count
    cell, front, prod = (cell.reshape(1, -1), front.reshape(1, -1), prod.reshape(1, -1))
    field = vmem(tx.shape)

    def planes(n):
        return vmem((n, width, long))

    pres, send = call(
        pres_kernel, (field, vmem((devices, 1, 3 * count))), (rhs, weights, cell, front, prod), far=range(5)
    )
    terms = everywhere(send)
    pres, tz, store = lax.optimization_barrier((pres, tz, store))
    answers, ends, tz_v, store_v = call(
        coef_kernel, (planes(2 * depth), planes(6)), (tz, store, pres), far=(0, 1), keep=(0, 1)
    )
    sib, tables = ([], [])
    last = answers
    for level in range(levels - 1):
        tables.append(answers)
        sib.append(flip(ends, level))
        ends, face, answers, last = call(
            functools.partial(join_kernel, level), (planes(6), planes(3), planes(2 * depth), field), (ends, sib[-1], answers)
        )
    tables.append(last)
    sib.append(flip(face, levels - 1))
    chunks = 8
    hbm_spec = pl.BlockSpec(memory_space=pltpu.HBM)
    terms, *tables = lax.optimization_barrier((terms, *tables))
    send = pl.pallas_call(
        front_kernel,
        out_shape=vmem((devices, 1, rows + 2 * levels * count)),
        in_specs=[VM, VM, VM, [VM] * len(tables), hbm_spec],
        out_specs=VM,
        scratch_shapes=[vmem(inverse.shape), pltpu.SemaphoreType.DMA((chunks,))],
        compiler_params=pltpu.CompilerParams(vmem_limit_bytes=LIMIT),
    )(terms, cell, prod, tables, pltpu.with_memory_space_constraint(inverse, pltpu.HBM))
    sol = everywhere(send)
    far = (tx, ty, rhs, block_diag, block_inv)
    args = (sol, terms, tz_v, store_v, pres, *sib)
    row3 = vmem((depth, 1, long))
    p, coupled_z, one, two, tx, ty, rhs, diag, binv = pl.pallas_call(
        functools.partial(pressure_kernel, levels),
        out_shape=(field, field, row3, row3) + tuple(vmem(a.shape) for a in far),
        in_specs=[VM] * len(args) + [hbm_spec] * len(far),
        out_specs=(VM,) * 9,
        scratch_shapes=[
            vmem((width * long // 128, lists), BF16),
            vmem((128, lists), BF16),
            vmem((rows, lists), BF16),
            vmem((1, lists), I32),
            pltpu.SemaphoreType.DMA((len(far),)),
        ],
        compiler_params=pltpu.CompilerParams(vmem_limit_bytes=LIMIT),
    )(
        *[pltpu.with_memory_space_constraint(a, pltpu.VMEM) for a in args],
        *[pltpu.with_memory_space_constraint(a, pltpu.HBM) for a in far],
    )
    one, two = (flip(one, 0, "tile"), neighbour(two, "tile"))
    row9 = vmem((3, depth, 1, long))
    plane3 = planes(3)
    s, row_one, row_two, inner, outer = call(
        search_kernel,
        (vmem(rhs.shape), row9, row9, plane3, plane3),
        (p, coupled_z, one, two, tx, ty, tz_v, rhs, diag, binv),
    )
    inner, outer = (flip(inner, 0), neighbour(outer))
    row_one, row_two = (flip(row_one, 0, "tile"), neighbour(row_two, "tile"))
    (part,) = call(inner_kernel, (vmem(rhs.shape),), (s, diag, tz_v, tx, ty))
    image, send = call(
        image_kernel,
        (vmem(rhs.shape), vmem((devices, 1, 128))),
        (part, row_one, row_two, inner, outer, rhs, tz_v, tx),
    )
    sums = everywhere(send)
    update, lin_res, ratio = call(
        finish_kernel, (hbm(rhs.shape), hbm(rhs.shape), hbm((1, 1))), (sums, s, image, rhs)
    )
    return (update, lin_res, ratio.reshape(()))


def solution(mesh):
    return jax.shard_map(
        shards,
        mesh=mesh,
        in_specs=(
            P(None, "layer", "tile", None),
            P(None, "layer", "tile", None),
            P(None, None, "layer", "tile", None),
            P(None, None, "layer", "tile", None),
            P("layer", "tile", None),
            P("layer", "tile", None),
            P("layer", "tile", None),
            P("layer", "tile", None),
            P(("tile", "layer")),
            P(("tile", "layer")),
            P(("tile", "layer")),
            P(("tile", "layer"), None),
        ),
        out_specs=(P(None, "layer", "tile", None), P(None, "layer", "tile", None), P()),
        check_vma=False,
    )
```

```python
import functools
import jax
import jax.numpy as jnp
from jax import lax
from jax.experimental import pallas as pl
from jax.experimental.pallas import tpu as pltpu
from jax.sharding import PartitionSpec as P

F32 = jnp.float32
BF16 = jnp.bfloat16
I32 = jnp.int32
BOTH = ("tile", "layer")
VM = pl.BlockSpec(memory_space=pltpu.VMEM)
LIMIT = 16 << 20
PARTS = 2


def hbm(shape):
    return jax.ShapeDtypeStruct(shape, F32)


def vmem(shape, dtype=F32):
    return pltpu.VMEM(shape, dtype)


def staged(kernel, where, outs, kept, column, *refs):
    count, sems = (len(where), refs[-1])
    held = list(refs[count + outs + len(kept) : -1])
    target = dict(zip(kept, refs[count + outs : count + outs + len(kept)]))
    operands, copies = ([], [])
    for i, far in enumerate(where):
        if far:
            to = target[i] if i in target else held.pop(0)
            part = refs[i].at[:, 0] if i in column else refs[i]
            copies.append(pltpu.make_async_copy(part, to, sems.at[len(copies)]))
            operands.append(to)
        else:
            operands.append(refs[i])
    for copy in copies:
        copy.start()
    for copy in copies:
        copy.wait()
    kernel(*operands, *refs[count : count + outs])


def call(kernel, outs, args, far=(), keep=(), column=(), limit=LIMIT):
    where = [i in far for i in range(len(args))]
    spaces = [pltpu.HBM if w else pltpu.VMEM for w in where]
    every = (*outs, *(vmem(args[i].shape, args[i].dtype) for i in keep))
    return pl.pallas_call(
        functools.partial(staged, kernel, where, len(outs), tuple(keep), tuple(column)),
        out_shape=every,
        in_specs=[pl.BlockSpec(memory_space=s) for s in spaces],
        out_specs=(VM,) * len(every),
        scratch_shapes=[
            vmem(a.shape[:1] + a.shape[2:] if i in column else a.shape, a.dtype)
            for i, a in enumerate(args)
            if where[i] and i not in keep
        ]
        + [pltpu.SemaphoreType.DMA((max(1, sum(where)),))],
        compiler_params=pltpu.CompilerParams(vmem_limit_bytes=limit),
    )(*[pltpu.with_memory_space_constraint(a, s) for a, s in zip(args, spaces)])


def nothing(*refs):
    pass


def load(*args):
    every = range(len(args))
    return call(nothing, (), args, far=every, keep=every, limit=1 << 20)


def iota(shape, dim):
    return lax.broadcasted_iota(I32, shape, dim)


def split(x):
    one = x.astype(BF16)
    rest = x - one.astype(F32)
    two = rest.astype(BF16)
    three = (rest - two.astype(F32)).astype(BF16)
    return [one, two, three]


def fold(x, parts=3):
    n = x.shape[0] // parts
    total = x[(parts - 1) * n :]
    for i in range(parts - 2, -1, -1):
        total = x[i * n : (i + 1) * n] + total
    return total


def onehot(index, size):
    return jnp.where(iota((size, index.shape[1]), 0) == index, 1.0, 0.0)


def dot(a, b):
    return lax.dot_general(a, b, (((1,), (0,)), ((), ())), preferred_element_type=F32)


def dot_nt(a, b):
    return lax.dot_general(a, b, (((1,), (1,)), ((), ())), preferred_element_type=F32)


def pick(tables, hi, hot):
    rows = tables[0].shape[0]
    parts = jnp.concatenate([p for table in tables for p in split(table)[:PARTS]], 0)
    got = dot(parts, hot)
    mask = onehot(hi, rows)
    n = PARTS * rows
    return [jnp.sum(fold(got[i * n : (i + 1) * n], PARTS) * mask, axis=0, keepdims=True) for i in range(len(tables))]


def pres_kernel(cell_in, front_in, prod_in, rhs_in, wts_in, tz_in, store_in, pres, send, ends, *scratch):
    (cell, front, prod, rhs, wts, tz, store), sems = scratch[:-1], scratch[-1]
    pairs = ((cell_in, cell), (front_in, front), (prod_in, prod), (rhs_in, rhs), (wts_in, wts), (tz_in, tz), (store_in, store))
    copies = [pltpu.make_async_copy(a, b, sems.at[i]) for i, (a, b) in enumerate(pairs)]
    for copy in copies:
        copy.start()
    for copy in copies[:3]:
        copy.wait()
    depth, width, long = pres.shape
    where = cell[...]
    hot = onehot(lax.rem(where, long), long).astype(BF16)
    for copy in copies[3:]:
        copy.wait()
    for z in range(depth):
        pres[z] = wts[0, z] * rhs[0, z] + wts[1, z] * rhs[1, z] + wts[2, z] * rhs[2, z]
    (found,) = pick([pres[...].reshape(depth * width, long)], lax.div(where, long), hot)
    both = jnp.concatenate([prod[...] * found, front[...].astype(F32), where.astype(F32)], 1)
    send[...] = jnp.broadcast_to(both[:, None], send.shape)
    tzs = [tz[z] for z in range(depth)]
    gs, invs, _, _, coefs = factors(tzs, [store[z] for z in range(depth)])
    y = local_solve([pres[z] for z in range(depth)], gs, invs, tzs)
    for i, value in enumerate((*coefs, y[0], y[-1], tzs[-1])):
        ends[i] = value


def is_right(level, axis="layer"):
    return (lax.axis_index(axis) >> level) % 2 == 1


def choose(level, mine, other, axis="layer"):
    right = is_right(level, axis)
    return (jnp.where(right, other, mine), jnp.where(right, mine, other))


def local_solve(rhs, upper, inv, tz):
    depth = len(rhs)
    y = [rhs[0] * inv[0]]
    for z in range(1, depth):
        y.append((rhs[z] + tz[z - 1] * y[-1]) * inv[z])
    for z in range(depth - 2, -1, -1):
        y[z] = y[z] + upper[z] * y[z + 1]
    return y


def factors(tz, store):
    depth = len(tz)
    gs, invs = ([], [])
    own = None
    for z in range(depth):
        own = store[z] if z == 0 else store[z] + gs[-1] * own
        invs.append(1.0 / (own + tz[z] if z < depth - 1 else own))
        gs.append(tz[z] * invs[-1])
    first = [invs[0]]
    for z in range(1, depth):
        first.append(tz[z - 1] * first[-1] * invs[z])
    final = [None] * depth
    final[-1] = invs[-1]
    for z in range(depth - 2, -1, -1):
        first[z] = first[z] + gs[z] * first[z + 1]
        final[z] = gs[z] * final[z + 1]
    return gs, invs, first, final, (first[0], first[-1], final[-1] + 1.0 / jnp.maximum(tz[-1], 1e-30))


def pair(level, own, sib):
    af, af_ = choose(level, own[0], sib[0])
    c, c_ = choose(level, own[1], sib[1])
    b, b_ = choose(level, own[2], sib[2])
    return af, c, b, af_, c_, b_, 1.0 / (b + af_)


def join_coefs(level, own, sib):
    af, c, _, _, c_, b_, g = pair(level, own, sib)
    return (af - c * c * g, c * c_ * g, b_ - c_ * c_ * g)


def join_ends(level, own, sib, mine, other):
    _, c, _, _, c_, _, g = pair(level, own, sib)
    yf, yf_ = choose(level, mine[0], other[0])
    yl, yl_ = choose(level, mine[1], other[1])
    flux = g * (yl - yf_)
    return (yf - c * flux, yl_ + c_ * flux)


def first_join_kernel(own, sib, tz, store, out, face, more, one, answers):
    depth = tz.shape[0]
    _, _, first, final, _ = factors([tz[z] for z in range(depth)], [store[z] for z in range(depth)])
    for z in range(depth):
        answers[z] = first[z]
        answers[depth + z] = final[z]
    join_kernel(0, own, sib, answers, out, face, more, one)


def join_kernel(level, own, sib, answers, out, face, more, one):
    depth, width, _ = more.shape
    depth = depth // 2
    _, c, _, _, c_, _, g = pair(level, own, sib)
    first, both, last = join_coefs(level, own, sib)
    yf, yl = join_ends(level, own, sib, (own[3], own[4]), (sib[3], sib[4]))
    out[0], out[1], out[2] = (first, both, last)
    out[3], out[4] = (yf, yl)
    lower = choose(level, own[5], sib[5])[1]
    out[5] = lower
    face[2] = lower
    right, later = (is_right(level), is_right(level + 1))
    face[0], face[1] = (jnp.where(later, first, last), jnp.where(later, yf, yl))
    cg, cg_ = (c * g, c_ * g)
    for z in range(depth):
        kf, kl = (answers[z], answers[depth + z])
        top = jnp.where(right, cg * kf, kf - cg * kl)
        bottom = jnp.where(right, kl - cg_ * kf, cg_ * kl)
        more[z] = top
        more[depth + z] = bottom
        one[z] = jnp.where(later, top, bottom)


def groups_of(levels):
    layers = lax.axis_size("layer")
    l = lax.axis_index("layer")
    base = lax.axis_index("tile") * layers
    out = [[base + l]]
    for level in range(levels):
        out.append([base + (((l >> level) ^ 1) << level) + i for i in range(1 << level)])
    return out


def front_kernel(recv, cell, prod, tables, inverse, send, held, sems):
    devices = recv.shape[0]
    count = recv.shape[2] // 3
    rows, length = inverse.shape
    lanes = 128
    chunks = sems.shape[0]
    wide = length // chunks
    cell, prod = (cell[...], prod[...])
    copies = [
        pltpu.make_async_copy(inverse.at[:, pl.ds(i * wide, wide)], held.at[:, pl.ds(i * wide, wide)], sems.at[i])
        for i in range(chunks)
    ]
    for copy in copies:
        copy.start()
    where, value = (cell, prod)
    depth, width, long = tables[-1].shape
    hi, lo = lax.div(where, long), lax.rem(where, long)
    stack = [t[k * depth : (k + 1) * depth].reshape(depth * width, long) for t in tables for k in range(t.shape[0] // depth)]
    found = [value * f for f in pick(stack, hi, onehot(lo, long).astype(BF16))]
    total = jnp.zeros((length // lanes, lanes), F32)
    group = 8
    for first in range(0, devices, group):
        lefts, rights = ([], [])
        for d in range(first, first + group):
            term = recv[d, :, :count]
            index = recv[d, :, count : 2 * count].astype(I32)
            hi, lo = lax.div(index, lanes), lax.rem(index, lanes)
            hit = iota((length // lanes, count), 0) == hi
            lefts.append(jnp.concatenate([jnp.where(hit, v.astype(F32), 0.0).astype(BF16) for v in split(term)], 0))
            rights.append(onehot(lo, lanes).astype(BF16))
        total = total + fold(dot_nt(jnp.concatenate(lefts, 1), jnp.concatenate(rights, 1)))
    acc = jnp.zeros((rows, lanes), F32)
    for i in range(chunks):
        copies[i].wait()
        for r in range(i * wide // lanes, (i + 1) * wide // lanes):
            acc = acc + held[:, r * lanes : (r + 1) * lanes] * total[r : r + 1]
    parts = jnp.concatenate(split(acc), 1)
    out = dot_nt(jnp.ones((8, parts.shape[1]), BF16), parts)
    send[...] = jnp.broadcast_to(jnp.concatenate([out[0:1], value, *found], 1)[:, None], send.shape)


def gathered(values, rows_hot, lanes_hot, start, size, ext, parts):
    hot = lanes_hot[:, start : start + size]
    pieces = [hot * p for v in values for p in split(v)[:parts]]
    got = dot_nt(rows_hot[:, start : start + size], jnp.concatenate(pieces, 0))
    planes = []
    lanes = hot.shape[0]
    for i in range(len(values)):
        plane = got[:, i * parts * lanes : (i * parts + 1) * lanes]
        for k in range(1, parts):
            j = i * parts + k
            plane = plane + got[:, j * lanes : (j + 1) * lanes]
        planes.append(jnp.concatenate([plane[r : r + ext] for r in range(0, plane.shape[0], ext)], 1))
    return planes


def beside(centre, tx, ty):
    width, long = centre.shape
    row, col = (iota(centre.shape, 0), iota(centre.shape, 1))
    total = tx * jnp.where(row == width - 1, 0.0, pltpu.roll(centre, width - 1, 0))
    total = total + jnp.where(row == 0, 0.0, pltpu.roll(tx * centre, 1, 0))
    total = total + ty * jnp.where(col == long - 1, 0.0, pltpu.roll(centre, long - 1, 1))
    return total + jnp.where(col == 0, 0.0, pltpu.roll(ty * centre, 1, 1))


def tile_rows(first, last, one, two):
    odd = is_right(0, "tile")
    one[...] = jnp.where(odd, first, last)
    two[...] = jnp.where(odd, last, first)


def pressure_kernel(levels, *refs):
    (recv, terms, pres), refs = (refs[:3], refs[3:])
    sib, refs = (refs[:levels], refs[levels:])
    far, refs = (refs[:3], refs[3:])
    (p, coupled_z, one, two), near_by, refs = (refs[:4], refs[4:7], refs[7:])
    rows_hot, lanes_hot, sol_hot, sol_row, sems = refs
    copies = [pltpu.make_async_copy(a, b, sems.at[i]) for i, (a, b) in enumerate(zip(far, near_by))]
    for copy in copies:
        copy.start()
    tz, store, tx = near_by
    depth, width, long = pres.shape
    rows = sol_hot.shape[0]
    count = terms.shape[2] // 3
    lanes = 128
    groups = groups_of(levels)
    at = 0
    layer = None
    for members in groups:
        for device in members:
            entry = terms[device]
            index = entry[:, count : 2 * count].astype(I32)
            cell = entry[:, 2 * count :].astype(I32)
            y, x = lax.rem(cell, long), lax.rem(lax.div(cell, long), width)
            here = pl.ds(at, count)
            rows_hot[:, here] = onehot(lax.div(y, lanes) * width + x, rows_hot.shape[0]).astype(BF16)
            lanes_hot[:, here] = onehot(lax.rem(y, lanes), lanes).astype(BF16)
            sol_hot[:, here] = onehot(lax.rem(index, rows), rows).astype(BF16)
            sol_row[:, here] = lax.div(index, rows)
            if layer is None:
                layer = lax.div(cell, long * width)
            at += count
    table = jnp.concatenate(split(recv[...].reshape(recv.shape[0], recv.shape[2])[:, :rows]), 0)
    sol = fold(dot(table, sol_hot[...]))
    sol = jnp.sum(jnp.where(iota(sol.shape, 0) == sol_row[...], sol, 0.0), axis=0, keepdims=True)

    def listed(group, column):
        at = rows + column * count
        return jnp.concatenate([recv[device][:, at : at + count] for device in group], 1)

    for copy in copies:
        copy.wait()
    tzs = [tz[z] for z in range(depth)]
    gs, invs, first, final, coefs = factors(tzs, [store[z] for z in range(depth)])
    own = [coefs]
    value = listed(groups[0], 0) * sol[:, :count]
    values = [jnp.where(layer == z, value, 0.0) for z in range(depth)]
    change = gathered(values, rows_hot, lanes_hot, 0, count, width, PARTS)
    y = local_solve([pres[z] - change[z] for z in range(depth)], gs, invs, tzs)
    mine = (y[0], y[-1])
    steps = []
    start = count
    for level in range(levels):
        size = len(groups[level + 1]) * count
        top = level == levels - 1
        columns = [1 + 2 * level] if top else [1 + 2 * level, 2 + 2 * level]
        values = [listed(groups[level + 1], c) * sol[:, start : start + size] for c in columns]
        change = gathered(values, rows_hot, lanes_hot, start, size, width, PARTS)
        start += size
        if top:
            other = sib[level][1] - change[0]
            steps.append((mine, (other, other)))
        else:
            other = (sib[level][3] - change[0], sib[level][4] - change[1])
            steps.append((mine, other))
            mine = join_ends(level, own[level], sib[level], mine, other)
            own.append(join_coefs(level, own[level], sib[level]))
    above = below = jnp.zeros((width, long), F32)
    tzp = jnp.zeros((width, long), F32)
    place = lax.axis_index("layer")
    for level in range(levels - 1, -1, -1):
        mine, other = steps[level]
        yl, _ = choose(level, mine[1], other[1])
        _, yf_ = choose(level, mine[0], other[0])
        flux = yl - yf_
        if level == levels - 1:
            b, _ = choose(level, own[level][2], sib[level][0])
            _, af_ = choose(level, own[level][0], sib[level][0])
            g = 1.0 / (b + af_)
            before = sib[level][2]
        else:
            _, c, _, _, c_, _, g = pair(level, own[level], sib[level])
            flux = flux + c * above - c_ * below
            before = sib[level][5]
        tzp = jnp.where(place % (2 << level) == 1 << level, before, tzp)
        flux = g * flux
        right = is_right(level)
        above, below = (jnp.where(right, flux, above), jnp.where(right, below, -flux))
    values = [y[z] + first[z] * above + final[z] * below for z in range(depth)]
    is_last = place == (1 << levels) - 1
    for z in range(depth):
        p[z] = values[z]
        total = above + tzp * values[z] if z == 0 else tzs[z - 1] * values[z - 1]
        if z == depth - 1:
            coupled_z[z] = total + jnp.where(is_last, 0.0, below + tzs[z] * values[z])
        else:
            coupled_z[z] = total + tzs[z] * values[z + 1]
    for z in range(depth):
        tile_rows(values[z][0:1], (tx[z] * values[z])[width - 1 :], one.at[z], two.at[z])


def search_kernel(p, coupled_z, one, two, tx, ty, tz, rhs, diag, binv, s, row_one, row_two, inner, outer):
    depth, width, _ = p.shape
    odd = is_right(0, "tile")
    right = is_right(0)
    row = iota(p.shape[1:], 0)
    for z in range(depth):
        centre = p[z]
        after = jnp.where(odd, two[z], one[z])
        before = jnp.where(odd, one[z], two[z])
        coupled = coupled_z[z] + beside(centre, tx[z], ty[z])
        coupled = coupled + jnp.where(row == 0, before, 0.0) + jnp.where(row == width - 1, tx[z] * after, 0.0)
        remain = [rhs[c, z] - diag[c, 0, z] * centre for c in range(3)]
        remain[0] = remain[0] + coupled
        for c in range(3):
            value = binv[c, 0, z] * remain[0] + binv[c, 1, z] * remain[1] + binv[c, 2, z] * remain[2]
            if c == 0:
                value = centre + value
            s[c, z] = value
            tile_rows(value[0:1], (tx[z] * value)[width - 1 :], row_one.at[c, z], row_two.at[c, z])
    for c in range(3):
        top, bottom = (s[c, 0], tz[depth - 1] * s[c, depth - 1])
        inner[c] = jnp.where(right, top, bottom)
        outer[c] = jnp.where(right, bottom, top)


def inner_kernel(s, diag, tz, tx, ty, image):
    depth = s.shape[1]
    for z in range(depth):
        for c in range(3):
            total = diag[c, 0, z] * s[0, z] + diag[c, 1, z] * s[1, z] + diag[c, 2, z] * s[2, z]
            total = total - beside(s[c, z], tx[z], ty[z])
            if z:
                total = total - tz[z - 1] * s[c, z - 1]
            if z < depth - 1:
                total = total - tz[z] * s[c, z + 1]
            image[c, z] = total


def image_kernel(part, row_one, row_two, inner, outer, rhs, tz, tx, image, send):
    depth, width = part.shape[1:3]
    right, odd = (is_right(0), is_right(0, "tile"))
    row = iota(part.shape[2:], 0)
    along = power = start = 0.0
    for z in range(depth):
        for c in range(3):
            value = part[c, z]
            if z == 0:
                value = value - jnp.where(right, inner[c], outer[c])
            if z == depth - 1:
                value = value - tz[z] * jnp.where(right, outer[c], inner[c])
            after = jnp.where(odd, row_two[c, z], row_one[c, z])
            before = jnp.where(odd, row_one[c, z], row_two[c, z])
            value = value - jnp.where(row == 0, before, 0.0) - jnp.where(row == width - 1, tx[z] * after, 0.0)
            image[c, z] = value
            given = rhs[c, z]
            along = along + value * given
            power = power + value * value
            start = start + given * given
    along, power, start = (jnp.sum(along), jnp.sum(power), jnp.sum(start))
    omega = along / jnp.where(power > 0.0, power, 1.0)
    square = cross = 0.0
    for z in range(depth):
        for c in range(3):
            value = image[c, z]
            left = rhs[c, z] - omega * value
            square = square + left * left
            cross = cross + left * value
    lane = iota((1, send.shape[2]), 1)
    out = jnp.zeros((1, send.shape[2]), F32)
    for i, value in enumerate((along, power, start, jnp.sum(square), jnp.sum(cross), omega)):
        out = jnp.where(lane == i, value, out)
    send[...] = jnp.broadcast_to(out[:, None], send.shape)


def finish_kernel(recv, s, image, rhs, update, lin_res, ratio):
    sums = recv[...].reshape(recv.shape[0], recv.shape[2])
    whole = jnp.sum(sums, axis=0, keepdims=True)
    omega = whole[:, 0:1] / whole[:, 1:2]
    shift = sums[:, 5:6] - omega
    square = sums[:, 3:4] + 2.0 * shift * sums[:, 4:5] + shift * shift * sums[:, 1:2]
    ratio[...] = jnp.sqrt(jnp.sum(square, axis=0, keepdims=True) / whole[:, 2:3])
    for c in range(3):
        for z in range(s.shape[1]):
            update[c, z] = omega * s[c, z]
            lin_res[c, z] = rhs[c, z] - omega * image[c, z]


def flip(x, level, axis="layer"):
    return lax.ppermute(x, axis, [(i, i ^ (1 << level)) for i in range(lax.axis_size(axis))])


def neighbour(x, axis="layer"):
    pairs = [(i, i + 1) for i in range(1, lax.axis_size(axis) - 1, 2)]
    return lax.ppermute(x, axis, pairs + [(j, i) for i, j in pairs])


def everywhere(x):
    return lax.all_to_all(x, BOTH, split_axis=0, concat_axis=0, tiled=True)


def shards(rhs, weights, block_diag, block_inv, tx, ty, tz, store, cell, front, prod, inverse):
    layers = lax.axis_size("layer")
    devices = lax.axis_size("tile") * layers
    levels = layers.bit_length() - 1
    depth, width, long = tx.shape
    count = cell.shape[0]
    rows = inverse.shape[0]
    lists = layers * count
    cell, front, prod = (cell.reshape(1, -1), front.reshape(1, -1), prod.reshape(1, -1))
    field = vmem(tx.shape)

    def planes(n):
        return vmem((n, width, long))

    hbm_spec = pl.BlockSpec(memory_space=pltpu.HBM)
    given = (cell, front, prod, rhs, weights, tz, store)
    pres, send, ends = pl.pallas_call(
        pres_kernel,
        out_shape=(field, vmem((devices, 1, 3 * count)), planes(6)),
        in_specs=[hbm_spec] * len(given),
        out_specs=(VM,) * 3,
        scratch_shapes=[vmem(a.shape, a.dtype) for a in given] + [pltpu.SemaphoreType.DMA((len(given),))],
        compiler_params=pltpu.CompilerParams(vmem_limit_bytes=LIMIT),
    )(*[pltpu.with_memory_space_constraint(a, pltpu.HBM) for a in given])
    terms = everywhere(send)
    sib, tables = ([], [])
    for level in range(levels - 1):
        sib.append(flip(ends, level))
        outs = (planes(6), planes(3), planes(2 * depth), field)
        if level == 0:
            ends, face, more, last, answers = call(
                first_join_kernel, (*outs, planes(2 * depth)), (ends, sib[-1], tz, store), far=(2, 3)
            )
        else:
            ends, face, more, last = call(functools.partial(join_kernel, level), outs, (ends, sib[-1], answers))
        tables.append(answers)
        answers = more
    tables.append(last)
    sib.append(flip(face, levels - 1))
    chunks = 8
    terms, *tables = lax.optimization_barrier((terms, *tables))
    send = pl.pallas_call(
        front_kernel,
        out_shape=vmem((devices, 1, rows + 2 * levels * count)),
        in_specs=[VM, VM, VM, [VM] * len(tables), hbm_spec],
        out_specs=VM,
        scratch_shapes=[vmem(inverse.shape), pltpu.SemaphoreType.DMA((chunks,))],
        compiler_params=pltpu.CompilerParams(vmem_limit_bytes=LIMIT),
    )(terms, cell, prod, tables, pltpu.with_memory_space_constraint(inverse, pltpu.HBM))
    sol = everywhere(send)
    far = (tz, store, tx)
    args = (sol, terms, pres, *sib)
    row3 = vmem((depth, 1, long))
    p, coupled_z, one, two, tz, _, tx = pl.pallas_call(
        functools.partial(pressure_kernel, levels),
        out_shape=(field, field, row3, row3) + tuple(vmem(a.shape) for a in far),
        in_specs=[VM] * len(args) + [hbm_spec] * len(far),
        out_specs=(VM,) * 7,
        scratch_shapes=[
            vmem((width * long // 128, lists), BF16),
            vmem((128, lists), BF16),
            vmem((rows, lists), BF16),
            vmem((1, lists), I32),
            pltpu.SemaphoreType.DMA((len(far),)),
        ],
        compiler_params=pltpu.CompilerParams(vmem_limit_bytes=LIMIT),
    )(
        *[pltpu.with_memory_space_constraint(a, pltpu.VMEM) for a in args],
        *[pltpu.with_memory_space_constraint(a, pltpu.HBM) for a in far],
    )
    ty, rhs, diag, binv = load(ty, rhs, block_diag, block_inv)
    one, two = (flip(one, 0, "tile"), neighbour(two, "tile"))
    row9 = vmem((3, depth, 1, long))
    plane3 = planes(3)
    s, row_one, row_two, inner, outer = call(
        search_kernel,
        (vmem(rhs.shape), row9, row9, plane3, plane3),
        (p, coupled_z, one, two, tx, ty, tz, rhs, diag, binv),
    )
    outer, inner = (neighbour(outer), flip(inner, 0))
    row_one, row_two = (flip(row_one, 0, "tile"), neighbour(row_two, "tile"))
    (part,) = call(inner_kernel, (vmem(rhs.shape),), (s, diag, tz, tx, ty))
    image, send = call(
        image_kernel,
        (vmem(rhs.shape), vmem((devices, 1, 128))),
        (part, row_one, row_two, inner, outer, rhs, tz, tx),
    )
    sums = everywhere(send)
    update, lin_res, ratio = call(
        finish_kernel, (hbm(rhs.shape), hbm(rhs.shape), hbm((1, 1))), (sums, s, image, rhs)
    )
    return (update, lin_res, ratio.reshape(()))


def solution(mesh):
    return jax.shard_map(
        shards,
        mesh=mesh,
        in_specs=(
            P(None, "layer", "tile", None),
            P(None, "layer", "tile", None),
            P(None, None, "layer", "tile", None),
            P(None, None, "layer", "tile", None),
            P("layer", "tile", None),
            P("layer", "tile", None),
            P("layer", "tile", None),
            P("layer", "tile", None),
            P(("tile", "layer")),
            P(("tile", "layer")),
            P(("tile", "layer")),
            P(("tile", "layer"), None),
        ),
        out_specs=(P(None, "layer", "tile", None), P(None, "layer", "tile", None), P()),
        check_vma=False,
    )
```

```python
import functools
import jax
import jax.numpy as jnp
from jax import lax
from jax.experimental import pallas as pl
from jax.experimental.pallas import tpu as pltpu
from jax.sharding import PartitionSpec as P

F32 = jnp.float32
BF16 = jnp.bfloat16
I32 = jnp.int32
BOTH = ("tile", "layer")
VM = pl.BlockSpec(memory_space=pltpu.VMEM)
LIMIT = 16 << 20
PARTS = 2


def hbm(shape):
    return jax.ShapeDtypeStruct(shape, F32)


def vmem(shape, dtype=F32):
    return pltpu.VMEM(shape, dtype)


def staged(kernel, where, outs, kept, column, *refs):
    count, sems = (len(where), refs[-1])
    held = list(refs[count + outs + len(kept) : -1])
    target_count = sum(where) - len(kept)
    held, extra = (held[:target_count], held[target_count:])
    target = dict(zip(kept, refs[count + outs : count + outs + len(kept)]))
    operands, copies = ([], [])
    for i, far in enumerate(where):
        if far:
            to = target[i] if i in target else held.pop(0)
            part = refs[i].at[:, 0] if i in column else refs[i]
            copies.append(pltpu.make_async_copy(part, to, sems.at[len(copies)]))
            operands.append(to)
        else:
            operands.append(refs[i])
    for copy in copies:
        copy.start()
    for copy in copies:
        copy.wait()
    kernel(*operands, *refs[count : count + outs], *extra)


def call(kernel, outs, args, far=(), keep=(), column=(), scratch=(), limit=LIMIT):
    where = [i in far for i in range(len(args))]
    spaces = [pltpu.HBM if w else pltpu.VMEM for w in where]
    every = (*outs, *(vmem(args[i].shape, args[i].dtype) for i in keep))
    return pl.pallas_call(
        functools.partial(staged, kernel, where, len(outs), tuple(keep), tuple(column)),
        out_shape=every,
        in_specs=[pl.BlockSpec(memory_space=s) for s in spaces],
        out_specs=(VM,) * len(every),
        scratch_shapes=[
            vmem(a.shape[:1] + a.shape[2:] if i in column else a.shape, a.dtype)
            for i, a in enumerate(args)
            if where[i] and i not in keep
        ]
        + [*scratch, pltpu.SemaphoreType.DMA((max(1, sum(where)),))],
        compiler_params=pltpu.CompilerParams(vmem_limit_bytes=limit),
    )(*[pltpu.with_memory_space_constraint(a, s) for a, s in zip(args, spaces)])


def iota(shape, dim):
    return lax.broadcasted_iota(I32, shape, dim)


def split(x):
    one = x.astype(BF16)
    rest = x - one.astype(F32)
    two = rest.astype(BF16)
    three = (rest - two.astype(F32)).astype(BF16)
    return [one, two, three]


def fold(x, parts=3):
    n = x.shape[0] // parts
    total = x[(parts - 1) * n :]
    for i in range(parts - 2, -1, -1):
        total = x[i * n : (i + 1) * n] + total
    return total


def onehot(index, size):
    return jnp.where(iota((size, index.shape[1]), 0) == index, 1.0, 0.0)


def dot(a, b):
    return lax.dot_general(a, b, (((1,), (0,)), ((), ())), preferred_element_type=F32)


def dot_nt(a, b):
    return lax.dot_general(a, b, (((1,), (1,)), ((), ())), preferred_element_type=F32)


def pick(tables, hi, hot):
    rows = tables[0].shape[0]
    parts = jnp.concatenate([p for table in tables for p in split(table)[:PARTS]], 0)
    got = dot(parts, hot)
    mask = onehot(hi, rows)
    n = PARTS * rows
    return [jnp.sum(fold(got[i * n : (i + 1) * n], PARTS) * mask, axis=0, keepdims=True) for i in range(len(tables))]


def pres_kernel(cell_in, front_in, prod_in, rhs_in, wts_in, tz_in, store_in, pres, send, ends, *scratch):
    (cell, front, prod, rhs, wts, tz, store), sems = scratch[:-1], scratch[-1]
    pairs = ((cell_in, cell), (front_in, front), (prod_in, prod), (rhs_in, rhs), (wts_in, wts), (tz_in, tz), (store_in, store))
    copies = [pltpu.make_async_copy(a, b, sems.at[i]) for i, (a, b) in enumerate(pairs)]
    for copy in copies:
        copy.start()
    for copy in copies[:3]:
        copy.wait()
    depth, width, long = pres.shape
    where = cell[...]
    hot = onehot(lax.rem(where, long), long).astype(BF16)
    for copy in copies[3:]:
        copy.wait()
    for z in range(depth):
        pres[z] = wts[0, z] * rhs[0, z] + wts[1, z] * rhs[1, z] + wts[2, z] * rhs[2, z]
    (found,) = pick([pres[...].reshape(depth * width, long)], lax.div(where, long), hot)
    both = jnp.concatenate([prod[...] * found, front[...].astype(F32), where.astype(F32)], 1)
    send[...] = jnp.broadcast_to(both[:, None], send.shape)
    tzs = [tz[z] for z in range(depth)]
    gs, invs, _, _, coefs = factors(tzs, [store[z] for z in range(depth)])
    y = local_solve([pres[z] for z in range(depth)], gs, invs, tzs)
    for i, value in enumerate((*coefs, y[0], y[-1], tzs[-1])):
        ends[i] = value


def is_right(level, axis="layer"):
    return (lax.axis_index(axis) >> level) % 2 == 1


def choose(level, mine, other, axis="layer"):
    right = is_right(level, axis)
    return (jnp.where(right, other, mine), jnp.where(right, mine, other))


def local_solve(rhs, upper, inv, tz):
    depth = len(rhs)
    y = [rhs[0] * inv[0]]
    for z in range(1, depth):
        y.append((rhs[z] + tz[z - 1] * y[-1]) * inv[z])
    for z in range(depth - 2, -1, -1):
        y[z] = y[z] + upper[z] * y[z + 1]
    return y


def factors(tz, store):
    depth = len(tz)
    gs, invs = ([], [])
    own = None
    for z in range(depth):
        own = store[z] if z == 0 else store[z] + gs[-1] * own
        invs.append(1.0 / (own + tz[z] if z < depth - 1 else own))
        gs.append(tz[z] * invs[-1])
    first = [invs[0]]
    for z in range(1, depth):
        first.append(tz[z - 1] * first[-1] * invs[z])
    final = [None] * depth
    final[-1] = invs[-1]
    for z in range(depth - 2, -1, -1):
        first[z] = first[z] + gs[z] * first[z + 1]
        final[z] = gs[z] * final[z + 1]
    return gs, invs, first, final, (first[0], first[-1], final[-1] + 1.0 / jnp.maximum(tz[-1], 1e-30))


def pair(level, own, sib):
    af, af_ = choose(level, own[0], sib[0])
    c, c_ = choose(level, own[1], sib[1])
    b, b_ = choose(level, own[2], sib[2])
    return af, c, b, af_, c_, b_, 1.0 / (b + af_)


def join_coefs(level, own, sib):
    af, c, _, _, c_, b_, g = pair(level, own, sib)
    return (af - c * c * g, c * c_ * g, b_ - c_ * c_ * g)


def join_ends(level, own, sib, mine, other):
    _, c, _, _, c_, _, g = pair(level, own, sib)
    yf, yf_ = choose(level, mine[0], other[0])
    yl, yl_ = choose(level, mine[1], other[1])
    flux = g * (yl - yf_)
    return (yf - c * flux, yl_ + c_ * flux)


def first_join_kernel(own, sib, tz, store, out, face, more, one, answers):
    depth = tz.shape[0]
    _, _, first, final, _ = factors([tz[z] for z in range(depth)], [store[z] for z in range(depth)])
    for z in range(depth):
        answers[z] = first[z]
        answers[depth + z] = final[z]
    join_kernel(0, own, sib, answers, out, face, more, one)


def join_kernel(level, own, sib, answers, out, face, more, one):
    depth, width, _ = more.shape
    depth = depth // 2
    _, c, _, _, c_, _, g = pair(level, own, sib)
    first, both, last = join_coefs(level, own, sib)
    yf, yl = join_ends(level, own, sib, (own[3], own[4]), (sib[3], sib[4]))
    out[0], out[1], out[2] = (first, both, last)
    out[3], out[4] = (yf, yl)
    lower = choose(level, own[5], sib[5])[1]
    out[5] = lower
    face[2] = lower
    right, later = (is_right(level), is_right(level + 1))
    face[0], face[1] = (jnp.where(later, first, last), jnp.where(later, yf, yl))
    cg, cg_ = (c * g, c_ * g)
    for z in range(depth):
        kf, kl = (answers[z], answers[depth + z])
        top = jnp.where(right, cg * kf, kf - cg * kl)
        bottom = jnp.where(right, kl - cg_ * kf, cg_ * kl)
        more[z] = top
        more[depth + z] = bottom
        one[z] = jnp.where(later, top, bottom)


def groups_of(levels):
    layers = lax.axis_size("layer")
    l = lax.axis_index("layer")
    base = lax.axis_index("tile") * layers
    out = [[base + l]]
    for level in range(levels):
        out.append([base + (((l >> level) ^ 1) << level) + i for i in range(1 << level)])
    return out


def front_kernel(recv, cell, prod, tables, inverse, send, held, sems):
    devices = recv.shape[0]
    count = recv.shape[2] // 3
    rows, length = inverse.shape
    lanes = 128
    chunks = sems.shape[0]
    wide = length // chunks
    cell, prod = (cell[...], prod[...])
    copies = [
        pltpu.make_async_copy(inverse.at[:, pl.ds(i * wide, wide)], held.at[:, pl.ds(i * wide, wide)], sems.at[i])
        for i in range(chunks)
    ]
    for copy in copies:
        copy.start()
    where, value = (cell, prod)
    depth, width, long = tables[-1].shape
    hi, lo = lax.div(where, long), lax.rem(where, long)
    stack = [t[k * depth : (k + 1) * depth].reshape(depth * width, long) for t in tables for k in range(t.shape[0] // depth)]
    found = [value * f for f in pick(stack, hi, onehot(lo, long).astype(BF16))]
    terms, index = (recv[:, 0, :count], recv[:, 0, count : 2 * count])
    high = jnp.floor(index * (1.0 / lanes))
    low = index - high * lanes
    parts = [p.astype(F32) for p in split(terms)[:PARTS]]
    row_of = iota((length // lanes, count), 0).astype(F32)
    lane_of = iota((lanes, count), 0).astype(F32)
    total = jnp.zeros((length // lanes, lanes), F32)
    for d in range(devices):
        hit = row_of == high[d : d + 1]
        left = jnp.concatenate([jnp.where(hit, p[d : d + 1], 0.0).astype(BF16) for p in parts], 0)
        right = jnp.where(lane_of == low[d : d + 1], 1.0, 0.0).astype(BF16)
        total = total + fold(dot_nt(left, right), PARTS)
    acc = jnp.zeros((rows, lanes), F32)
    for i in range(chunks):
        copies[i].wait()
        for r in range(i * wide // lanes, (i + 1) * wide // lanes):
            acc = acc + held[:, r * lanes : (r + 1) * lanes] * total[r : r + 1]
    parts = jnp.concatenate(split(acc), 1)
    out = dot_nt(jnp.ones((8, parts.shape[1]), BF16), parts)
    send[...] = jnp.broadcast_to(jnp.concatenate([out[0:1], value, *found], 1)[:, None], send.shape)


def gathered(values, rows_hot, lanes_hot, start, size, ext, parts):
    hot = lanes_hot[:, start : start + size]
    pieces = [hot * p for v in values for p in split(v)[:parts]]
    got = dot_nt(rows_hot[:, start : start + size], jnp.concatenate(pieces, 0))
    planes = []
    lanes = hot.shape[0]
    for i in range(len(values)):
        plane = got[:, i * parts * lanes : (i * parts + 1) * lanes]
        for k in range(1, parts):
            j = i * parts + k
            plane = plane + got[:, j * lanes : (j + 1) * lanes]
        planes.append(jnp.concatenate([plane[r : r + ext] for r in range(0, plane.shape[0], ext)], 1))
    return planes


def beside(centre, tx, ty):
    width, long = centre.shape
    row, col = (iota(centre.shape, 0), iota(centre.shape, 1))
    total = tx * jnp.where(row == width - 1, 0.0, pltpu.roll(centre, width - 1, 0))
    total = total + jnp.where(row == 0, 0.0, pltpu.roll(tx * centre, 1, 0))
    total = total + ty * jnp.where(col == long - 1, 0.0, pltpu.roll(centre, long - 1, 1))
    return total + jnp.where(col == 0, 0.0, pltpu.roll(ty * centre, 1, 1))


def tile_rows(first, last, one, two):
    odd = is_right(0, "tile")
    one[...] = jnp.where(odd, first, last)
    two[...] = jnp.where(odd, last, first)


def table_kernel(levels, shape, terms, rows_hot, lanes_hot, sol_hot, sol_row, layer):
    _, width, long = shape
    lanes = 128
    rows = sol_hot.shape[0]
    count = terms.shape[2] // 3
    at = 0
    for members in groups_of(levels):
        for device in members:
            entry = terms[device]
            index = entry[:, count : 2 * count].astype(I32)
            cell = entry[:, 2 * count :].astype(I32)
            y, x = lax.rem(cell, long), lax.rem(lax.div(cell, long), width)
            here = pl.ds(at, count)
            rows_hot[:, here] = onehot(lax.div(y, lanes) * width + x, rows_hot.shape[0]).astype(BF16)
            lanes_hot[:, here] = onehot(lax.rem(y, lanes), lanes).astype(BF16)
            sol_hot[:, here] = onehot(lax.rem(index, rows), rows).astype(BF16)
            sol_row[:, here] = lax.div(index, rows)
            if at == 0:
                layer[...] = lax.div(cell, long * width)
            at += count


def pressure_kernel(levels, recv, terms, pres, *refs):
    sib, (tz, store, tx, p, coupled_z, one, two, rows_hot, lanes_hot, sol_hot, sol_row, layer) = (refs[:levels], refs[levels:])
    depth, width, long = pres.shape
    table_kernel(levels, pres.shape, terms, rows_hot, lanes_hot, sol_hot, sol_row, layer)
    rows, count = (sol_hot.shape[0], layer.shape[1])
    groups = groups_of(levels)
    layer = layer[...]
    table = jnp.concatenate(split(recv[...].reshape(recv.shape[0], recv.shape[2])[:, :rows]), 0)
    sol = fold(dot(table, sol_hot[...]))
    sol = jnp.sum(jnp.where(iota(sol.shape, 0) == sol_row[...], sol, 0.0), axis=0, keepdims=True)

    def listed(group, column):
        at = rows + column * count
        return jnp.concatenate([recv[device][:, at : at + count] for device in group], 1)

    tzs = [tz[z] for z in range(depth)]
    gs, invs, first, final, coefs = factors(tzs, [store[z] for z in range(depth)])
    own = [coefs]
    value = listed(groups[0], 0) * sol[:, :count]
    values = [jnp.where(layer == z, value, 0.0) for z in range(depth)]
    change = gathered(values, rows_hot, lanes_hot, 0, count, width, PARTS)
    y = local_solve([pres[z] - change[z] for z in range(depth)], gs, invs, tzs)
    mine = (y[0], y[-1])
    steps = []
    start = count
    for level in range(levels):
        size = len(groups[level + 1]) * count
        top = level == levels - 1
        columns = [1 + 2 * level] if top else [1 + 2 * level, 2 + 2 * level]
        values = [listed(groups[level + 1], c) * sol[:, start : start + size] for c in columns]
        change = gathered(values, rows_hot, lanes_hot, start, size, width, PARTS)
        start += size
        if top:
            other = sib[level][1] - change[0]
            steps.append((mine, (other, other)))
        else:
            other = (sib[level][3] - change[0], sib[level][4] - change[1])
            steps.append((mine, other))
            mine = join_ends(level, own[level], sib[level], mine, other)
            own.append(join_coefs(level, own[level], sib[level]))
    above = below = jnp.zeros((width, long), F32)
    tzp = jnp.zeros((width, long), F32)
    place = lax.axis_index("layer")
    for level in range(levels - 1, -1, -1):
        mine, other = steps[level]
        yl, _ = choose(level, mine[1], other[1])
        _, yf_ = choose(level, mine[0], other[0])
        flux = yl - yf_
        if level == levels - 1:
            b, _ = choose(level, own[level][2], sib[level][0])
            _, af_ = choose(level, own[level][0], sib[level][0])
            g = 1.0 / (b + af_)
            before = sib[level][2]
        else:
            _, c, _, _, c_, _, g = pair(level, own[level], sib[level])
            flux = flux + c * above - c_ * below
            before = sib[level][5]
        tzp = jnp.where(place % (2 << level) == 1 << level, before, tzp)
        flux = g * flux
        right = is_right(level)
        above, below = (jnp.where(right, flux, above), jnp.where(right, below, -flux))
    values = [y[z] + first[z] * above + final[z] * below for z in range(depth)]
    is_last = place == (1 << levels) - 1
    for z in range(depth):
        p[z] = values[z]
        total = above + tzp * values[z] if z == 0 else tzs[z - 1] * values[z - 1]
        if z == depth - 1:
            coupled_z[z] = total + jnp.where(is_last, 0.0, below + tzs[z] * values[z])
        else:
            coupled_z[z] = total + tzs[z] * values[z + 1]
    for z in range(depth):
        tile_rows(values[z][0:1], (tx[z] * values[z])[width - 1 :], one.at[z], two.at[z])


def search_kernel(p, coupled_z, one, two, tx, ty, tz, rhs, diag, binv, s, row_one, row_two, inner, outer):
    depth, width, _ = p.shape
    odd = is_right(0, "tile")
    right = is_right(0)
    row = iota(p.shape[1:], 0)
    for z in range(depth):
        centre = p[z]
        after = jnp.where(odd, two[z], one[z])
        before = jnp.where(odd, one[z], two[z])
        coupled = coupled_z[z] + beside(centre, tx[z], ty[z])
        coupled = coupled + jnp.where(row == 0, before, 0.0) + jnp.where(row == width - 1, tx[z] * after, 0.0)
        remain = [rhs[c, z] - diag[c, 0, z] * centre for c in range(3)]
        remain[0] = remain[0] + coupled
        for c in range(3):
            value = binv[c, 0, z] * remain[0] + binv[c, 1, z] * remain[1] + binv[c, 2, z] * remain[2]
            if c == 0:
                value = centre + value
            s[c, z] = value
            tile_rows(value[0:1], (tx[z] * value)[width - 1 :], row_one.at[c, z], row_two.at[c, z])
    for c in range(3):
        top, bottom = (s[c, 0], tz[depth - 1] * s[c, depth - 1])
        inner[c] = jnp.where(right, top, bottom)
        outer[c] = jnp.where(right, bottom, top)


def inner_kernel(s, diag, tz, tx, ty, image):
    depth = s.shape[1]
    for z in range(depth):
        for c in range(3):
            total = diag[c, 0, z] * s[0, z] + diag[c, 1, z] * s[1, z] + diag[c, 2, z] * s[2, z]
            total = total - beside(s[c, z], tx[z], ty[z])
            if z:
                total = total - tz[z - 1] * s[c, z - 1]
            if z < depth - 1:
                total = total - tz[z] * s[c, z + 1]
            image[c, z] = total


def image_kernel(part, row_one, row_two, inner, outer, rhs, tz, tx, image, send):
    depth, width = part.shape[1:3]
    right, odd = (is_right(0), is_right(0, "tile"))
    row = iota(part.shape[2:], 0)
    along = power = start = 0.0
    for z in range(depth):
        for c in range(3):
            value = part[c, z]
            if z == 0:
                value = value - jnp.where(right, inner[c], outer[c])
            if z == depth - 1:
                value = value - tz[z] * jnp.where(right, outer[c], inner[c])
            after = jnp.where(odd, row_two[c, z], row_one[c, z])
            before = jnp.where(odd, row_one[c, z], row_two[c, z])
            value = value - jnp.where(row == 0, before, 0.0) - jnp.where(row == width - 1, tx[z] * after, 0.0)
            image[c, z] = value
            given = rhs[c, z]
            along = along + value * given
            power = power + value * value
            start = start + given * given
    along, power, start = (jnp.sum(along), jnp.sum(power), jnp.sum(start))
    omega = along / jnp.where(power > 0.0, power, 1.0)
    square = cross = 0.0
    for z in range(depth):
        for c in range(3):
            value = image[c, z]
            left = rhs[c, z] - omega * value
            square = square + left * left
            cross = cross + left * value
    lane = iota((1, send.shape[2]), 1)
    out = jnp.zeros((1, send.shape[2]), F32)
    for i, value in enumerate((along, power, start, jnp.sum(square), jnp.sum(cross), omega)):
        out = jnp.where(lane == i, value, out)
    send[...] = jnp.broadcast_to(out[:, None], send.shape)


def finish_kernel(recv, s, image, rhs, update, lin_res, ratio, held_update, held_res, sems):
    sums = recv[...].reshape(recv.shape[0], recv.shape[2])
    whole = jnp.sum(sums, axis=0, keepdims=True)
    omega = whole[:, 0:1] / whole[:, 1:2]
    copies = []
    for c in range(3):
        for z in range(s.shape[1]):
            held_update[c, z] = omega * s[c, z]
            held_res[c, z] = rhs[c, z] - omega * image[c, z]
        for held, out in ((held_update, update), (held_res, lin_res)):
            copies.append(pltpu.make_async_copy(held.at[c], out.at[c], sems.at[len(copies)]))
            copies[-1].start()
    shift = sums[:, 5:6] - omega
    square = sums[:, 3:4] + 2.0 * shift * sums[:, 4:5] + shift * shift * sums[:, 1:2]
    ratio[...] = jnp.sqrt(jnp.sum(square, axis=0, keepdims=True) / whole[:, 2:3])
    for copy in copies:
        copy.wait()


def flip(x, level, axis="layer"):
    return lax.ppermute(x, axis, [(i, i ^ (1 << level)) for i in range(lax.axis_size(axis))])


def neighbour(x, axis="layer"):
    pairs = [(i, i + 1) for i in range(1, lax.axis_size(axis) - 1, 2)]
    return lax.ppermute(x, axis, pairs + [(j, i) for i, j in pairs])


def everywhere(x):
    return lax.all_to_all(x, BOTH, split_axis=0, concat_axis=0, tiled=True)


def shards(rhs, weights, block_diag, block_inv, tx, ty, tz, store, cell, front, prod, inverse):
    layers = lax.axis_size("layer")
    devices = lax.axis_size("tile") * layers
    levels = layers.bit_length() - 1
    depth, width, long = tx.shape
    count = cell.shape[0]
    rows = inverse.shape[0]
    lists = layers * count
    cell, front, prod = (cell.reshape(1, -1), front.reshape(1, -1), prod.reshape(1, -1))
    field = vmem(tx.shape)

    def planes(n):
        return vmem((n, width, long))

    hbm_spec = pl.BlockSpec(memory_space=pltpu.HBM)
    given = (cell, front, prod, rhs, weights, tz, store)
    pres, send, ends = pl.pallas_call(
        pres_kernel,
        out_shape=(field, vmem((devices, 1, 3 * count)), planes(6)),
        in_specs=[hbm_spec] * len(given),
        out_specs=(VM,) * 3,
        scratch_shapes=[vmem(a.shape, a.dtype) for a in given] + [pltpu.SemaphoreType.DMA((len(given),))],
        compiler_params=pltpu.CompilerParams(vmem_limit_bytes=LIMIT),
    )(*[pltpu.with_memory_space_constraint(a, pltpu.HBM) for a in given])
    terms = everywhere(send)
    sib, tables = ([], [])
    for level in range(levels - 1):
        sib.append(flip(ends, level))
        outs = (planes(6), planes(3), planes(2 * depth), field)
        if level == 0:
            ends, face, more, last, answers = call(
                first_join_kernel, (*outs, planes(2 * depth)), (ends, sib[-1], tz, store), far=(2, 3)
            )
        else:
            ends, face, more, last = call(functools.partial(join_kernel, level), outs, (ends, sib[-1], answers))
        tables.append(answers)
        answers = more
    tables.append(last)
    sib.append(flip(face, levels - 1))
    chunks = 8
    terms, *tables = lax.optimization_barrier((terms, *tables))
    send = pl.pallas_call(
        front_kernel,
        out_shape=vmem((devices, 1, rows + 2 * levels * count)),
        in_specs=[VM, VM, VM, [VM] * len(tables), hbm_spec],
        out_specs=VM,
        scratch_shapes=[vmem(inverse.shape), pltpu.SemaphoreType.DMA((chunks,))],
        compiler_params=pltpu.CompilerParams(vmem_limit_bytes=LIMIT),
    )(terms, cell, prod, tables, pltpu.with_memory_space_constraint(inverse, pltpu.HBM))
    sol = everywhere(send)
    row3 = vmem((depth, 1, long))
    at = 3 + levels
    p, coupled_z, one, two, tz, _, tx = call(
        functools.partial(pressure_kernel, levels),
        (field, field, row3, row3),
        (sol, terms, pres, *sib, tz, store, tx),
        far=(at, at + 1, at + 2),
        keep=(at, at + 1, at + 2),
        scratch=(
            vmem((width * long // 128, lists), BF16),
            vmem((128, lists), BF16),
            vmem((rows, lists), BF16),
            vmem((1, lists), I32),
            vmem((1, count), I32),
        ),
    )
    one, two = (flip(one, 0, "tile"), neighbour(two, "tile"))
    row9 = vmem((3, depth, 1, long))
    plane3 = planes(3)
    s, row_one, row_two, inner, outer = call(
        search_kernel,
        (vmem(rhs.shape), row9, row9, plane3, plane3),
        (p, coupled_z, one, two, tx, ty, tz, rhs, block_diag, block_inv),
    )
    outer, inner = (neighbour(outer), flip(inner, 0))
    row_one, row_two = (flip(row_one, 0, "tile"), neighbour(row_two, "tile"))
    (part,) = call(inner_kernel, (vmem(rhs.shape),), (s, block_diag, tz, tx, ty))
    image, send = call(
        image_kernel,
        (vmem(rhs.shape), vmem((devices, 1, 128))),
        (part, row_one, row_two, inner, outer, rhs, tz, tx),
    )
    sums = everywhere(send)
    update, lin_res, ratio = pl.pallas_call(
        finish_kernel,
        out_shape=(hbm(rhs.shape), hbm(rhs.shape), hbm((1, 1))),
        in_specs=[VM] * 4,
        out_specs=(hbm_spec, hbm_spec, VM),
        scratch_shapes=[vmem(rhs.shape), vmem(rhs.shape), pltpu.SemaphoreType.DMA((6,))],
        compiler_params=pltpu.CompilerParams(vmem_limit_bytes=LIMIT),
    )(*[pltpu.with_memory_space_constraint(a, pltpu.VMEM) for a in (sums, s, image, rhs)])
    return (update, lin_res, ratio.reshape(()))


def solution(mesh):
    return jax.shard_map(
        shards,
        mesh=mesh,
        in_specs=(
            P(None, "layer", "tile", None),
            P(None, "layer", "tile", None),
            P(None, None, "layer", "tile", None),
            P(None, None, "layer", "tile", None),
            P("layer", "tile", None),
            P("layer", "tile", None),
            P("layer", "tile", None),
            P("layer", "tile", None),
            P(("tile", "layer")),
            P(("tile", "layer")),
            P(("tile", "layer")),
            P(("tile", "layer"), None),
        ),
        out_specs=(P(None, "layer", "tile", None), P(None, "layer", "tile", None), P()),
        check_vma=False,
    )
```

```python
import functools
import jax
import jax.numpy as jnp
from jax import lax
from jax.experimental import pallas as pl
from jax.experimental.pallas import tpu as pltpu
from jax.sharding import PartitionSpec as P

F32 = jnp.float32
BF16 = jnp.bfloat16
I32 = jnp.int32
BOTH = ("tile", "layer")
VM = pl.BlockSpec(memory_space=pltpu.VMEM)
LIMIT = 16 << 20
PARTS = 2


def hbm(shape):
    return jax.ShapeDtypeStruct(shape, F32)


def vmem(shape, dtype=F32):
    return pltpu.VMEM(shape, dtype)


def staged(kernel, where, outs, kept, column, *refs):
    count, sems = (len(where), refs[-1])
    held = list(refs[count + outs + len(kept) : -1])
    target_count = sum(where) - len(kept)
    held, extra = (held[:target_count], held[target_count:])
    target = dict(zip(kept, refs[count + outs : count + outs + len(kept)]))
    operands, copies = ([], [])
    for i, far in enumerate(where):
        if far:
            to = target[i] if i in target else held.pop(0)
            part = refs[i].at[:, 0] if i in column else refs[i]
            copies.append(pltpu.make_async_copy(part, to, sems.at[len(copies)]))
            operands.append(to)
        else:
            operands.append(refs[i])
    for copy in copies:
        copy.start()
    for copy in copies:
        copy.wait()
    kernel(*operands, *refs[count : count + outs], *extra)


def call(kernel, outs, args, far=(), keep=(), column=(), scratch=(), limit=LIMIT):
    where = [i in far for i in range(len(args))]
    spaces = [pltpu.HBM if w else pltpu.VMEM for w in where]
    every = (*outs, *(vmem(args[i].shape, args[i].dtype) for i in keep))
    return pl.pallas_call(
        functools.partial(staged, kernel, where, len(outs), tuple(keep), tuple(column)),
        out_shape=every,
        in_specs=[pl.BlockSpec(memory_space=s) for s in spaces],
        out_specs=(VM,) * len(every),
        scratch_shapes=[
            vmem(a.shape[:1] + a.shape[2:] if i in column else a.shape, a.dtype)
            for i, a in enumerate(args)
            if where[i] and i not in keep
        ]
        + [*scratch, pltpu.SemaphoreType.DMA((max(1, sum(where)),))],
        compiler_params=pltpu.CompilerParams(vmem_limit_bytes=limit),
    )(*[pltpu.with_memory_space_constraint(a, s) for a, s in zip(args, spaces)])


def iota(shape, dim):
    return lax.broadcasted_iota(I32, shape, dim)


def split(x):
    one = x.astype(BF16)
    rest = x - one.astype(F32)
    two = rest.astype(BF16)
    three = (rest - two.astype(F32)).astype(BF16)
    return [one, two, three]


def fold(x, parts=3):
    n = x.shape[0] // parts
    total = x[(parts - 1) * n :]
    for i in range(parts - 2, -1, -1):
        total = x[i * n : (i + 1) * n] + total
    return total


def onehot(index, size):
    return jnp.where(iota((size, index.shape[1]), 0) == index, 1.0, 0.0)


def dot(a, b):
    return lax.dot_general(a, b, (((1,), (0,)), ((), ())), preferred_element_type=F32)


def dot_nt(a, b):
    return lax.dot_general(a, b, (((1,), (1,)), ((), ())), preferred_element_type=F32)


def pick(tables, hi, hot):
    rows = tables[0].shape[0]
    parts = jnp.concatenate([p for table in tables for p in split(table)[:PARTS]], 0)
    got = dot(parts, hot)
    mask = onehot(hi, rows)
    n = PARTS * rows
    return [jnp.sum(fold(got[i * n : (i + 1) * n], PARTS) * mask, axis=0, keepdims=True) for i in range(len(tables))]


def pres_kernel(cell_in, front_in, prod_in, rhs_in, wts_in, tz_in, store_in, pres, send, ends, *scratch):
    (cell, front, prod, rhs, wts, tz, store), sems = scratch[:-1], scratch[-1]
    pairs = ((cell_in, cell), (front_in, front), (prod_in, prod), (rhs_in, rhs), (wts_in, wts), (tz_in, tz), (store_in, store))
    copies = [pltpu.make_async_copy(a, b, sems.at[i]) for i, (a, b) in enumerate(pairs)]
    for copy in copies:
        copy.start()
    for copy in copies[:3]:
        copy.wait()
    depth, width, long = pres.shape
    where = cell[...]
    hot = onehot(lax.rem(where, long), long).astype(BF16)
    for copy in copies[3:]:
        copy.wait()
    for z in range(depth):
        pres[z] = wts[0, z] * rhs[0, z] + wts[1, z] * rhs[1, z] + wts[2, z] * rhs[2, z]
    (found,) = pick([pres[...].reshape(depth * width, long)], lax.div(where, long), hot)
    both = jnp.concatenate([prod[...] * found, front[...].astype(F32), where.astype(F32)], 1)
    send[...] = jnp.broadcast_to(both[:, None], send.shape)
    tzs = [tz[z] for z in range(depth)]
    gs, invs, _, _, coefs = factors(tzs, [store[z] for z in range(depth)])
    y = local_solve([pres[z] for z in range(depth)], gs, invs, tzs)
    for i, value in enumerate((*coefs, y[0], y[-1], tzs[-1])):
        ends[i] = value


def is_right(level, axis="layer"):
    return (lax.axis_index(axis) >> level) % 2 == 1


def choose(level, mine, other, axis="layer"):
    right = is_right(level, axis)
    return (jnp.where(right, other, mine), jnp.where(right, mine, other))


def local_solve(rhs, upper, inv, tz):
    depth = len(rhs)
    y = [rhs[0] * inv[0]]
    for z in range(1, depth):
        y.append((rhs[z] + tz[z - 1] * y[-1]) * inv[z])
    for z in range(depth - 2, -1, -1):
        y[z] = y[z] + upper[z] * y[z + 1]
    return y


def factors(tz, store):
    depth = len(tz)
    gs, invs = ([], [])
    own = None
    for z in range(depth):
        own = store[z] if z == 0 else store[z] + gs[-1] * own
        invs.append(1.0 / (own + tz[z] if z < depth - 1 else own))
        gs.append(tz[z] * invs[-1])
    first = [invs[0]]
    for z in range(1, depth):
        first.append(tz[z - 1] * first[-1] * invs[z])
    final = [None] * depth
    final[-1] = invs[-1]
    for z in range(depth - 2, -1, -1):
        first[z] = first[z] + gs[z] * first[z + 1]
        final[z] = gs[z] * final[z + 1]
    return gs, invs, first, final, (first[0], first[-1], final[-1] + 1.0 / jnp.maximum(tz[-1], 1e-30))


def pair(level, own, sib):
    af, af_ = choose(level, own[0], sib[0])
    c, c_ = choose(level, own[1], sib[1])
    b, b_ = choose(level, own[2], sib[2])
    return af, c, b, af_, c_, b_, 1.0 / (b + af_)


def join_coefs(level, own, sib):
    af, c, _, _, c_, b_, g = pair(level, own, sib)
    return (af - c * c * g, c * c_ * g, b_ - c_ * c_ * g)


def join_ends(level, own, sib, mine, other):
    _, c, _, _, c_, _, g = pair(level, own, sib)
    yf, yf_ = choose(level, mine[0], other[0])
    yl, yl_ = choose(level, mine[1], other[1])
    flux = g * (yl - yf_)
    return (yf - c * flux, yl_ + c_ * flux)


def first_join_kernel(own, sib, tz, store, out, face, more, one, answers):
    depth = tz.shape[0]
    _, _, first, final, _ = factors([tz[z] for z in range(depth)], [store[z] for z in range(depth)])
    for z in range(depth):
        answers[z] = first[z]
        answers[depth + z] = final[z]
    join_kernel(0, own, sib, answers, out, face, more, one)


def join_kernel(level, own, sib, answers, out, face, more, one):
    depth, width, _ = more.shape
    depth = depth // 2
    _, c, _, _, c_, _, g = pair(level, own, sib)
    first, both, last = join_coefs(level, own, sib)
    yf, yl = join_ends(level, own, sib, (own[3], own[4]), (sib[3], sib[4]))
    out[0], out[1], out[2] = (first, both, last)
    out[3], out[4] = (yf, yl)
    lower = choose(level, own[5], sib[5])[1]
    out[5] = lower
    face[2] = lower
    right, later = (is_right(level), is_right(level + 1))
    face[0], face[1] = (jnp.where(later, first, last), jnp.where(later, yf, yl))
    cg, cg_ = (c * g, c_ * g)
    for z in range(depth):
        kf, kl = (answers[z], answers[depth + z])
        top = jnp.where(right, cg * kf, kf - cg * kl)
        bottom = jnp.where(right, kl - cg_ * kf, cg_ * kl)
        more[z] = top
        more[depth + z] = bottom
        one[z] = jnp.where(later, top, bottom)


def groups_of(levels):
    layers = lax.axis_size("layer")
    l = lax.axis_index("layer")
    base = lax.axis_index("tile") * layers
    out = [[base + l]]
    for level in range(levels):
        out.append([base + (((l >> level) ^ 1) << level) + i for i in range(1 << level)])
    return out


def front_kernel(recv, cell, prod, tables, inverse, send, held, sems):
    devices = recv.shape[0]
    count = recv.shape[2] // 3
    rows, length = inverse.shape
    lanes = 128
    chunks = sems.shape[0]
    wide = length // chunks
    cell, prod = (cell[...], prod[...])
    copies = [
        pltpu.make_async_copy(inverse.at[:, pl.ds(i * wide, wide)], held.at[:, pl.ds(i * wide, wide)], sems.at[i])
        for i in range(chunks)
    ]
    for copy in copies:
        copy.start()
    where, value = (cell, prod)
    depth, width, long = tables[-1].shape
    hi, lo = lax.div(where, long), lax.rem(where, long)
    stack = [t[k * depth : (k + 1) * depth].reshape(depth * width, long) for t in tables for k in range(t.shape[0] // depth)]
    found = [value * f for f in pick(stack, hi, onehot(lo, long).astype(BF16))]
    terms, index = (recv[:, 0, :count], recv[:, 0, count : 2 * count])
    high = jnp.floor(index * (1.0 / lanes))
    low = index - high * lanes
    parts = [p.astype(F32) for p in split(terms)[:PARTS]]
    row_of = iota((length // lanes, count), 0).astype(F32)
    lane_of = iota((lanes, count), 0).astype(F32)
    total = jnp.zeros((length // lanes, lanes), F32)
    for d in range(devices):
        hit = row_of == high[d : d + 1]
        left = jnp.concatenate([jnp.where(hit, p[d : d + 1], 0.0).astype(BF16) for p in parts], 0)
        right = jnp.where(lane_of == low[d : d + 1], 1.0, 0.0).astype(BF16)
        total = total + fold(dot_nt(left, right), PARTS)
    acc = jnp.zeros((rows, lanes), F32)
    for i in range(chunks):
        copies[i].wait()
        for r in range(i * wide // lanes, (i + 1) * wide // lanes):
            acc = acc + held[:, r * lanes : (r + 1) * lanes] * total[r : r + 1]
    parts = jnp.concatenate(split(acc), 1)
    out = dot_nt(jnp.ones((8, parts.shape[1]), BF16), parts)
    send[...] = jnp.broadcast_to(jnp.concatenate([out[0:1], value, *found], 1)[:, None], send.shape)


def gathered(values, rows_hot, lanes_hot, start, size, ext, parts):
    hot = lanes_hot[:, start : start + size]
    pieces = [hot * p for v in values for p in split(v)[:parts]]
    got = dot_nt(rows_hot[:, start : start + size], jnp.concatenate(pieces, 0))
    planes = []
    lanes = hot.shape[0]
    for i in range(len(values)):
        plane = got[:, i * parts * lanes : (i * parts + 1) * lanes]
        for k in range(1, parts):
            j = i * parts + k
            plane = plane + got[:, j * lanes : (j + 1) * lanes]
        planes.append(jnp.concatenate([plane[r : r + ext] for r in range(0, plane.shape[0], ext)], 1))
    return planes


def beside(centre, tx, ty):
    width, long = centre.shape
    row, col = (iota(centre.shape, 0), iota(centre.shape, 1))
    total = tx * jnp.where(row == width - 1, 0.0, pltpu.roll(centre, width - 1, 0))
    total = total + jnp.where(row == 0, 0.0, pltpu.roll(tx * centre, 1, 0))
    total = total + ty * jnp.where(col == long - 1, 0.0, pltpu.roll(centre, long - 1, 1))
    return total + jnp.where(col == 0, 0.0, pltpu.roll(ty * centre, 1, 1))


def tile_rows(first, last, one, two):
    odd = is_right(0, "tile")
    one[...] = jnp.where(odd, first, last)
    two[...] = jnp.where(odd, last, first)


def table_kernel(levels, shape, terms, rows_hot, lanes_hot, sol_hot, sol_row, layer):
    _, width, long = shape
    lanes = 128
    rows = sol_hot.shape[0]
    count = terms.shape[2] // 3
    at = 0
    for members in groups_of(levels):
        for device in members:
            entry = terms[device]
            index = entry[:, count : 2 * count].astype(I32)
            cell = entry[:, 2 * count :].astype(I32)
            y, x = lax.rem(cell, long), lax.rem(lax.div(cell, long), width)
            here = pl.ds(at, count)
            rows_hot[:, here] = onehot(lax.div(y, lanes) * width + x, rows_hot.shape[0]).astype(BF16)
            lanes_hot[:, here] = onehot(lax.rem(y, lanes), lanes).astype(BF16)
            sol_hot[:, here] = onehot(lax.rem(index, rows), rows).astype(BF16)
            sol_row[:, here] = lax.div(index, rows)
            if at == 0:
                layer[...] = lax.div(cell, long * width)
            at += count


def pressure_kernel(levels, recv, terms, pres, *refs):
    sib, (tz, store, tx, p, coupled_z, two, one, rows_hot, lanes_hot, sol_hot, sol_row, layer) = (refs[:levels], refs[levels:])
    depth, width, long = pres.shape
    table_kernel(levels, pres.shape, terms, rows_hot, lanes_hot, sol_hot, sol_row, layer)
    rows, count = (sol_hot.shape[0], layer.shape[1])
    groups = groups_of(levels)
    layer = layer[...]
    table = jnp.concatenate(split(recv[...].reshape(recv.shape[0], recv.shape[2])[:, :rows]), 0)
    sol = fold(dot(table, sol_hot[...]))
    sol = jnp.sum(jnp.where(iota(sol.shape, 0) == sol_row[...], sol, 0.0), axis=0, keepdims=True)

    def listed(group, column):
        at = rows + column * count
        return jnp.concatenate([recv[device][:, at : at + count] for device in group], 1)

    tzs = [tz[z] for z in range(depth)]
    gs, invs, first, final, coefs = factors(tzs, [store[z] for z in range(depth)])
    own = [coefs]
    value = listed(groups[0], 0) * sol[:, :count]
    values = [jnp.where(layer == z, value, 0.0) for z in range(depth)]
    change = gathered(values, rows_hot, lanes_hot, 0, count, width, PARTS)
    y = local_solve([pres[z] - change[z] for z in range(depth)], gs, invs, tzs)
    mine = (y[0], y[-1])
    steps = []
    start = count
    for level in range(levels):
        size = len(groups[level + 1]) * count
        top = level == levels - 1
        columns = [1 + 2 * level] if top else [1 + 2 * level, 2 + 2 * level]
        values = [listed(groups[level + 1], c) * sol[:, start : start + size] for c in columns]
        change = gathered(values, rows_hot, lanes_hot, start, size, width, PARTS)
        start += size
        if top:
            other = sib[level][1] - change[0]
            steps.append((mine, (other, other)))
        else:
            other = (sib[level][3] - change[0], sib[level][4] - change[1])
            steps.append((mine, other))
            mine = join_ends(level, own[level], sib[level], mine, other)
            own.append(join_coefs(level, own[level], sib[level]))
    above = below = jnp.zeros((width, long), F32)
    tzp = jnp.zeros((width, long), F32)
    place = lax.axis_index("layer")
    for level in range(levels - 1, -1, -1):
        mine, other = steps[level]
        yl, _ = choose(level, mine[1], other[1])
        _, yf_ = choose(level, mine[0], other[0])
        flux = yl - yf_
        if level == levels - 1:
            b, _ = choose(level, own[level][2], sib[level][0])
            _, af_ = choose(level, own[level][0], sib[level][0])
            g = 1.0 / (b + af_)
            before = sib[level][2]
        else:
            _, c, _, _, c_, _, g = pair(level, own[level], sib[level])
            flux = flux + c * above - c_ * below
            before = sib[level][5]
        tzp = jnp.where(place % (2 << level) == 1 << level, before, tzp)
        flux = g * flux
        right = is_right(level)
        above, below = (jnp.where(right, flux, above), jnp.where(right, below, -flux))
    values = [y[z] + first[z] * above + final[z] * below for z in range(depth)]
    is_last = place == (1 << levels) - 1
    for z in range(depth):
        p[z] = values[z]
        total = above + tzp * values[z] if z == 0 else tzs[z - 1] * values[z - 1]
        if z == depth - 1:
            coupled_z[z] = total + jnp.where(is_last, 0.0, below + tzs[z] * values[z])
        else:
            coupled_z[z] = total + tzs[z] * values[z + 1]
    for z in range(depth):
        tile_rows(values[z][0:1], (tx[z] * values[z])[width - 1 :], one.at[z], two.at[z])


def search_kernel(p, coupled_z, two, one, tx, ty, tz, rhs, diag, binv, s, outer, row_two, row_one, inner):
    depth, width, _ = p.shape
    odd = is_right(0, "tile")
    right = is_right(0)
    row = iota(p.shape[1:], 0)
    for z in range(depth):
        centre = p[z]
        after = jnp.where(odd, two[z], one[z])
        before = jnp.where(odd, one[z], two[z])
        coupled = coupled_z[z] + beside(centre, tx[z], ty[z])
        coupled = coupled + jnp.where(row == 0, before, 0.0) + jnp.where(row == width - 1, tx[z] * after, 0.0)
        remain = [rhs[c, z] - diag[c, 0, z] * centre for c in range(3)]
        remain[0] = remain[0] + coupled
        for c in range(3):
            value = binv[c, 0, z] * remain[0] + binv[c, 1, z] * remain[1] + binv[c, 2, z] * remain[2]
            if c == 0:
                value = centre + value
            s[c, z] = value
            tile_rows(value[0:1], (tx[z] * value)[width - 1 :], row_one.at[c, z], row_two.at[c, z])
    for c in range(3):
        top, bottom = (s[c, 0], tz[depth - 1] * s[c, depth - 1])
        inner[c] = jnp.where(right, top, bottom)
        outer[c] = jnp.where(right, bottom, top)


def inner_kernel(s, diag, tz, tx, ty, image):
    depth = s.shape[1]
    for z in range(depth):
        for c in range(3):
            total = diag[c, 0, z] * s[0, z] + diag[c, 1, z] * s[1, z] + diag[c, 2, z] * s[2, z]
            total = total - beside(s[c, z], tx[z], ty[z])
            if z:
                total = total - tz[z - 1] * s[c, z - 1]
            if z < depth - 1:
                total = total - tz[z] * s[c, z + 1]
            image[c, z] = total


def image_kernel(part, outer, row_two, row_one, inner, rhs, tz, tx, image, send):
    depth, width = part.shape[1:3]
    right, odd = (is_right(0), is_right(0, "tile"))
    row = iota(part.shape[2:], 0)
    along = power = start = 0.0
    for z in range(depth):
        for c in range(3):
            value = part[c, z]
            if z == 0:
                value = value - jnp.where(right, inner[c], outer[c])
            if z == depth - 1:
                value = value - tz[z] * jnp.where(right, outer[c], inner[c])
            after = jnp.where(odd, row_two[c, z], row_one[c, z])
            before = jnp.where(odd, row_one[c, z], row_two[c, z])
            value = value - jnp.where(row == 0, before, 0.0) - jnp.where(row == width - 1, tx[z] * after, 0.0)
            image[c, z] = value
            given = rhs[c, z]
            along = along + value * given
            power = power + value * value
            start = start + given * given
    along, power, start = (jnp.sum(along), jnp.sum(power), jnp.sum(start))
    omega = along / jnp.where(power > 0.0, power, 1.0)
    square = cross = 0.0
    for z in range(depth):
        for c in range(3):
            value = image[c, z]
            left = rhs[c, z] - omega * value
            square = square + left * left
            cross = cross + left * value
    lane = iota((1, send.shape[2]), 1)
    out = jnp.zeros((1, send.shape[2]), F32)
    for i, value in enumerate((along, power, start, jnp.sum(square), jnp.sum(cross), omega)):
        out = jnp.where(lane == i, value, out)
    send[...] = jnp.broadcast_to(out[:, None], send.shape)


def finish_kernel(recv, s, image, rhs, update, lin_res, ratio):
    sums = recv[...].reshape(recv.shape[0], recv.shape[2])
    whole = jnp.sum(sums, axis=0, keepdims=True)
    omega = whole[:, 0:1] / whole[:, 1:2]
    shift = sums[:, 5:6] - omega
    square = sums[:, 3:4] + 2.0 * shift * sums[:, 4:5] + shift * shift * sums[:, 1:2]
    ratio[...] = jnp.sqrt(jnp.sum(square, axis=0, keepdims=True) / whole[:, 2:3])
    for c in range(3):
        for z in range(s.shape[1]):
            update[c, z] = omega * s[c, z]
            lin_res[c, z] = rhs[c, z] - omega * image[c, z]


def flip(x, level, axis="layer"):
    return lax.ppermute(x, axis, [(i, i ^ (1 << level)) for i in range(lax.axis_size(axis))])


def neighbour(x, axis="layer"):
    pairs = [(i, i + 1) for i in range(1, lax.axis_size(axis) - 1, 2)]
    return lax.ppermute(x, axis, pairs + [(j, i) for i, j in pairs])


def everywhere(x):
    return lax.all_to_all(x, BOTH, split_axis=0, concat_axis=0, tiled=True)


def shards(rhs, weights, block_diag, block_inv, tx, ty, tz, store, cell, front, prod, inverse):
    layers = lax.axis_size("layer")
    devices = lax.axis_size("tile") * layers
    levels = layers.bit_length() - 1
    depth, width, long = tx.shape
    count = cell.shape[0]
    rows = inverse.shape[0]
    lists = layers * count
    cell, front, prod = (cell.reshape(1, -1), front.reshape(1, -1), prod.reshape(1, -1))
    field = vmem(tx.shape)

    def planes(n):
        return vmem((n, width, long))

    hbm_spec = pl.BlockSpec(memory_space=pltpu.HBM)
    given = (cell, front, prod, rhs, weights, tz, store)
    pres, send, ends = pl.pallas_call(
        pres_kernel,
        out_shape=(field, vmem((devices, 1, 3 * count)), planes(6)),
        in_specs=[hbm_spec] * len(given),
        out_specs=(VM,) * 3,
        scratch_shapes=[vmem(a.shape, a.dtype) for a in given] + [pltpu.SemaphoreType.DMA((len(given),))],
        compiler_params=pltpu.CompilerParams(vmem_limit_bytes=LIMIT),
    )(*[pltpu.with_memory_space_constraint(a, pltpu.HBM) for a in given])
    terms = everywhere(send)
    sib, tables = ([], [])
    for level in range(levels - 1):
        sib.append(flip(ends, level))
        outs = (planes(6), planes(3), planes(2 * depth), field)
        if level == 0:
            ends, face, more, last, answers = call(
                first_join_kernel, (*outs, planes(2 * depth)), (ends, sib[-1], tz, store), far=(2, 3)
            )
        else:
            ends, face, more, last = call(functools.partial(join_kernel, level), outs, (ends, sib[-1], answers))
        tables.append(answers)
        answers = more
    tables.append(last)
    sib.append(flip(face, levels - 1))
    chunks = 8
    terms, *tables = lax.optimization_barrier((terms, *tables))
    send = pl.pallas_call(
        front_kernel,
        out_shape=vmem((devices, 1, rows + 2 * levels * count)),
        in_specs=[VM, VM, VM, [VM] * len(tables), hbm_spec],
        out_specs=VM,
        scratch_shapes=[vmem(inverse.shape), pltpu.SemaphoreType.DMA((chunks,))],
        compiler_params=pltpu.CompilerParams(vmem_limit_bytes=LIMIT),
    )(terms, cell, prod, tables, pltpu.with_memory_space_constraint(inverse, pltpu.HBM))
    sol = everywhere(send)
    row3 = vmem((depth, 1, long))
    at = 3 + levels
    p, coupled_z, two, one, tz, _, tx = call(
        functools.partial(pressure_kernel, levels),
        (field, field, row3, row3),
        (sol, terms, pres, *sib, tz, store, tx),
        far=(at, at + 1, at + 2),
        keep=(at, at + 1, at + 2),
        scratch=(
            vmem((width * long // 128, lists), BF16),
            vmem((128, lists), BF16),
            vmem((rows, lists), BF16),
            vmem((1, lists), I32),
            vmem((1, count), I32),
        ),
    )
    two, one = (neighbour(two, "tile"), flip(one, 0, "tile"))
    row9 = vmem((3, depth, 1, long))
    plane3 = planes(3)
    s, outer, row_two, row_one, inner = call(
        search_kernel,
        (vmem(rhs.shape), plane3, row9, row9, plane3),
        (p, coupled_z, two, one, tx, ty, tz, rhs, block_diag, block_inv),
    )
    outer, row_two = (neighbour(outer), neighbour(row_two, "tile"))
    row_one, inner = (flip(row_one, 0, "tile"), flip(inner, 0))
    (part,) = call(inner_kernel, (vmem(rhs.shape),), (s, block_diag, tz, tx, ty))
    image, send = call(
        image_kernel,
        (vmem(rhs.shape), vmem((devices, 1, 128))),
        (part, outer, row_two, row_one, inner, rhs, tz, tx),
    )
    sums = everywhere(send)
    update, lin_res, ratio = call(
        finish_kernel, (hbm(rhs.shape), hbm(rhs.shape), hbm((1, 1))), (sums, s, image, rhs)
    )
    return (update, lin_res, ratio.reshape(()))


def solution(mesh):
    return jax.shard_map(
        shards,
        mesh=mesh,
        in_specs=(
            P(None, "layer", "tile", None),
            P(None, "layer", "tile", None),
            P(None, None, "layer", "tile", None),
            P(None, None, "layer", "tile", None),
            P("layer", "tile", None),
            P("layer", "tile", None),
            P("layer", "tile", None),
            P("layer", "tile", None),
            P(("tile", "layer")),
            P(("tile", "layer")),
            P(("tile", "layer")),
            P(("tile", "layer"), None),
        ),
        out_specs=(P(None, "layer", "tile", None), P(None, "layer", "tile", None), P()),
        check_vma=False,
    )
```

```python
import functools
import jax
import jax.numpy as jnp
from jax import lax
from jax.experimental import pallas as pl
from jax.experimental.pallas import tpu as pltpu
from jax.sharding import PartitionSpec as P

F32 = jnp.float32
BF16 = jnp.bfloat16
I32 = jnp.int32
BOTH = ("tile", "layer")
VM = pl.BlockSpec(memory_space=pltpu.VMEM)
LIMIT = 16 << 20
PARTS = 2


def hbm(shape):
    return jax.ShapeDtypeStruct(shape, F32)


def vmem(shape, dtype=F32):
    return pltpu.VMEM(shape, dtype)


def staged(kernel, where, outs, kept, column, *refs):
    count, sems = (len(where), refs[-1])
    held = list(refs[count + outs + len(kept) : -1])
    target_count = sum(where) - len(kept)
    held, extra = (held[:target_count], held[target_count:])
    target = dict(zip(kept, refs[count + outs : count + outs + len(kept)]))
    operands, copies = ([], [])
    for i, far in enumerate(where):
        if far:
            to = target[i] if i in target else held.pop(0)
            part = refs[i].at[:, 0] if i in column else refs[i]
            copies.append(pltpu.make_async_copy(part, to, sems.at[len(copies)]))
            operands.append(to)
        else:
            operands.append(refs[i])
    for copy in copies:
        copy.start()
    for copy in copies:
        copy.wait()
    kernel(*operands, *refs[count : count + outs], *extra)


def call(kernel, outs, args, far=(), keep=(), column=(), scratch=(), limit=LIMIT):
    where = [i in far for i in range(len(args))]
    spaces = [pltpu.HBM if w else pltpu.VMEM for w in where]
    every = (*outs, *(vmem(args[i].shape, args[i].dtype) for i in keep))
    return pl.pallas_call(
        functools.partial(staged, kernel, where, len(outs), tuple(keep), tuple(column)),
        out_shape=every,
        in_specs=[pl.BlockSpec(memory_space=s) for s in spaces],
        out_specs=(VM,) * len(every),
        scratch_shapes=[
            vmem(a.shape[:1] + a.shape[2:] if i in column else a.shape, a.dtype)
            for i, a in enumerate(args)
            if where[i] and i not in keep
        ]
        + [*scratch, pltpu.SemaphoreType.DMA((max(1, sum(where)),))],
        compiler_params=pltpu.CompilerParams(vmem_limit_bytes=limit),
    )(*[pltpu.with_memory_space_constraint(a, s) for a, s in zip(args, spaces)])


def iota(shape, dim):
    return lax.broadcasted_iota(I32, shape, dim)


def split(x):
    one = x.astype(BF16)
    rest = x - one.astype(F32)
    two = rest.astype(BF16)
    three = (rest - two.astype(F32)).astype(BF16)
    return [one, two, three]


def fold(x, parts=3):
    n = x.shape[0] // parts
    total = x[(parts - 1) * n :]
    for i in range(parts - 2, -1, -1):
        total = x[i * n : (i + 1) * n] + total
    return total


def onehot(index, size):
    return jnp.where(iota((size, index.shape[1]), 0) == index, 1.0, 0.0)


def dot(a, b):
    return lax.dot_general(a, b, (((1,), (0,)), ((), ())), preferred_element_type=F32)


def dot_nt(a, b):
    return lax.dot_general(a, b, (((1,), (1,)), ((), ())), preferred_element_type=F32)


def pick(tables, hi, hot):
    rows = tables[0].shape[0]
    parts = jnp.concatenate([p for table in tables for p in split(table)[:PARTS]], 0)
    got = dot(parts, hot)
    mask = onehot(hi, rows)
    n = PARTS * rows
    return [jnp.sum(fold(got[i * n : (i + 1) * n], PARTS) * mask, axis=0, keepdims=True) for i in range(len(tables))]


def pres_kernel(cell_in, front_in, prod_in, rhs_in, wts_in, tz_in, store_in, pres, send, ends, *scratch):
    (cell, front, prod, rhs, wts, tz, store), sems = scratch[:-1], scratch[-1]
    pairs = ((cell_in, cell), (front_in, front), (prod_in, prod), (rhs_in, rhs), (wts_in, wts), (tz_in, tz), (store_in, store))
    copies = [pltpu.make_async_copy(a, b, sems.at[i]) for i, (a, b) in enumerate(pairs)]
    for copy in copies:
        copy.start()
    for copy in copies[:3]:
        copy.wait()
    depth, width, long = pres.shape
    where = cell[...]
    hot = onehot(lax.rem(where, long), long).astype(BF16)
    for copy in copies[3:]:
        copy.wait()
    for z in range(depth):
        pres[z] = wts[0, z] * rhs[0, z] + wts[1, z] * rhs[1, z] + wts[2, z] * rhs[2, z]
    (found,) = pick([pres[...].reshape(depth * width, long)], lax.div(where, long), hot)
    both = jnp.concatenate([prod[...] * found, front[...].astype(F32), where.astype(F32)], 1)
    send[...] = jnp.broadcast_to(both[:, None], send.shape)
    tzs = [tz[z] for z in range(depth)]
    gs, invs, _, _, coefs = factors(tzs, [store[z] for z in range(depth)])
    y = local_solve([pres[z] for z in range(depth)], gs, invs, tzs)
    for i, value in enumerate((*coefs, y[0], y[-1], tzs[-1])):
        ends[i] = value


def is_right(level, axis="layer"):
    return (lax.axis_index(axis) >> level) % 2 == 1


def choose(level, mine, other, axis="layer"):
    right = is_right(level, axis)
    return (jnp.where(right, other, mine), jnp.where(right, mine, other))


def local_solve(rhs, upper, inv, tz):
    depth = len(rhs)
    y = [rhs[0] * inv[0]]
    for z in range(1, depth):
        y.append((rhs[z] + tz[z - 1] * y[-1]) * inv[z])
    for z in range(depth - 2, -1, -1):
        y[z] = y[z] + upper[z] * y[z + 1]
    return y


def factors(tz, store):
    depth = len(tz)
    gs, invs = ([], [])
    own = None
    for z in range(depth):
        own = store[z] if z == 0 else store[z] + gs[-1] * own
        invs.append(1.0 / (own + tz[z] if z < depth - 1 else own))
        gs.append(tz[z] * invs[-1])
    first = [invs[0]]
    for z in range(1, depth):
        first.append(tz[z - 1] * first[-1] * invs[z])
    final = [None] * depth
    final[-1] = invs[-1]
    for z in range(depth - 2, -1, -1):
        first[z] = first[z] + gs[z] * first[z + 1]
        final[z] = gs[z] * final[z + 1]
    return gs, invs, first, final, (first[0], first[-1], final[-1] + 1.0 / jnp.maximum(tz[-1], 1e-30))


def pair(level, own, sib):
    af, af_ = choose(level, own[0], sib[0])
    c, c_ = choose(level, own[1], sib[1])
    b, b_ = choose(level, own[2], sib[2])
    return af, c, b, af_, c_, b_, 1.0 / (b + af_)


def join_coefs(level, own, sib):
    af, c, _, _, c_, b_, g = pair(level, own, sib)
    return (af - c * c * g, c * c_ * g, b_ - c_ * c_ * g)


def join_ends(level, own, sib, mine, other):
    _, c, _, _, c_, _, g = pair(level, own, sib)
    yf, yf_ = choose(level, mine[0], other[0])
    yl, yl_ = choose(level, mine[1], other[1])
    flux = g * (yl - yf_)
    return (yf - c * flux, yl_ + c_ * flux)


def first_join_kernel(own, sib, tz, store, out, face, more, one, answers):
    depth = tz.shape[0]
    _, _, first, final, _ = factors([tz[z] for z in range(depth)], [store[z] for z in range(depth)])
    for z in range(depth):
        answers[z] = first[z]
        answers[depth + z] = final[z]
    join_kernel(0, own, sib, answers, out, face, more, one)


def join_kernel(level, own, sib, answers, out, face, more, one):
    depth, width, _ = more.shape
    depth = depth // 2
    _, c, _, _, c_, _, g = pair(level, own, sib)
    first, both, last = join_coefs(level, own, sib)
    yf, yl = join_ends(level, own, sib, (own[3], own[4]), (sib[3], sib[4]))
    out[0], out[1], out[2] = (first, both, last)
    out[3], out[4] = (yf, yl)
    lower = choose(level, own[5], sib[5])[1]
    out[5] = lower
    face[2] = lower
    right, later = (is_right(level), is_right(level + 1))
    face[0], face[1] = (jnp.where(later, first, last), jnp.where(later, yf, yl))
    cg, cg_ = (c * g, c_ * g)
    for z in range(depth):
        kf, kl = (answers[z], answers[depth + z])
        top = jnp.where(right, cg * kf, kf - cg * kl)
        bottom = jnp.where(right, kl - cg_ * kf, cg_ * kl)
        more[z] = top
        more[depth + z] = bottom
        one[z] = jnp.where(later, top, bottom)


def groups_of(levels):
    layers = lax.axis_size("layer")
    l = lax.axis_index("layer")
    base = lax.axis_index("tile") * layers
    out = [[base + l]]
    for level in range(levels):
        out.append([base + (((l >> level) ^ 1) << level) + i for i in range(1 << level)])
    return out


def front_kernel(recv, cell, prod, tables, inverse, send, held, sems):
    devices = recv.shape[0]
    count = recv.shape[2] // 3
    rows, length = inverse.shape
    lanes = 128
    chunks = sems.shape[0]
    wide = length // chunks
    cell, prod = (cell[...], prod[...])
    copies = [
        pltpu.make_async_copy(inverse.at[:, pl.ds(i * wide, wide)], held.at[:, pl.ds(i * wide, wide)], sems.at[i])
        for i in range(chunks)
    ]
    for copy in copies:
        copy.start()
    where, value = (cell, prod)
    depth, width, long = tables[-1].shape
    hi, lo = lax.div(where, long), lax.rem(where, long)
    stack = [t[k * depth : (k + 1) * depth].reshape(depth * width, long) for t in tables for k in range(t.shape[0] // depth)]
    found = [value * f for f in pick(stack, hi, onehot(lo, long).astype(BF16))]
    terms, index = (recv[:, 0, :count], recv[:, 0, count : 2 * count])
    high = jnp.floor(index * (1.0 / lanes))
    low = index - high * lanes
    parts = [p.astype(F32) for p in split(terms)[:PARTS]]
    row_of = iota((length // lanes, count), 0).astype(F32)
    lane_of = iota((lanes, count), 0).astype(F32)
    total = jnp.zeros((length // lanes, lanes), F32)
    for d in range(devices):
        hit = row_of == high[d : d + 1]
        left = jnp.concatenate([jnp.where(hit, p[d : d + 1], 0.0).astype(BF16) for p in parts], 0)
        right = jnp.where(lane_of == low[d : d + 1], 1.0, 0.0).astype(BF16)
        total = total + fold(dot_nt(left, right), PARTS)
    acc = jnp.zeros((rows, lanes), F32)
    for i in range(chunks):
        copies[i].wait()
        for r in range(i * wide // lanes, (i + 1) * wide // lanes):
            acc = acc + held[:, r * lanes : (r + 1) * lanes] * total[r : r + 1]
    parts = jnp.concatenate(split(acc), 1)
    out = dot_nt(jnp.ones((8, parts.shape[1]), BF16), parts)
    send[...] = jnp.broadcast_to(jnp.concatenate([out[0:1], value, *found], 1)[:, None], send.shape)


def gathered(values, rows_hot, lanes_hot, start, size, ext, parts):
    hot = lanes_hot[:, start : start + size]
    pieces = [hot * p for v in values for p in split(v)[:parts]]
    got = dot_nt(rows_hot[:, start : start + size], jnp.concatenate(pieces, 0))
    planes = []
    lanes = hot.shape[0]
    for i in range(len(values)):
        plane = got[:, i * parts * lanes : (i * parts + 1) * lanes]
        for k in range(1, parts):
            j = i * parts + k
            plane = plane + got[:, j * lanes : (j + 1) * lanes]
        planes.append(jnp.concatenate([plane[r : r + ext] for r in range(0, plane.shape[0], ext)], 1))
    return planes


def beside(centre, tx, ty):
    width, long = centre.shape
    row, col = (iota(centre.shape, 0), iota(centre.shape, 1))
    total = tx * jnp.where(row == width - 1, 0.0, pltpu.roll(centre, width - 1, 0))
    total = total + jnp.where(row == 0, 0.0, pltpu.roll(tx * centre, 1, 0))
    total = total + ty * jnp.where(col == long - 1, 0.0, pltpu.roll(centre, long - 1, 1))
    return total + jnp.where(col == 0, 0.0, pltpu.roll(ty * centre, 1, 1))


def tile_rows(first, last, one, two):
    odd = is_right(0, "tile")
    one[...] = jnp.where(odd, first, last)
    two[...] = jnp.where(odd, last, first)


def table_kernel(levels, shape, terms, rows_hot, lanes_hot, sol_hot, sol_row, layer):
    _, width, long = shape
    lanes = 128
    rows = sol_hot.shape[0]
    count = terms.shape[2] // 3
    at = 0
    for members in groups_of(levels):
        for device in members:
            entry = terms[device]
            index = entry[:, count : 2 * count].astype(I32)
            cell = entry[:, 2 * count :].astype(I32)
            y, x = lax.rem(cell, long), lax.rem(lax.div(cell, long), width)
            here = pl.ds(at, count)
            rows_hot[:, here] = onehot(lax.div(y, lanes) * width + x, rows_hot.shape[0]).astype(BF16)
            lanes_hot[:, here] = onehot(lax.rem(y, lanes), lanes).astype(BF16)
            sol_hot[:, here] = onehot(lax.rem(index, rows), rows).astype(BF16)
            sol_row[:, here] = lax.div(index, rows)
            if at == 0:
                layer[...] = lax.div(cell, long * width)
            at += count


def pressure_kernel(levels, recv, terms, pres, *refs):
    sib, (tz, store, tx, p, coupled_z, two, one, rows_hot, lanes_hot, sol_hot, sol_row, layer) = (refs[:levels], refs[levels:])
    depth, width, long = pres.shape
    table_kernel(levels, pres.shape, terms, rows_hot, lanes_hot, sol_hot, sol_row, layer)
    rows, count = (sol_hot.shape[0], layer.shape[1])
    groups = groups_of(levels)
    layer = layer[...]
    table = jnp.concatenate(split(recv[...].reshape(recv.shape[0], recv.shape[2])[:, :rows]), 0)
    sol = fold(dot(table, sol_hot[...]))
    sol = jnp.sum(jnp.where(iota(sol.shape, 0) == sol_row[...], sol, 0.0), axis=0, keepdims=True)

    def listed(group, column):
        at = rows + column * count
        return jnp.concatenate([recv[device][:, at : at + count] for device in group], 1)

    tzs = [tz[z] for z in range(depth)]
    gs, invs, first, final, coefs = factors(tzs, [store[z] for z in range(depth)])
    own = [coefs]
    value = listed(groups[0], 0) * sol[:, :count]
    values = [jnp.where(layer == z, value, 0.0) for z in range(depth)]
    change = gathered(values, rows_hot, lanes_hot, 0, count, width, PARTS)
    y = local_solve([pres[z] - change[z] for z in range(depth)], gs, invs, tzs)
    mine = (y[0], y[-1])
    steps = []
    start = count
    for level in range(levels):
        size = len(groups[level + 1]) * count
        top = level == levels - 1
        columns = [1 + 2 * level] if top else [1 + 2 * level, 2 + 2 * level]
        values = [listed(groups[level + 1], c) * sol[:, start : start + size] for c in columns]
        change = gathered(values, rows_hot, lanes_hot, start, size, width, PARTS)
        start += size
        if top:
            other = sib[level][1] - change[0]
            steps.append((mine, (other, other)))
        else:
            other = (sib[level][3] - change[0], sib[level][4] - change[1])
            steps.append((mine, other))
            mine = join_ends(level, own[level], sib[level], mine, other)
            own.append(join_coefs(level, own[level], sib[level]))
    above = below = jnp.zeros((width, long), F32)
    tzp = jnp.zeros((width, long), F32)
    place = lax.axis_index("layer")
    for level in range(levels - 1, -1, -1):
        mine, other = steps[level]
        yl, _ = choose(level, mine[1], other[1])
        _, yf_ = choose(level, mine[0], other[0])
        flux = yl - yf_
        if level == levels - 1:
            b, _ = choose(level, own[level][2], sib[level][0])
            _, af_ = choose(level, own[level][0], sib[level][0])
            g = 1.0 / (b + af_)
            before = sib[level][2]
        else:
            _, c, _, _, c_, _, g = pair(level, own[level], sib[level])
            flux = flux + c * above - c_ * below
            before = sib[level][5]
        tzp = jnp.where(place % (2 << level) == 1 << level, before, tzp)
        flux = g * flux
        right = is_right(level)
        above, below = (jnp.where(right, flux, above), jnp.where(right, below, -flux))
    values = [y[z] + first[z] * above + final[z] * below for z in range(depth)]
    is_last = place == (1 << levels) - 1
    for z in range(depth):
        p[z] = values[z]
        total = above + tzp * values[z] if z == 0 else tzs[z - 1] * values[z - 1]
        if z == depth - 1:
            coupled_z[z] = total + jnp.where(is_last, 0.0, below + tzs[z] * values[z])
        else:
            coupled_z[z] = total + tzs[z] * values[z + 1]
    for z in range(depth):
        tile_rows(values[z][0:1], (tx[z] * values[z])[width - 1 :], one.at[z], two.at[z])


def search_kernel(p, coupled_z, two, one, tx, ty, tz, rhs, diag, binv, s, outer, row_two, row_one, inner):
    depth, width, _ = p.shape
    odd = is_right(0, "tile")
    right = is_right(0)
    row = iota(p.shape[1:], 0)
    for z in range(depth):
        centre = p[z]
        after = jnp.where(odd, two[z], one[z])
        before = jnp.where(odd, one[z], two[z])
        coupled = coupled_z[z] + beside(centre, tx[z], ty[z])
        coupled = coupled + jnp.where(row == 0, before, 0.0) + jnp.where(row == width - 1, tx[z] * after, 0.0)
        remain = [rhs[c, z] - diag[c, 0, z] * centre for c in range(3)]
        remain[0] = remain[0] + coupled
        for c in range(3):
            value = binv[c, 0, z] * remain[0] + binv[c, 1, z] * remain[1] + binv[c, 2, z] * remain[2]
            if c == 0:
                value = centre + value
            s[c, z] = value
            tile_rows(value[0:1], (tx[z] * value)[width - 1 :], row_one.at[c, z], row_two.at[c, z])
    for c in range(3):
        top, bottom = (s[c, 0], tz[depth - 1] * s[c, depth - 1])
        inner[c] = jnp.where(right, top, bottom)
        outer[c] = jnp.where(right, bottom, top)


def inner_kernel(s, diag, tz, tx, ty, image):
    depth = s.shape[1]
    for z in range(depth):
        for c in range(3):
            total = diag[c, 0, z] * s[0, z] + diag[c, 1, z] * s[1, z] + diag[c, 2, z] * s[2, z]
            total = total - beside(s[c, z], tx[z], ty[z])
            if z:
                total = total - tz[z - 1] * s[c, z - 1]
            if z < depth - 1:
                total = total - tz[z] * s[c, z + 1]
            image[c, z] = total


def image_kernel(part, outer, row_one, row_two, inner, rhs, tz, tx, image, send):
    depth, width = part.shape[1:3]
    right, odd = (is_right(0), is_right(0, "tile"))
    row = iota(part.shape[2:], 0)
    along = power = start = 0.0
    for z in range(depth):
        for c in range(3):
            value = part[c, z]
            if z == 0:
                value = value - jnp.where(right, inner[c], outer[c])
            if z == depth - 1:
                value = value - tz[z] * jnp.where(right, outer[c], inner[c])
            after = jnp.where(odd, row_two[c, z], row_one[c, z])
            before = jnp.where(odd, row_one[c, z], row_two[c, z])
            value = value - jnp.where(row == 0, before, 0.0) - jnp.where(row == width - 1, tx[z] * after, 0.0)
            image[c, z] = value
            given = rhs[c, z]
            along = along + value * given
            power = power + value * value
            start = start + given * given
    along, power, start = (jnp.sum(along), jnp.sum(power), jnp.sum(start))
    omega = along / jnp.where(power > 0.0, power, 1.0)
    square = cross = 0.0
    for z in range(depth):
        for c in range(3):
            value = image[c, z]
            left = rhs[c, z] - omega * value
            square = square + left * left
            cross = cross + left * value
    lane = iota((1, send.shape[2]), 1)
    out = jnp.zeros((1, send.shape[2]), F32)
    for i, value in enumerate((along, power, start, jnp.sum(square), jnp.sum(cross), omega)):
        out = jnp.where(lane == i, value, out)
    send[...] = jnp.broadcast_to(out[:, None], send.shape)


def finish_kernel(recv, s, image, rhs, update, lin_res, ratio):
    sums = recv[...].reshape(recv.shape[0], recv.shape[2])
    whole = jnp.sum(sums, axis=0, keepdims=True)
    omega = whole[:, 0:1] / whole[:, 1:2]
    shift = sums[:, 5:6] - omega
    square = sums[:, 3:4] + 2.0 * shift * sums[:, 4:5] + shift * shift * sums[:, 1:2]
    ratio[...] = jnp.sqrt(jnp.sum(square, axis=0, keepdims=True) / whole[:, 2:3])
    for c in range(3):
        for z in range(s.shape[1]):
            update[c, z] = omega * s[c, z]
            lin_res[c, z] = rhs[c, z] - omega * image[c, z]


def flip(x, level, axis="layer"):
    return lax.ppermute(x, axis, [(i, i ^ (1 << level)) for i in range(lax.axis_size(axis))])


def neighbour(x, axis="layer"):
    pairs = [(i, i + 1) for i in range(1, lax.axis_size(axis) - 1, 2)]
    return lax.ppermute(x, axis, pairs + [(j, i) for i, j in pairs])


def everywhere(x):
    return lax.all_to_all(x, BOTH, split_axis=0, concat_axis=0, tiled=True)


def shards(rhs, weights, block_diag, block_inv, tx, ty, tz, store, cell, front, prod, inverse):
    layers = lax.axis_size("layer")
    devices = lax.axis_size("tile") * layers
    levels = layers.bit_length() - 1
    depth, width, long = tx.shape
    count = cell.shape[0]
    rows = inverse.shape[0]
    lists = layers * count
    cell, front, prod = (cell.reshape(1, -1), front.reshape(1, -1), prod.reshape(1, -1))
    field = vmem(tx.shape)

    def planes(n):
        return vmem((n, width, long))

    hbm_spec = pl.BlockSpec(memory_space=pltpu.HBM)
    given = (cell, front, prod, rhs, weights, tz, store)
    pres, send, ends = pl.pallas_call(
        pres_kernel,
        out_shape=(field, vmem((devices, 1, 3 * count)), planes(6)),
        in_specs=[hbm_spec] * len(given),
        out_specs=(VM,) * 3,
        scratch_shapes=[vmem(a.shape, a.dtype) for a in given] + [pltpu.SemaphoreType.DMA((len(given),))],
        compiler_params=pltpu.CompilerParams(vmem_limit_bytes=LIMIT),
    )(*[pltpu.with_memory_space_constraint(a, pltpu.HBM) for a in given])
    terms = everywhere(send)
    sib, tables = ([], [])
    for level in range(levels - 1):
        sib.append(flip(ends, level))
        outs = (planes(6), planes(3), planes(2 * depth), field)
        if level == 0:
            ends, face, more, last, answers = call(
                first_join_kernel, (*outs, planes(2 * depth)), (ends, sib[-1], tz, store), far=(2, 3)
            )
        else:
            ends, face, more, last = call(functools.partial(join_kernel, level), outs, (ends, sib[-1], answers))
        tables.append(answers)
        answers = more
    tables.append(last)
    sib.append(flip(face, levels - 1))
    chunks = 8
    terms, *tables = lax.optimization_barrier((terms, *tables))
    send = pl.pallas_call(
        front_kernel,
        out_shape=vmem((devices, 1, rows + 2 * levels * count)),
        in_specs=[VM, VM, VM, [VM] * len(tables), hbm_spec],
        out_specs=VM,
        scratch_shapes=[vmem(inverse.shape), pltpu.SemaphoreType.DMA((chunks,))],
        compiler_params=pltpu.CompilerParams(vmem_limit_bytes=LIMIT),
    )(terms, cell, prod, tables, pltpu.with_memory_space_constraint(inverse, pltpu.HBM))
    sol = everywhere(send)
    row3 = vmem((depth, 1, long))
    at = 3 + levels
    p, coupled_z, two, one, tz, _, tx = call(
        functools.partial(pressure_kernel, levels),
        (field, field, row3, row3),
        (sol, terms, pres, *sib, tz, store, tx),
        far=(at, at + 1, at + 2),
        keep=(at, at + 1, at + 2),
        scratch=(
            vmem((width * long // 128, lists), BF16),
            vmem((128, lists), BF16),
            vmem((rows, lists), BF16),
            vmem((1, lists), I32),
            vmem((1, count), I32),
        ),
    )
    two, one = (neighbour(two, "tile"), flip(one, 0, "tile"))
    row9 = vmem((3, depth, 1, long))
    plane3 = planes(3)
    s, outer, row_two, row_one, inner = call(
        search_kernel,
        (vmem(rhs.shape), plane3, row9, row9, plane3),
        (p, coupled_z, two, one, tx, ty, tz, rhs, block_diag, block_inv),
    )
    outer, row_two = (neighbour(outer), neighbour(row_two, "tile"))
    row_one, inner = (flip(row_one, 0, "tile"), flip(inner, 0))
    (part,) = call(inner_kernel, (vmem(rhs.shape),), (s, block_diag, tz, tx, ty))
    image, send = call(
        image_kernel,
        (vmem(rhs.shape), vmem((devices, 1, 128))),
        (part, outer, row_one, row_two, inner, rhs, tz, tx),
    )
    sums = everywhere(send)
    update, lin_res, ratio = call(
        finish_kernel, (hbm(rhs.shape), hbm(rhs.shape), hbm((1, 1))), (sums, s, image, rhs)
    )
    return (update, lin_res, ratio.reshape(()))


def solution(mesh):
    return jax.shard_map(
        shards,
        mesh=mesh,
        in_specs=(
            P(None, "layer", "tile", None),
            P(None, "layer", "tile", None),
            P(None, None, "layer", "tile", None),
            P(None, None, "layer", "tile", None),
            P("layer", "tile", None),
            P("layer", "tile", None),
            P("layer", "tile", None),
            P("layer", "tile", None),
            P(("tile", "layer")),
            P(("tile", "layer")),
            P(("tile", "layer")),
            P(("tile", "layer"), None),
        ),
        out_specs=(P(None, "layer", "tile", None), P(None, "layer", "tile", None), P()),
        check_vma=False,
    )
```

```python
import functools
import jax
import jax.numpy as jnp
from jax import lax
from jax.experimental import pallas as pl
from jax.experimental.pallas import tpu as pltpu
from jax.sharding import PartitionSpec as P

F32 = jnp.float32
BF16 = jnp.bfloat16
I32 = jnp.int32
BOTH = ("tile", "layer")
VM = pl.BlockSpec(memory_space=pltpu.VMEM)
LIMIT = 16 << 20
PARTS = 2


def hbm(shape):
    return jax.ShapeDtypeStruct(shape, F32)


def vmem(shape, dtype=F32):
    return pltpu.VMEM(shape, dtype)


def staged(kernel, where, outs, kept, column, late, *refs):
    count, sems = (len(where), refs[-1])
    held = list(refs[count + outs + len(kept) : -1])
    target_count = sum(where) - len(kept)
    held, extra = (held[:target_count], held[target_count:])
    target = dict(zip(kept, refs[count + outs : count + outs + len(kept)]))
    operands, copies = ([], [])
    for i, far in enumerate(where):
        if far:
            to = target[i] if i in target else held.pop(0)
            part = refs[i].at[:, 0] if i in column else refs[i]
            copies.append(pltpu.make_async_copy(part, to, sems.at[len(copies)]))
            operands.append(to)
        else:
            operands.append(refs[i])
    for copy in copies:
        copy.start()
    places = [i for i, far in enumerate(where) if far]
    rest = [copy for i, copy in zip(places, copies) if i in late]
    for i, copy in zip(places, copies):
        if i not in late:
            copy.wait()
    more = (lambda: [copy.wait() for copy in rest],) if late else ()
    kernel(*more, *operands, *refs[count : count + outs], *extra)


def call(kernel, outs, args, far=(), keep=(), column=(), late=(), scratch=(), limit=LIMIT):
    where = [i in far for i in range(len(args))]
    spaces = [pltpu.HBM if w else pltpu.VMEM for w in where]
    every = (*outs, *(vmem(args[i].shape, args[i].dtype) for i in keep))
    return pl.pallas_call(
        functools.partial(staged, kernel, where, len(outs), tuple(keep), tuple(column), tuple(late)),
        out_shape=every,
        in_specs=[pl.BlockSpec(memory_space=s) for s in spaces],
        out_specs=(VM,) * len(every),
        scratch_shapes=[
            vmem(a.shape[:1] + a.shape[2:] if i in column else a.shape, a.dtype)
            for i, a in enumerate(args)
            if where[i] and i not in keep
        ]
        + [*scratch, pltpu.SemaphoreType.DMA((max(1, sum(where)),))],
        compiler_params=pltpu.CompilerParams(vmem_limit_bytes=limit),
    )(*[pltpu.with_memory_space_constraint(a, s) for a, s in zip(args, spaces)])


def iota(shape, dim):
    return lax.broadcasted_iota(I32, shape, dim)


def split(x):
    one = x.astype(BF16)
    rest = x - one.astype(F32)
    two = rest.astype(BF16)
    three = (rest - two.astype(F32)).astype(BF16)
    return [one, two, three]


def fold(x, parts=3):
    n = x.shape[0] // parts
    total = x[(parts - 1) * n :]
    for i in range(parts - 2, -1, -1):
        total = x[i * n : (i + 1) * n] + total
    return total


def onehot(index, size):
    return jnp.where(iota((size, index.shape[1]), 0) == index, 1.0, 0.0)


def dot(a, b):
    return lax.dot_general(a, b, (((1,), (0,)), ((), ())), preferred_element_type=F32)


def dot_nt(a, b):
    return lax.dot_general(a, b, (((1,), (1,)), ((), ())), preferred_element_type=F32)


def pick(tables, hi, hot):
    rows = tables[0].shape[0]
    parts = jnp.concatenate([p for table in tables for p in split(table)[:PARTS]], 0)
    got = dot(parts, hot)
    mask = onehot(hi, rows)
    n = PARTS * rows
    return [jnp.sum(fold(got[i * n : (i + 1) * n], PARTS) * mask, axis=0, keepdims=True) for i in range(len(tables))]


def pres_kernel(cell_in, front_in, prod_in, rhs_in, wts_in, tz_in, store_in, pres, send, ends, *scratch):
    (cell, front, prod, rhs, wts, tz, store), sems = scratch[:-1], scratch[-1]
    pairs = ((cell_in, cell), (front_in, front), (prod_in, prod), (rhs_in, rhs), (wts_in, wts), (tz_in, tz), (store_in, store))
    copies = [pltpu.make_async_copy(a, b, sems.at[i]) for i, (a, b) in enumerate(pairs)]
    for copy in copies:
        copy.start()
    for copy in copies[:3]:
        copy.wait()
    depth, width, long = pres.shape
    where = cell[...]
    hot = onehot(lax.rem(where, long), long).astype(BF16)
    for copy in copies[3:]:
        copy.wait()
    for z in range(depth):
        pres[z] = wts[0, z] * rhs[0, z] + wts[1, z] * rhs[1, z] + wts[2, z] * rhs[2, z]
    (found,) = pick([pres[...].reshape(depth * width, long)], lax.div(where, long), hot)
    both = jnp.concatenate([prod[...] * found, front[...].astype(F32), where.astype(F32)], 1)
    send[...] = jnp.broadcast_to(both[:, None], send.shape)
    tzs = [tz[z] for z in range(depth)]
    gs, invs, _, _, coefs = factors(tzs, [store[z] for z in range(depth)])
    y = local_solve([pres[z] for z in range(depth)], gs, invs, tzs)
    for i, value in enumerate((*coefs, y[0], y[-1], tzs[-1])):
        ends[i] = value


def is_right(level, axis="layer"):
    return (lax.axis_index(axis) >> level) % 2 == 1


def choose(level, mine, other, axis="layer"):
    right = is_right(level, axis)
    return (jnp.where(right, other, mine), jnp.where(right, mine, other))


def local_solve(rhs, upper, inv, tz):
    depth = len(rhs)
    y = [rhs[0] * inv[0]]
    for z in range(1, depth):
        y.append((rhs[z] + tz[z - 1] * y[-1]) * inv[z])
    for z in range(depth - 2, -1, -1):
        y[z] = y[z] + upper[z] * y[z + 1]
    return y


def factors(tz, store):
    depth = len(tz)
    gs, invs = ([], [])
    own = None
    for z in range(depth):
        own = store[z] if z == 0 else store[z] + gs[-1] * own
        invs.append(1.0 / (own + tz[z] if z < depth - 1 else own))
        gs.append(tz[z] * invs[-1])
    first = [invs[0]]
    for z in range(1, depth):
        first.append(tz[z - 1] * first[-1] * invs[z])
    final = [None] * depth
    final[-1] = invs[-1]
    for z in range(depth - 2, -1, -1):
        first[z] = first[z] + gs[z] * first[z + 1]
        final[z] = gs[z] * final[z + 1]
    return gs, invs, first, final, (first[0], first[-1], final[-1] + 1.0 / jnp.maximum(tz[-1], 1e-30))


def pair(level, own, sib):
    af, af_ = choose(level, own[0], sib[0])
    c, c_ = choose(level, own[1], sib[1])
    b, b_ = choose(level, own[2], sib[2])
    return af, c, b, af_, c_, b_, 1.0 / (b + af_)


def join_coefs(level, own, sib):
    af, c, _, _, c_, b_, g = pair(level, own, sib)
    return (af - c * c * g, c * c_ * g, b_ - c_ * c_ * g)


def join_ends(level, own, sib, mine, other):
    _, c, _, _, c_, _, g = pair(level, own, sib)
    yf, yf_ = choose(level, mine[0], other[0])
    yl, yl_ = choose(level, mine[1], other[1])
    flux = g * (yl - yf_)
    return (yf - c * flux, yl_ + c_ * flux)


def first_join_kernel(final, own, sib, pres, tz, store, tx, cell, prod, low, high, *outs):
    depth, width, _ = tz.shape
    for k, ref in enumerate((tz, store, pres, tx)):
        for z in range(depth):
            low[k * depth + z] = ref[z, 0:1]
            high[k * depth + z] = ref[z, width - 1 : width]
    _, _, first, last, _ = factors([tz[z] for z in range(depth)], [store[z] for z in range(depth)])
    join(0, final, own, sib, first + last, cell, prod, *outs)


def join_kernel(level, final, own, sib, answers, cell, prod, *outs):
    join(level, final, own, sib, [answers[i] for i in range(answers.shape[0])], cell, prod, *outs)


def join(level, final, own, sib, answers, cell, prod, found, *outs):
    depth = len(answers) // 2
    width, long = answers[0].shape
    _, c, _, _, c_, _, g = pair(level, own, sib)
    first, both, last = join_coefs(level, own, sib)
    yf, yl = join_ends(level, own, sib, (own[3], own[4]), (sib[3], sib[4]))
    lower = choose(level, own[5], sib[5])[1]
    right, later = (is_right(level), is_right(level + 1))
    cg, cg_ = (c * g, c_ * g)
    tops, bottoms = ([], [])
    for z in range(depth):
        kf, kl = (answers[z], answers[depth + z])
        tops.append(jnp.where(right, cg * kf, kf - cg * kl))
        bottoms.append(jnp.where(right, kl - cg_ * kf, cg_ * kl))
    tables = [answers[:depth], answers[depth:]]
    if final:
        (face,) = outs
        face[0], face[1] = (jnp.where(later, first, last), jnp.where(later, yf, yl))
        face[2] = lower
        tables.append([jnp.where(later, tops[z], bottoms[z]) for z in range(depth)])
    else:
        out, more = outs
        for i, value in enumerate((first, both, last, yf, yl, lower)):
            out[i] = value
        for i, value in enumerate(tops + bottoms):
            more[i] = value
    where = cell[...]
    hot = onehot(lax.rem(where, long), long).astype(BF16)
    stack = [jnp.concatenate(t, 0) for t in tables]
    got = pick(stack, lax.div(where, long), hot)
    found[...] = jnp.concatenate([prod[...] * value for value in got], 1)


def groups_of(levels):
    layers = lax.axis_size("layer")
    l = lax.axis_index("layer")
    base = lax.axis_index("tile") * layers
    out = [[base + l]]
    for level in range(levels):
        out.append([base + (((l >> level) ^ 1) << level) + i for i in range(1 << level)])
    return out


def front_kernel(recv, found, inverse, send, held, sems):
    devices = recv.shape[0]
    count = recv.shape[2] // 3
    rows, length = inverse.shape
    lanes = 128
    chunks = sems.shape[0]
    wide = length // chunks
    found = found[...]
    copies = [
        pltpu.make_async_copy(inverse.at[:, pl.ds(i * wide, wide)], held.at[:, pl.ds(i * wide, wide)], sems.at[i])
        for i in range(chunks)
    ]
    for copy in copies:
        copy.start()
    terms, index = (recv[:, 0, :count], recv[:, 0, count : 2 * count])
    high = jnp.floor(index * (1.0 / lanes))
    low = index - high * lanes
    parts = [p.astype(F32) for p in split(terms)[:PARTS]]
    row_of = iota((length // lanes, count), 0).astype(F32)
    lane_of = iota((lanes, count), 0).astype(F32)
    total = jnp.zeros((length // lanes, lanes), F32)
    for d in range(devices):
        hit = row_of == high[d : d + 1]
        left = jnp.concatenate([jnp.where(hit, p[d : d + 1], 0.0).astype(BF16) for p in parts], 0)
        right = jnp.where(lane_of == low[d : d + 1], 1.0, 0.0).astype(BF16)
        total = total + fold(dot_nt(left, right), PARTS)
    acc = jnp.zeros((rows, lanes), F32)
    for i in range(chunks):
        copies[i].wait()
        for r in range(i * wide // lanes, (i + 1) * wide // lanes):
            acc = acc + held[:, r * lanes : (r + 1) * lanes] * total[r : r + 1]
    parts = jnp.concatenate(split(acc), 1)
    out = dot_nt(jnp.ones((8, parts.shape[1]), BF16), parts)
    send[...] = jnp.broadcast_to(jnp.concatenate([out[0:1], found], 1)[:, None], send.shape)


def gathered(values, rows_hot, lanes_hot, start, size, ext, parts):
    hot = lanes_hot[:, start : start + size]
    pieces = [hot * p for v in values for p in split(v)[:parts]]
    got = dot_nt(rows_hot[:, start : start + size], jnp.concatenate(pieces, 0))
    planes = []
    lanes = hot.shape[0]
    for i in range(len(values)):
        plane = got[:, i * parts * lanes : (i * parts + 1) * lanes]
        for k in range(1, parts):
            j = i * parts + k
            plane = plane + got[:, j * lanes : (j + 1) * lanes]
        planes.append(jnp.concatenate([plane[r : r + ext] for r in range(0, plane.shape[0], ext)], 1))
    return planes


def beside(centre, tx, ty):
    width, long = centre.shape
    row, col = (iota(centre.shape, 0), iota(centre.shape, 1))
    total = tx * jnp.where(row == width - 1, 0.0, pltpu.roll(centre, width - 1, 0))
    total = total + jnp.where(row == 0, 0.0, pltpu.roll(tx * centre, 1, 0))
    total = total + ty * jnp.where(col == long - 1, 0.0, pltpu.roll(centre, long - 1, 1))
    return total + jnp.where(col == 0, 0.0, pltpu.roll(ty * centre, 1, 1))


def tile_rows(first, last, one, two):
    odd = is_right(0, "tile")
    one[...] = jnp.where(odd, first, last)
    two[...] = jnp.where(odd, last, first)


def table_kernel(lists, shape, terms, hots, side=False):
    _, width, long = shape
    rows_hot, lanes_hot, sol_hot, sol_row, layer = hots
    lanes = 128
    rows = sol_hot.shape[0]
    count = terms.shape[2] // 3
    at = 0
    for members in lists:
        for k, device in enumerate(members):
            entry = terms[device]
            index = entry[:, count : 2 * count].astype(I32)
            cell = entry[:, 2 * count :].astype(I32)
            y, x = lax.rem(cell, long), lax.rem(lax.div(cell, long), width)
            if not side:
                row = lax.div(y, lanes) * width + x
            elif k % 2 == 0:
                row = jnp.where(x == 0, lax.div(y, lanes) * 8, -1)
            else:
                row = jnp.where(x == width - 1, lax.div(y, lanes) * 8 + 7, -1)
            here = pl.ds(at, count)
            rows_hot[:, here] = onehot(row, rows_hot.shape[0]).astype(BF16)
            lanes_hot[:, here] = onehot(lax.rem(y, lanes), lanes).astype(BF16)
            sol_hot[:, here] = onehot(lax.rem(index, rows), rows).astype(BF16)
            sol_row[:, here] = lax.div(index, rows)
            if at < layer.shape[1]:
                layer[:, here] = lax.div(cell, long * width)
            at += count


def column_solve(levels, recv, lists, hots, tz, store, pres, sib):
    rows_hot, lanes_hot, sol_hot, sol_row, layer = hots
    depth = len(tz)
    high = tz[0].shape[0]
    rows, count = (sol_hot.shape[0], recv.shape[2])
    count = (count - rows) // (2 * levels)
    table = jnp.concatenate(split(recv[...].reshape(recv.shape[0], recv.shape[2])[:, :rows]), 0)
    sol = fold(dot(table, sol_hot[...]))
    sol = jnp.sum(jnp.where(iota(sol.shape, 0) == sol_row[...], sol, 0.0), axis=0, keepdims=True)
    layer = layer[...]

    def listed(group, column):
        at = rows + column * count
        return jnp.concatenate([recv[device][:, at : at + count] for device in group], 1)

    gs, invs, first, final, coefs = factors(tz, store)
    own = [coefs]
    start = layer.shape[1]
    value = listed(lists[0], 0) * sol[:, :start]
    values = [jnp.where(layer == z, value, 0.0) for z in range(depth)]
    change = gathered(values, rows_hot, lanes_hot, 0, start, high, PARTS)
    y = local_solve([pres[z] - change[z] for z in range(depth)], gs, invs, tz)
    mine = (y[0], y[-1])
    steps = []
    for level in range(levels):
        size = len(lists[level + 1]) * count
        top = level == levels - 1
        columns = [1 + 2 * level] if top else [1 + 2 * level, 2 + 2 * level]
        values = [listed(lists[level + 1], c) * sol[:, start : start + size] for c in columns]
        change = gathered(values, rows_hot, lanes_hot, start, size, high, PARTS)
        start += size
        if top:
            other = sib[level][1] - change[0]
            steps.append((mine, (other, other)))
        else:
            other = (sib[level][3] - change[0], sib[level][4] - change[1])
            steps.append((mine, other))
            mine = join_ends(level, own[level], sib[level], mine, other)
            own.append(join_coefs(level, own[level], sib[level]))
    above = below = tzp = jnp.zeros(tz[0].shape, F32)
    place = lax.axis_index("layer")
    for level in range(levels - 1, -1, -1):
        mine, other = steps[level]
        yl, _ = choose(level, mine[1], other[1])
        _, yf_ = choose(level, mine[0], other[0])
        flux = yl - yf_
        if level == levels - 1:
            b, _ = choose(level, own[level][2], sib[level][0])
            _, af_ = choose(level, own[level][0], sib[level][0])
            g = 1.0 / (b + af_)
            before = sib[level][2]
        else:
            _, c, _, _, c_, _, g = pair(level, own[level], sib[level])
            flux = flux + c * above - c_ * below
            before = sib[level][5]
        tzp = jnp.where(place % (2 << level) == 1 << level, before, tzp)
        flux = g * flux
        right = is_right(level)
        above, below = (jnp.where(right, flux, above), jnp.where(right, below, -flux))
    return [y[z] + first[z] * above + final[z] * below for z in range(depth)], above, below, tzp


def pressure_kernel(levels, recv, terms, pres, *refs):
    sib, (tz, store, tx, binv, p, coupled_z, *hots) = (refs[:levels], refs[levels:])
    depth = pres.shape[0]
    lists = groups_of(levels)
    table_kernel(lists, pres.shape, terms, hots)
    tzs = [tz[z] for z in range(depth)]
    values, above, below, tzp = column_solve(
        levels, recv, lists, hots, tzs, [store[z] for z in range(depth)], [pres[z] for z in range(depth)], sib
    )
    is_last = lax.axis_index("layer") == (1 << levels) - 1
    for z in range(depth):
        p[z] = values[z]
        total = above + tzp * values[z] if z == 0 else tzs[z - 1] * values[z - 1]
        if z == depth - 1:
            coupled_z[z] = total + jnp.where(is_last, 0.0, below + tzs[z] * values[z])
        else:
            coupled_z[z] = total + tzs[z] * values[z + 1]


def edge_kernel(levels, low, high, *refs):
    sib, (one, two) = (refs[:levels], refs[levels:])
    for ref in (one, two):
        ref[...] = jnp.zeros(ref.shape, F32)
    n = low.shape[0]
    tile_rows(low[...], high[...], one.at[pl.ds(0, n)], two.at[pl.ds(0, n)])
    at = n
    for block in sib:
        width = block.shape[1]
        for i in range(block.shape[0]):
            tile_rows(block[i, 0:1], block[i, width - 1 : width], one.at[at], two.at[at])
            at += 1


def search_kernel(levels, shapes, ready, recv, terms, two, one, p, coupled_z, tx, tz, binv, rhs, diag, ty, *refs):
    (s, outer, row_two, row_one, inner), (planes, *hots) = (refs[:5], refs[5:])
    depth, width, long = p.shape
    tiles, layers = (lax.axis_size("tile"), lax.axis_size("layer"))
    tile = lax.axis_index("tile")
    odd, right = (is_right(0, "tile"), is_right(0))
    row = iota(p.shape[1:], 0)
    planes[...] = jnp.zeros(planes.shape, F32)
    for i in range(planes.shape[0]):
        planes[i, 0:1] = jnp.where(odd, two[i], one[i])
        planes[i, 7:8] = jnp.where(odd, one[i], two[i])
    lists = [
        [jnp.clip(device + step, 0, tiles * layers - 1) for device in members for step in (layers, -layers)]
        for members in groups_of(levels)
    ]
    table_kernel(lists, p.shape, terms, hots, side=True)
    has_next, has_last = ((tile < tiles - 1).astype(F32), (tile > 0).astype(F32))
    real = jnp.where(iota((8, long), 0) < 4, has_next, has_last)
    blocks = []
    at = 4 * depth
    for size in shapes:
        blocks.append([planes[at + i] for i in range(size)])
        at += size
    beyond, _, _, _ = column_solve(
        levels,
        recv,
        lists,
        hots,
        [planes[z] for z in range(depth)],
        [jnp.where(planes[depth + z] == 0.0, 1.0, planes[depth + z]) for z in range(depth)],
        [planes[2 * depth + z] for z in range(depth)],
        blocks,
    )
    ready()
    for z in range(depth):
        centre = p[z]
        far = jnp.where(real > 0.0, beyond[z], 0.0)
        after = far[0:1]
        before = (planes[3 * depth + z] * far)[7:8]
        coupled = coupled_z[z] + beside(centre, tx[z], ty[z])
        coupled = coupled + jnp.where(row == 0, before, 0.0) + jnp.where(row == width - 1, tx[z] * after, 0.0)
        remain = [rhs[c, z] - diag[c, 0, z] * centre for c in range(3)]
        remain[0] = remain[0] + coupled
        for c in range(3):
            value = binv[c, 0, z] * remain[0] + binv[c, 1, z] * remain[1] + binv[c, 2, z] * remain[2]
            if c == 0:
                value = centre + value
            s[c, z] = value
            tile_rows(value[0:1], (tx[z] * value)[width - 1 :], row_one.at[c, z], row_two.at[c, z])
    for c in range(3):
        top, bottom = (s[c, 0], tz[depth - 1] * s[c, depth - 1])
        inner[c] = jnp.where(right, top, bottom)
        outer[c] = jnp.where(right, bottom, top)


def inner_kernel(s, diag, tz, tx, ty, image):
    depth = s.shape[1]
    for z in range(depth):
        for c in range(3):
            total = diag[c, 0, z] * s[0, z] + diag[c, 1, z] * s[1, z] + diag[c, 2, z] * s[2, z]
            total = total - beside(s[c, z], tx[z], ty[z])
            if z:
                total = total - tz[z - 1] * s[c, z - 1]
            if z < depth - 1:
                total = total - tz[z] * s[c, z + 1]
            image[c, z] = total


def image_kernel(part, outer, row_two, row_one, inner, rhs, tz, tx, image, send):
    depth, width = part.shape[1:3]
    right, odd = (is_right(0), is_right(0, "tile"))
    row = iota(part.shape[2:], 0)
    along = power = start = 0.0
    for z in range(depth):
        for c in range(3):
            value = part[c, z]
            if z == 0:
                value = value - jnp.where(right, inner[c], outer[c])
            if z == depth - 1:
                value = value - tz[z] * jnp.where(right, outer[c], inner[c])
            after = jnp.where(odd, row_two[c, z], row_one[c, z])
            before = jnp.where(odd, row_one[c, z], row_two[c, z])
            value = value - jnp.where(row == 0, before, 0.0) - jnp.where(row == width - 1, tx[z] * after, 0.0)
            image[c, z] = value
            given = rhs[c, z]
            along = along + value * given
            power = power + value * value
            start = start + given * given
    along, power, start = (jnp.sum(along), jnp.sum(power), jnp.sum(start))
    omega = along / jnp.where(power > 0.0, power, 1.0)
    square = cross = 0.0
    for z in range(depth):
        for c in range(3):
            value = image[c, z]
            left = rhs[c, z] - omega * value
            square = square + left * left
            cross = cross + left * value
    lane = iota((1, send.shape[2]), 1)
    out = jnp.zeros((1, send.shape[2]), F32)
    for i, value in enumerate((along, power, start, jnp.sum(square), jnp.sum(cross), omega)):
        out = jnp.where(lane == i, value, out)
    send[...] = jnp.broadcast_to(out[:, None], send.shape)


def finish_kernel(recv, s, image, rhs, update, lin_res, ratio):
    sums = recv[...].reshape(recv.shape[0], recv.shape[2])
    whole = jnp.sum(sums, axis=0, keepdims=True)
    omega = whole[:, 0:1] / whole[:, 1:2]
    shift = sums[:, 5:6] - omega
    square = sums[:, 3:4] + 2.0 * shift * sums[:, 4:5] + shift * shift * sums[:, 1:2]
    ratio[...] = jnp.sqrt(jnp.sum(square, axis=0, keepdims=True) / whole[:, 2:3])
    for c in range(3):
        for z in range(s.shape[1]):
            update[c, z] = omega * s[c, z]
            lin_res[c, z] = rhs[c, z] - omega * image[c, z]


def flip(x, level, axis="layer"):
    return lax.ppermute(x, axis, [(i, i ^ (1 << level)) for i in range(lax.axis_size(axis))])


def neighbour(x, axis="layer"):
    pairs = [(i, i + 1) for i in range(1, lax.axis_size(axis) - 1, 2)]
    return lax.ppermute(x, axis, pairs + [(j, i) for i, j in pairs])


def everywhere(x):
    return lax.all_to_all(x, BOTH, split_axis=0, concat_axis=0, tiled=True)


def shards(rhs, weights, block_diag, block_inv, tx, ty, tz, store, cell, front, prod, inverse):
    layers = lax.axis_size("layer")
    devices = lax.axis_size("tile") * layers
    levels = layers.bit_length() - 1
    depth, width, long = tx.shape
    count = cell.shape[0]
    rows = inverse.shape[0]
    lists = layers * count
    cell, front, prod = (cell.reshape(1, -1), front.reshape(1, -1), prod.reshape(1, -1))
    field = vmem(tx.shape)

    def planes(n):
        return vmem((n, width, long))

    hbm_spec = pl.BlockSpec(memory_space=pltpu.HBM)
    given = (cell, front, prod, rhs, weights, tz, store)
    pres, send, ends = pl.pallas_call(
        pres_kernel,
        out_shape=(field, vmem((devices, 1, 3 * count)), planes(6)),
        in_specs=[hbm_spec] * len(given),
        out_specs=(VM,) * 3,
        scratch_shapes=[vmem(a.shape, a.dtype) for a in given] + [pltpu.SemaphoreType.DMA((len(given),))],
        compiler_params=pltpu.CompilerParams(vmem_limit_bytes=LIMIT),
    )(*[pltpu.with_memory_space_constraint(a, pltpu.HBM) for a in given])
    terms = everywhere(send)
    sib, found = ([], [prod])
    for level in range(levels - 1):
        sib.append(flip(ends, level))
        final = level == levels - 2
        outs = (vmem((1, (3 if final else 2) * count)), *((planes(3),) if final else (planes(6), planes(2 * depth))))
        if level == 0:
            rim = vmem((4 * depth, 1, long))
            low, high, *got = call(
                functools.partial(first_join_kernel, final),
                (rim, rim, *outs),
                (ends, sib[-1], pres, tz, store, tx, cell, prod),
                far=range(3, 8),
            )
        else:
            got = call(
                functools.partial(join_kernel, level, final), outs, (ends, sib[-1], answers, cell, prod), far=(3, 4)
            )
        found.append(got[0])
        if final:
            face = got[1]
        else:
            ends, answers = got[1:]
    found = jnp.concatenate(found, 1)
    terms, face, found = lax.optimization_barrier((terms, face, found))
    sib.append(flip(face, levels - 1))
    chunks = 8
    send = pl.pallas_call(
        front_kernel,
        out_shape=vmem((devices, 1, rows + 2 * levels * count)),
        in_specs=[VM, VM, hbm_spec],
        out_specs=VM,
        scratch_shapes=[vmem(inverse.shape), pltpu.SemaphoreType.DMA((chunks,))],
        compiler_params=pltpu.CompilerParams(vmem_limit_bytes=LIMIT),
    )(terms, found, pltpu.with_memory_space_constraint(inverse, pltpu.HBM))
    sizes = [block.shape[0] for block in sib]
    rim = vmem((4 * depth + sum(sizes), 1, long))
    send, low, high = lax.optimization_barrier((send, low, high))
    one, two = call(functools.partial(edge_kernel, levels), (rim, rim), (low, high, *sib))
    sol = everywhere(send)
    two, one = (neighbour(two, "tile"), flip(one, 0, "tile"))

    def hots(high, long_list, short_list):
        return (
            vmem((high * long // 128, long_list), BF16),
            vmem((128, long_list), BF16),
            vmem((rows, long_list), BF16),
            vmem((1, long_list), I32),
            vmem((1, short_list), I32),
        )

    at = 3 + levels
    p, coupled_z, tz, _, tx, block_inv = call(
        functools.partial(pressure_kernel, levels),
        (field, field),
        (sol, terms, pres, *sib, tz, store, tx, block_inv),
        far=range(at, at + 4),
        keep=range(at, at + 4),
        late=(),
        scratch=hots(width, lists, count),
    )
    row9 = vmem((3, depth, 1, long))
    plane3 = planes(3)
    s, outer, row_two, row_one, inner, rhs, block_diag, ty = call(
        functools.partial(search_kernel, levels, sizes),
        (vmem(rhs.shape), plane3, row9, row9, plane3),
        (sol, terms, two, one, p, coupled_z, tx, tz, block_inv, rhs, block_diag, ty),
        far=(9, 10, 11),
        keep=(9, 10, 11),
        late=(9, 10, 11),
        scratch=(vmem((4 * depth + sum(sizes), 8, long)), *hots(8, 2 * lists, 2 * count)),
    )
    outer, row_two = (neighbour(outer), neighbour(row_two, "tile"))
    row_one, inner = (flip(row_one, 0, "tile"), flip(inner, 0))
    (part,) = call(inner_kernel, (vmem(rhs.shape),), (s, block_diag, tz, tx, ty))
    image, send = call(
        image_kernel,
        (vmem(rhs.shape), vmem((devices, 1, 128))),
        (part, outer, row_two, row_one, inner, rhs, tz, tx),
    )
    sums = everywhere(send)
    update, lin_res, ratio = call(
        finish_kernel, (hbm(rhs.shape), hbm(rhs.shape), hbm((1, 1))), (sums, s, image, rhs)
    )
    return (update, lin_res, ratio.reshape(()))


def solution(mesh):
    return jax.shard_map(
        shards,
        mesh=mesh,
        in_specs=(
            P(None, "layer", "tile", None),
            P(None, "layer", "tile", None),
            P(None, None, "layer", "tile", None),
            P(None, None, "layer", "tile", None),
            P("layer", "tile", None),
            P("layer", "tile", None),
            P("layer", "tile", None),
            P("layer", "tile", None),
            P(("tile", "layer")),
            P(("tile", "layer")),
            P(("tile", "layer")),
            P(("tile", "layer"), None),
        ),
        out_specs=(P(None, "layer", "tile", None), P(None, "layer", "tile", None), P()),
        check_vma=False,
    )
```

```python
import functools
import jax
import jax.numpy as jnp
from jax import lax
from jax.experimental import pallas as pl
from jax.experimental.pallas import tpu as pltpu
from jax.sharding import PartitionSpec as P

F32 = jnp.float32
BF16 = jnp.bfloat16
I32 = jnp.int32
BOTH = ("tile", "layer")
VM = pl.BlockSpec(memory_space=pltpu.VMEM)
LIMIT = 16 << 20
PARTS = 2


def hbm(shape):
    return jax.ShapeDtypeStruct(shape, F32)


def vmem(shape, dtype=F32):
    return pltpu.VMEM(shape, dtype)


def staged(kernel, where, outs, kept, column, late, *refs):
    count, sems = (len(where), refs[-1])
    held = list(refs[count + outs + len(kept) : -1])
    target_count = sum(where) - len(kept)
    held, extra = (held[:target_count], held[target_count:])
    target = dict(zip(kept, refs[count + outs : count + outs + len(kept)]))
    operands, copies = ([], [])
    for i, far in enumerate(where):
        if far:
            to = target[i] if i in target else held.pop(0)
            part = refs[i].at[:, 0] if i in column else refs[i]
            copies.append(pltpu.make_async_copy(part, to, sems.at[len(copies)]))
            operands.append(to)
        else:
            operands.append(refs[i])
    for copy in copies:
        copy.start()
    places = [i for i, far in enumerate(where) if far]
    rest = [copy for i, copy in zip(places, copies) if i in late]
    for i, copy in zip(places, copies):
        if i not in late:
            copy.wait()
    more = (lambda: [copy.wait() for copy in rest],) if late else ()
    kernel(*more, *operands, *refs[count : count + outs], *extra)


def call(kernel, outs, args, far=(), keep=(), column=(), late=(), scratch=(), limit=LIMIT):
    where = [i in far for i in range(len(args))]
    spaces = [pltpu.HBM if w else pltpu.VMEM for w in where]
    every = (*outs, *(vmem(args[i].shape, args[i].dtype) for i in keep))
    return pl.pallas_call(
        functools.partial(staged, kernel, where, len(outs), tuple(keep), tuple(column), tuple(late)),
        out_shape=every,
        in_specs=[pl.BlockSpec(memory_space=s) for s in spaces],
        out_specs=(VM,) * len(every),
        scratch_shapes=[
            vmem(a.shape[:1] + a.shape[2:] if i in column else a.shape, a.dtype)
            for i, a in enumerate(args)
            if where[i] and i not in keep
        ]
        + [*scratch, pltpu.SemaphoreType.DMA((max(1, sum(where)),))],
        compiler_params=pltpu.CompilerParams(vmem_limit_bytes=limit),
    )(*[pltpu.with_memory_space_constraint(a, s) for a, s in zip(args, spaces)])


def iota(shape, dim):
    return lax.broadcasted_iota(I32, shape, dim)


def split(x):
    one = x.astype(BF16)
    rest = x - one.astype(F32)
    two = rest.astype(BF16)
    three = (rest - two.astype(F32)).astype(BF16)
    return [one, two, three]


def fold(x, parts=3):
    n = x.shape[0] // parts
    total = x[(parts - 1) * n :]
    for i in range(parts - 2, -1, -1):
        total = x[i * n : (i + 1) * n] + total
    return total


def onehot(index, size):
    return jnp.where(iota((size, index.shape[1]), 0) == index, 1.0, 0.0)


def dot(a, b):
    return lax.dot_general(a, b, (((1,), (0,)), ((), ())), preferred_element_type=F32)


def dot_nt(a, b):
    return lax.dot_general(a, b, (((1,), (1,)), ((), ())), preferred_element_type=F32)


def pick(tables, hi, hot):
    rows = tables[0].shape[0]
    parts = jnp.concatenate([p for table in tables for p in split(table)[:PARTS]], 0)
    got = dot(parts, hot)
    mask = onehot(hi, rows)
    n = PARTS * rows
    return [jnp.sum(fold(got[i * n : (i + 1) * n], PARTS) * mask, axis=0, keepdims=True) for i in range(len(tables))]


def pres_kernel(cell_in, front_in, prod_in, rhs_in, wts_in, tz_in, store_in, pres, send, ends, *scratch):
    (cell, front, prod, rhs, wts, tz, store), sems = scratch[:-1], scratch[-1]
    pairs = ((cell_in, cell), (front_in, front), (prod_in, prod), (rhs_in, rhs), (wts_in, wts), (tz_in, tz), (store_in, store))
    copies = [pltpu.make_async_copy(a, b, sems.at[i]) for i, (a, b) in enumerate(pairs)]
    for copy in copies:
        copy.start()
    for copy in copies[:3]:
        copy.wait()
    depth, width, long = pres.shape
    where = cell[...]
    hot = onehot(lax.rem(where, long), long).astype(BF16)
    for copy in copies[3:]:
        copy.wait()
    for z in range(depth):
        pres[z] = wts[0, z] * rhs[0, z] + wts[1, z] * rhs[1, z] + wts[2, z] * rhs[2, z]
    (found,) = pick([pres[...].reshape(depth * width, long)], lax.div(where, long), hot)
    both = jnp.concatenate([prod[...] * found, front[...].astype(F32), where.astype(F32)], 1)
    send[...] = jnp.broadcast_to(both[:, None], send.shape)
    tzs = [tz[z] for z in range(depth)]
    gs, invs, _, _, coefs = factors(tzs, [store[z] for z in range(depth)])
    y = local_solve([pres[z] for z in range(depth)], gs, invs, tzs)
    for i, value in enumerate((*coefs, y[0], y[-1], tzs[-1])):
        ends[i] = value


def is_right(level, axis="layer"):
    return (lax.axis_index(axis) >> level) % 2 == 1


def choose(level, mine, other, axis="layer"):
    right = is_right(level, axis)
    return (jnp.where(right, other, mine), jnp.where(right, mine, other))


def local_solve(rhs, upper, inv, tz):
    depth = len(rhs)
    y = [rhs[0] * inv[0]]
    for z in range(1, depth):
        y.append((rhs[z] + tz[z - 1] * y[-1]) * inv[z])
    for z in range(depth - 2, -1, -1):
        y[z] = y[z] + upper[z] * y[z + 1]
    return y


def factors(tz, store):
    depth = len(tz)
    gs, invs = ([], [])
    own = None
    for z in range(depth):
        own = store[z] if z == 0 else store[z] + gs[-1] * own
        invs.append(1.0 / (own + tz[z] if z < depth - 1 else own))
        gs.append(tz[z] * invs[-1])
    first = [invs[0]]
    for z in range(1, depth):
        first.append(tz[z - 1] * first[-1] * invs[z])
    final = [None] * depth
    final[-1] = invs[-1]
    for z in range(depth - 2, -1, -1):
        first[z] = first[z] + gs[z] * first[z + 1]
        final[z] = gs[z] * final[z + 1]
    return gs, invs, first, final, (first[0], first[-1], final[-1] + 1.0 / jnp.maximum(tz[-1], 1e-30))


def pair(level, own, sib):
    af, af_ = choose(level, own[0], sib[0])
    c, c_ = choose(level, own[1], sib[1])
    b, b_ = choose(level, own[2], sib[2])
    return af, c, b, af_, c_, b_, 1.0 / (b + af_)


def join_coefs(level, own, sib):
    af, c, _, _, c_, b_, g = pair(level, own, sib)
    return (af - c * c * g, c * c_ * g, b_ - c_ * c_ * g)


def join_ends(level, own, sib, mine, other):
    _, c, _, _, c_, _, g = pair(level, own, sib)
    yf, yf_ = choose(level, mine[0], other[0])
    yl, yl_ = choose(level, mine[1], other[1])
    flux = g * (yl - yf_)
    return (yf - c * flux, yl_ + c_ * flux)


def first_join_kernel(final, own, sib, pres, tz, store, tx, cell, prod, low, high, *outs):
    depth, width, _ = tz.shape
    for k, ref in enumerate((tz, store, pres, tx)):
        for z in range(depth):
            low[k * depth + z] = ref[z, 0:1]
            high[k * depth + z] = ref[z, width - 1 : width]
    _, _, first, last, _ = factors([tz[z] for z in range(depth)], [store[z] for z in range(depth)])
    join(0, final, own, sib, first + last, cell, prod, *outs)


def join_kernel(level, final, own, sib, answers, cell, prod, *outs):
    join(level, final, own, sib, [answers[i] for i in range(answers.shape[0])], cell, prod, *outs)


def join(level, final, own, sib, answers, cell, prod, found, *outs):
    depth = len(answers) // 2
    width, long = answers[0].shape
    _, c, _, _, c_, _, g = pair(level, own, sib)
    first, both, last = join_coefs(level, own, sib)
    yf, yl = join_ends(level, own, sib, (own[3], own[4]), (sib[3], sib[4]))
    lower = choose(level, own[5], sib[5])[1]
    right, later = (is_right(level), is_right(level + 1))
    cg, cg_ = (c * g, c_ * g)
    tops, bottoms = ([], [])
    for z in range(depth):
        kf, kl = (answers[z], answers[depth + z])
        tops.append(jnp.where(right, cg * kf, kf - cg * kl))
        bottoms.append(jnp.where(right, kl - cg_ * kf, cg_ * kl))
    tables = [answers[:depth], answers[depth:]]
    if final:
        (face,) = outs
        face[0], face[1] = (jnp.where(later, first, last), jnp.where(later, yf, yl))
        face[2] = lower
        tables.append([jnp.where(later, tops[z], bottoms[z]) for z in range(depth)])
    else:
        out, more = outs
        for i, value in enumerate((first, both, last, yf, yl, lower)):
            out[i] = value
        for i, value in enumerate(tops + bottoms):
            more[i] = value
    where = cell[...]
    hot = onehot(lax.rem(where, long), long).astype(BF16)
    stack = [jnp.concatenate(t, 0) for t in tables]
    got = pick(stack, lax.div(where, long), hot)
    found[...] = jnp.concatenate([prod[...] * value for value in got], 1)


def groups_of(levels):
    layers = lax.axis_size("layer")
    l = lax.axis_index("layer")
    base = lax.axis_index("tile") * layers
    out = [[base + l]]
    for level in range(levels):
        out.append([base + (((l >> level) ^ 1) << level) + i for i in range(1 << level)])
    return out


def front_kernel(recv, found, inverse, send, held, sems):
    devices = recv.shape[0]
    count = recv.shape[2] // 3
    rows, length = inverse.shape
    lanes = 128
    chunks = sems.shape[0]
    wide = length // chunks
    found = found[...]
    copies = [
        pltpu.make_async_copy(inverse.at[:, pl.ds(i * wide, wide)], held.at[:, pl.ds(i * wide, wide)], sems.at[i])
        for i in range(chunks)
    ]
    for copy in copies:
        copy.start()
    terms, index = (recv[:, 0, :count], recv[:, 0, count : 2 * count])
    high = jnp.floor(index * (1.0 / lanes))
    low = index - high * lanes
    parts = [p.astype(F32) for p in split(terms)[:PARTS]]
    row_of = iota((length // lanes, count), 0).astype(F32)
    lane_of = iota((lanes, count), 0).astype(F32)
    total = jnp.zeros((length // lanes, lanes), F32)
    for d in range(devices):
        hit = row_of == high[d : d + 1]
        left = jnp.concatenate([jnp.where(hit, p[d : d + 1], 0.0).astype(BF16) for p in parts], 0)
        right = jnp.where(lane_of == low[d : d + 1], 1.0, 0.0).astype(BF16)
        total = total + fold(dot_nt(left, right), PARTS)
    acc = jnp.zeros((rows, lanes), F32)
    for i in range(chunks):
        copies[i].wait()
        for r in range(i * wide // lanes, (i + 1) * wide // lanes):
            acc = acc + held[:, r * lanes : (r + 1) * lanes] * total[r : r + 1]
    parts = jnp.concatenate(split(acc), 1)
    out = dot_nt(jnp.ones((8, parts.shape[1]), BF16), parts)
    send[...] = jnp.broadcast_to(jnp.concatenate([out[0:1], found], 1)[:, None], send.shape)


def gathered(values, rows_hot, lanes_hot, start, size, ext, parts):
    hot = lanes_hot[:, start : start + size]
    pieces = [hot * p for v in values for p in split(v)[:parts]]
    got = dot_nt(rows_hot[:, start : start + size], jnp.concatenate(pieces, 0))
    planes = []
    lanes = hot.shape[0]
    for i in range(len(values)):
        plane = got[:, i * parts * lanes : (i * parts + 1) * lanes]
        for k in range(1, parts):
            j = i * parts + k
            plane = plane + got[:, j * lanes : (j + 1) * lanes]
        planes.append(jnp.concatenate([plane[r : r + ext] for r in range(0, plane.shape[0], ext)], 1))
    return planes


def beside(centre, tx, ty):
    width, long = centre.shape
    row, col = (iota(centre.shape, 0), iota(centre.shape, 1))
    total = tx * jnp.where(row == width - 1, 0.0, pltpu.roll(centre, width - 1, 0))
    total = total + jnp.where(row == 0, 0.0, pltpu.roll(tx * centre, 1, 0))
    total = total + ty * jnp.where(col == long - 1, 0.0, pltpu.roll(centre, long - 1, 1))
    return total + jnp.where(col == 0, 0.0, pltpu.roll(ty * centre, 1, 1))


def tile_rows(first, last, one, two):
    odd = is_right(0, "tile")
    one[...] = jnp.where(odd, first, last)
    two[...] = jnp.where(odd, last, first)


def table_kernel(lists, shape, terms, hots, only=None):
    _, width, long = shape
    rows_hot, lanes_hot, sol_hot, sol_row, layer = hots
    lanes = 128
    rows = sol_hot.shape[0]
    count = terms.shape[2] // 3
    at = 0
    for members in lists:
        for device in members:
            entry = terms[device]
            index = entry[:, count : 2 * count].astype(I32)
            cell = entry[:, 2 * count :].astype(I32)
            y, x = lax.rem(cell, long), lax.rem(lax.div(cell, long), width)
            if only is None:
                row = lax.div(y, lanes) * width + x
            else:
                row = jnp.where(x == only, lax.div(y, lanes) * 8, -1)
            here = pl.ds(at, count)
            rows_hot[:, here] = onehot(row, rows_hot.shape[0]).astype(BF16)
            lanes_hot[:, here] = onehot(lax.rem(y, lanes), lanes).astype(BF16)
            sol_hot[:, here] = onehot(lax.rem(index, rows), rows).astype(BF16)
            sol_row[:, here] = lax.div(index, rows)
            if at < layer.shape[1]:
                layer[:, here] = lax.div(cell, long * width)
            at += count


def column_solve(levels, recv, lists, hots, tz, store, pres, sib):
    rows_hot, lanes_hot, sol_hot, sol_row, layer = hots
    depth = len(tz)
    high = tz[0].shape[0]
    rows, count = (sol_hot.shape[0], recv.shape[2])
    count = (count - rows) // (2 * levels)
    table = jnp.concatenate(split(recv[...].reshape(recv.shape[0], recv.shape[2])[:, :rows]), 0)
    sol = fold(dot(table, sol_hot[...]))
    sol = jnp.sum(jnp.where(iota(sol.shape, 0) == sol_row[...], sol, 0.0), axis=0, keepdims=True)
    layer = layer[...]

    def listed(group, column):
        at = rows + column * count
        return jnp.concatenate([recv[device][:, at : at + count] for device in group], 1)

    gs, invs, first, final, coefs = factors(tz, store)
    own = [coefs]
    start = layer.shape[1]
    value = listed(lists[0], 0) * sol[:, :start]
    values = [jnp.where(layer == z, value, 0.0) for z in range(depth)]
    change = gathered(values, rows_hot, lanes_hot, 0, start, high, PARTS)
    y = local_solve([pres[z] - change[z] for z in range(depth)], gs, invs, tz)
    mine = (y[0], y[-1])
    steps = []
    for level in range(levels):
        size = len(lists[level + 1]) * count
        top = level == levels - 1
        columns = [1 + 2 * level] if top else [1 + 2 * level, 2 + 2 * level]
        values = [listed(lists[level + 1], c) * sol[:, start : start + size] for c in columns]
        change = gathered(values, rows_hot, lanes_hot, start, size, high, PARTS)
        start += size
        if top:
            other = sib[level][1] - change[0]
            steps.append((mine, (other, other)))
        else:
            other = (sib[level][3] - change[0], sib[level][4] - change[1])
            steps.append((mine, other))
            mine = join_ends(level, own[level], sib[level], mine, other)
            own.append(join_coefs(level, own[level], sib[level]))
    above = below = tzp = jnp.zeros(tz[0].shape, F32)
    place = lax.axis_index("layer")
    for level in range(levels - 1, -1, -1):
        mine, other = steps[level]
        yl, _ = choose(level, mine[1], other[1])
        _, yf_ = choose(level, mine[0], other[0])
        flux = yl - yf_
        if level == levels - 1:
            b, _ = choose(level, own[level][2], sib[level][0])
            _, af_ = choose(level, own[level][0], sib[level][0])
            g = 1.0 / (b + af_)
            before = sib[level][2]
        else:
            _, c, _, _, c_, _, g = pair(level, own[level], sib[level])
            flux = flux + c * above - c_ * below
            before = sib[level][5]
        tzp = jnp.where(place % (2 << level) == 1 << level, before, tzp)
        flux = g * flux
        right = is_right(level)
        above, below = (jnp.where(right, flux, above), jnp.where(right, below, -flux))
    return [y[z] + first[z] * above + final[z] * below for z in range(depth)], above, below, tzp


def pressure_kernel(levels, ready, recv, terms, pres, *refs):
    sib, (tz, store, tx, _, p, coupled_z, one, *hots) = (refs[:levels], refs[levels:])
    depth, width, _ = pres.shape
    odd = is_right(0, "tile")
    lists = groups_of(levels)
    table_kernel(lists, pres.shape, terms, hots)
    tzs = [tz[z] for z in range(depth)]
    values, above, below, tzp = column_solve(
        levels, recv, lists, hots, tzs, [store[z] for z in range(depth)], [pres[z] for z in range(depth)], sib
    )
    is_last = lax.axis_index("layer") == (1 << levels) - 1
    for z in range(depth):
        p[z] = values[z]
        one[z] = jnp.where(odd, values[z][0:1], (tx[z] * values[z])[width - 1 :])
        total = above + tzp * values[z] if z == 0 else tzs[z - 1] * values[z - 1]
        if z == depth - 1:
            coupled_z[z] = total + jnp.where(is_last, 0.0, below + tzs[z] * values[z])
        else:
            coupled_z[z] = total + tzs[z] * values[z + 1]
    ready()


def edge_kernel(levels, low, high, *refs):
    sib, two = (refs[:levels], refs[levels])
    odd = is_right(0, "tile")
    n = low.shape[0]
    two[pl.ds(0, n)] = jnp.where(odd, high[...], low[...])
    at = n
    for block in sib:
        width = block.shape[1]
        for i in range(block.shape[0]):
            two[at] = jnp.where(odd, block[i, width - 1 : width], block[i, 0:1])
            at += 1


def first_three(kernel, ready, one, two, three, _rhs, _diag, _ty, *rest):
    kernel(one, two, three, *rest)
    ready()


def beyond_kernel(levels, shapes, shape, recv, terms, two, row, planes, *hots):
    depth, width, long = shape
    tiles, layers = (lax.axis_size("tile"), lax.axis_size("layer"))
    tile = lax.axis_index("tile")
    odd = is_right(0, "tile")
    planes[...] = jnp.zeros(planes.shape, F32)
    for i in range(planes.shape[0]):
        planes[i, 0:1] = two[i]
    step = jnp.where(odd, layers, -layers)
    lists = [[jnp.clip(device + step, 0, tiles * layers - 1) for device in members] for members in groups_of(levels)]
    table_kernel(lists, shape, terms, hots, jnp.where(odd, 0, width - 1))
    exists = jnp.where(odd, (tile < tiles - 1).astype(F32), (tile > 0).astype(F32)) + jnp.zeros((1, long), F32)
    blocks = []
    at = 4 * depth
    for size in shapes:
        blocks.append([planes[at + i] for i in range(size)])
        at += size
    values, _, _, _ = column_solve(
        levels,
        recv,
        lists,
        hots,
        [planes[z] for z in range(depth)],
        [jnp.where(planes[depth + z] == 0.0, 1.0, planes[depth + z]) for z in range(depth)],
        [planes[2 * depth + z] for z in range(depth)],
        blocks,
    )
    for z in range(depth):
        found = jnp.where(exists > 0.0, values[z][0:1], 0.0)
        row[z] = jnp.where(odd, found, found * two[3 * depth + z])


def search_kernel(p, coupled_z, two, one, tx, ty, tz, rhs, diag, binv, s, outer, row_two, row_one, inner):
    depth, width, _ = p.shape
    odd = is_right(0, "tile")
    right = is_right(0)
    row = iota(p.shape[1:], 0)
    for z in range(depth):
        centre = p[z]
        after = jnp.where(odd, two[z], one[z])
        before = jnp.where(odd, one[z], two[z])
        coupled = coupled_z[z] + beside(centre, tx[z], ty[z])
        coupled = coupled + jnp.where(row == 0, before, 0.0) + jnp.where(row == width - 1, tx[z] * after, 0.0)
        remain = [rhs[c, z] - diag[c, 0, z] * centre for c in range(3)]
        remain[0] = remain[0] + coupled
        for c in range(3):
            value = binv[c, 0, z] * remain[0] + binv[c, 1, z] * remain[1] + binv[c, 2, z] * remain[2]
            if c == 0:
                value = centre + value
            s[c, z] = value
            tile_rows(value[0:1], (tx[z] * value)[width - 1 :], row_one.at[c, z], row_two.at[c, z])
    for c in range(3):
        top, bottom = (s[c, 0], tz[depth - 1] * s[c, depth - 1])
        inner[c] = jnp.where(right, top, bottom)
        outer[c] = jnp.where(right, bottom, top)


def inner_kernel(s, diag, tz, tx, ty, image):
    depth = s.shape[1]
    for z in range(depth):
        for c in range(3):
            total = diag[c, 0, z] * s[0, z] + diag[c, 1, z] * s[1, z] + diag[c, 2, z] * s[2, z]
            total = total - beside(s[c, z], tx[z], ty[z])
            if z:
                total = total - tz[z - 1] * s[c, z - 1]
            if z < depth - 1:
                total = total - tz[z] * s[c, z + 1]
            image[c, z] = total


def image_kernel(part, outer, row_two, row_one, inner, rhs, tz, tx, image, send):
    depth, width = part.shape[1:3]
    right, odd = (is_right(0), is_right(0, "tile"))
    row = iota(part.shape[2:], 0)
    along = power = start = 0.0
    for z in range(depth):
        for c in range(3):
            value = part[c, z]
            if z == 0:
                value = value - jnp.where(right, inner[c], outer[c])
            if z == depth - 1:
                value = value - tz[z] * jnp.where(right, outer[c], inner[c])
            after = jnp.where(odd, row_two[c, z], row_one[c, z])
            before = jnp.where(odd, row_one[c, z], row_two[c, z])
            value = value - jnp.where(row == 0, before, 0.0) - jnp.where(row == width - 1, tx[z] * after, 0.0)
            image[c, z] = value
            given = rhs[c, z]
            along = along + value * given
            power = power + value * value
            start = start + given * given
    along, power, start = (jnp.sum(along), jnp.sum(power), jnp.sum(start))
    omega = along / jnp.where(power > 0.0, power, 1.0)
    square = cross = 0.0
    for z in range(depth):
        for c in range(3):
            value = image[c, z]
            left = rhs[c, z] - omega * value
            square = square + left * left
            cross = cross + left * value
    lane = iota((1, send.shape[2]), 1)
    out = jnp.zeros((1, send.shape[2]), F32)
    for i, value in enumerate((along, power, start, jnp.sum(square), jnp.sum(cross), omega)):
        out = jnp.where(lane == i, value, out)
    send[...] = jnp.broadcast_to(out[:, None], send.shape)


def finish_kernel(recv, s, image, rhs, update, lin_res, ratio):
    sums = recv[...].reshape(recv.shape[0], recv.shape[2])
    whole = jnp.sum(sums, axis=0, keepdims=True)
    omega = whole[:, 0:1] / whole[:, 1:2]
    shift = sums[:, 5:6] - omega
    square = sums[:, 3:4] + 2.0 * shift * sums[:, 4:5] + shift * shift * sums[:, 1:2]
    ratio[...] = jnp.sqrt(jnp.sum(square, axis=0, keepdims=True) / whole[:, 2:3])
    for c in range(3):
        for z in range(s.shape[1]):
            update[c, z] = omega * s[c, z]
            lin_res[c, z] = rhs[c, z] - omega * image[c, z]


def flip(x, level, axis="layer"):
    return lax.ppermute(x, axis, [(i, i ^ (1 << level)) for i in range(lax.axis_size(axis))])


def neighbour(x, axis="layer"):
    pairs = [(i, i + 1) for i in range(1, lax.axis_size(axis) - 1, 2)]
    return lax.ppermute(x, axis, pairs + [(j, i) for i, j in pairs])


def everywhere(x):
    return lax.all_to_all(x, BOTH, split_axis=0, concat_axis=0, tiled=True)


def shards(rhs, weights, block_diag, block_inv, tx, ty, tz, store, cell, front, prod, inverse):
    layers = lax.axis_size("layer")
    devices = lax.axis_size("tile") * layers
    levels = layers.bit_length() - 1
    depth, width, long = tx.shape
    count = cell.shape[0]
    rows = inverse.shape[0]
    lists = layers * count
    cell, front, prod = (cell.reshape(1, -1), front.reshape(1, -1), prod.reshape(1, -1))
    field = vmem(tx.shape)

    def planes(n):
        return vmem((n, width, long))

    hbm_spec = pl.BlockSpec(memory_space=pltpu.HBM)
    given = (cell, front, prod, rhs, weights, tz, store)
    pres, send, ends = pl.pallas_call(
        pres_kernel,
        out_shape=(field, vmem((devices, 1, 3 * count)), planes(6)),
        in_specs=[hbm_spec] * len(given),
        out_specs=(VM,) * 3,
        scratch_shapes=[vmem(a.shape, a.dtype) for a in given] + [pltpu.SemaphoreType.DMA((len(given),))],
        compiler_params=pltpu.CompilerParams(vmem_limit_bytes=LIMIT),
    )(*[pltpu.with_memory_space_constraint(a, pltpu.HBM) for a in given])
    terms = everywhere(send)
    sib, found = ([], [prod])
    for level in range(levels - 1):
        sib.append(flip(ends, level))
        final = level == levels - 2
        outs = (vmem((1, (3 if final else 2) * count)), *((planes(3),) if final else (planes(6), planes(2 * depth))))
        if level == 0:
            rim = vmem((4 * depth, 1, long))
            low, high, *got = call(
                functools.partial(first_join_kernel, final),
                (rim, rim, *outs),
                (ends, sib[-1], pres, tz, store, tx, cell, prod),
                far=range(3, 8),
            )
        else:
            got = call(
                functools.partial(join_kernel, level, final), outs, (ends, sib[-1], answers, cell, prod), far=(3, 4)
            )
        found.append(got[0])
        if final:
            face = got[1]
        else:
            ends, answers = got[1:]
    found = jnp.concatenate(found, 1)
    terms, face, found = lax.optimization_barrier((terms, face, found))
    sib.append(flip(face, levels - 1))
    chunks = 8
    send = pl.pallas_call(
        front_kernel,
        out_shape=vmem((devices, 1, rows + 2 * levels * count)),
        in_specs=[VM, VM, hbm_spec],
        out_specs=VM,
        scratch_shapes=[vmem(inverse.shape), pltpu.SemaphoreType.DMA((chunks,))],
        compiler_params=pltpu.CompilerParams(vmem_limit_bytes=LIMIT),
    )(terms, found, pltpu.with_memory_space_constraint(inverse, pltpu.HBM))
    sizes = [block.shape[0] for block in sib]
    rim = vmem((4 * depth + sum(sizes), 1, long))
    send, low, high = lax.optimization_barrier((send, low, high))
    (two,) = call(functools.partial(edge_kernel, levels), (rim,), (low, high, *sib))
    sol = everywhere(send)
    two = neighbour(two, "tile")

    def hots(high):
        return (
            vmem((high * long // 128, lists), BF16),
            vmem((128, lists), BF16),
            vmem((rows, lists), BF16),
            vmem((1, lists), I32),
            vmem((1, count), I32),
        )

    at = 3 + levels
    row3 = vmem((depth, 1, long))
    p, coupled_z, one, tz, _, tx, block_inv = call(
        functools.partial(pressure_kernel, levels),
        (field, field, row3),
        (sol, terms, pres, *sib, tz, store, tx, block_inv),
        far=range(at, at + 4),
        keep=range(at, at + 4),
        late=(at + 3,),
        scratch=hots(width),
    )
    sol, one, terms = lax.optimization_barrier((sol, one, terms))
    one = flip(one, 0, "tile")
    two, rhs, block_diag, ty = call(
        functools.partial(first_three, functools.partial(beyond_kernel, levels, sizes, (depth, width, long))),
        (row3,),
        (sol, terms, two, rhs, block_diag, ty),
        far=(3, 4, 5),
        keep=(3, 4, 5),
        late=(3, 4, 5),
        scratch=(vmem((4 * depth + sum(sizes), 8, long)), *hots(8)),
    )
    row9 = vmem((3, depth, 1, long))
    plane3 = planes(3)
    s, outer, row_two, row_one, inner = call(
        search_kernel,
        (vmem(rhs.shape), plane3, row9, row9, plane3),
        (p, coupled_z, two, one, tx, ty, tz, rhs, block_diag, block_inv),
    )
    outer, row_two = (neighbour(outer), neighbour(row_two, "tile"))
    row_one, inner = (flip(row_one, 0, "tile"), flip(inner, 0))
    (part,) = call(inner_kernel, (vmem(rhs.shape),), (s, block_diag, tz, tx, ty))
    image, send = call(
        image_kernel,
        (vmem(rhs.shape), vmem((devices, 1, 128))),
        (part, outer, row_two, row_one, inner, rhs, tz, tx),
    )
    sums = everywhere(send)
    update, lin_res, ratio = call(
        finish_kernel, (hbm(rhs.shape), hbm(rhs.shape), hbm((1, 1))), (sums, s, image, rhs)
    )
    return (update, lin_res, ratio.reshape(()))


def solution(mesh):
    return jax.shard_map(
        shards,
        mesh=mesh,
        in_specs=(
            P(None, "layer", "tile", None),
            P(None, "layer", "tile", None),
            P(None, None, "layer", "tile", None),
            P(None, None, "layer", "tile", None),
            P("layer", "tile", None),
            P("layer", "tile", None),
            P("layer", "tile", None),
            P("layer", "tile", None),
            P(("tile", "layer")),
            P(("tile", "layer")),
            P(("tile", "layer")),
            P(("tile", "layer"), None),
        ),
        out_specs=(P(None, "layer", "tile", None), P(None, "layer", "tile", None), P()),
        check_vma=False,
    )
```

```python
import functools
import jax
import jax.numpy as jnp
from jax import lax
from jax.experimental import pallas as pl
from jax.experimental.pallas import tpu as pltpu
from jax.sharding import PartitionSpec as P

F32 = jnp.float32
BF16 = jnp.bfloat16
I32 = jnp.int32
BOTH = ("tile", "layer")
VM = pl.BlockSpec(memory_space=pltpu.VMEM)
LIMIT = 16 << 20
PARTS = 2


def hbm(shape):
    return jax.ShapeDtypeStruct(shape, F32)


def vmem(shape, dtype=F32):
    return pltpu.VMEM(shape, dtype)


def staged(kernel, where, outs, kept, column, late, *refs):
    count, sems = (len(where), refs[-1])
    held = list(refs[count + outs + len(kept) : -1])
    target_count = sum(where) - len(kept)
    held, extra = (held[:target_count], held[target_count:])
    target = dict(zip(kept, refs[count + outs : count + outs + len(kept)]))
    operands, copies = ([], [])
    for i, far in enumerate(where):
        if far:
            to = target[i] if i in target else held.pop(0)
            part = refs[i].at[:, 0] if i in column else refs[i]
            copies.append(pltpu.make_async_copy(part, to, sems.at[len(copies)]))
            operands.append(to)
        else:
            operands.append(refs[i])
    places = [i for i, far in enumerate(where) if far]
    rest = [copy for i, copy in zip(places, copies) if i in late]
    early = [copy for i, copy in zip(places, copies) if i not in late]
    for copy in early:
        copy.start()
    for copy in early:
        copy.wait()
    for copy in rest:
        copy.start()
    more = (lambda: [copy.wait() for copy in rest],) if late else ()
    kernel(*more, *operands, *refs[count : count + outs], *extra)


def call(kernel, outs, args, far=(), keep=(), column=(), late=(), scratch=(), limit=LIMIT):
    where = [i in far for i in range(len(args))]
    spaces = [pltpu.HBM if w else pltpu.VMEM for w in where]
    every = (*outs, *(vmem(args[i].shape, args[i].dtype) for i in keep))
    return pl.pallas_call(
        functools.partial(staged, kernel, where, len(outs), tuple(keep), tuple(column), tuple(late)),
        out_shape=every,
        in_specs=[pl.BlockSpec(memory_space=s) for s in spaces],
        out_specs=(VM,) * len(every),
        scratch_shapes=[
            vmem(a.shape[:1] + a.shape[2:] if i in column else a.shape, a.dtype)
            for i, a in enumerate(args)
            if where[i] and i not in keep
        ]
        + [*scratch, pltpu.SemaphoreType.DMA((max(1, sum(where)),))],
        compiler_params=pltpu.CompilerParams(vmem_limit_bytes=limit),
    )(*[pltpu.with_memory_space_constraint(a, s) for a, s in zip(args, spaces)])


def iota(shape, dim):
    return lax.broadcasted_iota(I32, shape, dim)


def split(x):
    one = x.astype(BF16)
    rest = x - one.astype(F32)
    two = rest.astype(BF16)
    three = (rest - two.astype(F32)).astype(BF16)
    return [one, two, three]


def fold(x, parts=3):
    n = x.shape[0] // parts
    total = x[(parts - 1) * n :]
    for i in range(parts - 2, -1, -1):
        total = x[i * n : (i + 1) * n] + total
    return total


def onehot(index, size):
    return jnp.where(iota((size, index.shape[1]), 0) == index, 1.0, 0.0)


def dot(a, b):
    return lax.dot_general(a, b, (((1,), (0,)), ((), ())), preferred_element_type=F32)


def dot_nt(a, b):
    return lax.dot_general(a, b, (((1,), (1,)), ((), ())), preferred_element_type=F32)


def pick(tables, hi, hot):
    rows = tables[0].shape[0]
    parts = jnp.concatenate([p for table in tables for p in split(table)[:PARTS]], 0)
    got = dot(parts, hot)
    mask = onehot(hi, rows)
    n = PARTS * rows
    return [jnp.sum(fold(got[i * n : (i + 1) * n], PARTS) * mask, axis=0, keepdims=True) for i in range(len(tables))]


def pres_kernel(cell_in, front_in, prod_in, rhs_in, wts_in, tz_in, store_in, pres, send, ends, *scratch):
    (cell, front, prod, rhs, wts, tz, store), sems = scratch[:-1], scratch[-1]
    pairs = ((cell_in, cell), (front_in, front), (prod_in, prod), (rhs_in, rhs), (wts_in, wts), (tz_in, tz), (store_in, store))
    copies = [pltpu.make_async_copy(a, b, sems.at[i]) for i, (a, b) in enumerate(pairs)]
    for copy in copies:
        copy.start()
    for copy in copies[:3]:
        copy.wait()
    depth, width, long = pres.shape
    where = cell[...]
    hot = onehot(lax.rem(where, long), long).astype(BF16)
    for copy in copies[3:]:
        copy.wait()
    for z in range(depth):
        pres[z] = wts[0, z] * rhs[0, z] + wts[1, z] * rhs[1, z] + wts[2, z] * rhs[2, z]
    (found,) = pick([pres[...].reshape(depth * width, long)], lax.div(where, long), hot)
    both = jnp.concatenate([prod[...] * found, front[...].astype(F32), where.astype(F32)], 1)
    send[...] = jnp.broadcast_to(both[:, None], send.shape)
    tzs = [tz[z] for z in range(depth)]
    gs, invs, _, _, coefs = factors(tzs, [store[z] for z in range(depth)])
    y = local_solve([pres[z] for z in range(depth)], gs, invs, tzs)
    for i, value in enumerate((*coefs, y[0], y[-1], tzs[-1])):
        ends[i] = value


def is_right(level, axis="layer"):
    return (lax.axis_index(axis) >> level) % 2 == 1


def choose(level, mine, other, axis="layer"):
    right = is_right(level, axis)
    return (jnp.where(right, other, mine), jnp.where(right, mine, other))


def local_solve(rhs, upper, inv, tz):
    depth = len(rhs)
    y = [rhs[0] * inv[0]]
    for z in range(1, depth):
        y.append((rhs[z] + tz[z - 1] * y[-1]) * inv[z])
    for z in range(depth - 2, -1, -1):
        y[z] = y[z] + upper[z] * y[z + 1]
    return y


def factors(tz, store):
    depth = len(tz)
    gs, invs = ([], [])
    own = None
    for z in range(depth):
        own = store[z] if z == 0 else store[z] + gs[-1] * own
        invs.append(1.0 / (own + tz[z] if z < depth - 1 else own))
        gs.append(tz[z] * invs[-1])
    first = [invs[0]]
    for z in range(1, depth):
        first.append(tz[z - 1] * first[-1] * invs[z])
    final = [None] * depth
    final[-1] = invs[-1]
    for z in range(depth - 2, -1, -1):
        first[z] = first[z] + gs[z] * first[z + 1]
        final[z] = gs[z] * final[z + 1]
    return gs, invs, first, final, (first[0], first[-1], final[-1] + 1.0 / jnp.maximum(tz[-1], 1e-30))


def pair(level, own, sib):
    af, af_ = choose(level, own[0], sib[0])
    c, c_ = choose(level, own[1], sib[1])
    b, b_ = choose(level, own[2], sib[2])
    return af, c, b, af_, c_, b_, 1.0 / (b + af_)


def join_coefs(level, own, sib):
    af, c, _, _, c_, b_, g = pair(level, own, sib)
    return (af - c * c * g, c * c_ * g, b_ - c_ * c_ * g)


def join_ends(level, own, sib, mine, other):
    _, c, _, _, c_, _, g = pair(level, own, sib)
    yf, yf_ = choose(level, mine[0], other[0])
    yl, yl_ = choose(level, mine[1], other[1])
    flux = g * (yl - yf_)
    return (yf - c * flux, yl_ + c_ * flux)


def first_join_kernel(final, own, sib, pres, tz, store, tx, cell, prod, low, high, *outs):
    depth, width, _ = tz.shape
    for k, ref in enumerate((tz, store, pres, tx)):
        for z in range(depth):
            low[k * depth + z] = ref[z, 0:1]
            high[k * depth + z] = ref[z, width - 1 : width]
    _, _, first, last, _ = factors([tz[z] for z in range(depth)], [store[z] for z in range(depth)])
    join(0, final, own, sib, first + last, cell, prod, *outs)


def join_kernel(level, final, own, sib, answers, cell, prod, *outs):
    join(level, final, own, sib, [answers[i] for i in range(answers.shape[0])], cell, prod, *outs)


def join(level, final, own, sib, answers, cell, prod, found, *outs):
    depth = len(answers) // 2
    width, long = answers[0].shape
    _, c, _, _, c_, _, g = pair(level, own, sib)
    first, both, last = join_coefs(level, own, sib)
    yf, yl = join_ends(level, own, sib, (own[3], own[4]), (sib[3], sib[4]))
    lower = choose(level, own[5], sib[5])[1]
    right, later = (is_right(level), is_right(level + 1))
    cg, cg_ = (c * g, c_ * g)
    tops, bottoms = ([], [])
    for z in range(depth):
        kf, kl = (answers[z], answers[depth + z])
        tops.append(jnp.where(right, cg * kf, kf - cg * kl))
        bottoms.append(jnp.where(right, kl - cg_ * kf, cg_ * kl))
    tables = [answers[:depth], answers[depth:]]
    if final:
        (face,) = outs
        face[0], face[1] = (jnp.where(later, first, last), jnp.where(later, yf, yl))
        face[2] = lower
        tables.append([jnp.where(later, tops[z], bottoms[z]) for z in range(depth)])
    else:
        out, more = outs
        for i, value in enumerate((first, both, last, yf, yl, lower)):
            out[i] = value
        for i, value in enumerate(tops + bottoms):
            more[i] = value
    where = cell[...]
    hot = onehot(lax.rem(where, long), long).astype(BF16)
    stack = [jnp.concatenate(t, 0) for t in tables]
    got = pick(stack, lax.div(where, long), hot)
    found[...] = jnp.concatenate([prod[...] * value for value in got], 1)


def groups_of(levels):
    layers = lax.axis_size("layer")
    l = lax.axis_index("layer")
    base = lax.axis_index("tile") * layers
    out = [[base + l]]
    for level in range(levels):
        out.append([base + (((l >> level) ^ 1) << level) + i for i in range(1 << level)])
    return out


def front_kernel(recv, found, inverse, send, held, sems):
    devices = recv.shape[0]
    count = recv.shape[2] // 3
    rows, length = inverse.shape
    lanes = 128
    chunks = sems.shape[0]
    wide = length // chunks
    found = found[...]
    copies = [
        pltpu.make_async_copy(inverse.at[:, pl.ds(i * wide, wide)], held.at[:, pl.ds(i * wide, wide)], sems.at[i])
        for i in range(chunks)
    ]
    for copy in copies:
        copy.start()
    terms, index = (recv[:, 0, :count], recv[:, 0, count : 2 * count])
    high = jnp.floor(index * (1.0 / lanes))
    low = index - high * lanes
    parts = [p.astype(F32) for p in split(terms)[:PARTS]]
    row_of = iota((length // lanes, count), 0).astype(F32)
    lane_of = iota((lanes, count), 0).astype(F32)
    total = jnp.zeros((length // lanes, lanes), F32)
    for d in range(devices):
        hit = row_of == high[d : d + 1]
        left = jnp.concatenate([jnp.where(hit, p[d : d + 1], 0.0).astype(BF16) for p in parts], 0)
        right = jnp.where(lane_of == low[d : d + 1], 1.0, 0.0).astype(BF16)
        total = total + fold(dot_nt(left, right), PARTS)
    acc = jnp.zeros((rows, lanes), F32)
    for i in range(chunks):
        copies[i].wait()
        for r in range(i * wide // lanes, (i + 1) * wide // lanes):
            acc = acc + held[:, r * lanes : (r + 1) * lanes] * total[r : r + 1]
    parts = jnp.concatenate(split(acc), 1)
    out = dot_nt(jnp.ones((8, parts.shape[1]), BF16), parts)
    send[...] = jnp.broadcast_to(jnp.concatenate([out[0:1], found], 1)[:, None], send.shape)


def gathered(values, rows_hot, lanes_hot, start, size, ext, parts):
    hot = lanes_hot[:, start : start + size]
    pieces = [hot * p for v in values for p in split(v)[:parts]]
    got = dot_nt(rows_hot[:, start : start + size], jnp.concatenate(pieces, 0))
    planes = []
    lanes = hot.shape[0]
    for i in range(len(values)):
        plane = got[:, i * parts * lanes : (i * parts + 1) * lanes]
        for k in range(1, parts):
            j = i * parts + k
            plane = plane + got[:, j * lanes : (j + 1) * lanes]
        planes.append(jnp.concatenate([plane[r : r + ext] for r in range(0, plane.shape[0], ext)], 1))
    return planes


def beside(centre, tx, ty):
    width, long = centre.shape
    row, col = (iota(centre.shape, 0), iota(centre.shape, 1))
    total = tx * jnp.where(row == width - 1, 0.0, pltpu.roll(centre, width - 1, 0))
    total = total + jnp.where(row == 0, 0.0, pltpu.roll(tx * centre, 1, 0))
    total = total + ty * jnp.where(col == long - 1, 0.0, pltpu.roll(centre, long - 1, 1))
    return total + jnp.where(col == 0, 0.0, pltpu.roll(ty * centre, 1, 1))


def tile_rows(first, last, one, two):
    odd = is_right(0, "tile")
    one[...] = jnp.where(odd, first, last)
    two[...] = jnp.where(odd, last, first)


def table_kernel(lists, shape, terms, hots, only=None):
    _, width, long = shape
    rows_hot, lanes_hot, sol_hot, sol_row, layer = hots
    lanes = 128
    rows = sol_hot.shape[0]
    count = terms.shape[2] // 3
    at = 0
    for members in lists:
        for device in members:
            entry = terms[device]
            index = entry[:, count : 2 * count].astype(I32)
            cell = entry[:, 2 * count :].astype(I32)
            y, x = lax.rem(cell, long), lax.rem(lax.div(cell, long), width)
            if only is None:
                row = lax.div(y, lanes) * width + x
            else:
                row = jnp.where(x == only, lax.div(y, lanes) * 8, -1)
            here = pl.ds(at, count)
            rows_hot[:, here] = onehot(row, rows_hot.shape[0]).astype(BF16)
            lanes_hot[:, here] = onehot(lax.rem(y, lanes), lanes).astype(BF16)
            sol_hot[:, here] = onehot(lax.rem(index, rows), rows).astype(BF16)
            sol_row[:, here] = lax.div(index, rows)
            if at < layer.shape[1]:
                layer[:, here] = lax.div(cell, long * width)
            at += count


def column_solve(levels, recv, lists, hots, tz, store, pres, sib):
    rows_hot, lanes_hot, sol_hot, sol_row, layer = hots
    depth = len(tz)
    high = tz[0].shape[0]
    rows, count = (sol_hot.shape[0], recv.shape[2])
    count = (count - rows) // (2 * levels)
    table = jnp.concatenate(split(recv[...].reshape(recv.shape[0], recv.shape[2])[:, :rows]), 0)
    sol = fold(dot(table, sol_hot[...]))
    sol = jnp.sum(jnp.where(iota(sol.shape, 0) == sol_row[...], sol, 0.0), axis=0, keepdims=True)
    layer = layer[...]

    def listed(group, column):
        at = rows + column * count
        return jnp.concatenate([recv[device][:, at : at + count] for device in group], 1)

    gs, invs, first, final, coefs = factors(tz, store)
    own = [coefs]
    start = layer.shape[1]
    value = listed(lists[0], 0) * sol[:, :start]
    values = [jnp.where(layer == z, value, 0.0) for z in range(depth)]
    change = gathered(values, rows_hot, lanes_hot, 0, start, high, PARTS)
    y = local_solve([pres[z] - change[z] for z in range(depth)], gs, invs, tz)
    mine = (y[0], y[-1])
    steps = []
    for level in range(levels):
        size = len(lists[level + 1]) * count
        top = level == levels - 1
        columns = [1 + 2 * level] if top else [1 + 2 * level, 2 + 2 * level]
        values = [listed(lists[level + 1], c) * sol[:, start : start + size] for c in columns]
        change = gathered(values, rows_hot, lanes_hot, start, size, high, PARTS)
        start += size
        if top:
            other = sib[level][1] - change[0]
            steps.append((mine, (other, other)))
        else:
            other = (sib[level][3] - change[0], sib[level][4] - change[1])
            steps.append((mine, other))
            mine = join_ends(level, own[level], sib[level], mine, other)
            own.append(join_coefs(level, own[level], sib[level]))
    above = below = tzp = jnp.zeros(tz[0].shape, F32)
    place = lax.axis_index("layer")
    for level in range(levels - 1, -1, -1):
        mine, other = steps[level]
        yl, _ = choose(level, mine[1], other[1])
        _, yf_ = choose(level, mine[0], other[0])
        flux = yl - yf_
        if level == levels - 1:
            b, _ = choose(level, own[level][2], sib[level][0])
            _, af_ = choose(level, own[level][0], sib[level][0])
            g = 1.0 / (b + af_)
            before = sib[level][2]
        else:
            _, c, _, _, c_, _, g = pair(level, own[level], sib[level])
            flux = flux + c * above - c_ * below
            before = sib[level][5]
        tzp = jnp.where(place % (2 << level) == 1 << level, before, tzp)
        flux = g * flux
        right = is_right(level)
        above, below = (jnp.where(right, flux, above), jnp.where(right, below, -flux))
    return [y[z] + first[z] * above + final[z] * below for z in range(depth)], above, below, tzp


def pressure_kernel(levels, ready, recv, terms, pres, *refs):
    sib, (tz, store, tx, _, p, coupled_z, one, *hots) = (refs[:levels], refs[levels:])
    depth, width, _ = pres.shape
    odd = is_right(0, "tile")
    lists = groups_of(levels)
    table_kernel(lists, pres.shape, terms, hots)
    tzs = [tz[z] for z in range(depth)]
    values, above, below, tzp = column_solve(
        levels, recv, lists, hots, tzs, [store[z] for z in range(depth)], [pres[z] for z in range(depth)], sib
    )
    is_last = lax.axis_index("layer") == (1 << levels) - 1
    for z in range(depth):
        p[z] = values[z]
        one[z] = jnp.where(odd, values[z][0:1], (tx[z] * values[z])[width - 1 :])
        total = above + tzp * values[z] if z == 0 else tzs[z - 1] * values[z - 1]
        if z == depth - 1:
            coupled_z[z] = total + jnp.where(is_last, 0.0, below + tzs[z] * values[z])
        else:
            coupled_z[z] = total + tzs[z] * values[z + 1]
    ready()


def edge_kernel(levels, low, high, *refs):
    sib, two = (refs[:levels], refs[levels])
    odd = is_right(0, "tile")
    n = low.shape[0]
    two[pl.ds(0, n)] = jnp.where(odd, high[...], low[...])
    at = n
    for block in sib:
        width = block.shape[1]
        for i in range(block.shape[0]):
            two[at] = jnp.where(odd, block[i, width - 1 : width], block[i, 0:1])
            at += 1


def first_three(kernel, ready, one, two, three, _rhs, _diag, _ty, *rest):
    kernel(one, two, three, *rest)
    ready()


def beyond_kernel(levels, shapes, shape, recv, terms, two, row, planes, *hots):
    depth, width, long = shape
    tiles, layers = (lax.axis_size("tile"), lax.axis_size("layer"))
    tile = lax.axis_index("tile")
    odd = is_right(0, "tile")
    planes[...] = jnp.zeros(planes.shape, F32)
    for i in range(planes.shape[0]):
        planes[i, 0:1] = two[i]
    step = jnp.where(odd, layers, -layers)
    lists = [[jnp.clip(device + step, 0, tiles * layers - 1) for device in members] for members in groups_of(levels)]
    table_kernel(lists, shape, terms, hots, jnp.where(odd, 0, width - 1))
    exists = jnp.where(odd, (tile < tiles - 1).astype(F32), (tile > 0).astype(F32)) + jnp.zeros((1, long), F32)
    blocks = []
    at = 4 * depth
    for size in shapes:
        blocks.append([planes[at + i] for i in range(size)])
        at += size
    values, _, _, _ = column_solve(
        levels,
        recv,
        lists,
        hots,
        [planes[z] for z in range(depth)],
        [jnp.where(planes[depth + z] == 0.0, 1.0, planes[depth + z]) for z in range(depth)],
        [planes[2 * depth + z] for z in range(depth)],
        blocks,
    )
    for z in range(depth):
        found = jnp.where(exists > 0.0, values[z][0:1], 0.0)
        row[z] = jnp.where(odd, found, found * two[3 * depth + z])


def search_kernel(p, coupled_z, two, one, tx, ty, tz, rhs, diag, binv, s, outer, row_two, row_one, inner):
    depth, width, _ = p.shape
    odd = is_right(0, "tile")
    right = is_right(0)
    row = iota(p.shape[1:], 0)
    for z in range(depth):
        centre = p[z]
        after = jnp.where(odd, two[z], one[z])
        before = jnp.where(odd, one[z], two[z])
        coupled = coupled_z[z] + beside(centre, tx[z], ty[z])
        coupled = coupled + jnp.where(row == 0, before, 0.0) + jnp.where(row == width - 1, tx[z] * after, 0.0)
        remain = [rhs[c, z] - diag[c, 0, z] * centre for c in range(3)]
        remain[0] = remain[0] + coupled
        for c in range(3):
            value = binv[c, 0, z] * remain[0] + binv[c, 1, z] * remain[1] + binv[c, 2, z] * remain[2]
            if c == 0:
                value = centre + value
            s[c, z] = value
            tile_rows(value[0:1], (tx[z] * value)[width - 1 :], row_one.at[c, z], row_two.at[c, z])
    for c in range(3):
        top, bottom = (s[c, 0], tz[depth - 1] * s[c, depth - 1])
        inner[c] = jnp.where(right, top, bottom)
        outer[c] = jnp.where(right, bottom, top)


def inner_kernel(s, diag, tz, tx, ty, image):
    depth = s.shape[1]
    for z in range(depth):
        for c in range(3):
            total = diag[c, 0, z] * s[0, z] + diag[c, 1, z] * s[1, z] + diag[c, 2, z] * s[2, z]
            total = total - beside(s[c, z], tx[z], ty[z])
            if z:
                total = total - tz[z - 1] * s[c, z - 1]
            if z < depth - 1:
                total = total - tz[z] * s[c, z + 1]
            image[c, z] = total


def image_kernel(part, outer, row_two, row_one, inner, rhs, tz, tx, image, send):
    depth, width = part.shape[1:3]
    right, odd = (is_right(0), is_right(0, "tile"))
    row = iota(part.shape[2:], 0)
    along = power = start = 0.0
    for z in range(depth):
        for c in range(3):
            value = part[c, z]
            if z == 0:
                value = value - jnp.where(right, inner[c], outer[c])
            if z == depth - 1:
                value = value - tz[z] * jnp.where(right, outer[c], inner[c])
            after = jnp.where(odd, row_two[c, z], row_one[c, z])
            before = jnp.where(odd, row_one[c, z], row_two[c, z])
            value = value - jnp.where(row == 0, before, 0.0) - jnp.where(row == width - 1, tx[z] * after, 0.0)
            image[c, z] = value
            given = rhs[c, z]
            along = along + value * given
            power = power + value * value
            start = start + given * given
    along, power, start = (jnp.sum(along), jnp.sum(power), jnp.sum(start))
    omega = along / jnp.where(power > 0.0, power, 1.0)
    square = cross = 0.0
    for z in range(depth):
        for c in range(3):
            value = image[c, z]
            left = rhs[c, z] - omega * value
            square = square + left * left
            cross = cross + left * value
    lane = iota((1, send.shape[2]), 1)
    out = jnp.zeros((1, send.shape[2]), F32)
    for i, value in enumerate((along, power, start, jnp.sum(square), jnp.sum(cross), omega)):
        out = jnp.where(lane == i, value, out)
    send[...] = jnp.broadcast_to(out[:, None], send.shape)


def finish_kernel(recv, s, image, rhs, update, lin_res, ratio):
    sums = recv[...].reshape(recv.shape[0], recv.shape[2])
    whole = jnp.sum(sums, axis=0, keepdims=True)
    omega = whole[:, 0:1] / whole[:, 1:2]
    shift = sums[:, 5:6] - omega
    square = sums[:, 3:4] + 2.0 * shift * sums[:, 4:5] + shift * shift * sums[:, 1:2]
    ratio[...] = jnp.sqrt(jnp.sum(square, axis=0, keepdims=True) / whole[:, 2:3])
    for c in range(3):
        for z in range(s.shape[1]):
            update[c, z] = omega * s[c, z]
            lin_res[c, z] = rhs[c, z] - omega * image[c, z]


def flip(x, level, axis="layer"):
    return lax.ppermute(x, axis, [(i, i ^ (1 << level)) for i in range(lax.axis_size(axis))])


def neighbour(x, axis="layer"):
    pairs = [(i, i + 1) for i in range(1, lax.axis_size(axis) - 1, 2)]
    return lax.ppermute(x, axis, pairs + [(j, i) for i, j in pairs])


def everywhere(x):
    return lax.all_to_all(x, BOTH, split_axis=0, concat_axis=0, tiled=True)


def shards(rhs, weights, block_diag, block_inv, tx, ty, tz, store, cell, front, prod, inverse):
    layers = lax.axis_size("layer")
    devices = lax.axis_size("tile") * layers
    levels = layers.bit_length() - 1
    depth, width, long = tx.shape
    count = cell.shape[0]
    rows = inverse.shape[0]
    lists = layers * count
    cell, front, prod = (cell.reshape(1, -1), front.reshape(1, -1), prod.reshape(1, -1))
    field = vmem(tx.shape)

    def planes(n):
        return vmem((n, width, long))

    hbm_spec = pl.BlockSpec(memory_space=pltpu.HBM)
    given = (cell, front, prod, rhs, weights, tz, store)
    pres, send, ends = pl.pallas_call(
        pres_kernel,
        out_shape=(field, vmem((devices, 1, 3 * count)), planes(6)),
        in_specs=[hbm_spec] * len(given),
        out_specs=(VM,) * 3,
        scratch_shapes=[vmem(a.shape, a.dtype) for a in given] + [pltpu.SemaphoreType.DMA((len(given),))],
        compiler_params=pltpu.CompilerParams(vmem_limit_bytes=LIMIT),
    )(*[pltpu.with_memory_space_constraint(a, pltpu.HBM) for a in given])
    terms = everywhere(send)
    sib, found = ([], [prod])
    for level in range(levels - 1):
        sib.append(flip(ends, level))
        final = level == levels - 2
        outs = (vmem((1, (3 if final else 2) * count)), *((planes(3),) if final else (planes(6), planes(2 * depth))))
        if level == 0:
            rim = vmem((4 * depth, 1, long))
            low, high, *got = call(
                functools.partial(first_join_kernel, final),
                (rim, rim, *outs),
                (ends, sib[-1], pres, tz, store, tx, cell, prod),
                far=range(3, 8),
            )
        else:
            got = call(
                functools.partial(join_kernel, level, final), outs, (ends, sib[-1], answers, cell, prod), far=(3, 4)
            )
        found.append(got[0])
        if final:
            face = got[1]
        else:
            ends, answers = got[1:]
    found = jnp.concatenate(found, 1)
    terms, face, found = lax.optimization_barrier((terms, face, found))
    sib.append(flip(face, levels - 1))
    chunks = 8
    send = pl.pallas_call(
        front_kernel,
        out_shape=vmem((devices, 1, rows + 2 * levels * count)),
        in_specs=[VM, VM, hbm_spec],
        out_specs=VM,
        scratch_shapes=[vmem(inverse.shape), pltpu.SemaphoreType.DMA((chunks,))],
        compiler_params=pltpu.CompilerParams(vmem_limit_bytes=LIMIT),
    )(terms, found, pltpu.with_memory_space_constraint(inverse, pltpu.HBM))
    sizes = [block.shape[0] for block in sib]
    rim = vmem((4 * depth + sum(sizes), 1, long))
    send, low, high = lax.optimization_barrier((send, low, high))
    (two,) = call(functools.partial(edge_kernel, levels), (rim,), (low, high, *sib))
    sol = everywhere(send)
    two = neighbour(two, "tile")

    def hots(high):
        return (
            vmem((high * long // 128, lists), BF16),
            vmem((128, lists), BF16),
            vmem((rows, lists), BF16),
            vmem((1, lists), I32),
            vmem((1, count), I32),
        )

    at = 3 + levels
    row3 = vmem((depth, 1, long))
    p, coupled_z, one, tz, _, tx, block_inv = call(
        functools.partial(pressure_kernel, levels),
        (field, field, row3),
        (sol, terms, pres, *sib, tz, store, tx, block_inv),
        far=range(at, at + 4),
        keep=range(at, at + 4),
        late=(at + 3,),
        scratch=hots(width),
    )
    sol, one, terms = lax.optimization_barrier((sol, one, terms))
    one = flip(one, 0, "tile")
    two, rhs, block_diag, ty = call(
        functools.partial(first_three, functools.partial(beyond_kernel, levels, sizes, (depth, width, long))),
        (row3,),
        (sol, terms, two, rhs, block_diag, ty),
        far=(3, 4, 5),
        keep=(3, 4, 5),
        late=(3, 4, 5),
        scratch=(vmem((4 * depth + sum(sizes), 8, long)), *hots(8)),
    )
    row9 = vmem((3, depth, 1, long))
    plane3 = planes(3)
    s, outer, row_two, row_one, inner = call(
        search_kernel,
        (vmem(rhs.shape), plane3, row9, row9, plane3),
        (p, coupled_z, two, one, tx, ty, tz, rhs, block_diag, block_inv),
    )
    outer, row_two = (neighbour(outer), neighbour(row_two, "tile"))
    row_one, inner = (flip(row_one, 0, "tile"), flip(inner, 0))
    (part,) = call(inner_kernel, (vmem(rhs.shape),), (s, block_diag, tz, tx, ty))
    image, send = call(
        image_kernel,
        (vmem(rhs.shape), vmem((devices, 1, 128))),
        (part, outer, row_two, row_one, inner, rhs, tz, tx),
    )
    sums = everywhere(send)
    update, lin_res, ratio = call(
        finish_kernel, (hbm(rhs.shape), hbm(rhs.shape), hbm((1, 1))), (sums, s, image, rhs)
    )
    return (update, lin_res, ratio.reshape(()))


def solution(mesh):
    return jax.shard_map(
        shards,
        mesh=mesh,
        in_specs=(
            P(None, "layer", "tile", None),
            P(None, "layer", "tile", None),
            P(None, None, "layer", "tile", None),
            P(None, None, "layer", "tile", None),
            P("layer", "tile", None),
            P("layer", "tile", None),
            P("layer", "tile", None),
            P("layer", "tile", None),
            P(("tile", "layer")),
            P(("tile", "layer")),
            P(("tile", "layer")),
            P(("tile", "layer"), None),
        ),
        out_specs=(P(None, "layer", "tile", None), P(None, "layer", "tile", None), P()),
        check_vma=False,
    )
```

```python
import functools
import jax
import jax.numpy as jnp
from jax import lax
from jax.experimental import pallas as pl
from jax.experimental.pallas import tpu as pltpu
from jax.sharding import PartitionSpec as P

F32 = jnp.float32
BF16 = jnp.bfloat16
I32 = jnp.int32
BOTH = ("tile", "layer")
VM = pl.BlockSpec(memory_space=pltpu.VMEM)
LIMIT = 16 << 20
PARTS = 2


def hbm(shape):
    return jax.ShapeDtypeStruct(shape, F32)


def vmem(shape, dtype=F32):
    return pltpu.VMEM(shape, dtype)


def staged(kernel, where, outs, kept, column, late, *refs):
    count, sems = (len(where), refs[-1])
    held = list(refs[count + outs + len(kept) : -1])
    target_count = sum(where) - len(kept)
    held, extra = (held[:target_count], held[target_count:])
    target = dict(zip(kept, refs[count + outs : count + outs + len(kept)]))
    operands, copies = ([], [])
    for i, far in enumerate(where):
        if far:
            to = target[i] if i in target else held.pop(0)
            part = refs[i].at[:, 0] if i in column else refs[i]
            copies.append(pltpu.make_async_copy(part, to, sems.at[len(copies)]))
            operands.append(to)
        else:
            operands.append(refs[i])
    places = [i for i, far in enumerate(where) if far]
    for copy in copies:
        copy.start()
    for i, copy in zip(places, copies):
        if not any(i in group for group in late):
            copy.wait()

    def ready(k):
        for i, copy in zip(places, copies):
            if i in late[k]:
                copy.wait()

    more = (ready,) if late else ()
    kernel(*more, *operands, *refs[count : count + outs], *extra)


def call(kernel, outs, args, far=(), keep=(), column=(), late=(), scratch=(), limit=LIMIT):
    where = [i in far for i in range(len(args))]
    spaces = [pltpu.HBM if w else pltpu.VMEM for w in where]
    every = (*outs, *(vmem(args[i].shape, args[i].dtype) for i in keep))
    return pl.pallas_call(
        functools.partial(staged, kernel, where, len(outs), tuple(keep), tuple(column), tuple(late)),
        out_shape=every,
        in_specs=[pl.BlockSpec(memory_space=s) for s in spaces],
        out_specs=(VM,) * len(every),
        scratch_shapes=[
            vmem(a.shape[:1] + a.shape[2:] if i in column else a.shape, a.dtype)
            for i, a in enumerate(args)
            if where[i] and i not in keep
        ]
        + [*scratch, pltpu.SemaphoreType.DMA((max(1, sum(where)),))],
        compiler_params=pltpu.CompilerParams(vmem_limit_bytes=limit),
    )(*[pltpu.with_memory_space_constraint(a, s) for a, s in zip(args, spaces)])


def iota(shape, dim):
    return lax.broadcasted_iota(I32, shape, dim)


def split(x):
    one = x.astype(BF16)
    rest = x - one.astype(F32)
    two = rest.astype(BF16)
    three = (rest - two.astype(F32)).astype(BF16)
    return [one, two, three]


def fold(x, parts=3):
    n = x.shape[0] // parts
    total = x[(parts - 1) * n :]
    for i in range(parts - 2, -1, -1):
        total = x[i * n : (i + 1) * n] + total
    return total


def onehot(index, size):
    return jnp.where(iota((size, index.shape[1]), 0) == index, 1.0, 0.0)


def dot(a, b):
    return lax.dot_general(a, b, (((1,), (0,)), ((), ())), preferred_element_type=F32)


def dot_nt(a, b):
    return lax.dot_general(a, b, (((1,), (1,)), ((), ())), preferred_element_type=F32)


def pick(tables, hi, hot):
    rows = tables[0].shape[0]
    parts = jnp.concatenate([p for table in tables for p in split(table)[:PARTS]], 0)
    got = dot(parts, hot)
    mask = onehot(hi, rows)
    n = PARTS * rows
    return [jnp.sum(fold(got[i * n : (i + 1) * n], PARTS) * mask, axis=0, keepdims=True) for i in range(len(tables))]


def pres_kernel(cell_in, front_in, prod_in, rhs_in, wts_in, tz_in, store_in, pres, send, ends, *scratch):
    (cell, front, prod, rhs, wts, tz, store), sems = scratch[:-1], scratch[-1]
    pairs = ((cell_in, cell), (front_in, front), (prod_in, prod), (rhs_in, rhs), (wts_in, wts), (tz_in, tz), (store_in, store))
    copies = [pltpu.make_async_copy(a, b, sems.at[i]) for i, (a, b) in enumerate(pairs)]
    for copy in copies:
        copy.start()
    for copy in copies[:3]:
        copy.wait()
    depth, width, long = pres.shape
    where = cell[...]
    hot = onehot(lax.rem(where, long), long).astype(BF16)
    for copy in copies[3:]:
        copy.wait()
    for z in range(depth):
        pres[z] = wts[0, z] * rhs[0, z] + wts[1, z] * rhs[1, z] + wts[2, z] * rhs[2, z]
    (found,) = pick([pres[...].reshape(depth * width, long)], lax.div(where, long), hot)
    both = jnp.concatenate([prod[...] * found, front[...].astype(F32), where.astype(F32)], 1)
    send[...] = jnp.broadcast_to(both[:, None], send.shape)
    tzs = [tz[z] for z in range(depth)]
    gs, invs, _, _, coefs = factors(tzs, [store[z] for z in range(depth)])
    y = local_solve([pres[z] for z in range(depth)], gs, invs, tzs)
    for i, value in enumerate((*coefs, y[0], y[-1], tzs[-1])):
        ends[i] = value


def is_right(level, axis="layer"):
    return (lax.axis_index(axis) >> level) % 2 == 1


def choose(level, mine, other, axis="layer"):
    right = is_right(level, axis)
    return (jnp.where(right, other, mine), jnp.where(right, mine, other))


def local_solve(rhs, upper, inv, tz):
    depth = len(rhs)
    y = [rhs[0] * inv[0]]
    for z in range(1, depth):
        y.append((rhs[z] + tz[z - 1] * y[-1]) * inv[z])
    for z in range(depth - 2, -1, -1):
        y[z] = y[z] + upper[z] * y[z + 1]
    return y


def factors(tz, store):
    depth = len(tz)
    gs, invs = ([], [])
    own = None
    for z in range(depth):
        own = store[z] if z == 0 else store[z] + gs[-1] * own
        invs.append(1.0 / (own + tz[z] if z < depth - 1 else own))
        gs.append(tz[z] * invs[-1])
    first = [invs[0]]
    for z in range(1, depth):
        first.append(tz[z - 1] * first[-1] * invs[z])
    final = [None] * depth
    final[-1] = invs[-1]
    for z in range(depth - 2, -1, -1):
        first[z] = first[z] + gs[z] * first[z + 1]
        final[z] = gs[z] * final[z + 1]
    return gs, invs, first, final, (first[0], first[-1], final[-1] + 1.0 / jnp.maximum(tz[-1], 1e-30))


def pair(level, own, sib):
    af, af_ = choose(level, own[0], sib[0])
    c, c_ = choose(level, own[1], sib[1])
    b, b_ = choose(level, own[2], sib[2])
    return af, c, b, af_, c_, b_, 1.0 / (b + af_)


def join_coefs(level, own, sib):
    af, c, _, _, c_, b_, g = pair(level, own, sib)
    return (af - c * c * g, c * c_ * g, b_ - c_ * c_ * g)


def join_ends(level, own, sib, mine, other):
    _, c, _, _, c_, _, g = pair(level, own, sib)
    yf, yf_ = choose(level, mine[0], other[0])
    yl, yl_ = choose(level, mine[1], other[1])
    flux = g * (yl - yf_)
    return (yf - c * flux, yl_ + c_ * flux)


def first_join_kernel(final, own, sib, pres, tz, store, tx, cell, prod, low, high, *outs):
    depth, width, _ = tz.shape
    for k, ref in enumerate((tz, store, pres, tx)):
        for z in range(depth):
            low[k * depth + z] = ref[z, 0:1]
            high[k * depth + z] = ref[z, width - 1 : width]
    _, _, first, last, _ = factors([tz[z] for z in range(depth)], [store[z] for z in range(depth)])
    join(0, final, own, sib, first + last, cell, prod, *outs)


def join_kernel(level, final, own, sib, answers, cell, prod, *outs):
    join(level, final, own, sib, [answers[i] for i in range(answers.shape[0])], cell, prod, *outs)


def join(level, final, own, sib, answers, cell, prod, found, *outs):
    depth = len(answers) // 2
    width, long = answers[0].shape
    _, c, _, _, c_, _, g = pair(level, own, sib)
    first, both, last = join_coefs(level, own, sib)
    yf, yl = join_ends(level, own, sib, (own[3], own[4]), (sib[3], sib[4]))
    lower = choose(level, own[5], sib[5])[1]
    right, later = (is_right(level), is_right(level + 1))
    cg, cg_ = (c * g, c_ * g)
    tops, bottoms = ([], [])
    for z in range(depth):
        kf, kl = (answers[z], answers[depth + z])
        tops.append(jnp.where(right, cg * kf, kf - cg * kl))
        bottoms.append(jnp.where(right, kl - cg_ * kf, cg_ * kl))
    tables = [answers[:depth], answers[depth:]]
    if final:
        (face,) = outs
        face[0], face[1] = (jnp.where(later, first, last), jnp.where(later, yf, yl))
        face[2] = lower
        tables.append([jnp.where(later, tops[z], bottoms[z]) for z in range(depth)])
    else:
        out, more = outs
        for i, value in enumerate((first, both, last, yf, yl, lower)):
            out[i] = value
        for i, value in enumerate(tops + bottoms):
            more[i] = value
    where = cell[...]
    hot = onehot(lax.rem(where, long), long).astype(BF16)
    stack = [jnp.concatenate(t, 0) for t in tables]
    got = pick(stack, lax.div(where, long), hot)
    found[...] = jnp.concatenate([prod[...] * value for value in got], 1)


def groups_of(levels):
    layers = lax.axis_size("layer")
    l = lax.axis_index("layer")
    base = lax.axis_index("tile") * layers
    out = [[base + l]]
    for level in range(levels):
        out.append([base + (((l >> level) ^ 1) << level) + i for i in range(1 << level)])
    return out


def front_kernel(recv, found, inverse, send, held, sems):
    devices = recv.shape[0]
    count = recv.shape[2] // 3
    rows, length = inverse.shape
    lanes = 128
    chunks = sems.shape[0]
    wide = length // chunks
    found = found[...]
    copies = [
        pltpu.make_async_copy(inverse.at[:, pl.ds(i * wide, wide)], held.at[:, pl.ds(i * wide, wide)], sems.at[i])
        for i in range(chunks)
    ]
    for copy in copies:
        copy.start()
    terms, index = (recv[:, 0, :count], recv[:, 0, count : 2 * count])
    high = jnp.floor(index * (1.0 / lanes))
    low = index - high * lanes
    parts = [p.astype(F32) for p in split(terms)[:PARTS]]
    row_of = iota((length // lanes, count), 0).astype(F32)
    lane_of = iota((lanes, count), 0).astype(F32)
    total = jnp.zeros((length // lanes, lanes), F32)
    for d in range(devices):
        hit = row_of == high[d : d + 1]
        left = jnp.concatenate([jnp.where(hit, p[d : d + 1], 0.0).astype(BF16) for p in parts], 0)
        right = jnp.where(lane_of == low[d : d + 1], 1.0, 0.0).astype(BF16)
        total = total + fold(dot_nt(left, right), PARTS)
    acc = jnp.zeros((rows, lanes), F32)
    for i in range(chunks):
        copies[i].wait()
        for r in range(i * wide // lanes, (i + 1) * wide // lanes):
            acc = acc + held[:, r * lanes : (r + 1) * lanes] * total[r : r + 1]
    parts = jnp.concatenate(split(acc), 1)
    out = dot_nt(jnp.ones((8, parts.shape[1]), BF16), parts)
    send[...] = jnp.broadcast_to(jnp.concatenate([out[0:1], found], 1)[:, None], send.shape)


def gathered(values, rows_hot, lanes_hot, start, size, ext, parts):
    hot = lanes_hot[:, start : start + size]
    pieces = [hot * p for v in values for p in split(v)[:parts]]
    got = dot_nt(rows_hot[:, start : start + size], jnp.concatenate(pieces, 0))
    planes = []
    lanes = hot.shape[0]
    for i in range(len(values)):
        plane = got[:, i * parts * lanes : (i * parts + 1) * lanes]
        for k in range(1, parts):
            j = i * parts + k
            plane = plane + got[:, j * lanes : (j + 1) * lanes]
        planes.append(jnp.concatenate([plane[r : r + ext] for r in range(0, plane.shape[0], ext)], 1))
    return planes


def beside(centre, tx, ty):
    width, long = centre.shape
    row, col = (iota(centre.shape, 0), iota(centre.shape, 1))
    total = tx * jnp.where(row == width - 1, 0.0, pltpu.roll(centre, width - 1, 0))
    total = total + jnp.where(row == 0, 0.0, pltpu.roll(tx * centre, 1, 0))
    total = total + ty * jnp.where(col == long - 1, 0.0, pltpu.roll(centre, long - 1, 1))
    return total + jnp.where(col == 0, 0.0, pltpu.roll(ty * centre, 1, 1))


def tile_rows(first, last, one, two):
    odd = is_right(0, "tile")
    one[...] = jnp.where(odd, first, last)
    two[...] = jnp.where(odd, last, first)


def table_kernel(lists, shape, terms, hots, only=None):
    _, width, long = shape
    rows_hot, lanes_hot, sol_hot, sol_row, layer = hots
    lanes = 128
    rows = sol_hot.shape[0]
    count = terms.shape[2] // 3
    at = 0
    for members in lists:
        for device in members:
            entry = terms[device]
            index = entry[:, count : 2 * count].astype(I32)
            cell = entry[:, 2 * count :].astype(I32)
            y, x = lax.rem(cell, long), lax.rem(lax.div(cell, long), width)
            if only is None:
                row = lax.div(y, lanes) * width + x
            else:
                row = jnp.where(x == only, lax.div(y, lanes) * 8, -1)
            here = pl.ds(at, count)
            rows_hot[:, here] = onehot(row, rows_hot.shape[0]).astype(BF16)
            lanes_hot[:, here] = onehot(lax.rem(y, lanes), lanes).astype(BF16)
            sol_hot[:, here] = onehot(lax.rem(index, rows), rows).astype(BF16)
            sol_row[:, here] = lax.div(index, rows)
            if at < layer.shape[1]:
                layer[:, here] = lax.div(cell, long * width)
            at += count


def column_solve(levels, recv, lists, hots, planes_of, sib):
    rows_hot, lanes_hot, sol_hot, sol_row, layer = hots
    rows, count = (sol_hot.shape[0], recv.shape[2])
    count = (count - rows) // (2 * levels)
    table = jnp.concatenate(split(recv[...].reshape(recv.shape[0], recv.shape[2])[:, :rows]), 0)
    sol = fold(dot(table, sol_hot[...]))
    sol = jnp.sum(jnp.where(iota(sol.shape, 0) == sol_row[...], sol, 0.0), axis=0, keepdims=True)
    layer = layer[...]

    def listed(group, column):
        at = rows + column * count
        return jnp.concatenate([recv[device][:, at : at + count] for device in group], 1)

    tz, store, pres = planes_of()
    depth = len(tz)
    high = tz[0].shape[0]
    gs, invs, first, final, coefs = factors(tz, store)
    own = [coefs]
    start = layer.shape[1]
    value = listed(lists[0], 0) * sol[:, :start]
    values = [jnp.where(layer == z, value, 0.0) for z in range(depth)]
    change = gathered(values, rows_hot, lanes_hot, 0, start, high, PARTS)
    y = local_solve([pres[z] - change[z] for z in range(depth)], gs, invs, tz)
    mine = (y[0], y[-1])
    steps = []
    for level in range(levels):
        size = len(lists[level + 1]) * count
        top = level == levels - 1
        columns = [1 + 2 * level] if top else [1 + 2 * level, 2 + 2 * level]
        values = [listed(lists[level + 1], c) * sol[:, start : start + size] for c in columns]
        change = gathered(values, rows_hot, lanes_hot, start, size, high, PARTS)
        start += size
        if top:
            other = sib[level][1] - change[0]
            steps.append((mine, (other, other)))
        else:
            other = (sib[level][3] - change[0], sib[level][4] - change[1])
            steps.append((mine, other))
            mine = join_ends(level, own[level], sib[level], mine, other)
            own.append(join_coefs(level, own[level], sib[level]))
    above = below = tzp = jnp.zeros(tz[0].shape, F32)
    place = lax.axis_index("layer")
    for level in range(levels - 1, -1, -1):
        mine, other = steps[level]
        yl, _ = choose(level, mine[1], other[1])
        _, yf_ = choose(level, mine[0], other[0])
        flux = yl - yf_
        if level == levels - 1:
            b, _ = choose(level, own[level][2], sib[level][0])
            _, af_ = choose(level, own[level][0], sib[level][0])
            g = 1.0 / (b + af_)
            before = sib[level][2]
        else:
            _, c, _, _, c_, _, g = pair(level, own[level], sib[level])
            flux = flux + c * above - c_ * below
            before = sib[level][5]
        tzp = jnp.where(place % (2 << level) == 1 << level, before, tzp)
        flux = g * flux
        right = is_right(level)
        above, below = (jnp.where(right, flux, above), jnp.where(right, below, -flux))
    return [y[z] + first[z] * above + final[z] * below for z in range(depth)], above, below, tzp


def pressure_kernel(levels, ready, recv, terms, pres, *refs):
    sib, (tz, store, tx, _, p, coupled_z, one, *hots) = (refs[:levels], refs[levels:])
    depth, width, _ = pres.shape
    odd = is_right(0, "tile")
    lists = groups_of(levels)
    table_kernel(lists, pres.shape, terms, hots)

    def planes_of():
        ready(0)
        return tuple([ref[z] for z in range(depth)] for ref in (tz, store, pres))

    values, above, below, tzp = column_solve(levels, recv, lists, hots, planes_of, sib)
    tzs = [tz[z] for z in range(depth)]
    is_last = lax.axis_index("layer") == (1 << levels) - 1
    for z in range(depth):
        p[z] = values[z]
        one[z] = jnp.where(odd, values[z][0:1], (tx[z] * values[z])[width - 1 :])
        total = above + tzp * values[z] if z == 0 else tzs[z - 1] * values[z - 1]
        if z == depth - 1:
            coupled_z[z] = total + jnp.where(is_last, 0.0, below + tzs[z] * values[z])
        else:
            coupled_z[z] = total + tzs[z] * values[z + 1]
    ready(1)


def edge_kernel(levels, low, high, *refs):
    sib, two = (refs[:levels], refs[levels])
    odd = is_right(0, "tile")
    n = low.shape[0]
    two[pl.ds(0, n)] = jnp.where(odd, high[...], low[...])
    at = n
    for block in sib:
        width = block.shape[1]
        for i in range(block.shape[0]):
            two[at] = jnp.where(odd, block[i, width - 1 : width], block[i, 0:1])
            at += 1


def first_three(kernel, ready, one, two, three, _rhs, _diag, _ty, *rest):
    kernel(one, two, three, *rest)
    ready(0)


def beyond_kernel(levels, shapes, shape, recv, terms, two, row, planes, *hots):
    depth, width, long = shape
    tiles, layers = (lax.axis_size("tile"), lax.axis_size("layer"))
    tile = lax.axis_index("tile")
    odd = is_right(0, "tile")
    planes[...] = jnp.zeros(planes.shape, F32)
    for i in range(planes.shape[0]):
        planes[i, 0:1] = two[i]
    step = jnp.where(odd, layers, -layers)
    lists = [[jnp.clip(device + step, 0, tiles * layers - 1) for device in members] for members in groups_of(levels)]
    table_kernel(lists, shape, terms, hots, jnp.where(odd, 0, width - 1))
    exists = jnp.where(odd, (tile < tiles - 1).astype(F32), (tile > 0).astype(F32)) + jnp.zeros((1, long), F32)
    blocks = []
    at = 4 * depth
    for size in shapes:
        blocks.append([planes[at + i] for i in range(size)])
        at += size

    def planes_of():
        kept = [planes[depth + z] for z in range(depth)]
        return (
            [planes[z] for z in range(depth)],
            [jnp.where(value == 0.0, 1.0, value) for value in kept],
            [planes[2 * depth + z] for z in range(depth)],
        )

    values, _, _, _ = column_solve(levels, recv, lists, hots, planes_of, blocks)
    for z in range(depth):
        found = jnp.where(exists > 0.0, values[z][0:1], 0.0)
        row[z] = jnp.where(odd, found, found * two[3 * depth + z])


def search_kernel(p, coupled_z, two, one, tx, ty, tz, rhs, diag, binv, s, outer, row_two, row_one, inner):
    depth, width, _ = p.shape
    odd = is_right(0, "tile")
    right = is_right(0)
    row = iota(p.shape[1:], 0)
    for z in range(depth):
        centre = p[z]
        after = jnp.where(odd, two[z], one[z])
        before = jnp.where(odd, one[z], two[z])
        coupled = coupled_z[z] + beside(centre, tx[z], ty[z])
        coupled = coupled + jnp.where(row == 0, before, 0.0) + jnp.where(row == width - 1, tx[z] * after, 0.0)
        remain = [rhs[c, z] - diag[c, 0, z] * centre for c in range(3)]
        remain[0] = remain[0] + coupled
        for c in range(3):
            value = binv[c, 0, z] * remain[0] + binv[c, 1, z] * remain[1] + binv[c, 2, z] * remain[2]
            if c == 0:
                value = centre + value
            s[c, z] = value
            tile_rows(value[0:1], (tx[z] * value)[width - 1 :], row_one.at[c, z], row_two.at[c, z])
    for c in range(3):
        top, bottom = (s[c, 0], tz[depth - 1] * s[c, depth - 1])
        inner[c] = jnp.where(right, top, bottom)
        outer[c] = jnp.where(right, bottom, top)


def inner_kernel(s, diag, tz, tx, ty, image):
    depth = s.shape[1]
    for z in range(depth):
        for c in range(3):
            total = diag[c, 0, z] * s[0, z] + diag[c, 1, z] * s[1, z] + diag[c, 2, z] * s[2, z]
            total = total - beside(s[c, z], tx[z], ty[z])
            if z:
                total = total - tz[z - 1] * s[c, z - 1]
            if z < depth - 1:
                total = total - tz[z] * s[c, z + 1]
            image[c, z] = total


def image_kernel(part, outer, row_two, row_one, inner, rhs, tz, tx, image, send):
    depth, width = part.shape[1:3]
    right, odd = (is_right(0), is_right(0, "tile"))
    row = iota(part.shape[2:], 0)
    along = power = start = 0.0
    for z in range(depth):
        for c in range(3):
            value = part[c, z]
            if z == 0:
                value = value - jnp.where(right, inner[c], outer[c])
            if z == depth - 1:
                value = value - tz[z] * jnp.where(right, outer[c], inner[c])
            after = jnp.where(odd, row_two[c, z], row_one[c, z])
            before = jnp.where(odd, row_one[c, z], row_two[c, z])
            value = value - jnp.where(row == 0, before, 0.0) - jnp.where(row == width - 1, tx[z] * after, 0.0)
            image[c, z] = value
            given = rhs[c, z]
            along = along + value * given
            power = power + value * value
            start = start + given * given
    along, power, start = (jnp.sum(along), jnp.sum(power), jnp.sum(start))
    omega = along / jnp.where(power > 0.0, power, 1.0)
    square = cross = 0.0
    for z in range(depth):
        for c in range(3):
            value = image[c, z]
            left = rhs[c, z] - omega * value
            square = square + left * left
            cross = cross + left * value
    lane = iota((1, send.shape[2]), 1)
    out = jnp.zeros((1, send.shape[2]), F32)
    for i, value in enumerate((along, power, start, jnp.sum(square), jnp.sum(cross), omega)):
        out = jnp.where(lane == i, value, out)
    send[...] = jnp.broadcast_to(out[:, None], send.shape)


def finish_kernel(recv, s, image, rhs, update, lin_res, ratio):
    sums = recv[...].reshape(recv.shape[0], recv.shape[2])
    whole = jnp.sum(sums, axis=0, keepdims=True)
    omega = whole[:, 0:1] / whole[:, 1:2]
    shift = sums[:, 5:6] - omega
    square = sums[:, 3:4] + 2.0 * shift * sums[:, 4:5] + shift * shift * sums[:, 1:2]
    ratio[...] = jnp.sqrt(jnp.sum(square, axis=0, keepdims=True) / whole[:, 2:3])
    for c in range(3):
        for z in range(s.shape[1]):
            update[c, z] = omega * s[c, z]
            lin_res[c, z] = rhs[c, z] - omega * image[c, z]


def flip(x, level, axis="layer"):
    return lax.ppermute(x, axis, [(i, i ^ (1 << level)) for i in range(lax.axis_size(axis))])


def neighbour(x, axis="layer"):
    pairs = [(i, i + 1) for i in range(1, lax.axis_size(axis) - 1, 2)]
    return lax.ppermute(x, axis, pairs + [(j, i) for i, j in pairs])


def everywhere(x):
    return lax.all_to_all(x, BOTH, split_axis=0, concat_axis=0, tiled=True)


def shards(rhs, weights, block_diag, block_inv, tx, ty, tz, store, cell, front, prod, inverse):
    layers = lax.axis_size("layer")
    devices = lax.axis_size("tile") * layers
    levels = layers.bit_length() - 1
    depth, width, long = tx.shape
    count = cell.shape[0]
    rows = inverse.shape[0]
    lists = layers * count
    cell, front, prod = (cell.reshape(1, -1), front.reshape(1, -1), prod.reshape(1, -1))
    field = vmem(tx.shape)

    def planes(n):
        return vmem((n, width, long))

    hbm_spec = pl.BlockSpec(memory_space=pltpu.HBM)
    given = (cell, front, prod, rhs, weights, tz, store)
    pres, send, ends = pl.pallas_call(
        pres_kernel,
        out_shape=(field, vmem((devices, 1, 3 * count)), planes(6)),
        in_specs=[hbm_spec] * len(given),
        out_specs=(VM,) * 3,
        scratch_shapes=[vmem(a.shape, a.dtype) for a in given] + [pltpu.SemaphoreType.DMA((len(given),))],
        compiler_params=pltpu.CompilerParams(vmem_limit_bytes=LIMIT),
    )(*[pltpu.with_memory_space_constraint(a, pltpu.HBM) for a in given])
    terms = everywhere(send)
    sib, found = ([], [prod])
    for level in range(levels - 1):
        sib.append(flip(ends, level))
        final = level == levels - 2
        outs = (vmem((1, (3 if final else 2) * count)), *((planes(3),) if final else (planes(6), planes(2 * depth))))
        if level == 0:
            rim = vmem((4 * depth, 1, long))
            low, high, *got = call(
                functools.partial(first_join_kernel, final),
                (rim, rim, *outs),
                (ends, sib[-1], pres, tz, store, tx, cell, prod),
                far=range(3, 8),
            )
        else:
            got = call(
                functools.partial(join_kernel, level, final), outs, (ends, sib[-1], answers, cell, prod), far=(3, 4)
            )
        found.append(got[0])
        if final:
            face = got[1]
        else:
            ends, answers = got[1:]
    found = jnp.concatenate(found, 1)
    terms, face, found = lax.optimization_barrier((terms, face, found))
    sib.append(flip(face, levels - 1))
    chunks = 8
    send = pl.pallas_call(
        front_kernel,
        out_shape=vmem((devices, 1, rows + 2 * levels * count)),
        in_specs=[VM, VM, hbm_spec],
        out_specs=VM,
        scratch_shapes=[vmem(inverse.shape), pltpu.SemaphoreType.DMA((chunks,))],
        compiler_params=pltpu.CompilerParams(vmem_limit_bytes=LIMIT),
    )(terms, found, pltpu.with_memory_space_constraint(inverse, pltpu.HBM))
    sizes = [block.shape[0] for block in sib]
    rim = vmem((4 * depth + sum(sizes), 1, long))
    send, low, high = lax.optimization_barrier((send, low, high))
    (two,) = call(functools.partial(edge_kernel, levels), (rim,), (low, high, *sib))
    sol = everywhere(send)
    two = neighbour(two, "tile")

    def hots(high):
        return (
            vmem((high * long // 128, lists), BF16),
            vmem((128, lists), BF16),
            vmem((rows, lists), BF16),
            vmem((1, lists), I32),
            vmem((1, count), I32),
        )

    at = 3 + levels
    row3 = vmem((depth, 1, long))
    p, coupled_z, one, tz, _, tx, block_inv = call(
        functools.partial(pressure_kernel, levels),
        (field, field, row3),
        (sol, terms, pres, *sib, tz, store, tx, block_inv),
        far=range(at, at + 4),
        keep=range(at, at + 4),
        late=(range(at, at + 3), (at + 3,)),
        scratch=hots(width),
    )
    sol, one, terms = lax.optimization_barrier((sol, one, terms))
    one = flip(one, 0, "tile")
    two, rhs, block_diag, ty = call(
        functools.partial(first_three, functools.partial(beyond_kernel, levels, sizes, (depth, width, long))),
        (row3,),
        (sol, terms, two, rhs, block_diag, ty),
        far=(3, 4, 5),
        keep=(3, 4, 5),
        late=((3, 4, 5),),
        scratch=(vmem((4 * depth + sum(sizes), 8, long)), *hots(8)),
    )
    row9 = vmem((3, depth, 1, long))
    plane3 = planes(3)
    s, outer, row_two, row_one, inner = call(
        search_kernel,
        (vmem(rhs.shape), plane3, row9, row9, plane3),
        (p, coupled_z, two, one, tx, ty, tz, rhs, block_diag, block_inv),
    )
    outer, row_two = (neighbour(outer), neighbour(row_two, "tile"))
    row_one, inner = (flip(row_one, 0, "tile"), flip(inner, 0))
    (part,) = call(inner_kernel, (vmem(rhs.shape),), (s, block_diag, tz, tx, ty))
    image, send = call(
        image_kernel,
        (vmem(rhs.shape), vmem((devices, 1, 128))),
        (part, outer, row_two, row_one, inner, rhs, tz, tx),
    )
    sums = everywhere(send)
    update, lin_res, ratio = call(
        finish_kernel, (hbm(rhs.shape), hbm(rhs.shape), hbm((1, 1))), (sums, s, image, rhs)
    )
    return (update, lin_res, ratio.reshape(()))


def solution(mesh):
    return jax.shard_map(
        shards,
        mesh=mesh,
        in_specs=(
            P(None, "layer", "tile", None),
            P(None, "layer", "tile", None),
            P(None, None, "layer", "tile", None),
            P(None, None, "layer", "tile", None),
            P("layer", "tile", None),
            P("layer", "tile", None),
            P("layer", "tile", None),
            P("layer", "tile", None),
            P(("tile", "layer")),
            P(("tile", "layer")),
            P(("tile", "layer")),
            P(("tile", "layer"), None),
        ),
        out_specs=(P(None, "layer", "tile", None), P(None, "layer", "tile", None), P()),
        check_vma=False,
    )
```

```python
import functools
import jax
import jax.numpy as jnp
from jax import lax
from jax.experimental import pallas as pl
from jax.experimental.pallas import tpu as pltpu
from jax.sharding import PartitionSpec as P

F32 = jnp.float32
BF16 = jnp.bfloat16
I32 = jnp.int32
BOTH = ("tile", "layer")
VM = pl.BlockSpec(memory_space=pltpu.VMEM)
LIMIT = 16 << 20
PARTS = 2


def hbm(shape):
    return jax.ShapeDtypeStruct(shape, F32)


def vmem(shape, dtype=F32):
    return pltpu.VMEM(shape, dtype)


def staged(kernel, where, outs, kept, column, late, *refs):
    count, sems = (len(where), refs[-1])
    held = list(refs[count + outs + len(kept) : -1])
    target_count = sum(where) - len(kept)
    held, extra = (held[:target_count], held[target_count:])
    target = dict(zip(kept, refs[count + outs : count + outs + len(kept)]))
    operands, copies = ([], [])
    for i, far in enumerate(where):
        if far:
            to = target[i] if i in target else held.pop(0)
            part = refs[i].at[:, 0] if i in column else refs[i]
            copies.append(pltpu.make_async_copy(part, to, sems.at[len(copies)]))
            operands.append(to)
        else:
            operands.append(refs[i])
    places = [i for i, far in enumerate(where) if far]
    for copy in copies:
        copy.start()
    for i, copy in zip(places, copies):
        if not any(i in group for group in late):
            copy.wait()

    def ready(k):
        for i, copy in zip(places, copies):
            if i in late[k]:
                copy.wait()

    more = (ready,) if late else ()
    kernel(*more, *operands, *refs[count : count + outs], *extra)


def call(kernel, outs, args, far=(), keep=(), column=(), late=(), scratch=(), limit=LIMIT):
    where = [i in far for i in range(len(args))]
    spaces = [pltpu.HBM if w else pltpu.VMEM for w in where]
    every = (*outs, *(vmem(args[i].shape, args[i].dtype) for i in keep))
    return pl.pallas_call(
        functools.partial(staged, kernel, where, len(outs), tuple(keep), tuple(column), tuple(late)),
        out_shape=every,
        in_specs=[pl.BlockSpec(memory_space=s) for s in spaces],
        out_specs=(VM,) * len(every),
        scratch_shapes=[
            vmem(a.shape[:1] + a.shape[2:] if i in column else a.shape, a.dtype)
            for i, a in enumerate(args)
            if where[i] and i not in keep
        ]
        + [*scratch, pltpu.SemaphoreType.DMA((max(1, sum(where)),))],
        compiler_params=pltpu.CompilerParams(vmem_limit_bytes=limit),
    )(*[pltpu.with_memory_space_constraint(a, s) for a, s in zip(args, spaces)])


def iota(shape, dim):
    return lax.broadcasted_iota(I32, shape, dim)


def split(x):
    one = x.astype(BF16)
    rest = x - one.astype(F32)
    two = rest.astype(BF16)
    three = (rest - two.astype(F32)).astype(BF16)
    return [one, two, three]


def fold(x, parts=3):
    n = x.shape[0] // parts
    total = x[(parts - 1) * n :]
    for i in range(parts - 2, -1, -1):
        total = x[i * n : (i + 1) * n] + total
    return total


def onehot(index, size):
    return jnp.where(iota((size, index.shape[1]), 0) == index, 1.0, 0.0)


def dot(a, b):
    return lax.dot_general(a, b, (((1,), (0,)), ((), ())), preferred_element_type=F32)


def dot_nt(a, b):
    return lax.dot_general(a, b, (((1,), (1,)), ((), ())), preferred_element_type=F32)


def pick(tables, hi, hot):
    rows = tables[0].shape[0]
    parts = jnp.concatenate([p for table in tables for p in split(table)[:PARTS]], 0)
    got = dot(parts, hot)
    mask = onehot(hi, rows)
    n = PARTS * rows
    return [jnp.sum(fold(got[i * n : (i + 1) * n], PARTS) * mask, axis=0, keepdims=True) for i in range(len(tables))]


def pres_kernel(cell_in, front_in, prod_in, rhs_in, wts_in, tz_in, store_in, pres, send, ends, *scratch):
    (cell, front, prod, rhs, wts, tz, store), sems = scratch[:-1], scratch[-1]
    pairs = ((cell_in, cell), (front_in, front), (prod_in, prod), (rhs_in, rhs), (wts_in, wts), (tz_in, tz), (store_in, store))
    copies = [pltpu.make_async_copy(a, b, sems.at[i]) for i, (a, b) in enumerate(pairs)]
    for copy in copies:
        copy.start()
    for copy in copies[:3]:
        copy.wait()
    depth, width, long = pres.shape
    where = cell[...]
    hot = onehot(lax.rem(where, long), long).astype(BF16)
    for copy in copies[3:]:
        copy.wait()
    for z in range(depth):
        pres[z] = wts[0, z] * rhs[0, z] + wts[1, z] * rhs[1, z] + wts[2, z] * rhs[2, z]
    tzs = [tz[z] for z in range(depth)]
    gs, invs, first, final, coefs = factors(tzs, [store[z] for z in range(depth)])
    tables = [pres[...].reshape(depth * width, long), jnp.concatenate(first, 0), jnp.concatenate(final, 0)]
    found, kf, kl = pick(tables, lax.div(where, long), hot)
    both = jnp.concatenate([prod[...] * found, front[...].astype(F32), where.astype(F32)], 1)
    send[...] = jnp.broadcast_to(both[:, None], send.shape)
    y = local_solve([pres[z] for z in range(depth)], gs, invs, tzs)
    for i, value in enumerate((*coefs, y[0], y[-1], tzs[-1])):
        ends[i] = value
    ends[6] = jnp.zeros((width, long), F32)
    ends[6, 0:1, : 2 * where.shape[1]] = jnp.concatenate([prod[...] * kf, prod[...] * kl], 1)


def is_right(level, axis="layer"):
    return (lax.axis_index(axis) >> level) % 2 == 1


def choose(level, mine, other, axis="layer"):
    right = is_right(level, axis)
    return (jnp.where(right, other, mine), jnp.where(right, mine, other))


def local_solve(rhs, upper, inv, tz):
    depth = len(rhs)
    y = [rhs[0] * inv[0]]
    for z in range(1, depth):
        y.append((rhs[z] + tz[z - 1] * y[-1]) * inv[z])
    for z in range(depth - 2, -1, -1):
        y[z] = y[z] + upper[z] * y[z + 1]
    return y


def factors(tz, store):
    depth = len(tz)
    gs, invs = ([], [])
    own = None
    for z in range(depth):
        own = store[z] if z == 0 else store[z] + gs[-1] * own
        invs.append(1.0 / (own + tz[z] if z < depth - 1 else own))
        gs.append(tz[z] * invs[-1])
    first = [invs[0]]
    for z in range(1, depth):
        first.append(tz[z - 1] * first[-1] * invs[z])
    final = [None] * depth
    final[-1] = invs[-1]
    for z in range(depth - 2, -1, -1):
        first[z] = first[z] + gs[z] * first[z + 1]
        final[z] = gs[z] * final[z + 1]
    return gs, invs, first, final, block_ends(first, final, tz)


def block_ends(first, final, tz):
    return (first[0], first[-1], final[-1] + 1.0 / jnp.maximum(tz[-1], 1e-30))


def pair(level, own, sib):
    af, af_ = choose(level, own[0], sib[0])
    c, c_ = choose(level, own[1], sib[1])
    b, b_ = choose(level, own[2], sib[2])
    return af, c, b, af_, c_, b_, 1.0 / (b + af_)


def join_coefs(level, own, sib):
    af, c, _, _, c_, b_, g = pair(level, own, sib)
    return (af - c * c * g, c * c_ * g, b_ - c_ * c_ * g)


def join_ends(level, own, sib, mine, other):
    _, c, _, _, c_, _, g = pair(level, own, sib)
    yf, yf_ = choose(level, mine[0], other[0])
    yl, yl_ = choose(level, mine[1], other[1])
    flux = g * (yl - yf_)
    return (yf - c * flux, yl_ + c_ * flux)


def first_join_kernel(final, own, sib, pres, tz, store, tx, cell, prod, kept, low, high, *outs):
    depth, width, _ = tz.shape
    for k, ref in enumerate((tz, store, pres, tx)):
        for z in range(depth):
            low[k * depth + z] = ref[z, 0:1]
            high[k * depth + z] = ref[z, width - 1 : width]
    gs, invs, first, last, _ = factors([tz[z] for z in range(depth)], [store[z] for z in range(depth)])
    for i, value in enumerate(gs + invs + first + last):
        kept[i] = value
    join(0, final, own, sib, first + last, cell, prod, *outs)


def join_kernel(level, final, own, sib, answers, cell, prod, *outs):
    join(level, final, own, sib, [answers[i] for i in range(answers.shape[0])], cell, prod, *outs)


def join(level, final, own, sib, answers, cell, prod, found, *outs):
    depth = len(answers) // 2
    width, long = answers[0].shape
    _, c, _, _, c_, _, g = pair(level, own, sib)
    first, both, last = join_coefs(level, own, sib)
    yf, yl = join_ends(level, own, sib, (own[3], own[4]), (sib[3], sib[4]))
    lower = choose(level, own[5], sib[5])[1]
    right, later = (is_right(level), is_right(level + 1))
    cg, cg_ = (c * g, c_ * g)
    tops, bottoms = ([], [])
    for z in range(depth):
        kf, kl = (answers[z], answers[depth + z])
        tops.append(jnp.where(right, cg * kf, kf - cg * kl))
        bottoms.append(jnp.where(right, kl - cg_ * kf, cg_ * kl))
    tables = [answers[:depth], answers[depth:]] if level else []
    if final:
        (face,) = outs
        face[0], face[1] = (jnp.where(later, first, last), jnp.where(later, yf, yl))
        face[2] = lower
        tables.append([jnp.where(later, tops[z], bottoms[z]) for z in range(depth)])
    else:
        out, more = outs
        for i, value in enumerate((first, both, last, yf, yl, lower)):
            out[i] = value
        for i, value in enumerate(tops + bottoms):
            more[i] = value
    if tables:
        where = cell[...]
        hot = onehot(lax.rem(where, long), long).astype(BF16)
        got = pick([jnp.concatenate(t, 0) for t in tables], lax.div(where, long), hot)
        found[...] = jnp.concatenate([prod[...] * value for value in got], 1)
    else:
        found[...] = jnp.zeros(found.shape, F32)


def groups_of(levels):
    layers = lax.axis_size("layer")
    l = lax.axis_index("layer")
    base = lax.axis_index("tile") * layers
    out = [[base + l]]
    for level in range(levels):
        out.append([base + (((l >> level) ^ 1) << level) + i for i in range(1 << level)])
    return out


def front_kernel(recv, found, inverse, send, held, sems):
    devices = recv.shape[0]
    count = recv.shape[2] // 3
    rows, length = inverse.shape
    lanes = 128
    chunks = sems.shape[0]
    wide = length // chunks
    found = found[...]
    copies = [
        pltpu.make_async_copy(inverse.at[:, pl.ds(i * wide, wide)], held.at[:, pl.ds(i * wide, wide)], sems.at[i])
        for i in range(chunks)
    ]
    for copy in copies:
        copy.start()
    terms, index = (recv[:, 0, :count], recv[:, 0, count : 2 * count])
    high = jnp.floor(index * (1.0 / lanes))
    low = index - high * lanes
    parts = [p.astype(F32) for p in split(terms)[:PARTS]]
    row_of = iota((length // lanes, count), 0).astype(F32)
    lane_of = iota((lanes, count), 0).astype(F32)
    total = jnp.zeros((length // lanes, lanes), F32)
    for d in range(devices):
        hit = row_of == high[d : d + 1]
        left = jnp.concatenate([jnp.where(hit, p[d : d + 1], 0.0).astype(BF16) for p in parts], 0)
        right = jnp.where(lane_of == low[d : d + 1], 1.0, 0.0).astype(BF16)
        total = total + fold(dot_nt(left, right), PARTS)
    acc = jnp.zeros((rows, lanes), F32)
    for i in range(chunks):
        copies[i].wait()
        for r in range(i * wide // lanes, (i + 1) * wide // lanes):
            acc = acc + held[:, r * lanes : (r + 1) * lanes] * total[r : r + 1]
    parts = jnp.concatenate(split(acc), 1)
    out = dot_nt(jnp.ones((8, parts.shape[1]), BF16), parts)
    pad = send.shape[2] - out.shape[1] - found.shape[1]
    pieces = [out[0:1], found] + ([jnp.zeros((1, pad), F32)] if pad else [])
    send[...] = jnp.broadcast_to(jnp.concatenate(pieces, 1)[:, None], send.shape)


def gathered(values, rows_hot, lanes_hot, start, size, ext, parts):
    hot = lanes_hot[:, start : start + size]
    pieces = [hot * p for v in values for p in split(v)[:parts]]
    got = dot_nt(rows_hot[:, start : start + size], jnp.concatenate(pieces, 0))
    planes = []
    lanes = hot.shape[0]
    for i in range(len(values)):
        plane = got[:, i * parts * lanes : (i * parts + 1) * lanes]
        for k in range(1, parts):
            j = i * parts + k
            plane = plane + got[:, j * lanes : (j + 1) * lanes]
        planes.append(jnp.concatenate([plane[r : r + ext] for r in range(0, plane.shape[0], ext)], 1))
    return planes


def beside(centre, tx, ty):
    width, long = centre.shape
    row, col = (iota(centre.shape, 0), iota(centre.shape, 1))
    total = tx * jnp.where(row == width - 1, 0.0, pltpu.roll(centre, width - 1, 0))
    total = total + jnp.where(row == 0, 0.0, pltpu.roll(tx * centre, 1, 0))
    total = total + ty * jnp.where(col == long - 1, 0.0, pltpu.roll(centre, long - 1, 1))
    return total + jnp.where(col == 0, 0.0, pltpu.roll(ty * centre, 1, 1))


def tile_rows(first, last, one, two):
    odd = is_right(0, "tile")
    one[...] = jnp.where(odd, first, last)
    two[...] = jnp.where(odd, last, first)


def table_kernel(lists, shape, terms, hots, only=None):
    _, width, long = shape
    rows_hot, lanes_hot, sol_hot, sol_row, layer = hots
    lanes = 128
    rows = sol_hot.shape[0]
    count = terms.shape[2] // 3
    at = 0
    for members in lists:
        for device in members:
            entry = terms[device]
            index = entry[:, count : 2 * count].astype(I32)
            cell = entry[:, 2 * count :].astype(I32)
            y, x = lax.rem(cell, long), lax.rem(lax.div(cell, long), width)
            if only is None:
                row = lax.div(y, lanes) * width + x
            else:
                row = jnp.where(x == only, lax.div(y, lanes) * 8, -1)
            here = pl.ds(at, count)
            rows_hot[:, here] = onehot(row, rows_hot.shape[0]).astype(BF16)
            lanes_hot[:, here] = onehot(lax.rem(y, lanes), lanes).astype(BF16)
            sol_hot[:, here] = onehot(lax.rem(index, rows), rows).astype(BF16)
            sol_row[:, here] = lax.div(index, rows)
            if at < layer.shape[1]:
                layer[:, here] = lax.div(cell, long * width)
            at += count


def column_solve(levels, recv, lists, hots, listing, planes_of, sib):
    rows_hot, lanes_hot, sol_hot, sol_row, layer = hots
    rows, count = (sol_hot.shape[0], layer.shape[1])
    table = jnp.concatenate(split(recv[...].reshape(recv.shape[0], recv.shape[2])[:, :rows]), 0)
    sol = fold(dot(table, sol_hot[...]))
    sol = jnp.sum(jnp.where(iota(sol.shape, 0) == sol_row[...], sol, 0.0), axis=0, keepdims=True)
    layer = layer[...]

    def listed(group, column):
        at = rows + column * count
        return jnp.concatenate([recv[device][:, at : at + count] for device in group], 1)

    mine_list, sib_list = listing
    tz, pres, (gs, invs, first, final, coefs) = planes_of()
    depth = len(tz)
    high = tz[0].shape[0]
    own = [coefs]
    start = layer.shape[1]
    value = mine_list * sol[:, :start]
    values = [jnp.where(layer == z, value, 0.0) for z in range(depth)]
    change = gathered(values, rows_hot, lanes_hot, 0, start, high, PARTS)
    y = local_solve([pres[z] - change[z] for z in range(depth)], gs, invs, tz)
    mine = (y[0], y[-1])
    steps = []
    for level in range(levels):
        size = len(lists[level + 1]) * count
        top = level == levels - 1
        if level:
            columns = [2 * level - 2] if top else [2 * level - 2, 2 * level - 1]
            values = [listed(lists[level + 1], c) for c in columns]
        else:
            values = [sib_list[:, i * count : (i + 1) * count] for i in range(2)]
        values = [value * sol[:, start : start + size] for value in values]
        change = gathered(values, rows_hot, lanes_hot, start, size, high, PARTS)
        start += size
        if top:
            other = sib[level][1] - change[0]
            steps.append((mine, (other, other)))
        else:
            other = (sib[level][3] - change[0], sib[level][4] - change[1])
            steps.append((mine, other))
            mine = join_ends(level, own[level], sib[level], mine, other)
            own.append(join_coefs(level, own[level], sib[level]))
    above = below = tzp = jnp.zeros(tz[0].shape, F32)
    place = lax.axis_index("layer")
    for level in range(levels - 1, -1, -1):
        mine, other = steps[level]
        yl, _ = choose(level, mine[1], other[1])
        _, yf_ = choose(level, mine[0], other[0])
        flux = yl - yf_
        if level == levels - 1:
            b, _ = choose(level, own[level][2], sib[level][0])
            _, af_ = choose(level, own[level][0], sib[level][0])
            g = 1.0 / (b + af_)
            before = sib[level][2]
        else:
            _, c, _, _, c_, _, g = pair(level, own[level], sib[level])
            flux = flux + c * above - c_ * below
            before = sib[level][5]
        tzp = jnp.where(place % (2 << level) == 1 << level, before, tzp)
        flux = g * flux
        right = is_right(level)
        above, below = (jnp.where(right, flux, above), jnp.where(right, below, -flux))
    return [y[z] + first[z] * above + final[z] * below for z in range(depth)], above, below, tzp


def pressure_kernel(levels, ready, recv, terms, pres, *refs):
    sib, (tz, kept, tx, prod, _, p, coupled_z, one, *hots) = (refs[:levels], refs[levels:])
    depth, width, _ = pres.shape
    odd = is_right(0, "tile")
    lists = groups_of(levels)
    table_kernel(lists, pres.shape, terms, hots)

    def planes_of():
        tzs, pressures = ([ref[z] for z in range(depth)] for ref in (tz, pres))
        gs, invs, first, final = ([kept[k * depth + z] for z in range(depth)] for k in range(4))
        return tzs, pressures, (gs, invs, first, final, block_ends(first, final, tzs))

    ready(0)
    listing = (prod[...], sib[0][6, 0:1])
    values, above, below, tzp = column_solve(levels, recv, lists, hots, listing, planes_of, sib)
    tzs = [tz[z] for z in range(depth)]
    is_last = lax.axis_index("layer") == (1 << levels) - 1
    for z in range(depth):
        p[z] = values[z]
        one[z] = jnp.where(odd, values[z][0:1], (tx[z] * values[z])[width - 1 :])
        total = above + tzp * values[z] if z == 0 else tzs[z - 1] * values[z - 1]
        if z == depth - 1:
            coupled_z[z] = total + jnp.where(is_last, 0.0, below + tzs[z] * values[z])
        else:
            coupled_z[z] = total + tzs[z] * values[z + 1]
    ready(1)


def edge_kernel(levels, low, high, prod, *refs):
    sib, two = (refs[:levels], refs[levels])
    odd = is_right(0, "tile")
    n = low.shape[0]
    two[pl.ds(0, n)] = jnp.where(odd, high[...], low[...])
    at = n
    for block in sib:
        width = block.shape[1]
        for i in range(min(6, block.shape[0])):
            two[at] = jnp.where(odd, block[i, width - 1 : width], block[i, 0:1])
            at += 1
    two[at] = sib[0][6, 0:1]
    two[at + 1] = jnp.zeros((1, two.shape[2]), F32)
    two[at + 1, :, : prod.shape[1]] = prod[...]


def first_three(kernel, ready, one, two, three, _rhs, _diag, _ty, *rest):
    kernel(one, two, three, *rest)
    ready(0)


def beyond_kernel(levels, shapes, shape, recv, terms, two, row, planes, *hots):
    depth, width, long = shape
    tiles, layers = (lax.axis_size("tile"), lax.axis_size("layer"))
    tile = lax.axis_index("tile")
    odd = is_right(0, "tile")
    planes[...] = jnp.zeros(planes.shape, F32)
    count = planes.shape[0]
    for i in range(count):
        planes[i, 0:1] = two[i]
    step = jnp.where(odd, layers, -layers)
    lists = [[jnp.clip(device + step, 0, tiles * layers - 1) for device in members] for members in groups_of(levels)]
    table_kernel(lists, shape, terms, hots, jnp.where(odd, 0, width - 1))
    exists = jnp.where(odd, (tile < tiles - 1).astype(F32), (tile > 0).astype(F32)) + jnp.zeros((1, long), F32)
    blocks = []
    at = 4 * depth
    for size in shapes:
        blocks.append([planes[at + i] for i in range(size)])
        at += size

    def planes_of():
        kept = [planes[depth + z] for z in range(depth)]
        tzs = [planes[z] for z in range(depth)]
        found = factors(tzs, [jnp.where(value == 0.0, 1.0, value) for value in kept])
        return tzs, [planes[2 * depth + z] for z in range(depth)], found

    listing = (two[count + 1, :, : terms.shape[2] // 3], two[count])
    values, _, _, _ = column_solve(levels, recv, lists, hots, listing, planes_of, blocks)
    for z in range(depth):
        found = jnp.where(exists > 0.0, values[z][0:1], 0.0)
        row[z] = jnp.where(odd, found, found * two[3 * depth + z])


def search_kernel(p, coupled_z, two, one, tx, ty, tz, rhs, diag, binv, s, outer, row_two, row_one, inner):
    depth, width, _ = p.shape
    odd = is_right(0, "tile")
    right = is_right(0)
    row = iota(p.shape[1:], 0)
    for z in range(depth):
        centre = p[z]
        after = jnp.where(odd, two[z], one[z])
        before = jnp.where(odd, one[z], two[z])
        coupled = coupled_z[z] + beside(centre, tx[z], ty[z])
        coupled = coupled + jnp.where(row == 0, before, 0.0) + jnp.where(row == width - 1, tx[z] * after, 0.0)
        remain = [rhs[c, z] - diag[c, 0, z] * centre for c in range(3)]
        remain[0] = remain[0] + coupled
        for c in range(3):
            value = binv[c, 0, z] * remain[0] + binv[c, 1, z] * remain[1] + binv[c, 2, z] * remain[2]
            if c == 0:
                value = centre + value
            s[c, z] = value
            tile_rows(value[0:1], (tx[z] * value)[width - 1 :], row_one.at[c, z], row_two.at[c, z])
    for c in range(3):
        top, bottom = (s[c, 0], tz[depth - 1] * s[c, depth - 1])
        inner[c] = jnp.where(right, top, bottom)
        outer[c] = jnp.where(right, bottom, top)


def inner_kernel(s, diag, tz, tx, ty, image):
    depth = s.shape[1]
    for z in range(depth):
        for c in range(3):
            total = diag[c, 0, z] * s[0, z] + diag[c, 1, z] * s[1, z] + diag[c, 2, z] * s[2, z]
            total = total - beside(s[c, z], tx[z], ty[z])
            if z:
                total = total - tz[z - 1] * s[c, z - 1]
            if z < depth - 1:
                total = total - tz[z] * s[c, z + 1]
            image[c, z] = total


def image_kernel(part, outer, row_two, row_one, inner, rhs, tz, tx, image, send):
    depth, width = part.shape[1:3]
    right, odd = (is_right(0), is_right(0, "tile"))
    row = iota(part.shape[2:], 0)
    along = power = start = 0.0
    for z in range(depth):
        for c in range(3):
            value = part[c, z]
            if z == 0:
                value = value - jnp.where(right, inner[c], outer[c])
            if z == depth - 1:
                value = value - tz[z] * jnp.where(right, outer[c], inner[c])
            after = jnp.where(odd, row_two[c, z], row_one[c, z])
            before = jnp.where(odd, row_one[c, z], row_two[c, z])
            value = value - jnp.where(row == 0, before, 0.0) - jnp.where(row == width - 1, tx[z] * after, 0.0)
            image[c, z] = value
            given = rhs[c, z]
            along = along + value * given
            power = power + value * value
            start = start + given * given
    along, power, start = (jnp.sum(along), jnp.sum(power), jnp.sum(start))
    omega = along / jnp.where(power > 0.0, power, 1.0)
    square = cross = 0.0
    for z in range(depth):
        for c in range(3):
            value = image[c, z]
            left = rhs[c, z] - omega * value
            square = square + left * left
            cross = cross + left * value
    lane = iota((1, send.shape[2]), 1)
    out = jnp.zeros((1, send.shape[2]), F32)
    for i, value in enumerate((along, power, start, jnp.sum(square), jnp.sum(cross), omega)):
        out = jnp.where(lane == i, value, out)
    send[...] = jnp.broadcast_to(out[:, None], send.shape)


def finish_kernel(recv, s, image, rhs, update, lin_res, ratio):
    sums = recv[...].reshape(recv.shape[0], recv.shape[2])
    whole = jnp.sum(sums, axis=0, keepdims=True)
    omega = whole[:, 0:1] / whole[:, 1:2]
    shift = sums[:, 5:6] - omega
    square = sums[:, 3:4] + 2.0 * shift * sums[:, 4:5] + shift * shift * sums[:, 1:2]
    ratio[...] = jnp.sqrt(jnp.sum(square, axis=0, keepdims=True) / whole[:, 2:3])
    for c in range(3):
        for z in range(s.shape[1]):
            update[c, z] = omega * s[c, z]
            lin_res[c, z] = rhs[c, z] - omega * image[c, z]


def flip(x, level, axis="layer"):
    return lax.ppermute(x, axis, [(i, i ^ (1 << level)) for i in range(lax.axis_size(axis))])


def neighbour(x, axis="layer"):
    pairs = [(i, i + 1) for i in range(1, lax.axis_size(axis) - 1, 2)]
    return lax.ppermute(x, axis, pairs + [(j, i) for i, j in pairs])


def everywhere(x):
    return lax.all_to_all(x, BOTH, split_axis=0, concat_axis=0, tiled=True)


def shards(rhs, weights, block_diag, block_inv, tx, ty, tz, store, cell, front, prod, inverse):
    layers = lax.axis_size("layer")
    devices = lax.axis_size("tile") * layers
    levels = layers.bit_length() - 1
    depth, width, long = tx.shape
    count = cell.shape[0]
    rows = inverse.shape[0]
    lists = layers * count
    cell, front, prod = (cell.reshape(1, -1), front.reshape(1, -1), prod.reshape(1, -1))
    field = vmem(tx.shape)

    def planes(n):
        return vmem((n, width, long))

    hbm_spec = pl.BlockSpec(memory_space=pltpu.HBM)
    given = (cell, front, prod, rhs, weights, tz, store)
    pres, send, ends = pl.pallas_call(
        pres_kernel,
        out_shape=(field, vmem((devices, 1, 3 * count)), planes(7)),
        in_specs=[hbm_spec] * len(given),
        out_specs=(VM,) * 3,
        scratch_shapes=[vmem(a.shape, a.dtype) for a in given] + [pltpu.SemaphoreType.DMA((len(given),))],
        compiler_params=pltpu.CompilerParams(vmem_limit_bytes=LIMIT),
    )(*[pltpu.with_memory_space_constraint(a, pltpu.HBM) for a in given])
    terms = everywhere(send)
    sib, found = ([], [])
    for level in range(levels - 1):
        sib.append(flip(ends, level))
        final = level == levels - 2
        many = (2 if level else 0) + (1 if final else 0)
        outs = (vmem((1, max(1, many) * count)), *((planes(3),) if final else (planes(6), planes(2 * depth))))
        if level == 0:
            rim = vmem((4 * depth, 1, long))
            kept, low, high, *got = call(
                functools.partial(first_join_kernel, final),
                (hbm((4 * depth, width, long)), rim, rim, *outs),
                (ends, sib[-1], pres, tz, store, tx, cell, prod),
                far=range(3, 8),
            )
        else:
            got = call(
                functools.partial(join_kernel, level, final), outs, (ends, sib[-1], answers, cell, prod), far=(3, 4)
            )
        if many:
            found.append(got[0])
        if final:
            face = got[1]
        else:
            ends, answers = got[1:]
    found = found[0] if len(found) == 1 else jnp.concatenate(found, 1)
    terms, face, found = lax.optimization_barrier((terms, face, found))
    sib.append(flip(face, levels - 1))
    chunks = 8
    send = pl.pallas_call(
        front_kernel,
        out_shape=vmem((devices, 1, max(rows + found.shape[1], 3 * count))),
        in_specs=[VM, VM, hbm_spec],
        out_specs=VM,
        scratch_shapes=[vmem(inverse.shape), pltpu.SemaphoreType.DMA((chunks,))],
        compiler_params=pltpu.CompilerParams(vmem_limit_bytes=LIMIT),
    )(terms, found, pltpu.with_memory_space_constraint(inverse, pltpu.HBM))
    sizes = [min(6, block.shape[0]) for block in sib]
    rim = vmem((4 * depth + sum(sizes) + 2, 1, long))
    send, low, high = lax.optimization_barrier((send, low, high))
    (two,) = call(functools.partial(edge_kernel, levels), (rim,), (low, high, prod, *sib))
    sol = everywhere(send)
    two = neighbour(two, "tile")

    def hots(high):
        return (
            vmem((high * long // 128, lists), BF16),
            vmem((128, lists), BF16),
            vmem((rows, lists), BF16),
            vmem((1, lists), I32),
            vmem((1, count), I32),
        )

    at = 3 + levels
    row3 = vmem((depth, 1, long))
    p, coupled_z, one, tz, tx, block_inv = call(
        functools.partial(pressure_kernel, levels),
        (field, field, row3),
        (sol, terms, pres, *sib, tz, kept, tx, prod, block_inv),
        far=range(at, at + 5),
        keep=(at, at + 2, at + 4),
        late=(range(at, at + 4), (at + 4,)),
        scratch=hots(width),
    )
    sol, one, terms = lax.optimization_barrier((sol, one, terms))
    one = flip(one, 0, "tile")
    two, rhs, block_diag, ty = call(
        functools.partial(first_three, functools.partial(beyond_kernel, levels, sizes, (depth, width, long))),
        (row3,),
        (sol, terms, two, rhs, block_diag, ty),
        far=(3, 4, 5),
        keep=(3, 4, 5),
        late=((3, 4, 5),),
        scratch=(vmem((4 * depth + sum(sizes), 8, long)), *hots(8)),
    )
    row9 = vmem((3, depth, 1, long))
    plane3 = planes(3)
    s, outer, row_two, row_one, inner = call(
        search_kernel,
        (vmem(rhs.shape), plane3, row9, row9, plane3),
        (p, coupled_z, two, one, tx, ty, tz, rhs, block_diag, block_inv),
    )
    outer, row_two = (neighbour(outer), neighbour(row_two, "tile"))
    row_one, inner = (flip(row_one, 0, "tile"), flip(inner, 0))
    (part,) = call(inner_kernel, (vmem(rhs.shape),), (s, block_diag, tz, tx, ty))
    image, send = call(
        image_kernel,
        (vmem(rhs.shape), vmem((devices, 1, 128))),
        (part, outer, row_two, row_one, inner, rhs, tz, tx),
    )
    sums = everywhere(send)
    update, lin_res, ratio = call(
        finish_kernel, (hbm(rhs.shape), hbm(rhs.shape), hbm((1, 1))), (sums, s, image, rhs)
    )
    return (update, lin_res, ratio.reshape(()))


def solution(mesh):
    return jax.shard_map(
        shards,
        mesh=mesh,
        in_specs=(
            P(None, "layer", "tile", None),
            P(None, "layer", "tile", None),
            P(None, None, "layer", "tile", None),
            P(None, None, "layer", "tile", None),
            P("layer", "tile", None),
            P("layer", "tile", None),
            P("layer", "tile", None),
            P("layer", "tile", None),
            P(("tile", "layer")),
            P(("tile", "layer")),
            P(("tile", "layer")),
            P(("tile", "layer"), None),
        ),
        out_specs=(P(None, "layer", "tile", None), P(None, "layer", "tile", None), P()),
        check_vma=False,
    )
```

```python
import functools
import jax
import jax.numpy as jnp
from jax import lax
from jax.experimental import pallas as pl
from jax.experimental.pallas import tpu as pltpu
from jax.sharding import PartitionSpec as P

F32 = jnp.float32
BF16 = jnp.bfloat16
I32 = jnp.int32
BOTH = ("tile", "layer")
VM = pl.BlockSpec(memory_space=pltpu.VMEM)
LIMIT = 16 << 20
PARTS = 2


def hbm(shape):
    return jax.ShapeDtypeStruct(shape, F32)


def vmem(shape, dtype=F32):
    return pltpu.VMEM(shape, dtype)


def staged(kernel, where, outs, kept, column, late, *refs):
    count, sems = (len(where), refs[-1])
    held = list(refs[count + outs + len(kept) : -1])
    target_count = sum(where) - len(kept)
    held, extra = (held[:target_count], held[target_count:])
    target = dict(zip(kept, refs[count + outs : count + outs + len(kept)]))
    operands, copies = ([], [])
    for i, far in enumerate(where):
        if far:
            to = target[i] if i in target else held.pop(0)
            part = refs[i].at[:, 0] if i in column else refs[i]
            copies.append(pltpu.make_async_copy(part, to, sems.at[len(copies)]))
            operands.append(to)
        else:
            operands.append(refs[i])
    places = [i for i, far in enumerate(where) if far]
    for copy in copies:
        copy.start()
    for i, copy in zip(places, copies):
        if not any(i in group for group in late):
            copy.wait()

    def ready(k):
        for i, copy in zip(places, copies):
            if i in late[k]:
                copy.wait()

    more = (ready,) if late else ()
    kernel(*more, *operands, *refs[count : count + outs], *extra)


def call(kernel, outs, args, far=(), keep=(), column=(), late=(), scratch=(), limit=LIMIT):
    where = [i in far for i in range(len(args))]
    spaces = [pltpu.HBM if w else pltpu.VMEM for w in where]
    shapes = [a.shape[:1] + a.shape[2:] if i in column else a.shape for i, a in enumerate(args)]
    every = (*outs, *(vmem(shapes[i], args[i].dtype) for i in keep))
    return pl.pallas_call(
        functools.partial(staged, kernel, where, len(outs), tuple(keep), tuple(column), tuple(late)),
        out_shape=every,
        in_specs=[pl.BlockSpec(memory_space=s) for s in spaces],
        out_specs=(VM,) * len(every),
        scratch_shapes=[vmem(shapes[i], a.dtype) for i, a in enumerate(args) if where[i] and i not in keep]
        + [*scratch, pltpu.SemaphoreType.DMA((max(1, sum(where)),))],
        compiler_params=pltpu.CompilerParams(vmem_limit_bytes=limit),
    )(*[pltpu.with_memory_space_constraint(a, s) for a, s in zip(args, spaces)])


def iota(shape, dim):
    return lax.broadcasted_iota(I32, shape, dim)


def split(x):
    one = x.astype(BF16)
    rest = x - one.astype(F32)
    two = rest.astype(BF16)
    three = (rest - two.astype(F32)).astype(BF16)
    return [one, two, three]


def fold(x, parts=3):
    n = x.shape[0] // parts
    total = x[(parts - 1) * n :]
    for i in range(parts - 2, -1, -1):
        total = x[i * n : (i + 1) * n] + total
    return total


def onehot(index, size):
    return jnp.where(iota((size, index.shape[1]), 0) == index, 1.0, 0.0)


def dot(a, b):
    return lax.dot_general(a, b, (((1,), (0,)), ((), ())), preferred_element_type=F32)


def dot_nt(a, b):
    return lax.dot_general(a, b, (((1,), (1,)), ((), ())), preferred_element_type=F32)


def pick(tables, hi, hot):
    rows = tables[0].shape[0]
    parts = jnp.concatenate([p for table in tables for p in split(table)[:PARTS]], 0)
    got = dot(parts, hot)
    mask = onehot(hi, rows)
    n = PARTS * rows
    return [jnp.sum(fold(got[i * n : (i + 1) * n], PARTS) * mask, axis=0, keepdims=True) for i in range(len(tables))]


def pres_kernel(cell_in, front_in, prod_in, rhs_in, wts_in, tz_in, store_in, pres, send, ends, *scratch):
    (cell, front, prod, rhs, wts, tz, store), sems = scratch[:-1], scratch[-1]
    pairs = ((cell_in, cell), (front_in, front), (prod_in, prod), (tz_in, tz), (store_in, store), (rhs_in, rhs), (wts_in, wts))
    copies = [pltpu.make_async_copy(a, b, sems.at[i]) for i, (a, b) in enumerate(pairs)]
    for copy in copies:
        copy.start()
    for copy in copies[:3]:
        copy.wait()
    depth, width, long = pres.shape
    where = cell[...]
    hot = onehot(lax.rem(where, long), long).astype(BF16)
    for copy in copies[3:5]:
        copy.wait()
    tzs = [tz[z] for z in range(depth)]
    gs, invs, first, final, coefs = factors(tzs, [store[z] for z in range(depth)])
    for copy in copies[5:]:
        copy.wait()
    for z in range(depth):
        pres[z] = wts[0, z] * rhs[0, z] + wts[1, z] * rhs[1, z] + wts[2, z] * rhs[2, z]
    tables = [pres[...].reshape(depth * width, long), jnp.concatenate(first, 0), jnp.concatenate(final, 0)]
    found, kf, kl = pick(tables, lax.div(where, long), hot)
    both = jnp.concatenate([prod[...] * found, front[...].astype(F32), where.astype(F32)], 1)
    send[...] = jnp.broadcast_to(both[:, None], send.shape)
    y = local_solve([pres[z] for z in range(depth)], gs, invs, tzs)
    for i, value in enumerate((*coefs, y[0], y[-1], tzs[-1])):
        ends[i] = value
    ends[6] = jnp.zeros((width, long), F32)
    ends[6, 0:1, : 2 * where.shape[1]] = jnp.concatenate([prod[...] * kf, prod[...] * kl], 1)


def is_right(level, axis="layer"):
    return (lax.axis_index(axis) >> level) % 2 == 1


def choose(level, mine, other, axis="layer"):
    right = is_right(level, axis)
    return (jnp.where(right, other, mine), jnp.where(right, mine, other))


def local_solve(rhs, upper, inv, tz):
    depth = len(rhs)
    y = [rhs[0] * inv[0]]
    for z in range(1, depth):
        y.append((rhs[z] + tz[z - 1] * y[-1]) * inv[z])
    for z in range(depth - 2, -1, -1):
        y[z] = y[z] + upper[z] * y[z + 1]
    return y


def factors(tz, store):
    depth = len(tz)
    gs, invs = ([], [])
    own = None
    for z in range(depth):
        own = store[z] if z == 0 else store[z] + gs[-1] * own
        invs.append(1.0 / (own + tz[z] if z < depth - 1 else own))
        gs.append(tz[z] * invs[-1])
    first = [invs[0]]
    for z in range(1, depth):
        first.append(tz[z - 1] * first[-1] * invs[z])
    final = [None] * depth
    final[-1] = invs[-1]
    for z in range(depth - 2, -1, -1):
        first[z] = first[z] + gs[z] * first[z + 1]
        final[z] = gs[z] * final[z + 1]
    return gs, invs, first, final, block_ends(first, final, tz)


def block_ends(first, final, tz):
    return (first[0], first[-1], final[-1] + 1.0 / jnp.maximum(tz[-1], 1e-30))


def pair(level, own, sib):
    af, af_ = choose(level, own[0], sib[0])
    c, c_ = choose(level, own[1], sib[1])
    b, b_ = choose(level, own[2], sib[2])
    return af, c, b, af_, c_, b_, 1.0 / (b + af_)


def join_coefs(level, own, sib):
    af, c, _, _, c_, b_, g = pair(level, own, sib)
    return (af - c * c * g, c * c_ * g, b_ - c_ * c_ * g)


def join_ends(level, own, sib, mine, other):
    _, c, _, _, c_, _, g = pair(level, own, sib)
    yf, yf_ = choose(level, mine[0], other[0])
    yl, yl_ = choose(level, mine[1], other[1])
    flux = g * (yl - yf_)
    return (yf - c * flux, yl_ + c_ * flux)


def first_join_kernel(final, own, sib, pres, tz, store, tx, cell, prod, kept, low, high, *outs):
    depth, width, _ = tz.shape
    for k, ref in enumerate((tz, store, pres, tx)):
        for z in range(depth):
            low[k * depth + z] = ref[z, 0:1]
            high[k * depth + z] = ref[z, width - 1 : width]
    gs, invs, first, last, _ = factors([tz[z] for z in range(depth)], [store[z] for z in range(depth)])
    for i, value in enumerate(gs + invs + first + last):
        kept[i] = value
    join(0, final, own, sib, first + last, cell, prod, *outs)


def join_kernel(level, final, own, sib, answers, cell, prod, *outs):
    join(level, final, own, sib, [answers[i] for i in range(answers.shape[0])], cell, prod, *outs)


def join(level, final, own, sib, answers, cell, prod, found, *outs):
    depth = len(answers) // 2
    width, long = answers[0].shape
    _, c, _, _, c_, _, g = pair(level, own, sib)
    first, both, last = join_coefs(level, own, sib)
    yf, yl = join_ends(level, own, sib, (own[3], own[4]), (sib[3], sib[4]))
    lower = choose(level, own[5], sib[5])[1]
    right, later = (is_right(level), is_right(level + 1))
    cg, cg_ = (c * g, c_ * g)
    tops, bottoms = ([], [])
    for z in range(depth):
        kf, kl = (answers[z], answers[depth + z])
        tops.append(jnp.where(right, cg * kf, kf - cg * kl))
        bottoms.append(jnp.where(right, kl - cg_ * kf, cg_ * kl))
    tables = [answers[:depth], answers[depth:]] if level else []
    if final:
        (face,) = outs
        face[0], face[1] = (jnp.where(later, first, last), jnp.where(later, yf, yl))
        face[2] = lower
        tables.append([jnp.where(later, tops[z], bottoms[z]) for z in range(depth)])
    else:
        out, more = outs
        for i, value in enumerate((first, both, last, yf, yl, lower)):
            out[i] = value
        for i, value in enumerate(tops + bottoms):
            more[i] = value
    if tables:
        where = cell[...]
        hot = onehot(lax.rem(where, long), long).astype(BF16)
        got = pick([jnp.concatenate(t, 0) for t in tables], lax.div(where, long), hot)
        found[...] = jnp.concatenate([prod[...] * value for value in got], 1)
    else:
        found[...] = jnp.zeros(found.shape, F32)


def groups_of(levels):
    layers = lax.axis_size("layer")
    l = lax.axis_index("layer")
    base = lax.axis_index("tile") * layers
    out = [[base + l]]
    for level in range(levels):
        out.append([base + (((l >> level) ^ 1) << level) + i for i in range(1 << level)])
    return out


def front_kernel(recv, found, inverse, send, held, sems):
    devices = recv.shape[0]
    count = recv.shape[2] // 3
    rows, length = inverse.shape
    lanes = 128
    chunks = sems.shape[0]
    wide = length // chunks
    found = found[...]
    copies = [
        pltpu.make_async_copy(inverse.at[:, pl.ds(i * wide, wide)], held.at[:, pl.ds(i * wide, wide)], sems.at[i])
        for i in range(chunks)
    ]
    for copy in copies:
        copy.start()
    terms, index = (recv[:, 0, :count], recv[:, 0, count : 2 * count])
    high = jnp.floor(index * (1.0 / lanes))
    low = index - high * lanes
    parts = [p.astype(F32) for p in split(terms)[:PARTS]]
    row_of = iota((length // lanes, count), 0).astype(F32)
    lane_of = iota((lanes, count), 0).astype(F32)
    total = jnp.zeros((length // lanes, lanes), F32)
    for d in range(devices):
        hit = row_of == high[d : d + 1]
        left = jnp.concatenate([jnp.where(hit, p[d : d + 1], 0.0).astype(BF16) for p in parts], 0)
        right = jnp.where(lane_of == low[d : d + 1], 1.0, 0.0).astype(BF16)
        total = total + fold(dot_nt(left, right), PARTS)
    acc = jnp.zeros((rows, lanes), F32)
    for i in range(chunks):
        copies[i].wait()
        for r in range(i * wide // lanes, (i + 1) * wide // lanes):
            acc = acc + held[:, r * lanes : (r + 1) * lanes] * total[r : r + 1]
    parts = jnp.concatenate(split(acc), 1)
    out = dot_nt(jnp.ones((8, parts.shape[1]), BF16), parts)
    pad = send.shape[2] - out.shape[1] - found.shape[1]
    pieces = [out[0:1], found] + ([jnp.zeros((1, pad), F32)] if pad else [])
    send[...] = jnp.broadcast_to(jnp.concatenate(pieces, 1)[:, None], send.shape)


def gathered(values, rows_hot, lanes_hot, start, size, ext, parts):
    hot = lanes_hot[:, start : start + size]
    pieces = [hot * p for v in values for p in split(v)[:parts]]
    got = dot_nt(rows_hot[:, start : start + size], jnp.concatenate(pieces, 0))
    planes = []
    lanes = hot.shape[0]
    for i in range(len(values)):
        plane = got[:, i * parts * lanes : (i * parts + 1) * lanes]
        for k in range(1, parts):
            j = i * parts + k
            plane = plane + got[:, j * lanes : (j + 1) * lanes]
        planes.append(jnp.concatenate([plane[r : r + ext] for r in range(0, plane.shape[0], ext)], 1))
    return planes


def beside(centre, tx, ty):
    width, long = centre.shape
    row, col = (iota(centre.shape, 0), iota(centre.shape, 1))
    total = tx * jnp.where(row == width - 1, 0.0, pltpu.roll(centre, width - 1, 0))
    total = total + jnp.where(row == 0, 0.0, pltpu.roll(tx * centre, 1, 0))
    total = total + ty * jnp.where(col == long - 1, 0.0, pltpu.roll(centre, long - 1, 1))
    return total + jnp.where(col == 0, 0.0, pltpu.roll(ty * centre, 1, 1))


def tile_rows(first, last, one, two):
    odd = is_right(0, "tile")
    one[...] = jnp.where(odd, first, last)
    two[...] = jnp.where(odd, last, first)


def table_kernel(lists, shape, terms, hots, only=None):
    _, width, long = shape
    rows_hot, lanes_hot, sol_hot, sol_row, layer = hots
    lanes = 128
    rows = sol_hot.shape[0]
    count = terms.shape[2] // 3
    at = 0
    for members in lists:
        for device in members:
            entry = terms[device]
            index = entry[:, count : 2 * count].astype(I32)
            cell = entry[:, 2 * count :].astype(I32)
            y, x = lax.rem(cell, long), lax.rem(lax.div(cell, long), width)
            if only is None:
                row = lax.div(y, lanes) * width + x
            else:
                row = jnp.where(x == only, lax.div(y, lanes), -1)
            here = pl.ds(at, count)
            rows_hot[:, here] = onehot(row, rows_hot.shape[0]).astype(BF16)
            lanes_hot[:, here] = onehot(lax.rem(y, lanes), lanes).astype(BF16)
            sol_hot[:, here] = onehot(lax.rem(index, rows), rows).astype(BF16)
            sol_row[:, here] = lax.div(index, rows)
            if at < layer.shape[1]:
                layer[:, here] = lax.div(cell, long * width)
            at += count


def column_solve(levels, recv, lists, hots, listing, planes_of, sib):
    rows_hot, lanes_hot, sol_hot, sol_row, layer = hots
    rows, count = (sol_hot.shape[0], layer.shape[1])
    table = jnp.concatenate(split(recv[...].reshape(recv.shape[0], recv.shape[2])[:, :rows]), 0)
    sol = fold(dot(table, sol_hot[...]))
    sol = jnp.sum(jnp.where(iota(sol.shape, 0) == sol_row[...], sol, 0.0), axis=0, keepdims=True)
    layer = layer[...]

    def listed(group, column):
        at = rows + column * count
        return jnp.concatenate([recv[device][:, at : at + count] for device in group], 1)

    mine_list, sib_list = listing
    tz, pres, (gs, invs, first, final, coefs) = planes_of()
    depth = len(tz)
    high = tz[0].shape[0]
    own = [coefs]
    start = layer.shape[1]
    value = mine_list * sol[:, :start]
    values = [jnp.where(layer == z, value, 0.0) for z in range(depth)]
    change = gathered(values, rows_hot, lanes_hot, 0, start, high, PARTS)
    y = local_solve([pres[z] - change[z] for z in range(depth)], gs, invs, tz)
    mine = (y[0], y[-1])
    steps = []
    for level in range(levels):
        size = len(lists[level + 1]) * count
        top = level == levels - 1
        if level:
            columns = [2 * level - 2] if top else [2 * level - 2, 2 * level - 1]
            values = [listed(lists[level + 1], c) for c in columns]
        else:
            values = [sib_list[:, i * count : (i + 1) * count] for i in range(2)]
        values = [value * sol[:, start : start + size] for value in values]
        change = gathered(values, rows_hot, lanes_hot, start, size, high, PARTS)
        start += size
        if top:
            other = sib[level][1] - change[0]
            steps.append((mine, (other, other)))
        else:
            other = (sib[level][3] - change[0], sib[level][4] - change[1])
            steps.append((mine, other))
            mine = join_ends(level, own[level], sib[level], mine, other)
            own.append(join_coefs(level, own[level], sib[level]))
    above = below = tzp = jnp.zeros(tz[0].shape, F32)
    place = lax.axis_index("layer")
    for level in range(levels - 1, -1, -1):
        mine, other = steps[level]
        yl, _ = choose(level, mine[1], other[1])
        _, yf_ = choose(level, mine[0], other[0])
        flux = yl - yf_
        if level == levels - 1:
            b, _ = choose(level, own[level][2], sib[level][0])
            _, af_ = choose(level, own[level][0], sib[level][0])
            g = 1.0 / (b + af_)
            before = sib[level][2]
        else:
            _, c, _, _, c_, _, g = pair(level, own[level], sib[level])
            flux = flux + c * above - c_ * below
            before = sib[level][5]
        tzp = jnp.where(place % (2 << level) == 1 << level, before, tzp)
        flux = g * flux
        right = is_right(level)
        above, below = (jnp.where(right, flux, above), jnp.where(right, below, -flux))
    return [y[z] + first[z] * above + final[z] * below for z in range(depth)], above, below, tzp


def pressure_kernel(levels, ready, recv, terms, pres, *refs):
    sib, (tz, kept, tx, prod, _, p, coupled_z, one, *hots) = (refs[:levels], refs[levels:])
    depth, width, _ = pres.shape
    odd = is_right(0, "tile")
    lists = groups_of(levels)
    table_kernel(lists, pres.shape, terms, hots)

    def planes_of():
        tzs, pressures = ([ref[z] for z in range(depth)] for ref in (tz, pres))
        gs, invs, first, final = ([kept[k * depth + z] for z in range(depth)] for k in range(4))
        return tzs, pressures, (gs, invs, first, final, block_ends(first, final, tzs))

    ready(0)
    listing = (prod[...], sib[0][6, 0:1])
    values, above, below, tzp = column_solve(levels, recv, lists, hots, listing, planes_of, sib)
    tzs = [tz[z] for z in range(depth)]
    is_last = lax.axis_index("layer") == (1 << levels) - 1
    for z in range(depth):
        p[z] = values[z]
        one[z] = jnp.where(odd, values[z][0:1], (tx[z] * values[z])[width - 1 :])
        total = above + tzp * values[z] if z == 0 else tzs[z - 1] * values[z - 1]
        if z == depth - 1:
            coupled_z[z] = total + jnp.where(is_last, 0.0, below + tzs[z] * values[z])
        else:
            coupled_z[z] = total + tzs[z] * values[z + 1]
    ready(1)


def edge_kernel(levels, low, high, prod, *refs):
    sib, two = (refs[:levels], refs[levels])
    odd = is_right(0, "tile")
    n = low.shape[0]
    two[pl.ds(0, n)] = jnp.where(odd, high[...], low[...])
    at = n
    for block in sib:
        width = block.shape[1]
        for i in range(min(6, block.shape[0])):
            two[at] = jnp.where(odd, block[i, width - 1 : width], block[i, 0:1])
            at += 1
    two[at] = sib[0][6, 0:1]
    two[at + 1] = jnp.zeros((1, two.shape[2]), F32)
    two[at + 1, :, : prod.shape[1]] = prod[...]


def first_three(kernel, ready, one, two, three, _rhs, _diag, _ty, *rest):
    kernel(one, two, three, *rest)
    ready(0)


def beyond_kernel(levels, shapes, shape, recv, terms, two, row, *hots):
    depth, width, long = shape
    tiles, layers = (lax.axis_size("tile"), lax.axis_size("layer"))
    tile = lax.axis_index("tile")
    odd = is_right(0, "tile")
    count = 4 * depth + sum(shapes)
    planes = [two[i] for i in range(count)]
    step = jnp.where(odd, layers, -layers)
    lists = [[jnp.clip(device + step, 0, tiles * layers - 1) for device in members] for members in groups_of(levels)]
    table_kernel(lists, shape, terms, hots, jnp.where(odd, 0, width - 1))
    exists = jnp.where(odd, (tile < tiles - 1).astype(F32), (tile > 0).astype(F32)) + jnp.zeros((1, long), F32)
    blocks = []
    at = 4 * depth
    for size in shapes:
        blocks.append([planes[at + i] for i in range(size)])
        at += size

    def planes_of():
        kept = [planes[depth + z] for z in range(depth)]
        tzs = [planes[z] for z in range(depth)]
        found = factors(tzs, [jnp.where(value == 0.0, 1.0, value) for value in kept])
        return tzs, [planes[2 * depth + z] for z in range(depth)], found

    listing = (two[count + 1, :, : terms.shape[2] // 3], two[count])
    values, _, _, _ = column_solve(levels, recv, lists, hots, listing, planes_of, blocks)
    for z in range(depth):
        found = jnp.where(exists > 0.0, values[z], 0.0)
        row[z] = jnp.where(odd, found, found * two[3 * depth + z])


def search_kernel(p, coupled_z, two, one, tx, ty, tz, rhs, column, binv, s, outer, row_two, row_one, inner):
    depth, width, _ = p.shape
    odd = is_right(0, "tile")
    right = is_right(0)
    row = iota(p.shape[1:], 0)
    for z in range(depth):
        centre = p[z]
        after = jnp.where(odd, two[z], one[z])
        before = jnp.where(odd, one[z], two[z])
        coupled = coupled_z[z] + beside(centre, tx[z], ty[z])
        coupled = coupled + jnp.where(row == 0, before, 0.0) + jnp.where(row == width - 1, tx[z] * after, 0.0)
        remain = [rhs[c, z] - column[c, z] * centre for c in range(3)]
        remain[0] = remain[0] + coupled
        for c in range(3):
            value = binv[c, 0, z] * remain[0] + binv[c, 1, z] * remain[1] + binv[c, 2, z] * remain[2]
            if c == 0:
                value = centre + value
            s[c, z] = value
            tile_rows(value[0:1], (tx[z] * value)[width - 1 :], row_one.at[c, z], row_two.at[c, z])
    for c in range(3):
        top, bottom = (s[c, 0], tz[depth - 1] * s[c, depth - 1])
        inner[c] = jnp.where(right, top, bottom)
        outer[c] = jnp.where(right, bottom, top)


def inner_kernel(ready, s, diag, tz, tx, ty, image):
    depth = s.shape[1]
    for z in range(depth):
        for c in range(3):
            total = beside(s[c, z], tx[z], ty[z])
            if z:
                total = total + tz[z - 1] * s[c, z - 1]
            if z < depth - 1:
                total = total + tz[z] * s[c, z + 1]
            image[c, z] = total
    ready(0)
    for z in range(depth):
        for c in range(3):
            total = diag[c, 0, z] * s[0, z] + diag[c, 1, z] * s[1, z] + diag[c, 2, z] * s[2, z]
            image[c, z] = total - image[c, z]


def image_kernel(part, outer, row_two, row_one, inner, rhs, tz, tx, image, send):
    depth, width = part.shape[1:3]
    right, odd = (is_right(0), is_right(0, "tile"))
    row = iota(part.shape[2:], 0)
    along = power = start = 0.0
    for z in range(depth):
        for c in range(3):
            value = part[c, z]
            if z == 0:
                value = value - jnp.where(right, inner[c], outer[c])
            if z == depth - 1:
                value = value - tz[z] * jnp.where(right, outer[c], inner[c])
            after = jnp.where(odd, row_two[c, z], row_one[c, z])
            before = jnp.where(odd, row_one[c, z], row_two[c, z])
            value = value - jnp.where(row == 0, before, 0.0) - jnp.where(row == width - 1, tx[z] * after, 0.0)
            image[c, z] = value
            given = rhs[c, z]
            along = along + value * given
            power = power + value * value
            start = start + given * given
    along, power, start = (jnp.sum(along), jnp.sum(power), jnp.sum(start))
    omega = along / jnp.where(power > 0.0, power, 1.0)
    square = cross = 0.0
    for z in range(depth):
        for c in range(3):
            value = image[c, z]
            left = rhs[c, z] - omega * value
            square = square + left * left
            cross = cross + left * value
    lane = iota((1, send.shape[2]), 1)
    out = jnp.zeros((1, send.shape[2]), F32)
    for i, value in enumerate((along, power, start, jnp.sum(square), jnp.sum(cross), omega)):
        out = jnp.where(lane == i, value, out)
    send[...] = jnp.broadcast_to(out[:, None], send.shape)


def finish_kernel(recv, s, image, rhs, update, lin_res, ratio):
    sums = recv[...].reshape(recv.shape[0], recv.shape[2])
    whole = jnp.sum(sums, axis=0, keepdims=True)
    omega = whole[:, 0:1] / whole[:, 1:2]
    shift = sums[:, 5:6] - omega
    square = sums[:, 3:4] + 2.0 * shift * sums[:, 4:5] + shift * shift * sums[:, 1:2]
    ratio[...] = jnp.sqrt(jnp.sum(square, axis=0, keepdims=True) / whole[:, 2:3])
    for c in range(3):
        for z in range(s.shape[1]):
            update[c, z] = omega * s[c, z]
            lin_res[c, z] = rhs[c, z] - omega * image[c, z]


def flip(x, level, axis="layer"):
    return lax.ppermute(x, axis, [(i, i ^ (1 << level)) for i in range(lax.axis_size(axis))])


def neighbour(x, axis="layer"):
    pairs = [(i, i + 1) for i in range(1, lax.axis_size(axis) - 1, 2)]
    return lax.ppermute(x, axis, pairs + [(j, i) for i, j in pairs])


def everywhere(x):
    return lax.all_to_all(x, BOTH, split_axis=0, concat_axis=0, tiled=True)


def shards(rhs, weights, block_diag, block_inv, tx, ty, tz, store, cell, front, prod, inverse):
    layers = lax.axis_size("layer")
    devices = lax.axis_size("tile") * layers
    levels = layers.bit_length() - 1
    depth, width, long = tx.shape
    count = cell.shape[0]
    rows = inverse.shape[0]
    lists = layers * count
    cell, front, prod = (cell.reshape(1, -1), front.reshape(1, -1), prod.reshape(1, -1))
    field = vmem(tx.shape)

    def planes(n):
        return vmem((n, width, long))

    hbm_spec = pl.BlockSpec(memory_space=pltpu.HBM)
    given = (cell, front, prod, rhs, weights, tz, store)
    pres, send, ends = pl.pallas_call(
        pres_kernel,
        out_shape=(field, vmem((devices, 1, 3 * count)), planes(7)),
        in_specs=[hbm_spec] * len(given),
        out_specs=(VM,) * 3,
        scratch_shapes=[vmem(a.shape, a.dtype) for a in given] + [pltpu.SemaphoreType.DMA((len(given),))],
        compiler_params=pltpu.CompilerParams(vmem_limit_bytes=LIMIT),
    )(*[pltpu.with_memory_space_constraint(a, pltpu.HBM) for a in given])
    terms = everywhere(send)
    sib, found = ([], [])
    for level in range(levels - 1):
        sib.append(flip(ends, level))
        final = level == levels - 2
        many = (2 if level else 0) + (1 if final else 0)
        outs = (vmem((1, max(1, many) * count)), *((planes(3),) if final else (planes(6), planes(2 * depth))))
        if level == 0:
            rim = vmem((4 * depth, 1, long))
            kept, low, high, *got = call(
                functools.partial(first_join_kernel, final),
                (hbm((4 * depth, width, long)), rim, rim, *outs),
                (ends, sib[-1], pres, tz, store, tx, cell, prod),
                far=range(3, 8),
            )
        else:
            got = call(
                functools.partial(join_kernel, level, final), outs, (ends, sib[-1], answers, cell, prod), far=(3, 4)
            )
        if many:
            found.append(got[0])
        if final:
            face = got[1]
        else:
            ends, answers = got[1:]
    found = found[0] if len(found) == 1 else jnp.concatenate(found, 1)
    terms, face, found = lax.optimization_barrier((terms, face, found))
    sib.append(flip(face, levels - 1))
    chunks = 8
    send = pl.pallas_call(
        front_kernel,
        out_shape=vmem((devices, 1, max(rows + found.shape[1], 3 * count))),
        in_specs=[VM, VM, hbm_spec],
        out_specs=VM,
        scratch_shapes=[vmem(inverse.shape), pltpu.SemaphoreType.DMA((chunks,))],
        compiler_params=pltpu.CompilerParams(vmem_limit_bytes=LIMIT),
    )(terms, found, pltpu.with_memory_space_constraint(inverse, pltpu.HBM))
    sizes = [min(6, block.shape[0]) for block in sib]
    rim = vmem((4 * depth + sum(sizes) + 2, 1, long))
    send, low, high = lax.optimization_barrier((send, low, high))
    (two,) = call(functools.partial(edge_kernel, levels), (rim,), (low, high, prod, *sib))
    sol = everywhere(send)
    two = neighbour(two, "tile")

    def hots(high):
        return (
            vmem((high * long // 128, lists), BF16),
            vmem((128, lists), BF16),
            vmem((rows, lists), BF16),
            vmem((1, lists), I32),
            vmem((1, count), I32),
        )

    at = 3 + levels
    row3 = vmem((depth, 1, long))
    p, coupled_z, one, tz, tx, block_inv = call(
        functools.partial(pressure_kernel, levels),
        (field, field, row3),
        (sol, terms, pres, *sib, tz, kept, tx, prod, block_inv),
        far=range(at, at + 5),
        keep=(at, at + 2, at + 4),
        late=(range(at, at + 4), (at + 4,)),
        scratch=hots(width),
    )
    sol, one, terms = lax.optimization_barrier((sol, one, terms))
    one = flip(one, 0, "tile")
    two, rhs, first_column, ty = call(
        functools.partial(first_three, functools.partial(beyond_kernel, levels, sizes, (depth, width, long))),
        (row3,),
        (sol, terms, two, rhs, block_diag, ty),
        far=(3, 4, 5),
        keep=(3, 4, 5),
        column=(4,),
        late=((3, 4, 5),),
        scratch=hots(1),
    )
    row9 = vmem((3, depth, 1, long))
    plane3 = planes(3)
    s, outer, row_two, row_one, inner = call(
        search_kernel,
        (vmem(rhs.shape), plane3, row9, row9, plane3),
        (p, coupled_z, two, one, tx, ty, tz, rhs, first_column, block_inv),
    )
    outer, row_two = (neighbour(outer), neighbour(row_two, "tile"))
    row_one, inner = (flip(row_one, 0, "tile"), flip(inner, 0))
    (part,) = call(inner_kernel, (vmem(rhs.shape),), (s, block_diag, tz, tx, ty), far=(1,), late=((1,),))
    image, send = call(
        image_kernel,
        (vmem(rhs.shape), vmem((devices, 1, 128))),
        (part, outer, row_two, row_one, inner, rhs, tz, tx),
    )
    sums = everywhere(send)
    update, lin_res, ratio = call(
        finish_kernel, (hbm(rhs.shape), hbm(rhs.shape), hbm((1, 1))), (sums, s, image, rhs)
    )
    return (update, lin_res, ratio.reshape(()))


def solution(mesh):
    return jax.shard_map(
        shards,
        mesh=mesh,
        in_specs=(
            P(None, "layer", "tile", None),
            P(None, "layer", "tile", None),
            P(None, None, "layer", "tile", None),
            P(None, None, "layer", "tile", None),
            P("layer", "tile", None),
            P("layer", "tile", None),
            P("layer", "tile", None),
            P("layer", "tile", None),
            P(("tile", "layer")),
            P(("tile", "layer")),
            P(("tile", "layer")),
            P(("tile", "layer"), None),
        ),
        out_specs=(P(None, "layer", "tile", None), P(None, "layer", "tile", None), P()),
        check_vma=False,
    )
```

```python
import functools
import jax
import jax.numpy as jnp
from jax import lax
from jax.experimental import pallas as pl
from jax.experimental.pallas import tpu as pltpu
from jax.sharding import PartitionSpec as P

F32 = jnp.float32
BF16 = jnp.bfloat16
I32 = jnp.int32
BOTH = ("tile", "layer")
VM = pl.BlockSpec(memory_space=pltpu.VMEM)
LIMIT = 16 << 20
PARTS = 2


def hbm(shape):
    return jax.ShapeDtypeStruct(shape, F32)


def vmem(shape, dtype=F32):
    return pltpu.VMEM(shape, dtype)


def staged(kernel, where, outs, kept, column, late, *refs):
    count, sems = (len(where), refs[-1])
    held = list(refs[count + outs + len(kept) : -1])
    target_count = sum(where) - len(kept)
    held, extra = (held[:target_count], held[target_count:])
    target = dict(zip(kept, refs[count + outs : count + outs + len(kept)]))
    operands, copies = ([], [])
    for i, far in enumerate(where):
        if far:
            to = target[i] if i in target else held.pop(0)
            part = refs[i].at[:, 0] if i in column else refs[i]
            copies.append(pltpu.make_async_copy(part, to, sems.at[len(copies)]))
            operands.append(to)
        else:
            operands.append(refs[i])
    places = [i for i, far in enumerate(where) if far]
    for copy in copies:
        copy.start()
    for i, copy in zip(places, copies):
        if not any(i in group for group in late):
            copy.wait()

    def ready(k):
        for i, copy in zip(places, copies):
            if i in late[k]:
                copy.wait()

    more = (ready,) if late else ()
    kernel(*more, *operands, *refs[count : count + outs], *extra)


def call(kernel, outs, args, far=(), keep=(), column=(), late=(), scratch=(), limit=LIMIT):
    where = [i in far for i in range(len(args))]
    spaces = [pltpu.HBM if w else pltpu.VMEM for w in where]
    shapes = [a.shape[:1] + a.shape[2:] if i in column else a.shape for i, a in enumerate(args)]
    every = (*outs, *(vmem(shapes[i], args[i].dtype) for i in keep))
    return pl.pallas_call(
        functools.partial(staged, kernel, where, len(outs), tuple(keep), tuple(column), tuple(late)),
        out_shape=every,
        in_specs=[pl.BlockSpec(memory_space=s) for s in spaces],
        out_specs=(VM,) * len(every),
        scratch_shapes=[vmem(shapes[i], a.dtype) for i, a in enumerate(args) if where[i] and i not in keep]
        + [*scratch, pltpu.SemaphoreType.DMA((max(1, sum(where)),))],
        compiler_params=pltpu.CompilerParams(vmem_limit_bytes=limit),
    )(*[pltpu.with_memory_space_constraint(a, s) for a, s in zip(args, spaces)])


def iota(shape, dim):
    return lax.broadcasted_iota(I32, shape, dim)


def split(x):
    one = x.astype(BF16)
    rest = x - one.astype(F32)
    two = rest.astype(BF16)
    three = (rest - two.astype(F32)).astype(BF16)
    return [one, two, three]


def fold(x, parts=3):
    n = x.shape[0] // parts
    total = x[(parts - 1) * n :]
    for i in range(parts - 2, -1, -1):
        total = x[i * n : (i + 1) * n] + total
    return total


def onehot(index, size):
    return jnp.where(iota((size, index.shape[1]), 0) == index, 1.0, 0.0)


def dot(a, b):
    return lax.dot_general(a, b, (((1,), (0,)), ((), ())), preferred_element_type=F32)


def dot_nt(a, b):
    return lax.dot_general(a, b, (((1,), (1,)), ((), ())), preferred_element_type=F32)


def pick(tables, hi, hot):
    rows = tables[0].shape[0]
    parts = jnp.concatenate([p for table in tables for p in split(table)[:PARTS]], 0)
    got = dot(parts, hot)
    mask = onehot(hi, rows)
    n = PARTS * rows
    return [jnp.sum(fold(got[i * n : (i + 1) * n], PARTS) * mask, axis=0, keepdims=True) for i in range(len(tables))]


def pres_kernel(cell_in, front_in, prod_in, rhs_in, wts_in, tz_in, store_in, pres, send, ends, *scratch):
    (cell, front, prod, rhs, wts, tz, store), sems = scratch[:-1], scratch[-1]
    pairs = ((cell_in, cell), (front_in, front), (prod_in, prod), (tz_in, tz), (store_in, store), (rhs_in, rhs), (wts_in, wts))
    copies = [pltpu.make_async_copy(a, b, sems.at[i]) for i, (a, b) in enumerate(pairs)]
    for copy in copies:
        copy.start()
    for copy in copies[:3]:
        copy.wait()
    depth, width, long = pres.shape
    where = cell[...]
    hot = onehot(lax.rem(where, long), long).astype(BF16)
    for copy in copies[3:5]:
        copy.wait()
    tzs = [tz[z] for z in range(depth)]
    gs, invs, first, final, coefs = factors(tzs, [store[z] for z in range(depth)])
    row = lax.div(where, long)
    kf, kl = pick([jnp.concatenate(first, 0), jnp.concatenate(final, 0)], row, hot)
    for copy in copies[5:]:
        copy.wait()
    for z in range(depth):
        pres[z] = wts[0, z] * rhs[0, z] + wts[1, z] * rhs[1, z] + wts[2, z] * rhs[2, z]
    (found,) = pick([pres[...].reshape(depth * width, long)], row, hot)
    both = jnp.concatenate([prod[...] * found, front[...].astype(F32), where.astype(F32)], 1)
    send[...] = jnp.broadcast_to(both[:, None], send.shape)
    y = local_solve([pres[z] for z in range(depth)], gs, invs, tzs)
    for i, value in enumerate((*coefs, y[0], y[-1], tzs[-1])):
        ends[i] = value
    ends[6] = jnp.zeros((width, long), F32)
    ends[6, 0:1, : 2 * where.shape[1]] = jnp.concatenate([prod[...] * kf, prod[...] * kl], 1)


def is_right(level, axis="layer"):
    return (lax.axis_index(axis) >> level) % 2 == 1


def choose(level, mine, other, axis="layer"):
    right = is_right(level, axis)
    return (jnp.where(right, other, mine), jnp.where(right, mine, other))


def local_solve(rhs, upper, inv, tz):
    depth = len(rhs)
    y = [rhs[0] * inv[0]]
    for z in range(1, depth):
        y.append((rhs[z] + tz[z - 1] * y[-1]) * inv[z])
    for z in range(depth - 2, -1, -1):
        y[z] = y[z] + upper[z] * y[z + 1]
    return y


def factors(tz, store):
    depth = len(tz)
    gs, invs = ([], [])
    own = None
    for z in range(depth):
        own = store[z] if z == 0 else store[z] + gs[-1] * own
        invs.append(1.0 / (own + tz[z] if z < depth - 1 else own))
        gs.append(tz[z] * invs[-1])
    first = [invs[0]]
    for z in range(1, depth):
        first.append(tz[z - 1] * first[-1] * invs[z])
    final = [None] * depth
    final[-1] = invs[-1]
    for z in range(depth - 2, -1, -1):
        first[z] = first[z] + gs[z] * first[z + 1]
        final[z] = gs[z] * final[z + 1]
    return gs, invs, first, final, block_ends(first, final, tz)


def block_ends(first, final, tz):
    return (first[0], first[-1], final[-1] + 1.0 / jnp.maximum(tz[-1], 1e-30))


def pair(level, own, sib):
    af, af_ = choose(level, own[0], sib[0])
    c, c_ = choose(level, own[1], sib[1])
    b, b_ = choose(level, own[2], sib[2])
    return af, c, b, af_, c_, b_, 1.0 / (b + af_)


def join_coefs(level, own, sib):
    af, c, _, _, c_, b_, g = pair(level, own, sib)
    return (af - c * c * g, c * c_ * g, b_ - c_ * c_ * g)


def join_ends(level, own, sib, mine, other):
    _, c, _, _, c_, _, g = pair(level, own, sib)
    yf, yf_ = choose(level, mine[0], other[0])
    yl, yl_ = choose(level, mine[1], other[1])
    flux = g * (yl - yf_)
    return (yf - c * flux, yl_ + c_ * flux)


def first_join_kernel(final, own, sib, pres, tz, store, tx, cell, prod, kept, low, high, *outs):
    depth, width, _ = tz.shape
    for k, ref in enumerate((tz, store, pres, tx)):
        for z in range(depth):
            low[k * depth + z] = ref[z, 0:1]
            high[k * depth + z] = ref[z, width - 1 : width]
    gs, invs, first, last, _ = factors([tz[z] for z in range(depth)], [store[z] for z in range(depth)])
    for i, value in enumerate(gs + invs + first + last):
        kept[i] = value
    join(0, final, own, sib, first + last, cell, prod, *outs)


def join_kernel(level, final, own, sib, answers, cell, prod, *outs):
    join(level, final, own, sib, [answers[i] for i in range(answers.shape[0])], cell, prod, *outs)


def join(level, final, own, sib, answers, cell, prod, found, *outs):
    depth = len(answers) // 2
    width, long = answers[0].shape
    _, c, _, _, c_, _, g = pair(level, own, sib)
    first, both, last = join_coefs(level, own, sib)
    yf, yl = join_ends(level, own, sib, (own[3], own[4]), (sib[3], sib[4]))
    lower = choose(level, own[5], sib[5])[1]
    right, later = (is_right(level), is_right(level + 1))
    cg, cg_ = (c * g, c_ * g)
    tops, bottoms = ([], [])
    for z in range(depth):
        kf, kl = (answers[z], answers[depth + z])
        tops.append(jnp.where(right, cg * kf, kf - cg * kl))
        bottoms.append(jnp.where(right, kl - cg_ * kf, cg_ * kl))
    tables = [answers[:depth], answers[depth:]] if level else []
    if final:
        (face,) = outs
        face[0], face[1] = (jnp.where(later, first, last), jnp.where(later, yf, yl))
        face[2] = lower
        tables.append([jnp.where(later, tops[z], bottoms[z]) for z in range(depth)])
    else:
        out, more = outs
        for i, value in enumerate((first, both, last, yf, yl, lower)):
            out[i] = value
        for i, value in enumerate(tops + bottoms):
            more[i] = value
    if tables:
        where = cell[...]
        hot = onehot(lax.rem(where, long), long).astype(BF16)
        got = pick([jnp.concatenate(t, 0) for t in tables], lax.div(where, long), hot)
        found[...] = jnp.concatenate([prod[...] * value for value in got], 1)
    else:
        found[...] = jnp.zeros(found.shape, F32)


def groups_of(levels):
    layers = lax.axis_size("layer")
    l = lax.axis_index("layer")
    base = lax.axis_index("tile") * layers
    out = [[base + l]]
    for level in range(levels):
        out.append([base + (((l >> level) ^ 1) << level) + i for i in range(1 << level)])
    return out


def front_kernel(recv, found, inverse, send, held, sems):
    devices = recv.shape[0]
    count = recv.shape[2] // 3
    rows, length = inverse.shape
    lanes = 128
    chunks = sems.shape[0]
    wide = length // chunks
    found = found[...]
    copies = [
        pltpu.make_async_copy(inverse.at[:, pl.ds(i * wide, wide)], held.at[:, pl.ds(i * wide, wide)], sems.at[i])
        for i in range(chunks)
    ]
    for copy in copies:
        copy.start()
    terms, index = (recv[:, 0, :count], recv[:, 0, count : 2 * count])
    high = jnp.floor(index * (1.0 / lanes))
    low = index - high * lanes
    parts = [p.astype(F32) for p in split(terms)[:PARTS]]
    row_of = iota((length // lanes, count), 0).astype(F32)
    lane_of = iota((lanes, count), 0).astype(F32)
    total = jnp.zeros((length // lanes, lanes), F32)
    for d in range(devices):
        hit = row_of == high[d : d + 1]
        left = jnp.concatenate([jnp.where(hit, p[d : d + 1], 0.0).astype(BF16) for p in parts], 0)
        right = jnp.where(lane_of == low[d : d + 1], 1.0, 0.0).astype(BF16)
        total = total + fold(dot_nt(left, right), PARTS)
    acc = jnp.zeros((rows, lanes), F32)
    for i in range(chunks):
        copies[i].wait()
        for r in range(i * wide // lanes, (i + 1) * wide // lanes):
            acc = acc + held[:, r * lanes : (r + 1) * lanes] * total[r : r + 1]
    parts = jnp.concatenate(split(acc), 1)
    out = dot_nt(jnp.ones((8, parts.shape[1]), BF16), parts)
    pad = send.shape[2] - out.shape[1] - found.shape[1]
    pieces = [out[0:1], found] + ([jnp.zeros((1, pad), F32)] if pad else [])
    send[...] = jnp.broadcast_to(jnp.concatenate(pieces, 1)[:, None], send.shape)


def gathered(values, rows_hot, lanes_hot, start, size, ext, parts):
    hot = lanes_hot[:, start : start + size]
    pieces = [hot * p for v in values for p in split(v)[:parts]]
    got = dot_nt(rows_hot[:, start : start + size], jnp.concatenate(pieces, 0))
    planes = []
    lanes = hot.shape[0]
    for i in range(len(values)):
        plane = got[:, i * parts * lanes : (i * parts + 1) * lanes]
        for k in range(1, parts):
            j = i * parts + k
            plane = plane + got[:, j * lanes : (j + 1) * lanes]
        planes.append(jnp.concatenate([plane[r : r + ext] for r in range(0, plane.shape[0], ext)], 1))
    return planes


def beside(centre, tx, ty):
    width, long = centre.shape
    row, col = (iota(centre.shape, 0), iota(centre.shape, 1))
    total = tx * jnp.where(row == width - 1, 0.0, pltpu.roll(centre, width - 1, 0))
    total = total + jnp.where(row == 0, 0.0, pltpu.roll(tx * centre, 1, 0))
    total = total + ty * jnp.where(col == long - 1, 0.0, pltpu.roll(centre, long - 1, 1))
    return total + jnp.where(col == 0, 0.0, pltpu.roll(ty * centre, 1, 1))


def tile_rows(first, last, one, two):
    odd = is_right(0, "tile")
    one[...] = jnp.where(odd, first, last)
    two[...] = jnp.where(odd, last, first)


def table_kernel(lists, shape, terms, hots, only=None):
    _, width, long = shape
    rows_hot, lanes_hot, sol_hot, sol_row, layer = hots
    lanes = 128
    rows = sol_hot.shape[0]
    count = terms.shape[2] // 3
    at = 0
    for members in lists:
        for device in members:
            entry = terms[device]
            index = entry[:, count : 2 * count].astype(I32)
            cell = entry[:, 2 * count :].astype(I32)
            y, x = lax.rem(cell, long), lax.rem(lax.div(cell, long), width)
            if only is None:
                row = lax.div(y, lanes) * width + x
            else:
                row = jnp.where(x == only, lax.div(y, lanes), -1)
            here = pl.ds(at, count)
            rows_hot[:, here] = onehot(row, rows_hot.shape[0]).astype(BF16)
            lanes_hot[:, here] = onehot(lax.rem(y, lanes), lanes).astype(BF16)
            sol_hot[:, here] = onehot(lax.rem(index, rows), rows).astype(BF16)
            sol_row[:, here] = lax.div(index, rows)
            if at < layer.shape[1]:
                layer[:, here] = lax.div(cell, long * width)
            at += count


def column_solve(levels, recv, lists, hots, listing, planes_of, sib):
    rows_hot, lanes_hot, sol_hot, sol_row, layer = hots
    rows, count = (sol_hot.shape[0], layer.shape[1])
    table = jnp.concatenate(split(recv[...].reshape(recv.shape[0], recv.shape[2])[:, :rows]), 0)
    sol = fold(dot(table, sol_hot[...]))
    sol = jnp.sum(jnp.where(iota(sol.shape, 0) == sol_row[...], sol, 0.0), axis=0, keepdims=True)
    layer = layer[...]

    def listed(group, column):
        at = rows + column * count
        return jnp.concatenate([recv[device][:, at : at + count] for device in group], 1)

    mine_list, sib_list = listing
    tz, pres, (gs, invs, first, final, coefs) = planes_of()
    depth = len(tz)
    high = tz[0].shape[0]
    own = [coefs]
    start = layer.shape[1]
    value = mine_list * sol[:, :start]
    values = [jnp.where(layer == z, value, 0.0) for z in range(depth)]
    change = gathered(values, rows_hot, lanes_hot, 0, start, high, PARTS)
    y = local_solve([pres[z] - change[z] for z in range(depth)], gs, invs, tz)
    mine = (y[0], y[-1])
    steps = []
    for level in range(levels):
        size = len(lists[level + 1]) * count
        top = level == levels - 1
        if level:
            columns = [2 * level - 2] if top else [2 * level - 2, 2 * level - 1]
            values = [listed(lists[level + 1], c) for c in columns]
        else:
            values = [sib_list[:, i * count : (i + 1) * count] for i in range(2)]
        values = [value * sol[:, start : start + size] for value in values]
        change = gathered(values, rows_hot, lanes_hot, start, size, high, PARTS)
        start += size
        if top:
            other = sib[level][1] - change[0]
            steps.append((mine, (other, other)))
        else:
            other = (sib[level][3] - change[0], sib[level][4] - change[1])
            steps.append((mine, other))
            mine = join_ends(level, own[level], sib[level], mine, other)
            own.append(join_coefs(level, own[level], sib[level]))
    above = below = tzp = jnp.zeros(tz[0].shape, F32)
    place = lax.axis_index("layer")
    for level in range(levels - 1, -1, -1):
        mine, other = steps[level]
        yl, _ = choose(level, mine[1], other[1])
        _, yf_ = choose(level, mine[0], other[0])
        flux = yl - yf_
        if level == levels - 1:
            b, _ = choose(level, own[level][2], sib[level][0])
            _, af_ = choose(level, own[level][0], sib[level][0])
            g = 1.0 / (b + af_)
            before = sib[level][2]
        else:
            _, c, _, _, c_, _, g = pair(level, own[level], sib[level])
            flux = flux + c * above - c_ * below
            before = sib[level][5]
        tzp = jnp.where(place % (2 << level) == 1 << level, before, tzp)
        flux = g * flux
        right = is_right(level)
        above, below = (jnp.where(right, flux, above), jnp.where(right, below, -flux))
    return [y[z] + first[z] * above + final[z] * below for z in range(depth)], above, below, tzp


def pressure_kernel(levels, ready, recv, terms, pres, *refs):
    sib, (tz, kept, tx, prod, _, p, coupled_z, one, *hots) = (refs[:levels], refs[levels:])
    depth, width, _ = pres.shape
    odd = is_right(0, "tile")
    lists = groups_of(levels)
    table_kernel(lists, pres.shape, terms, hots)

    def planes_of():
        tzs, pressures = ([ref[z] for z in range(depth)] for ref in (tz, pres))
        gs, invs, first, final = ([kept[k * depth + z] for z in range(depth)] for k in range(4))
        return tzs, pressures, (gs, invs, first, final, block_ends(first, final, tzs))

    ready(0)
    listing = (prod[...], sib[0][6, 0:1])
    values, above, below, tzp = column_solve(levels, recv, lists, hots, listing, planes_of, sib)
    tzs = [tz[z] for z in range(depth)]
    is_last = lax.axis_index("layer") == (1 << levels) - 1
    for z in range(depth):
        p[z] = values[z]
        one[z] = jnp.where(odd, values[z][0:1], (tx[z] * values[z])[width - 1 :])
        total = above + tzp * values[z] if z == 0 else tzs[z - 1] * values[z - 1]
        if z == depth - 1:
            coupled_z[z] = total + jnp.where(is_last, 0.0, below + tzs[z] * values[z])
        else:
            coupled_z[z] = total + tzs[z] * values[z + 1]
    ready(1)


def edge_kernel(levels, low, high, prod, *refs):
    sib, two = (refs[:levels], refs[levels])
    odd = is_right(0, "tile")
    n = low.shape[0]
    two[pl.ds(0, n)] = jnp.where(odd, high[...], low[...])
    at = n
    for block in sib:
        width = block.shape[1]
        for i in range(min(6, block.shape[0])):
            two[at] = jnp.where(odd, block[i, width - 1 : width], block[i, 0:1])
            at += 1
    two[at] = sib[0][6, 0:1]
    two[at + 1] = jnp.zeros((1, two.shape[2]), F32)
    two[at + 1, :, : prod.shape[1]] = prod[...]


def first_three(kernel, ready, one, two, three, _rhs, _diag, _ty, *rest):
    kernel(one, two, three, *rest)
    ready(0)


def beyond_kernel(levels, shapes, shape, recv, terms, two, row, *hots):
    depth, width, long = shape
    tiles, layers = (lax.axis_size("tile"), lax.axis_size("layer"))
    tile = lax.axis_index("tile")
    odd = is_right(0, "tile")
    count = 4 * depth + sum(shapes)
    planes = [two[i] for i in range(count)]
    step = jnp.where(odd, layers, -layers)
    lists = [[jnp.clip(device + step, 0, tiles * layers - 1) for device in members] for members in groups_of(levels)]
    table_kernel(lists, shape, terms, hots, jnp.where(odd, 0, width - 1))
    exists = jnp.where(odd, (tile < tiles - 1).astype(F32), (tile > 0).astype(F32)) + jnp.zeros((1, long), F32)
    blocks = []
    at = 4 * depth
    for size in shapes:
        blocks.append([planes[at + i] for i in range(size)])
        at += size

    def planes_of():
        kept = [planes[depth + z] for z in range(depth)]
        tzs = [planes[z] for z in range(depth)]
        found = factors(tzs, [jnp.where(value == 0.0, 1.0, value) for value in kept])
        return tzs, [planes[2 * depth + z] for z in range(depth)], found

    listing = (two[count + 1, :, : terms.shape[2] // 3], two[count])
    values, _, _, _ = column_solve(levels, recv, lists, hots, listing, planes_of, blocks)
    for z in range(depth):
        found = jnp.where(exists > 0.0, values[z], 0.0)
        row[z] = jnp.where(odd, found, found * two[3 * depth + z])


def search_kernel(p, coupled_z, two, one, tx, ty, tz, rhs, column, binv, s, outer, row_two, row_one, inner):
    depth, width, _ = p.shape
    odd = is_right(0, "tile")
    right = is_right(0)
    row = iota(p.shape[1:], 0)
    for z in range(depth):
        centre = p[z]
        after = jnp.where(odd, two[z], one[z])
        before = jnp.where(odd, one[z], two[z])
        coupled = coupled_z[z] + beside(centre, tx[z], ty[z])
        coupled = coupled + jnp.where(row == 0, before, 0.0) + jnp.where(row == width - 1, tx[z] * after, 0.0)
        remain = [rhs[c, z] - column[c, z] * centre for c in range(3)]
        remain[0] = remain[0] + coupled
        for c in range(3):
            value = binv[c, 0, z] * remain[0] + binv[c, 1, z] * remain[1] + binv[c, 2, z] * remain[2]
            if c == 0:
                value = centre + value
            s[c, z] = value
            tile_rows(value[0:1], (tx[z] * value)[width - 1 :], row_one.at[c, z], row_two.at[c, z])
    for c in range(3):
        top, bottom = (s[c, 0], tz[depth - 1] * s[c, depth - 1])
        inner[c] = jnp.where(right, top, bottom)
        outer[c] = jnp.where(right, bottom, top)


def inner_kernel(ready, s, diag, tz, tx, ty, image):
    depth = s.shape[1]
    for z in range(depth):
        for c in range(3):
            total = beside(s[c, z], tx[z], ty[z])
            if z:
                total = total + tz[z - 1] * s[c, z - 1]
            if z < depth - 1:
                total = total + tz[z] * s[c, z + 1]
            image[c, z] = total
    ready(0)
    for z in range(depth):
        for c in range(3):
            total = diag[c, 0, z] * s[0, z] + diag[c, 1, z] * s[1, z] + diag[c, 2, z] * s[2, z]
            image[c, z] = total - image[c, z]


def image_kernel(part, inner, outer, row_two, row_one, rhs, tz, tx, image, send):
    depth, width = part.shape[1:3]
    right, odd = (is_right(0), is_right(0, "tile"))
    row = iota(part.shape[2:], 0)
    along = power = start = 0.0
    for z in range(depth):
        for c in range(3):
            value = part[c, z]
            if z == 0:
                value = value - jnp.where(right, inner[c], outer[c])
            if z == depth - 1:
                value = value - tz[z] * jnp.where(right, outer[c], inner[c])
            after = jnp.where(odd, row_two[c, z], row_one[c, z])
            before = jnp.where(odd, row_one[c, z], row_two[c, z])
            value = value - jnp.where(row == 0, before, 0.0) - jnp.where(row == width - 1, tx[z] * after, 0.0)
            image[c, z] = value
            given = rhs[c, z]
            along = along + value * given
            power = power + value * value
            start = start + given * given
    along, power, start = (jnp.sum(along), jnp.sum(power), jnp.sum(start))
    omega = along / jnp.where(power > 0.0, power, 1.0)
    square = cross = 0.0
    for z in range(depth):
        for c in range(3):
            value = image[c, z]
            left = rhs[c, z] - omega * value
            square = square + left * left
            cross = cross + left * value
    lane = iota((1, send.shape[2]), 1)
    out = jnp.zeros((1, send.shape[2]), F32)
    for i, value in enumerate((along, power, start, jnp.sum(square), jnp.sum(cross), omega)):
        out = jnp.where(lane == i, value, out)
    send[...] = jnp.broadcast_to(out[:, None], send.shape)


def finish_kernel(recv, s, image, rhs, update, lin_res, ratio):
    sums = recv[...].reshape(recv.shape[0], recv.shape[2])
    whole = jnp.sum(sums, axis=0, keepdims=True)
    omega = whole[:, 0:1] / whole[:, 1:2]
    shift = sums[:, 5:6] - omega
    square = sums[:, 3:4] + 2.0 * shift * sums[:, 4:5] + shift * shift * sums[:, 1:2]
    ratio[...] = jnp.sqrt(jnp.sum(square, axis=0, keepdims=True) / whole[:, 2:3])
    for c in range(3):
        for z in range(s.shape[1]):
            update[c, z] = omega * s[c, z]
            lin_res[c, z] = rhs[c, z] - omega * image[c, z]


def flip(x, level, axis="layer"):
    return lax.ppermute(x, axis, [(i, i ^ (1 << level)) for i in range(lax.axis_size(axis))])


def neighbour(x, axis="layer"):
    pairs = [(i, i + 1) for i in range(1, lax.axis_size(axis) - 1, 2)]
    return lax.ppermute(x, axis, pairs + [(j, i) for i, j in pairs])


def everywhere(x):
    return lax.all_to_all(x, BOTH, split_axis=0, concat_axis=0, tiled=True)


def shards(rhs, weights, block_diag, block_inv, tx, ty, tz, store, cell, front, prod, inverse):
    layers = lax.axis_size("layer")
    devices = lax.axis_size("tile") * layers
    levels = layers.bit_length() - 1
    depth, width, long = tx.shape
    count = cell.shape[0]
    rows = inverse.shape[0]
    lists = layers * count
    cell, front, prod = (cell.reshape(1, -1), front.reshape(1, -1), prod.reshape(1, -1))
    field = vmem(tx.shape)

    def planes(n):
        return vmem((n, width, long))

    hbm_spec = pl.BlockSpec(memory_space=pltpu.HBM)
    given = (cell, front, prod, rhs, weights, tz, store)
    pres, send, ends = pl.pallas_call(
        pres_kernel,
        out_shape=(field, vmem((devices, 1, 3 * count)), planes(7)),
        in_specs=[hbm_spec] * len(given),
        out_specs=(VM,) * 3,
        scratch_shapes=[vmem(a.shape, a.dtype) for a in given] + [pltpu.SemaphoreType.DMA((len(given),))],
        compiler_params=pltpu.CompilerParams(vmem_limit_bytes=LIMIT),
    )(*[pltpu.with_memory_space_constraint(a, pltpu.HBM) for a in given])
    terms = everywhere(send)
    sib, found = ([], [])
    for level in range(levels - 1):
        sib.append(flip(ends, level))
        final = level == levels - 2
        many = (2 if level else 0) + (1 if final else 0)
        outs = (vmem((1, max(1, many) * count)), *((planes(3),) if final else (planes(6), planes(2 * depth))))
        if level == 0:
            rim = vmem((4 * depth, 1, long))
            kept, low, high, *got = call(
                functools.partial(first_join_kernel, final),
                (hbm((4 * depth, width, long)), rim, rim, *outs),
                (ends, sib[-1], pres, tz, store, tx, cell, prod),
                far=range(3, 8),
            )
        else:
            got = call(
                functools.partial(join_kernel, level, final), outs, (ends, sib[-1], answers, cell, prod), far=(3, 4)
            )
        if many:
            found.append(got[0])
        if final:
            face = got[1]
        else:
            ends, answers = got[1:]
    found = found[0] if len(found) == 1 else jnp.concatenate(found, 1)
    terms, face, found = lax.optimization_barrier((terms, face, found))
    sib.append(flip(face, levels - 1))
    chunks = 8
    send = pl.pallas_call(
        front_kernel,
        out_shape=vmem((devices, 1, max(rows + found.shape[1], 3 * count))),
        in_specs=[VM, VM, hbm_spec],
        out_specs=VM,
        scratch_shapes=[vmem(inverse.shape), pltpu.SemaphoreType.DMA((chunks,))],
        compiler_params=pltpu.CompilerParams(vmem_limit_bytes=LIMIT),
    )(terms, found, pltpu.with_memory_space_constraint(inverse, pltpu.HBM))
    sizes = [min(6, block.shape[0]) for block in sib]
    rim = vmem((4 * depth + sum(sizes) + 2, 1, long))
    send, low, high = lax.optimization_barrier((send, low, high))
    (two,) = call(functools.partial(edge_kernel, levels), (rim,), (low, high, prod, *sib))
    sol = everywhere(send)
    two = neighbour(two, "tile")

    def hots(high):
        return (
            vmem((high * long // 128, lists), BF16),
            vmem((128, lists), BF16),
            vmem((rows, lists), BF16),
            vmem((1, lists), I32),
            vmem((1, count), I32),
        )

    at = 3 + levels
    row3 = vmem((depth, 1, long))
    p, coupled_z, one, tz, tx, block_inv = call(
        functools.partial(pressure_kernel, levels),
        (field, field, row3),
        (sol, terms, pres, *sib, tz, kept, tx, prod, block_inv),
        far=range(at, at + 5),
        keep=(at, at + 2, at + 4),
        late=(range(at, at + 4), (at + 4,)),
        scratch=hots(width),
    )
    sol, one, terms = lax.optimization_barrier((sol, one, terms))
    one = flip(one, 0, "tile")
    two, rhs, first_column, ty = call(
        functools.partial(first_three, functools.partial(beyond_kernel, levels, sizes, (depth, width, long))),
        (row3,),
        (sol, terms, two, rhs, block_diag, ty),
        far=(3, 4, 5),
        keep=(3, 4, 5),
        column=(4,),
        late=((3, 4, 5),),
        scratch=hots(1),
    )
    row9 = vmem((3, depth, 1, long))
    plane3 = planes(3)
    s, outer, row_two, row_one, inner = call(
        search_kernel,
        (vmem(rhs.shape), plane3, row9, row9, plane3),
        (p, coupled_z, two, one, tx, ty, tz, rhs, first_column, block_inv),
    )
    outer, row_two = (neighbour(outer), neighbour(row_two, "tile"))
    row_one, inner = (flip(row_one, 0, "tile"), flip(inner, 0))
    (part,) = call(inner_kernel, (vmem(rhs.shape),), (s, block_diag, tz, tx, ty), far=(1,), late=((1,),))
    image, send = call(
        image_kernel,
        (vmem(rhs.shape), vmem((devices, 1, 128))),
        (part, inner, outer, row_two, row_one, rhs, tz, tx),
    )
    sums = everywhere(send)
    update, lin_res, ratio = call(
        finish_kernel, (hbm(rhs.shape), hbm(rhs.shape), hbm((1, 1))), (sums, s, image, rhs)
    )
    return (update, lin_res, ratio.reshape(()))


def solution(mesh):
    return jax.shard_map(
        shards,
        mesh=mesh,
        in_specs=(
            P(None, "layer", "tile", None),
            P(None, "layer", "tile", None),
            P(None, None, "layer", "tile", None),
            P(None, None, "layer", "tile", None),
            P("layer", "tile", None),
            P("layer", "tile", None),
            P("layer", "tile", None),
            P("layer", "tile", None),
            P(("tile", "layer")),
            P(("tile", "layer")),
            P(("tile", "layer")),
            P(("tile", "layer"), None),
        ),
        out_specs=(P(None, "layer", "tile", None), P(None, "layer", "tile", None), P()),
        check_vma=False,
    )
```

```python
import functools
import jax
import jax.numpy as jnp
from jax import lax
from jax.experimental import pallas as pl
from jax.experimental.pallas import tpu as pltpu
from jax.sharding import PartitionSpec as P

F32 = jnp.float32
BF16 = jnp.bfloat16
I32 = jnp.int32
BOTH = ("tile", "layer")
VM = pl.BlockSpec(memory_space=pltpu.VMEM)
LIMIT = 16 << 20
PARTS = 2


def hbm(shape):
    return jax.ShapeDtypeStruct(shape, F32)


def vmem(shape, dtype=F32):
    return pltpu.VMEM(shape, dtype)


def staged(kernel, where, outs, kept, column, cut, late, *refs):
    count, sems = (len(where), refs[-1])
    held = list(refs[count + outs + len(kept) : -1])
    target_count = sum(where) - len(kept)
    held, extra = (held[:target_count], held[target_count:])
    target = dict(zip(kept, refs[count + outs : count + outs + len(kept)]))
    operands, copies = ([], [])
    for i, far in enumerate(where):
        if far:
            to = target[i] if i in target else held.pop(0)
            part = refs[i].at[:, 0] if i in column else refs[i].at[cut[i][0] : cut[i][1]] if i in cut else refs[i]
            copies.append(pltpu.make_async_copy(part, to, sems.at[len(copies)]))
            operands.append(to)
        else:
            operands.append(refs[i])
    places = [i for i, far in enumerate(where) if far]
    for copy in copies:
        copy.start()
    for i, copy in zip(places, copies):
        if not any(i in group for group in late):
            copy.wait()

    def ready(k):
        for i, copy in zip(places, copies):
            if i in late[k]:
                copy.wait()

    more = (ready,) if late else ()
    kernel(*more, *operands, *refs[count : count + outs], *extra)


def call(kernel, outs, args, far=(), keep=(), column=(), cut={}, late=(), scratch=(), limit=LIMIT):
    where = [i in far for i in range(len(args))]
    spaces = [pltpu.HBM if w else pltpu.VMEM for w in where]
    shapes = [a.shape[:1] + a.shape[2:] if i in column else a.shape for i, a in enumerate(args)]
    shapes = [(cut[i][1] - cut[i][0], *a[1:]) if i in cut else a for i, a in enumerate(shapes)]
    every = (*outs, *(vmem(shapes[i], args[i].dtype) for i in keep))
    return pl.pallas_call(
        functools.partial(staged, kernel, where, len(outs), tuple(keep), tuple(column), cut, tuple(late)),
        out_shape=every,
        in_specs=[pl.BlockSpec(memory_space=s) for s in spaces],
        out_specs=(VM,) * len(every),
        scratch_shapes=[vmem(shapes[i], a.dtype) for i, a in enumerate(args) if where[i] and i not in keep]
        + [*scratch, pltpu.SemaphoreType.DMA((max(1, sum(where)),))],
        compiler_params=pltpu.CompilerParams(vmem_limit_bytes=limit),
    )(*[pltpu.with_memory_space_constraint(a, s) for a, s in zip(args, spaces)])


def iota(shape, dim):
    return lax.broadcasted_iota(I32, shape, dim)


def split(x):
    one = x.astype(BF16)
    rest = x - one.astype(F32)
    two = rest.astype(BF16)
    three = (rest - two.astype(F32)).astype(BF16)
    return [one, two, three]


def fold(x, parts=3):
    n = x.shape[0] // parts
    total = x[(parts - 1) * n :]
    for i in range(parts - 2, -1, -1):
        total = x[i * n : (i + 1) * n] + total
    return total


def onehot(index, size):
    return jnp.where(iota((size, index.shape[1]), 0) == index, 1.0, 0.0)


def dot(a, b):
    return lax.dot_general(a, b, (((1,), (0,)), ((), ())), preferred_element_type=F32)


def dot_nt(a, b):
    return lax.dot_general(a, b, (((1,), (1,)), ((), ())), preferred_element_type=F32)


def pick(tables, hi, hot):
    rows = tables[0].shape[0]
    parts = jnp.concatenate([p for table in tables for p in split(table)[:PARTS]], 0)
    got = dot(parts, hot)
    mask = onehot(hi, rows)
    n = PARTS * rows
    return [jnp.sum(fold(got[i * n : (i + 1) * n], PARTS) * mask, axis=0, keepdims=True) for i in range(len(tables))]


def pres_kernel(cell_in, front_in, prod_in, rhs_in, wts_in, tz_in, store_in, pres, send, ends, *scratch):
    (cell, front, prod, rhs, wts, tz, store), sems = scratch[:-1], scratch[-1]
    pairs = ((cell_in, cell), (front_in, front), (prod_in, prod), (tz_in, tz), (store_in, store), (rhs_in, rhs), (wts_in, wts))
    copies = [pltpu.make_async_copy(a, b, sems.at[i]) for i, (a, b) in enumerate(pairs)]
    for copy in copies:
        copy.start()
    for copy in copies[:3]:
        copy.wait()
    depth, width, long = pres.shape
    where = cell[...]
    hot = onehot(lax.rem(where, long), long).astype(BF16)
    for copy in copies[3:5]:
        copy.wait()
    tzs = [tz[z] for z in range(depth)]
    gs, invs, first, final, coefs = factors(tzs, [store[z] for z in range(depth)])
    row = lax.div(where, long)
    kf, kl = pick([jnp.concatenate(first, 0), jnp.concatenate(final, 0)], row, hot)
    for copy in copies[5:]:
        copy.wait()
    for z in range(depth):
        pres[z] = wts[0, z] * rhs[0, z] + wts[1, z] * rhs[1, z] + wts[2, z] * rhs[2, z]
    (found,) = pick([pres[...].reshape(depth * width, long)], row, hot)
    both = jnp.concatenate([prod[...] * found, front[...].astype(F32), where.astype(F32)], 1)
    send[...] = jnp.broadcast_to(both[:, None], send.shape)
    y = local_solve([pres[z] for z in range(depth)], gs, invs, tzs)
    for i, value in enumerate((*coefs, y[0], y[-1], tzs[-1])):
        ends[i] = value
    ends[6] = jnp.zeros((width, long), F32)
    ends[6, 0:1, : 2 * where.shape[1]] = jnp.concatenate([prod[...] * kf, prod[...] * kl], 1)


def is_right(level, axis="layer"):
    return (lax.axis_index(axis) >> level) % 2 == 1


def choose(level, mine, other, axis="layer"):
    right = is_right(level, axis)
    return (jnp.where(right, other, mine), jnp.where(right, mine, other))


def local_solve(rhs, upper, inv, tz):
    depth = len(rhs)
    y = [rhs[0] * inv[0]]
    for z in range(1, depth):
        y.append((rhs[z] + tz[z - 1] * y[-1]) * inv[z])
    for z in range(depth - 2, -1, -1):
        y[z] = y[z] + upper[z] * y[z + 1]
    return y


def factors(tz, store):
    depth = len(tz)
    gs, invs = ([], [])
    own = None
    for z in range(depth):
        own = store[z] if z == 0 else store[z] + gs[-1] * own
        invs.append(1.0 / (own + tz[z] if z < depth - 1 else own))
        gs.append(tz[z] * invs[-1])
    first = [invs[0]]
    for z in range(1, depth):
        first.append(tz[z - 1] * first[-1] * invs[z])
    final = [None] * depth
    final[-1] = invs[-1]
    for z in range(depth - 2, -1, -1):
        first[z] = first[z] + gs[z] * first[z + 1]
        final[z] = gs[z] * final[z + 1]
    return gs, invs, first, final, block_ends(first, final, tz)


def block_ends(first, final, tz):
    return (first[0], first[-1], final[-1] + 1.0 / jnp.maximum(tz[-1], 1e-30))


def pair(level, own, sib):
    af, af_ = choose(level, own[0], sib[0])
    c, c_ = choose(level, own[1], sib[1])
    b, b_ = choose(level, own[2], sib[2])
    return af, c, b, af_, c_, b_, 1.0 / (b + af_)


def join_coefs(level, own, sib):
    af, c, _, _, c_, b_, g = pair(level, own, sib)
    return (af - c * c * g, c * c_ * g, b_ - c_ * c_ * g)


def join_ends(level, own, sib, mine, other):
    _, c, _, _, c_, _, g = pair(level, own, sib)
    yf, yf_ = choose(level, mine[0], other[0])
    yl, yl_ = choose(level, mine[1], other[1])
    flux = g * (yl - yf_)
    return (yf - c * flux, yl_ + c_ * flux)


def first_join_kernel(final, own, sib, pres, tz, store, tx, cell, prod, kept, low, high, *outs):
    depth, width, _ = tz.shape
    for k, ref in enumerate((tz, store, pres, tx)):
        for z in range(depth):
            low[k * depth + z] = ref[z, 0:1]
            high[k * depth + z] = ref[z, width - 1 : width]
    gs, invs, first, last, _ = factors([tz[z] for z in range(depth)], [store[z] for z in range(depth)])
    for i, value in enumerate(gs + invs + first + last):
        kept[i] = value
    join(0, final, own, sib, first + last, cell, prod, *outs)


def join_kernel(level, final, own, sib, answers, cell, prod, *outs):
    join(level, final, own, sib, [answers[i] for i in range(answers.shape[0])], cell, prod, *outs)


def join(level, final, own, sib, answers, cell, prod, found, *outs):
    depth = len(answers) // 2
    width, long = answers[0].shape
    _, c, _, _, c_, _, g = pair(level, own, sib)
    first, both, last = join_coefs(level, own, sib)
    yf, yl = join_ends(level, own, sib, (own[3], own[4]), (sib[3], sib[4]))
    lower = choose(level, own[5], sib[5])[1]
    right, later = (is_right(level), is_right(level + 1))
    cg, cg_ = (c * g, c_ * g)
    tops, bottoms = ([], [])
    for z in range(depth):
        kf, kl = (answers[z], answers[depth + z])
        tops.append(jnp.where(right, cg * kf, kf - cg * kl))
        bottoms.append(jnp.where(right, kl - cg_ * kf, cg_ * kl))
    tables = [answers[:depth], answers[depth:]] if level else []
    if final:
        (face,) = outs
        face[0], face[1] = (jnp.where(later, first, last), jnp.where(later, yf, yl))
        face[2] = lower
        tables.append([jnp.where(later, tops[z], bottoms[z]) for z in range(depth)])
    else:
        out, more = outs
        for i, value in enumerate((first, both, last, yf, yl, lower)):
            out[i] = value
        for i, value in enumerate(tops + bottoms):
            more[i] = value
    if tables:
        where = cell[...]
        hot = onehot(lax.rem(where, long), long).astype(BF16)
        got = pick([jnp.concatenate(t, 0) for t in tables], lax.div(where, long), hot)
        found[...] = jnp.concatenate([prod[...] * value for value in got], 1)
    else:
        found[...] = jnp.zeros(found.shape, F32)


def groups_of(levels):
    layers = lax.axis_size("layer")
    l = lax.axis_index("layer")
    base = lax.axis_index("tile") * layers
    out = [[base + l]]
    for level in range(levels):
        out.append([base + (((l >> level) ^ 1) << level) + i for i in range(1 << level)])
    return out


def front_kernel(recv, found, inverse, send, held, sems):
    devices = recv.shape[0]
    count = recv.shape[2] // 3
    rows, length = inverse.shape
    lanes = 128
    chunks = sems.shape[0]
    wide = length // chunks
    found = found[...]
    copies = [
        pltpu.make_async_copy(inverse.at[:, pl.ds(i * wide, wide)], held.at[:, pl.ds(i * wide, wide)], sems.at[i])
        for i in range(chunks)
    ]
    for copy in copies:
        copy.start()
    terms, index = (recv[:, 0, :count], recv[:, 0, count : 2 * count])
    high = jnp.floor(index * (1.0 / lanes))
    low = index - high * lanes
    parts = [p.astype(F32) for p in split(terms)[:PARTS]]
    row_of = iota((length // lanes, count), 0).astype(F32)
    lane_of = iota((lanes, count), 0).astype(F32)
    flipped = jnp.zeros((lanes, PARTS * (length // lanes)), F32)
    for d in range(devices):
        hit = row_of == high[d : d + 1]
        left = jnp.concatenate([jnp.where(hit, p[d : d + 1], 0.0).astype(BF16) for p in parts], 0)
        right = jnp.where(lane_of == low[d : d + 1], 1.0, 0.0).astype(BF16)
        flipped = flipped + dot_nt(right, left)
    total = fold(jnp.transpose(flipped), PARTS)
    acc = jnp.zeros((rows, lanes), F32)
    for i in range(chunks):
        copies[i].wait()
        for r in range(i * wide // lanes, (i + 1) * wide // lanes):
            acc = acc + held[:, r * lanes : (r + 1) * lanes] * total[r : r + 1]
    out = jnp.transpose(jnp.broadcast_to(jnp.sum(acc, axis=1, keepdims=True), (rows, lanes)))
    pad = send.shape[2] - out.shape[1] - found.shape[1]
    pieces = [out[0:1], found] + ([jnp.zeros((1, pad), F32)] if pad else [])
    send[...] = jnp.broadcast_to(jnp.concatenate(pieces, 1)[:, None], send.shape)


def gathered(values, rows_hot, lanes_hot, start, size, ext, parts):
    hot = lanes_hot[:, start : start + size]
    pieces = [hot * p for v in values for p in split(v)[:parts]]
    got = dot_nt(rows_hot[:, start : start + size], jnp.concatenate(pieces, 0))
    planes = []
    lanes = hot.shape[0]
    for i in range(len(values)):
        plane = got[:, i * parts * lanes : (i * parts + 1) * lanes]
        for k in range(1, parts):
            j = i * parts + k
            plane = plane + got[:, j * lanes : (j + 1) * lanes]
        planes.append(jnp.concatenate([plane[r : r + ext] for r in range(0, plane.shape[0], ext)], 1))
    return planes


def beside(centre, tx, ty):
    width, long = centre.shape
    row, col = (iota(centre.shape, 0), iota(centre.shape, 1))
    total = tx * jnp.where(row == width - 1, 0.0, pltpu.roll(centre, width - 1, 0))
    total = total + jnp.where(row == 0, 0.0, pltpu.roll(tx * centre, 1, 0))
    total = total + ty * jnp.where(col == long - 1, 0.0, pltpu.roll(centre, long - 1, 1))
    return total + jnp.where(col == 0, 0.0, pltpu.roll(ty * centre, 1, 1))


def tile_rows(first, last, one, two):
    odd = is_right(0, "tile")
    one[...] = jnp.where(odd, first, last)
    two[...] = jnp.where(odd, last, first)


def table_kernel(lists, shape, terms, hots, only=None):
    _, width, long = shape
    rows_hot, lanes_hot, sol_hot, sol_row, layer = hots
    lanes = 128
    rows = sol_hot.shape[0]
    count = terms.shape[2] // 3
    at = 0
    for members in lists:
        for device in members:
            entry = terms[device]
            index = entry[:, count : 2 * count].astype(I32)
            cell = entry[:, 2 * count :].astype(I32)
            y, x = lax.rem(cell, long), lax.rem(lax.div(cell, long), width)
            if only is None:
                row = lax.div(y, lanes) * width + x
            else:
                row = jnp.where(x == only, lax.div(y, lanes), -1)
            here = pl.ds(at, count)
            rows_hot[:, here] = onehot(row, rows_hot.shape[0]).astype(BF16)
            lanes_hot[:, here] = onehot(lax.rem(y, lanes), lanes).astype(BF16)
            sol_hot[:, here] = onehot(lax.rem(index, rows), rows).astype(BF16)
            sol_row[:, here] = lax.div(index, rows)
            if at < layer.shape[1]:
                layer[:, here] = lax.div(cell, long * width)
            at += count


def column_solve(levels, recv, lists, hots, listing, planes_of, sib):
    rows_hot, lanes_hot, sol_hot, sol_row, layer = hots
    rows, count = (sol_hot.shape[0], layer.shape[1])
    table = jnp.concatenate(split(recv[...].reshape(recv.shape[0], recv.shape[2])[:, :rows]), 0)
    sol = fold(dot(table, sol_hot[...]))
    sol = jnp.sum(jnp.where(iota(sol.shape, 0) == sol_row[...], sol, 0.0), axis=0, keepdims=True)
    layer = layer[...]

    def listed(group, column):
        at = rows + column * count
        return jnp.concatenate([recv[device][:, at : at + count] for device in group], 1)

    mine_list, sib_list = listing
    tz, pres, (gs, invs, first, final, coefs) = planes_of()
    depth = len(tz)
    high = tz[0].shape[0]
    own = [coefs]
    start = layer.shape[1]
    value = mine_list * sol[:, :start]
    values = [jnp.where(layer == z, value, 0.0) for z in range(depth)]
    change = gathered(values, rows_hot, lanes_hot, 0, start, high, PARTS)
    y = local_solve([pres[z] - change[z] for z in range(depth)], gs, invs, tz)
    mine = (y[0], y[-1])
    steps = []
    for level in range(levels):
        size = len(lists[level + 1]) * count
        top = level == levels - 1
        if level:
            columns = [2 * level - 2] if top else [2 * level - 2, 2 * level - 1]
            values = [listed(lists[level + 1], c) for c in columns]
        else:
            values = [sib_list[:, i * count : (i + 1) * count] for i in range(2)]
        values = [value * sol[:, start : start + size] for value in values]
        change = gathered(values, rows_hot, lanes_hot, start, size, high, PARTS)
        start += size
        if top:
            other = sib[level][1] - change[0]
            steps.append((mine, (other, other)))
        else:
            other = (sib[level][3] - change[0], sib[level][4] - change[1])
            steps.append((mine, other))
            mine = join_ends(level, own[level], sib[level], mine, other)
            own.append(join_coefs(level, own[level], sib[level]))
    above = below = tzp = jnp.zeros(tz[0].shape, F32)
    place = lax.axis_index("layer")
    for level in range(levels - 1, -1, -1):
        mine, other = steps[level]
        yl, _ = choose(level, mine[1], other[1])
        _, yf_ = choose(level, mine[0], other[0])
        flux = yl - yf_
        if level == levels - 1:
            b, _ = choose(level, own[level][2], sib[level][0])
            _, af_ = choose(level, own[level][0], sib[level][0])
            g = 1.0 / (b + af_)
            before = sib[level][2]
        else:
            _, c, _, _, c_, _, g = pair(level, own[level], sib[level])
            flux = flux + c * above - c_ * below
            before = sib[level][5]
        tzp = jnp.where(place % (2 << level) == 1 << level, before, tzp)
        flux = g * flux
        right = is_right(level)
        above, below = (jnp.where(right, flux, above), jnp.where(right, below, -flux))
    return [y[z] + first[z] * above + final[z] * below for z in range(depth)], above, below, tzp


def pressure_kernel(levels, ready, recv, terms, pres, *refs):
    sib, (tz, kept, tx, prod, _, p, coupled_z, one, *hots) = (refs[:levels], refs[levels:])
    depth, width, _ = pres.shape
    odd = is_right(0, "tile")
    lists = groups_of(levels)
    table_kernel(lists, pres.shape, terms, hots)

    def planes_of():
        tzs, pressures = ([ref[z] for z in range(depth)] for ref in (tz, pres))
        gs, invs, first, final = ([kept[k * depth + z] for z in range(depth)] for k in range(4))
        return tzs, pressures, (gs, invs, first, final, block_ends(first, final, tzs))

    ready(0)
    listing = (prod[...], sib[0][6, 0:1])
    values, above, below, tzp = column_solve(levels, recv, lists, hots, listing, planes_of, sib)
    tzs = [tz[z] for z in range(depth)]
    is_last = lax.axis_index("layer") == (1 << levels) - 1
    for z in range(depth):
        p[z] = values[z]
        one[z] = jnp.where(odd, values[z][0:1], (tx[z] * values[z])[width - 1 :])
        total = above + tzp * values[z] if z == 0 else tzs[z - 1] * values[z - 1]
        if z == depth - 1:
            coupled_z[z] = total + jnp.where(is_last, 0.0, below + tzs[z] * values[z])
        else:
            coupled_z[z] = total + tzs[z] * values[z + 1]
    ready(1)


def edge_kernel(levels, low, high, prod, *refs):
    sib, two = (refs[:levels], refs[levels])
    odd = is_right(0, "tile")
    n = low.shape[0]
    two[pl.ds(0, n)] = jnp.where(odd, high[...], low[...])
    at = n
    for block in sib:
        width = block.shape[1]
        for i in range(min(6, block.shape[0])):
            two[at] = jnp.where(odd, block[i, width - 1 : width], block[i, 0:1])
            at += 1
    two[at] = sib[0][6, 0:1]
    two[at + 1] = jnp.zeros((1, two.shape[2]), F32)
    two[at + 1, :, : prod.shape[1]] = prod[...]


def first_three(kernel, ready, one, two, three, _rhs, _diag, _ty, _binv, *rest):
    kernel(one, two, three, *rest)
    ready(0)


def beyond_kernel(levels, shapes, shape, recv, terms, two, row, *hots):
    depth, width, long = shape
    tiles, layers = (lax.axis_size("tile"), lax.axis_size("layer"))
    tile = lax.axis_index("tile")
    odd = is_right(0, "tile")
    count = 4 * depth + sum(shapes)
    planes = [two[i] for i in range(count)]
    step = jnp.where(odd, layers, -layers)
    lists = [[jnp.clip(device + step, 0, tiles * layers - 1) for device in members] for members in groups_of(levels)]
    table_kernel(lists, shape, terms, hots, jnp.where(odd, 0, width - 1))
    exists = jnp.where(odd, (tile < tiles - 1).astype(F32), (tile > 0).astype(F32)) + jnp.zeros((1, long), F32)
    blocks = []
    at = 4 * depth
    for size in shapes:
        blocks.append([planes[at + i] for i in range(size)])
        at += size

    def planes_of():
        kept = [planes[depth + z] for z in range(depth)]
        tzs = [planes[z] for z in range(depth)]
        found = factors(tzs, [jnp.where(value == 0.0, 1.0, value) for value in kept])
        return tzs, [planes[2 * depth + z] for z in range(depth)], found

    listing = (two[count + 1, :, : terms.shape[2] // 3], two[count])
    values, _, _, _ = column_solve(levels, recv, lists, hots, listing, planes_of, blocks)
    for z in range(depth):
        found = jnp.where(exists > 0.0, values[z], 0.0)
        row[z] = jnp.where(odd, found, found * two[3 * depth + z])


def search_kernel(p, coupled_z, two, one, tx, ty, tz, rhs, column, first_inv, later_inv, s, outer, row_two, row_one, inner):
    depth, width, _ = p.shape
    odd = is_right(0, "tile")
    right = is_right(0)
    row = iota(p.shape[1:], 0)
    for z in range(depth):
        centre = p[z]
        after = jnp.where(odd, two[z], one[z])
        before = jnp.where(odd, one[z], two[z])
        coupled = coupled_z[z] + beside(centre, tx[z], ty[z])
        coupled = coupled + jnp.where(row == 0, before, 0.0) + jnp.where(row == width - 1, tx[z] * after, 0.0)
        remain = [rhs[c, z] - column[c, z] * centre for c in range(3)]
        remain[0] = remain[0] + coupled
        for c in range(3):
            binv = [later_inv[c - 1, d, z] if c else first_inv[0, d, z] for d in range(3)]
            value = binv[0] * remain[0] + binv[1] * remain[1] + binv[2] * remain[2]
            if c == 0:
                value = centre + value
            s[c, z] = value
            tile_rows(value[0:1], (tx[z] * value)[width - 1 :], row_one.at[c, z], row_two.at[c, z])
    for c in range(3):
        top, bottom = (s[c, 0], tz[depth - 1] * s[c, depth - 1])
        inner[c] = jnp.where(right, top, bottom)
        outer[c] = jnp.where(right, bottom, top)


def inner_kernel(ready, s, diag, tz, tx, ty, image):
    depth = s.shape[1]
    for z in range(depth):
        for c in range(3):
            total = beside(s[c, z], tx[z], ty[z])
            if z:
                total = total + tz[z - 1] * s[c, z - 1]
            if z < depth - 1:
                total = total + tz[z] * s[c, z + 1]
            image[c, z] = total
    ready(0)
    for z in range(depth):
        for c in range(3):
            total = diag[c, 0, z] * s[0, z] + diag[c, 1, z] * s[1, z] + diag[c, 2, z] * s[2, z]
            image[c, z] = total - image[c, z]


def image_kernel(part, inner, outer, row_two, row_one, rhs, tz, tx, image, send):
    depth, width = part.shape[1:3]
    right, odd = (is_right(0), is_right(0, "tile"))
    row = iota(part.shape[2:], 0)
    along = power = start = 0.0
    for z in range(depth):
        for c in range(3):
            value = part[c, z]
            if z == 0:
                value = value - jnp.where(right, inner[c], outer[c])
            if z == depth - 1:
                value = value - tz[z] * jnp.where(right, outer[c], inner[c])
            after = jnp.where(odd, row_two[c, z], row_one[c, z])
            before = jnp.where(odd, row_one[c, z], row_two[c, z])
            value = value - jnp.where(row == 0, before, 0.0) - jnp.where(row == width - 1, tx[z] * after, 0.0)
            image[c, z] = value
            given = rhs[c, z]
            along = along + value * given
            power = power + value * value
            start = start + given * given
    along, power, start = (jnp.sum(along), jnp.sum(power), jnp.sum(start))
    omega = along / jnp.where(power > 0.0, power, 1.0)
    square = cross = 0.0
    for z in range(depth):
        for c in range(3):
            value = image[c, z]
            left = rhs[c, z] - omega * value
            square = square + left * left
            cross = cross + left * value
    lane = iota((1, send.shape[2]), 1)
    out = jnp.zeros((1, send.shape[2]), F32)
    for i, value in enumerate((along, power, start, jnp.sum(square), jnp.sum(cross), omega)):
        out = jnp.where(lane == i, value, out)
    send[...] = jnp.broadcast_to(out[:, None], send.shape)


def finish_kernel(recv, s, image, rhs, update, lin_res, ratio):
    sums = recv[...].reshape(recv.shape[0], recv.shape[2])
    whole = jnp.sum(sums, axis=0, keepdims=True)
    omega = whole[:, 0:1] / whole[:, 1:2]
    shift = sums[:, 5:6] - omega
    square = sums[:, 3:4] + 2.0 * shift * sums[:, 4:5] + shift * shift * sums[:, 1:2]
    ratio[...] = jnp.sqrt(jnp.sum(square, axis=0, keepdims=True) / whole[:, 2:3])
    for c in range(3):
        for z in range(s.shape[1]):
            update[c, z] = omega * s[c, z]
            lin_res[c, z] = rhs[c, z] - omega * image[c, z]


def flip(x, level, axis="layer"):
    return lax.ppermute(x, axis, [(i, i ^ (1 << level)) for i in range(lax.axis_size(axis))])


def neighbour(x, axis="layer"):
    pairs = [(i, i + 1) for i in range(1, lax.axis_size(axis) - 1, 2)]
    return lax.ppermute(x, axis, pairs + [(j, i) for i, j in pairs])


def everywhere(x):
    return lax.all_to_all(x, BOTH, split_axis=0, concat_axis=0, tiled=True)


def shards(rhs, weights, block_diag, block_inv, tx, ty, tz, store, cell, front, prod, inverse):
    layers = lax.axis_size("layer")
    devices = lax.axis_size("tile") * layers
    levels = layers.bit_length() - 1
    depth, width, long = tx.shape
    count = cell.shape[0]
    rows = inverse.shape[0]
    lists = layers * count
    cell, front, prod = (cell.reshape(1, -1), front.reshape(1, -1), prod.reshape(1, -1))
    field = vmem(tx.shape)

    def planes(n):
        return vmem((n, width, long))

    hbm_spec = pl.BlockSpec(memory_space=pltpu.HBM)
    given = (cell, front, prod, rhs, weights, tz, store)
    pres, send, ends = pl.pallas_call(
        pres_kernel,
        out_shape=(field, vmem((devices, 1, 3 * count)), planes(7)),
        in_specs=[hbm_spec] * len(given),
        out_specs=(VM,) * 3,
        scratch_shapes=[vmem(a.shape, a.dtype) for a in given] + [pltpu.SemaphoreType.DMA((len(given),))],
        compiler_params=pltpu.CompilerParams(vmem_limit_bytes=LIMIT),
    )(*[pltpu.with_memory_space_constraint(a, pltpu.HBM) for a in given])
    terms = everywhere(send)
    sib, found = ([], [])
    for level in range(levels - 1):
        sib.append(flip(ends, level))
        final = level == levels - 2
        many = (2 if level else 0) + (1 if final else 0)
        outs = (vmem((1, max(1, many) * count)), *((planes(3),) if final else (planes(6), planes(2 * depth))))
        if level == 0:
            rim = vmem((4 * depth, 1, long))
            kept, low, high, *got = call(
                functools.partial(first_join_kernel, final),
                (hbm((4 * depth, width, long)), rim, rim, *outs),
                (ends, sib[-1], pres, tz, store, tx, cell, prod),
                far=range(3, 8),
            )
        else:
            got = call(
                functools.partial(join_kernel, level, final), outs, (ends, sib[-1], answers, cell, prod), far=(3, 4)
            )
        if many:
            found.append(got[0])
        if final:
            face = got[1]
        else:
            ends, answers = got[1:]
    found = found[0] if len(found) == 1 else jnp.concatenate(found, 1)
    terms, face, found = lax.optimization_barrier((terms, face, found))
    sib.append(flip(face, levels - 1))
    chunks = 8
    send = pl.pallas_call(
        front_kernel,
        out_shape=vmem((devices, 1, max(rows + found.shape[1], 3 * count))),
        in_specs=[VM, VM, hbm_spec],
        out_specs=VM,
        scratch_shapes=[vmem(inverse.shape), pltpu.SemaphoreType.DMA((chunks,))],
        compiler_params=pltpu.CompilerParams(vmem_limit_bytes=LIMIT),
    )(terms, found, pltpu.with_memory_space_constraint(inverse, pltpu.HBM))
    sizes = [min(6, block.shape[0]) for block in sib]
    rim = vmem((4 * depth + sum(sizes) + 2, 1, long))
    send, low, high = lax.optimization_barrier((send, low, high))
    (two,) = call(functools.partial(edge_kernel, levels), (rim,), (low, high, prod, *sib))
    sol = everywhere(send)
    two = neighbour(two, "tile")

    def hots(high):
        return (
            vmem((high * long // 128, lists), BF16),
            vmem((128, lists), BF16),
            vmem((rows, lists), BF16),
            vmem((1, lists), I32),
            vmem((1, count), I32),
        )

    at = 3 + levels
    row3 = vmem((depth, 1, long))
    p, coupled_z, one, tz, tx, later_inv = call(
        functools.partial(pressure_kernel, levels),
        (field, field, row3),
        (sol, terms, pres, *sib, tz, kept, tx, prod, block_inv),
        far=range(at, at + 5),
        keep=(at, at + 2, at + 4),
        cut={at + 4: (1, 3)},
        late=(range(at, at + 4), (at + 4,)),
        scratch=hots(width),
    )
    sol, one, terms = lax.optimization_barrier((sol, one, terms))
    one = flip(one, 0, "tile")
    two, rhs, first_column, ty, first_inv = call(
        functools.partial(first_three, functools.partial(beyond_kernel, levels, sizes, (depth, width, long))),
        (row3,),
        (sol, terms, two, rhs, block_diag, ty, block_inv),
        far=(3, 4, 5, 6),
        keep=(3, 4, 5, 6),
        column=(4,),
        cut={6: (0, 1)},
        late=((3, 4, 5, 6),),
        scratch=hots(1),
    )
    row9 = vmem((3, depth, 1, long))
    plane3 = planes(3)
    s, outer, row_two, row_one, inner = call(
        search_kernel,
        (vmem(rhs.shape), plane3, row9, row9, plane3),
        (p, coupled_z, two, one, tx, ty, tz, rhs, first_column, first_inv, later_inv),
    )
    outer, row_two = (neighbour(outer), neighbour(row_two, "tile"))
    row_one, inner = (flip(row_one, 0, "tile"), flip(inner, 0))
    (part,) = call(inner_kernel, (vmem(rhs.shape),), (s, block_diag, tz, tx, ty), far=(1,), late=((1,),))
    image, send = call(
        image_kernel,
        (vmem(rhs.shape), vmem((devices, 1, 128))),
        (part, inner, outer, row_two, row_one, rhs, tz, tx),
    )
    sums = everywhere(send)
    update, lin_res, ratio = call(
        finish_kernel, (hbm(rhs.shape), hbm(rhs.shape), hbm((1, 1))), (sums, s, image, rhs)
    )
    return (update, lin_res, ratio.reshape(()))


def solution(mesh):
    return jax.shard_map(
        shards,
        mesh=mesh,
        in_specs=(
            P(None, "layer", "tile", None),
            P(None, "layer", "tile", None),
            P(None, None, "layer", "tile", None),
            P(None, None, "layer", "tile", None),
            P("layer", "tile", None),
            P("layer", "tile", None),
            P("layer", "tile", None),
            P("layer", "tile", None),
            P(("tile", "layer")),
            P(("tile", "layer")),
            P(("tile", "layer")),
            P(("tile", "layer"), None),
        ),
        out_specs=(P(None, "layer", "tile", None), P(None, "layer", "tile", None), P()),
        check_vma=False,
    )
```

```python
import functools
import jax
import jax.numpy as jnp
from jax import lax
from jax.experimental import pallas as pl
from jax.experimental.pallas import tpu as pltpu
from jax.sharding import PartitionSpec as P

F32 = jnp.float32
BF16 = jnp.bfloat16
I32 = jnp.int32
BOTH = ("tile", "layer")
VM = pl.BlockSpec(memory_space=pltpu.VMEM)
LIMIT = 16 << 20
PARTS = 2


def hbm(shape):
    return jax.ShapeDtypeStruct(shape, F32)


def vmem(shape, dtype=F32):
    return pltpu.VMEM(shape, dtype)


def staged(kernel, where, outs, kept, column, late, *refs):
    count, sems = (len(where), refs[-1])
    held = list(refs[count + outs + len(kept) : -1])
    target_count = sum(where) - len(kept)
    held, extra = (held[:target_count], held[target_count:])
    target = dict(zip(kept, refs[count + outs : count + outs + len(kept)]))
    operands, copies = ([], [])
    for i, far in enumerate(where):
        if far:
            to = target[i] if i in target else held.pop(0)
            part = refs[i].at[:, 0] if i in column else refs[i]
            copies.append(pltpu.make_async_copy(part, to, sems.at[len(copies)]))
            operands.append(to)
        else:
            operands.append(refs[i])
    places = [i for i, far in enumerate(where) if far]
    for copy in copies:
        copy.start()
    for i, copy in zip(places, copies):
        if not any(i in group for group in late):
            copy.wait()

    def ready(k):
        for i, copy in zip(places, copies):
            if i in late[k]:
                copy.wait()

    more = (ready,) if late else ()
    kernel(*more, *operands, *refs[count : count + outs], *extra)


def call(kernel, outs, args, far=(), keep=(), column=(), late=(), scratch=(), limit=LIMIT):
    where = [i in far for i in range(len(args))]
    spaces = [pltpu.HBM if w else pltpu.VMEM for w in where]
    shapes = [a.shape[:1] + a.shape[2:] if i in column else a.shape for i, a in enumerate(args)]
    every = (*outs, *(vmem(shapes[i], args[i].dtype) for i in keep))
    return pl.pallas_call(
        functools.partial(staged, kernel, where, len(outs), tuple(keep), tuple(column), tuple(late)),
        out_shape=every,
        in_specs=[pl.BlockSpec(memory_space=s) for s in spaces],
        out_specs=(VM,) * len(every),
        scratch_shapes=[vmem(shapes[i], a.dtype) for i, a in enumerate(args) if where[i] and i not in keep]
        + [*scratch, pltpu.SemaphoreType.DMA((max(1, sum(where)),))],
        compiler_params=pltpu.CompilerParams(vmem_limit_bytes=limit),
    )(*[pltpu.with_memory_space_constraint(a, s) for a, s in zip(args, spaces)])


def iota(shape, dim):
    return lax.broadcasted_iota(I32, shape, dim)


def split(x):
    one = x.astype(BF16)
    rest = x - one.astype(F32)
    two = rest.astype(BF16)
    three = (rest - two.astype(F32)).astype(BF16)
    return [one, two, three]


def fold(x, parts=3):
    n = x.shape[0] // parts
    total = x[(parts - 1) * n :]
    for i in range(parts - 2, -1, -1):
        total = x[i * n : (i + 1) * n] + total
    return total


def onehot(index, size):
    return jnp.where(iota((size, index.shape[1]), 0) == index, 1.0, 0.0)


def dot(a, b):
    return lax.dot_general(a, b, (((1,), (0,)), ((), ())), preferred_element_type=F32)


def dot_nt(a, b):
    return lax.dot_general(a, b, (((1,), (1,)), ((), ())), preferred_element_type=F32)


def pick(tables, hi, hot):
    rows = tables[0].shape[0]
    parts = jnp.concatenate([p for table in tables for p in split(table)[:PARTS]], 0)
    got = dot(parts, hot)
    mask = onehot(hi, rows)
    n = PARTS * rows
    return [jnp.sum(fold(got[i * n : (i + 1) * n], PARTS) * mask, axis=0, keepdims=True) for i in range(len(tables))]


def pres_kernel(cell_in, front_in, prod_in, rhs_in, wts_in, tz_in, store_in, pres, send, ends, *scratch):
    (cell, front, prod, rhs, wts, tz, store), sems = scratch[:-1], scratch[-1]
    pairs = ((cell_in, cell), (front_in, front), (prod_in, prod), (tz_in, tz), (store_in, store), (rhs_in, rhs), (wts_in, wts))
    copies = [pltpu.make_async_copy(a, b, sems.at[i]) for i, (a, b) in enumerate(pairs)]
    for copy in copies:
        copy.start()
    for copy in copies[:3]:
        copy.wait()
    depth, width, long = pres.shape
    where = cell[...]
    hot = onehot(lax.rem(where, long), long).astype(BF16)
    for copy in copies[3:5]:
        copy.wait()
    tzs = [tz[z] for z in range(depth)]
    gs, invs, first, final, coefs = factors(tzs, [store[z] for z in range(depth)])
    row = lax.div(where, long)
    kf, kl = pick([jnp.concatenate(first, 0), jnp.concatenate(final, 0)], row, hot)
    for copy in copies[5:]:
        copy.wait()
    for z in range(depth):
        pres[z] = wts[0, z] * rhs[0, z] + wts[1, z] * rhs[1, z] + wts[2, z] * rhs[2, z]
    (found,) = pick([pres[...].reshape(depth * width, long)], row, hot)
    both = jnp.concatenate([prod[...] * found, front[...].astype(F32), where.astype(F32)], 1)
    send[...] = jnp.broadcast_to(both[:, None], send.shape)
    y = local_solve([pres[z] for z in range(depth)], gs, invs, tzs)
    for i, value in enumerate((*coefs, y[0], y[-1], tzs[-1])):
        ends[i] = value
    ends[6] = jnp.zeros((width, long), F32)
    ends[6, 0:1, : 2 * where.shape[1]] = jnp.concatenate([prod[...] * kf, prod[...] * kl], 1)


def is_right(level, axis="layer"):
    return (lax.axis_index(axis) >> level) % 2 == 1


def choose(level, mine, other, axis="layer"):
    right = is_right(level, axis)
    return (jnp.where(right, other, mine), jnp.where(right, mine, other))


def local_solve(rhs, upper, inv, tz):
    depth = len(rhs)
    y = [rhs[0] * inv[0]]
    for z in range(1, depth):
        y.append((rhs[z] + tz[z - 1] * y[-1]) * inv[z])
    for z in range(depth - 2, -1, -1):
        y[z] = y[z] + upper[z] * y[z + 1]
    return y


def factors(tz, store):
    depth = len(tz)
    gs, invs = ([], [])
    own = None
    for z in range(depth):
        own = store[z] if z == 0 else store[z] + gs[-1] * own
        invs.append(1.0 / (own + tz[z] if z < depth - 1 else own))
        gs.append(tz[z] * invs[-1])
    first = [invs[0]]
    for z in range(1, depth):
        first.append(tz[z - 1] * first[-1] * invs[z])
    final = [None] * depth
    final[-1] = invs[-1]
    for z in range(depth - 2, -1, -1):
        first[z] = first[z] + gs[z] * first[z + 1]
        final[z] = gs[z] * final[z + 1]
    return gs, invs, first, final, block_ends(first, final, tz)


def block_ends(first, final, tz):
    return (first[0], first[-1], final[-1] + 1.0 / jnp.maximum(tz[-1], 1e-30))


def pair(level, own, sib):
    af, af_ = choose(level, own[0], sib[0])
    c, c_ = choose(level, own[1], sib[1])
    b, b_ = choose(level, own[2], sib[2])
    return af, c, b, af_, c_, b_, 1.0 / (b + af_)


def join_coefs(level, own, sib):
    af, c, _, _, c_, b_, g = pair(level, own, sib)
    return (af - c * c * g, c * c_ * g, b_ - c_ * c_ * g)


def join_ends(level, own, sib, mine, other):
    _, c, _, _, c_, _, g = pair(level, own, sib)
    yf, yf_ = choose(level, mine[0], other[0])
    yl, yl_ = choose(level, mine[1], other[1])
    flux = g * (yl - yf_)
    return (yf - c * flux, yl_ + c_ * flux)


def first_join_kernel(final, own, sib, pres, tz, store, tx, cell, prod, kept, low, high, *outs):
    depth, width, _ = tz.shape
    for k, ref in enumerate((tz, store, pres, tx)):
        for z in range(depth):
            low[k * depth + z] = ref[z, 0:1]
            high[k * depth + z] = ref[z, width - 1 : width]
    gs, invs, first, last, _ = factors([tz[z] for z in range(depth)], [store[z] for z in range(depth)])
    for i, value in enumerate(gs + invs + first + last):
        kept[i] = value
    join(0, final, own, sib, first + last, cell, prod, *outs)


def join_kernel(level, final, own, sib, answers, cell, prod, *outs):
    join(level, final, own, sib, [answers[i] for i in range(answers.shape[0])], cell, prod, *outs)


def join(level, final, own, sib, answers, cell, prod, found, *outs):
    depth = len(answers) // 2
    width, long = answers[0].shape
    _, c, _, _, c_, _, g = pair(level, own, sib)
    first, both, last = join_coefs(level, own, sib)
    yf, yl = join_ends(level, own, sib, (own[3], own[4]), (sib[3], sib[4]))
    lower = choose(level, own[5], sib[5])[1]
    right, later = (is_right(level), is_right(level + 1))
    cg, cg_ = (c * g, c_ * g)
    tops, bottoms = ([], [])
    for z in range(depth):
        kf, kl = (answers[z], answers[depth + z])
        tops.append(jnp.where(right, cg * kf, kf - cg * kl))
        bottoms.append(jnp.where(right, kl - cg_ * kf, cg_ * kl))
    tables = [answers[:depth], answers[depth:]] if level else []
    if final:
        (face,) = outs
        face[0], face[1] = (jnp.where(later, first, last), jnp.where(later, yf, yl))
        face[2] = lower
        tables.append([jnp.where(later, tops[z], bottoms[z]) for z in range(depth)])
    else:
        out, more = outs
        for i, value in enumerate((first, both, last, yf, yl, lower)):
            out[i] = value
        for i, value in enumerate(tops + bottoms):
            more[i] = value
    if tables:
        where = cell[...]
        hot = onehot(lax.rem(where, long), long).astype(BF16)
        got = pick([jnp.concatenate(t, 0) for t in tables], lax.div(where, long), hot)
        found[...] = jnp.concatenate([prod[...] * value for value in got], 1)
    else:
        found[...] = jnp.zeros(found.shape, F32)


def groups_of(levels):
    layers = lax.axis_size("layer")
    l = lax.axis_index("layer")
    base = lax.axis_index("tile") * layers
    out = [[base + l]]
    for level in range(levels):
        out.append([base + (((l >> level) ^ 1) << level) + i for i in range(1 << level)])
    return out


def front_kernel(recv, found, inverse, send, held, sems):
    devices = recv.shape[0]
    count = recv.shape[2] // 3
    rows, length = inverse.shape
    lanes = 128
    chunks = sems.shape[0]
    wide = length // chunks
    found = found[...]
    copies = [
        pltpu.make_async_copy(inverse.at[:, pl.ds(i * wide, wide)], held.at[:, pl.ds(i * wide, wide)], sems.at[i])
        for i in range(chunks)
    ]
    for copy in copies:
        copy.start()
    terms, index = (recv[:, 0, :count], recv[:, 0, count : 2 * count])
    high = jnp.floor(index * (1.0 / lanes))
    low = index - high * lanes
    parts = [p.astype(F32) for p in split(terms)[:PARTS]]
    row_of = iota((length // lanes, count), 0).astype(F32)
    lane_of = iota((lanes, count), 0).astype(F32)
    flipped = jnp.zeros((lanes, PARTS * (length // lanes)), F32)
    for d in range(devices):
        hit = row_of == high[d : d + 1]
        left = jnp.concatenate([jnp.where(hit, p[d : d + 1], 0.0).astype(BF16) for p in parts], 0)
        right = jnp.where(lane_of == low[d : d + 1], 1.0, 0.0).astype(BF16)
        flipped = flipped + dot_nt(right, left)
    total = fold(jnp.transpose(flipped), PARTS)
    acc = jnp.zeros((rows, lanes), F32)
    for i in range(chunks):
        copies[i].wait()
        for r in range(i * wide // lanes, (i + 1) * wide // lanes):
            acc = acc + held[:, r * lanes : (r + 1) * lanes] * total[r : r + 1]
    out = jnp.transpose(jnp.broadcast_to(jnp.sum(acc, axis=1, keepdims=True), (rows, lanes)))
    pad = send.shape[2] - out.shape[1] - found.shape[1]
    pieces = [out[0:1], found] + ([jnp.zeros((1, pad), F32)] if pad else [])
    send[...] = jnp.broadcast_to(jnp.concatenate(pieces, 1)[:, None], send.shape)


def gathered(values, rows_hot, lanes_hot, start, size, ext, parts):
    hot = lanes_hot[:, start : start + size]
    pieces = [hot * p for v in values for p in split(v)[:parts]]
    got = dot_nt(rows_hot[:, start : start + size], jnp.concatenate(pieces, 0))
    planes = []
    lanes = hot.shape[0]
    for i in range(len(values)):
        plane = got[:, i * parts * lanes : (i * parts + 1) * lanes]
        for k in range(1, parts):
            j = i * parts + k
            plane = plane + got[:, j * lanes : (j + 1) * lanes]
        planes.append(jnp.concatenate([plane[r : r + ext] for r in range(0, plane.shape[0], ext)], 1))
    return planes


def beside(centre, tx, ty):
    width, long = centre.shape
    row, col = (iota(centre.shape, 0), iota(centre.shape, 1))
    total = tx * jnp.where(row == width - 1, 0.0, pltpu.roll(centre, width - 1, 0))
    total = total + jnp.where(row == 0, 0.0, pltpu.roll(tx * centre, 1, 0))
    total = total + ty * jnp.where(col == long - 1, 0.0, pltpu.roll(centre, long - 1, 1))
    return total + jnp.where(col == 0, 0.0, pltpu.roll(ty * centre, 1, 1))


def tile_rows(first, last, one, two):
    odd = is_right(0, "tile")
    one[...] = jnp.where(odd, first, last)
    two[...] = jnp.where(odd, last, first)


def table_kernel(lists, shape, terms, hots, only=None):
    _, width, long = shape
    rows_hot, lanes_hot, sol_hot, sol_row, layer = hots
    lanes = 128
    rows = sol_hot.shape[0]
    count = terms.shape[2] // 3
    at = 0
    for members in lists:
        for device in members:
            entry = terms[device]
            index = entry[:, count : 2 * count].astype(I32)
            cell = entry[:, 2 * count :].astype(I32)
            y, x = lax.rem(cell, long), lax.rem(lax.div(cell, long), width)
            if only is None:
                row = lax.div(y, lanes) * width + x
            else:
                row = jnp.where(x == only, lax.div(y, lanes), -1)
            here = pl.ds(at, count)
            rows_hot[:, here] = onehot(row, rows_hot.shape[0]).astype(BF16)
            lanes_hot[:, here] = onehot(lax.rem(y, lanes), lanes).astype(BF16)
            sol_hot[:, here] = onehot(lax.rem(index, rows), rows).astype(BF16)
            sol_row[:, here] = lax.div(index, rows)
            if at < layer.shape[1]:
                layer[:, here] = lax.div(cell, long * width)
            at += count


def column_solve(levels, recv, lists, hots, listing, planes_of, sib):
    rows_hot, lanes_hot, sol_hot, sol_row, layer = hots
    rows, count = (sol_hot.shape[0], layer.shape[1])
    table = jnp.concatenate(split(recv[...].reshape(recv.shape[0], recv.shape[2])[:, :rows]), 0)
    sol = fold(dot(table, sol_hot[...]))
    sol = jnp.sum(jnp.where(iota(sol.shape, 0) == sol_row[...], sol, 0.0), axis=0, keepdims=True)
    layer = layer[...]

    def listed(group, column):
        at = rows + column * count
        return jnp.concatenate([recv[device][:, at : at + count] for device in group], 1)

    mine_list, sib_list = listing
    tz, pres, (gs, invs, first, final, coefs) = planes_of()
    depth = len(tz)
    high = tz[0].shape[0]
    own = [coefs]
    start = layer.shape[1]
    value = mine_list * sol[:, :start]
    values = [jnp.where(layer == z, value, 0.0) for z in range(depth)]
    change = gathered(values, rows_hot, lanes_hot, 0, start, high, PARTS)
    y = local_solve([pres[z] - change[z] for z in range(depth)], gs, invs, tz)
    mine = (y[0], y[-1])
    steps = []
    for level in range(levels):
        size = len(lists[level + 1]) * count
        top = level == levels - 1
        if level:
            columns = [2 * level - 2] if top else [2 * level - 2, 2 * level - 1]
            values = [listed(lists[level + 1], c) for c in columns]
        else:
            values = [sib_list[:, i * count : (i + 1) * count] for i in range(2)]
        values = [value * sol[:, start : start + size] for value in values]
        change = gathered(values, rows_hot, lanes_hot, start, size, high, PARTS)
        start += size
        if top:
            other = sib[level][1] - change[0]
            steps.append((mine, (other, other)))
        else:
            other = (sib[level][3] - change[0], sib[level][4] - change[1])
            steps.append((mine, other))
            mine = join_ends(level, own[level], sib[level], mine, other)
            own.append(join_coefs(level, own[level], sib[level]))
    above = below = tzp = jnp.zeros(tz[0].shape, F32)
    place = lax.axis_index("layer")
    for level in range(levels - 1, -1, -1):
        mine, other = steps[level]
        yl, _ = choose(level, mine[1], other[1])
        _, yf_ = choose(level, mine[0], other[0])
        flux = yl - yf_
        if level == levels - 1:
            b, _ = choose(level, own[level][2], sib[level][0])
            _, af_ = choose(level, own[level][0], sib[level][0])
            g = 1.0 / (b + af_)
            before = sib[level][2]
        else:
            _, c, _, _, c_, _, g = pair(level, own[level], sib[level])
            flux = flux + c * above - c_ * below
            before = sib[level][5]
        tzp = jnp.where(place % (2 << level) == 1 << level, before, tzp)
        flux = g * flux
        right = is_right(level)
        above, below = (jnp.where(right, flux, above), jnp.where(right, below, -flux))
    return [y[z] + first[z] * above + final[z] * below for z in range(depth)], above, below, tzp


def pressure_kernel(levels, ready, recv, pres, *refs):
    hots, sib, (tz, kept, tx, prod, _, p, coupled_z, one) = (refs[:5], refs[5 : 5 + levels], refs[5 + levels :])
    depth, width, _ = pres.shape
    odd = is_right(0, "tile")
    lists = groups_of(levels)

    def planes_of():
        tzs, pressures = ([ref[z] for z in range(depth)] for ref in (tz, pres))
        gs, invs, first, final = ([kept[k * depth + z] for z in range(depth)] for k in range(4))
        return tzs, pressures, (gs, invs, first, final, block_ends(first, final, tzs))

    ready(0)
    listing = (prod[...], sib[0][6, 0:1])
    values, above, below, tzp = column_solve(levels, recv, lists, hots, listing, planes_of, sib)
    tzs = [tz[z] for z in range(depth)]
    is_last = lax.axis_index("layer") == (1 << levels) - 1
    for z in range(depth):
        p[z] = values[z]
        one[z] = jnp.where(odd, values[z][0:1], (tx[z] * values[z])[width - 1 :])
        total = above + tzp * values[z] if z == 0 else tzs[z - 1] * values[z - 1]
        if z == depth - 1:
            coupled_z[z] = total + jnp.where(is_last, 0.0, below + tzs[z] * values[z])
        else:
            coupled_z[z] = total + tzs[z] * values[z + 1]
    ready(1)


def edge_kernel(levels, shape, low, high, prod, terms, *refs):
    sib, two, hots = (refs[:levels], refs[levels], refs[levels + 1 :])
    table_kernel(groups_of(levels), shape, terms, hots)
    odd = is_right(0, "tile")
    n = low.shape[0]
    two[pl.ds(0, n)] = jnp.where(odd, high[...], low[...])
    at = n
    for block in sib:
        width = block.shape[1]
        for i in range(min(6, block.shape[0])):
            two[at] = jnp.where(odd, block[i, width - 1 : width], block[i, 0:1])
            at += 1
    two[at] = sib[0][6, 0:1]
    two[at + 1] = jnp.zeros((1, two.shape[2]), F32)
    two[at + 1, :, : prod.shape[1]] = prod[...]


def first_three(kernel, ready, one, two, three, _rhs, _diag, _ty, *rest):
    kernel(one, two, three, *rest)
    ready(0)


def beyond_kernel(levels, shapes, shape, recv, terms, two, row, *hots):
    depth, width, long = shape
    tiles, layers = (lax.axis_size("tile"), lax.axis_size("layer"))
    tile = lax.axis_index("tile")
    odd = is_right(0, "tile")
    count = 4 * depth + sum(shapes)
    planes = [two[i] for i in range(count)]
    step = jnp.where(odd, layers, -layers)
    lists = [[jnp.clip(device + step, 0, tiles * layers - 1) for device in members] for members in groups_of(levels)]
    table_kernel(lists, shape, terms, hots, jnp.where(odd, 0, width - 1))
    exists = jnp.where(odd, (tile < tiles - 1).astype(F32), (tile > 0).astype(F32)) + jnp.zeros((1, long), F32)
    blocks = []
    at = 4 * depth
    for size in shapes:
        blocks.append([planes[at + i] for i in range(size)])
        at += size

    def planes_of():
        kept = [planes[depth + z] for z in range(depth)]
        tzs = [planes[z] for z in range(depth)]
        found = factors(tzs, [jnp.where(value == 0.0, 1.0, value) for value in kept])
        return tzs, [planes[2 * depth + z] for z in range(depth)], found

    listing = (two[count + 1, :, : terms.shape[2] // 3], two[count])
    values, _, _, _ = column_solve(levels, recv, lists, hots, listing, planes_of, blocks)
    for z in range(depth):
        found = jnp.where(exists > 0.0, values[z], 0.0)
        row[z] = jnp.where(odd, found, found * two[3 * depth + z])


def search_kernel(p, coupled_z, two, one, tx, ty, tz, rhs, column, binv, s, outer, row_two, row_one, inner):
    depth, width, _ = p.shape
    odd = is_right(0, "tile")
    right = is_right(0)
    row = iota(p.shape[1:], 0)
    for z in range(depth):
        centre = p[z]
        after = jnp.where(odd, two[z], one[z])
        before = jnp.where(odd, one[z], two[z])
        coupled = coupled_z[z] + beside(centre, tx[z], ty[z])
        coupled = coupled + jnp.where(row == 0, before, 0.0) + jnp.where(row == width - 1, tx[z] * after, 0.0)
        remain = [rhs[c, z] - column[c, z] * centre for c in range(3)]
        remain[0] = remain[0] + coupled
        for c in range(3):
            value = binv[c, 0, z] * remain[0] + binv[c, 1, z] * remain[1] + binv[c, 2, z] * remain[2]
            if c == 0:
                value = centre + value
            s[c, z] = value
            tile_rows(value[0:1], (tx[z] * value)[width - 1 :], row_one.at[c, z], row_two.at[c, z])
    for c in range(3):
        top, bottom = (s[c, 0], tz[depth - 1] * s[c, depth - 1])
        inner[c] = jnp.where(right, top, bottom)
        outer[c] = jnp.where(right, bottom, top)


def inner_kernel(ready, s, diag, tz, tx, ty, image):
    depth = s.shape[1]
    for z in range(depth):
        for c in range(3):
            total = beside(s[c, z], tx[z], ty[z])
            if z:
                total = total + tz[z - 1] * s[c, z - 1]
            if z < depth - 1:
                total = total + tz[z] * s[c, z + 1]
            image[c, z] = total
    ready(0)
    for z in range(depth):
        for c in range(3):
            total = diag[c, 0, z] * s[0, z] + diag[c, 1, z] * s[1, z] + diag[c, 2, z] * s[2, z]
            image[c, z] = total - image[c, z]


def image_kernel(part, inner, outer, row_two, row_one, rhs, tz, tx, image, send):
    depth, width = part.shape[1:3]
    right, odd = (is_right(0), is_right(0, "tile"))
    row = iota(part.shape[2:], 0)
    along = power = start = 0.0
    for z in range(depth):
        for c in range(3):
            value = part[c, z]
            if z == 0:
                value = value - jnp.where(right, inner[c], outer[c])
            if z == depth - 1:
                value = value - tz[z] * jnp.where(right, outer[c], inner[c])
            after = jnp.where(odd, row_two[c, z], row_one[c, z])
            before = jnp.where(odd, row_one[c, z], row_two[c, z])
            value = value - jnp.where(row == 0, before, 0.0) - jnp.where(row == width - 1, tx[z] * after, 0.0)
            image[c, z] = value
            given = rhs[c, z]
            along = along + value * given
            power = power + value * value
            start = start + given * given
    along, power, start = (jnp.sum(along), jnp.sum(power), jnp.sum(start))
    omega = along / jnp.where(power > 0.0, power, 1.0)
    square = cross = 0.0
    for z in range(depth):
        for c in range(3):
            value = image[c, z]
            left = rhs[c, z] - omega * value
            square = square + left * left
            cross = cross + left * value
    lane = iota((1, send.shape[2]), 1)
    out = jnp.zeros((1, send.shape[2]), F32)
    for i, value in enumerate((along, power, start, jnp.sum(square), jnp.sum(cross), omega)):
        out = jnp.where(lane == i, value, out)
    send[...] = jnp.broadcast_to(out[:, None], send.shape)


def finish_kernel(recv, s, image, rhs, update, lin_res, ratio):
    sums = recv[...].reshape(recv.shape[0], recv.shape[2])
    whole = jnp.sum(sums, axis=0, keepdims=True)
    omega = whole[:, 0:1] / whole[:, 1:2]
    shift = sums[:, 5:6] - omega
    square = sums[:, 3:4] + 2.0 * shift * sums[:, 4:5] + shift * shift * sums[:, 1:2]
    ratio[...] = jnp.sqrt(jnp.sum(square, axis=0, keepdims=True) / whole[:, 2:3])
    for c in range(3):
        for z in range(s.shape[1]):
            update[c, z] = omega * s[c, z]
            lin_res[c, z] = rhs[c, z] - omega * image[c, z]


def flip(x, level, axis="layer"):
    return lax.ppermute(x, axis, [(i, i ^ (1 << level)) for i in range(lax.axis_size(axis))])


def neighbour(x, axis="layer"):
    pairs = [(i, i + 1) for i in range(1, lax.axis_size(axis) - 1, 2)]
    return lax.ppermute(x, axis, pairs + [(j, i) for i, j in pairs])


def everywhere(x):
    return lax.all_to_all(x, BOTH, split_axis=0, concat_axis=0, tiled=True)


def shards(rhs, weights, block_diag, block_inv, tx, ty, tz, store, cell, front, prod, inverse):
    layers = lax.axis_size("layer")
    devices = lax.axis_size("tile") * layers
    levels = layers.bit_length() - 1
    depth, width, long = tx.shape
    count = cell.shape[0]
    rows = inverse.shape[0]
    lists = layers * count
    cell, front, prod = (cell.reshape(1, -1), front.reshape(1, -1), prod.reshape(1, -1))
    field = vmem(tx.shape)

    def planes(n):
        return vmem((n, width, long))

    hbm_spec = pl.BlockSpec(memory_space=pltpu.HBM)
    given = (cell, front, prod, rhs, weights, tz, store)
    pres, send, ends = pl.pallas_call(
        pres_kernel,
        out_shape=(field, vmem((devices, 1, 3 * count)), planes(7)),
        in_specs=[hbm_spec] * len(given),
        out_specs=(VM,) * 3,
        scratch_shapes=[vmem(a.shape, a.dtype) for a in given] + [pltpu.SemaphoreType.DMA((len(given),))],
        compiler_params=pltpu.CompilerParams(vmem_limit_bytes=LIMIT),
    )(*[pltpu.with_memory_space_constraint(a, pltpu.HBM) for a in given])
    terms = everywhere(send)
    sib, found = ([], [])
    for level in range(levels - 1):
        sib.append(flip(ends, level))
        final = level == levels - 2
        many = (2 if level else 0) + (1 if final else 0)
        outs = (vmem((1, max(1, many) * count)), *((planes(3),) if final else (planes(6), planes(2 * depth))))
        if level == 0:
            rim = vmem((4 * depth, 1, long))
            kept, low, high, *got = call(
                functools.partial(first_join_kernel, final),
                (hbm((4 * depth, width, long)), rim, rim, *outs),
                (ends, sib[-1], pres, tz, store, tx, cell, prod),
                far=range(3, 8),
            )
        else:
            got = call(
                functools.partial(join_kernel, level, final), outs, (ends, sib[-1], answers, cell, prod), far=(3, 4)
            )
        if many:
            found.append(got[0])
        if final:
            face = got[1]
        else:
            ends, answers = got[1:]
    found = found[0] if len(found) == 1 else jnp.concatenate(found, 1)
    terms, face, found = lax.optimization_barrier((terms, face, found))
    sib.append(flip(face, levels - 1))
    chunks = 8
    send = pl.pallas_call(
        front_kernel,
        out_shape=vmem((devices, 1, max(rows + found.shape[1], 3 * count))),
        in_specs=[VM, VM, hbm_spec],
        out_specs=VM,
        scratch_shapes=[vmem(inverse.shape), pltpu.SemaphoreType.DMA((chunks,))],
        compiler_params=pltpu.CompilerParams(vmem_limit_bytes=LIMIT),
    )(terms, found, pltpu.with_memory_space_constraint(inverse, pltpu.HBM))
    sizes = [min(6, block.shape[0]) for block in sib]
    rim = vmem((4 * depth + sum(sizes) + 2, 1, long))
    send, low, high = lax.optimization_barrier((send, low, high))

    def hots(high):
        return (
            vmem((high * long // 128, lists), BF16),
            vmem((128, lists), BF16),
            vmem((rows, lists), BF16),
            vmem((1, lists), I32),
            vmem((1, count), I32),
        )

    two, *made = call(
        functools.partial(edge_kernel, levels, (depth, width, long)),
        (rim, *hots(width)),
        (low, high, prod, terms, *sib),
    )
    sol = everywhere(send)
    two = neighbour(two, "tile")
    at = 7 + levels
    row3 = vmem((depth, 1, long))
    p, coupled_z, one, tz, tx, block_inv = call(
        functools.partial(pressure_kernel, levels),
        (field, field, row3),
        (sol, pres, *made, *sib, tz, kept, tx, prod, block_inv),
        far=range(at, at + 5),
        keep=(at, at + 2, at + 4),
        late=(range(at, at + 4), (at + 4,)),
    )
    sol, one, terms = lax.optimization_barrier((sol, one, terms))
    one = flip(one, 0, "tile")
    two, rhs, first_column, ty = call(
        functools.partial(first_three, functools.partial(beyond_kernel, levels, sizes, (depth, width, long))),
        (row3,),
        (sol, terms, two, rhs, block_diag, ty),
        far=(3, 4, 5),
        keep=(3, 4, 5),
        column=(4,),
        late=((3, 4, 5),),
        scratch=hots(1),
    )
    row9 = vmem((3, depth, 1, long))
    plane3 = planes(3)
    s, outer, row_two, row_one, inner = call(
        search_kernel,
        (vmem(rhs.shape), plane3, row9, row9, plane3),
        (p, coupled_z, two, one, tx, ty, tz, rhs, first_column, block_inv),
    )
    outer, row_two = (neighbour(outer), neighbour(row_two, "tile"))
    row_one, inner = (flip(row_one, 0, "tile"), flip(inner, 0))
    (part,) = call(inner_kernel, (vmem(rhs.shape),), (s, block_diag, tz, tx, ty), far=(1,), late=((1,),))
    image, send = call(
        image_kernel,
        (vmem(rhs.shape), vmem((devices, 1, 128))),
        (part, inner, outer, row_two, row_one, rhs, tz, tx),
    )
    sums = everywhere(send)
    update, lin_res, ratio = call(
        finish_kernel, (hbm(rhs.shape), hbm(rhs.shape), hbm((1, 1))), (sums, s, image, rhs)
    )
    return (update, lin_res, ratio.reshape(()))


def solution(mesh):
    return jax.shard_map(
        shards,
        mesh=mesh,
        in_specs=(
            P(None, "layer", "tile", None),
            P(None, "layer", "tile", None),
            P(None, None, "layer", "tile", None),
            P(None, None, "layer", "tile", None),
            P("layer", "tile", None),
            P("layer", "tile", None),
            P("layer", "tile", None),
            P("layer", "tile", None),
            P(("tile", "layer")),
            P(("tile", "layer")),
            P(("tile", "layer")),
            P(("tile", "layer"), None),
        ),
        out_specs=(P(None, "layer", "tile", None), P(None, "layer", "tile", None), P()),
        check_vma=False,
    )
```

```python
import functools
import jax
import jax.numpy as jnp
from jax import lax
from jax.experimental import pallas as pl
from jax.experimental.pallas import tpu as pltpu
from jax.sharding import PartitionSpec as P

F32 = jnp.float32
BF16 = jnp.bfloat16
I32 = jnp.int32
BOTH = ("tile", "layer")
VM = pl.BlockSpec(memory_space=pltpu.VMEM)
LIMIT = 16 << 20
PARTS = 2


def hbm(shape):
    return jax.ShapeDtypeStruct(shape, F32)


def vmem(shape, dtype=F32):
    return pltpu.VMEM(shape, dtype)


def staged(kernel, where, outs, kept, column, cut, late, *refs):
    count, sems = (len(where), refs[-1])
    held = list(refs[count + outs + len(kept) : -1])
    target_count = sum(where) - len(kept)
    held, extra = (held[:target_count], held[target_count:])
    target = dict(zip(kept, refs[count + outs : count + outs + len(kept)]))
    operands, copies = ([], [])
    for i, far in enumerate(where):
        if far:
            to = target[i] if i in target else held.pop(0)
            part = refs[i].at[:, 0] if i in column else refs[i].at[cut[i][0] : cut[i][1]] if i in cut else refs[i]
            copies.append(pltpu.make_async_copy(part, to, sems.at[len(copies)]))
            operands.append(to)
        else:
            operands.append(refs[i])
    places = [i for i, far in enumerate(where) if far]
    for copy in copies:
        copy.start()
    for i, copy in zip(places, copies):
        if not any(i in group for group in late):
            copy.wait()

    def ready(k):
        for i, copy in zip(places, copies):
            if i in late[k]:
                copy.wait()

    more = (ready,) if late else ()
    kernel(*more, *operands, *refs[count : count + outs], *extra)


def call(kernel, outs, args, far=(), keep=(), column=(), cut={}, late=(), scratch=(), limit=LIMIT):
    where = [i in far for i in range(len(args))]
    spaces = [pltpu.HBM if w else pltpu.VMEM for w in where]
    shapes = [a.shape[:1] + a.shape[2:] if i in column else a.shape for i, a in enumerate(args)]
    shapes = [(cut[i][1] - cut[i][0], *a[1:]) if i in cut else a for i, a in enumerate(shapes)]
    every = (*outs, *(vmem(shapes[i], args[i].dtype) for i in keep))
    return pl.pallas_call(
        functools.partial(staged, kernel, where, len(outs), tuple(keep), tuple(column), cut, tuple(late)),
        out_shape=every,
        in_specs=[pl.BlockSpec(memory_space=s) for s in spaces],
        out_specs=(VM,) * len(every),
        scratch_shapes=[vmem(shapes[i], a.dtype) for i, a in enumerate(args) if where[i] and i not in keep]
        + [*scratch, pltpu.SemaphoreType.DMA((max(1, sum(where)),))],
        compiler_params=pltpu.CompilerParams(vmem_limit_bytes=limit),
    )(*[pltpu.with_memory_space_constraint(a, s) for a, s in zip(args, spaces)])


def iota(shape, dim):
    return lax.broadcasted_iota(I32, shape, dim)


def split(x):
    one = x.astype(BF16)
    rest = x - one.astype(F32)
    two = rest.astype(BF16)
    three = (rest - two.astype(F32)).astype(BF16)
    return [one, two, three]


def fold(x, parts=3):
    n = x.shape[0] // parts
    total = x[(parts - 1) * n :]
    for i in range(parts - 2, -1, -1):
        total = x[i * n : (i + 1) * n] + total
    return total


def onehot(index, size):
    return jnp.where(iota((size, index.shape[1]), 0) == index, 1.0, 0.0)


def dot(a, b):
    return lax.dot_general(a, b, (((1,), (0,)), ((), ())), preferred_element_type=F32)


def dot_nt(a, b):
    return lax.dot_general(a, b, (((1,), (1,)), ((), ())), preferred_element_type=F32)


def pick(tables, hi, hot):
    rows = tables[0].shape[0]
    parts = jnp.concatenate([p for table in tables for p in split(table)[:PARTS]], 0)
    got = dot(parts, hot)
    mask = onehot(hi, rows)
    n = PARTS * rows
    return [jnp.sum(fold(got[i * n : (i + 1) * n], PARTS) * mask, axis=0, keepdims=True) for i in range(len(tables))]


def pres_kernel(cell_in, front_in, prod_in, rhs_in, wts_in, tz_in, store_in, pres, send, ends, *scratch):
    (cell, front, prod, rhs, wts, tz, store), sems = scratch[:-1], scratch[-1]
    pairs = ((cell_in, cell), (front_in, front), (prod_in, prod), (tz_in, tz), (store_in, store), (rhs_in, rhs), (wts_in, wts))
    copies = [pltpu.make_async_copy(a, b, sems.at[i]) for i, (a, b) in enumerate(pairs)]
    for copy in copies:
        copy.start()
    for copy in copies[:3]:
        copy.wait()
    depth, width, long = pres.shape
    where = cell[...]
    hot = onehot(lax.rem(where, long), long).astype(BF16)
    for copy in copies[3:5]:
        copy.wait()
    tzs = [tz[z] for z in range(depth)]
    gs, invs, first, final, coefs = factors(tzs, [store[z] for z in range(depth)])
    row = lax.div(where, long)
    kf, kl = pick([jnp.concatenate(first, 0), jnp.concatenate(final, 0)], row, hot)
    for copy in copies[5:]:
        copy.wait()
    for z in range(depth):
        pres[z] = wts[0, z] * rhs[0, z] + wts[1, z] * rhs[1, z] + wts[2, z] * rhs[2, z]
    (found,) = pick([pres[...].reshape(depth * width, long)], row, hot)
    both = jnp.concatenate([prod[...] * found, front[...].astype(F32), where.astype(F32)], 1)
    send[...] = jnp.broadcast_to(both[:, None], send.shape)
    y = local_solve([pres[z] for z in range(depth)], gs, invs, tzs)
    for i, value in enumerate((*coefs, y[0], y[-1], tzs[-1])):
        ends[i] = value
    ends[6] = jnp.zeros((width, long), F32)
    ends[6, 0:1, : 2 * where.shape[1]] = jnp.concatenate([prod[...] * kf, prod[...] * kl], 1)


def is_right(level, axis="layer"):
    return (lax.axis_index(axis) >> level) % 2 == 1


def choose(level, mine, other, axis="layer"):
    right = is_right(level, axis)
    return (jnp.where(right, other, mine), jnp.where(right, mine, other))


def local_solve(rhs, upper, inv, tz):
    depth = len(rhs)
    y = [rhs[0] * inv[0]]
    for z in range(1, depth):
        y.append((rhs[z] + tz[z - 1] * y[-1]) * inv[z])
    for z in range(depth - 2, -1, -1):
        y[z] = y[z] + upper[z] * y[z + 1]
    return y


def factors(tz, store):
    depth = len(tz)
    gs, invs = ([], [])
    own = None
    for z in range(depth):
        own = store[z] if z == 0 else store[z] + gs[-1] * own
        invs.append(1.0 / (own + tz[z] if z < depth - 1 else own))
        gs.append(tz[z] * invs[-1])
    first = [invs[0]]
    for z in range(1, depth):
        first.append(tz[z - 1] * first[-1] * invs[z])
    final = [None] * depth
    final[-1] = invs[-1]
    for z in range(depth - 2, -1, -1):
        first[z] = first[z] + gs[z] * first[z + 1]
        final[z] = gs[z] * final[z + 1]
    return gs, invs, first, final, block_ends(first, final, tz)


def block_ends(first, final, tz):
    return (first[0], first[-1], final[-1] + 1.0 / jnp.maximum(tz[-1], 1e-30))


def pair(level, own, sib):
    af, af_ = choose(level, own[0], sib[0])
    c, c_ = choose(level, own[1], sib[1])
    b, b_ = choose(level, own[2], sib[2])
    return af, c, b, af_, c_, b_, 1.0 / (b + af_)


def join_coefs(level, own, sib):
    af, c, _, _, c_, b_, g = pair(level, own, sib)
    return (af - c * c * g, c * c_ * g, b_ - c_ * c_ * g)


def join_ends(level, own, sib, mine, other):
    _, c, _, _, c_, _, g = pair(level, own, sib)
    yf, yf_ = choose(level, mine[0], other[0])
    yl, yl_ = choose(level, mine[1], other[1])
    flux = g * (yl - yf_)
    return (yf - c * flux, yl_ + c_ * flux)


def first_join_kernel(final, own, sib, pres, tz, store, tx, cell, prod, kept, low, high, *outs):
    depth, width, _ = tz.shape
    for k, ref in enumerate((tz, store, pres, tx)):
        for z in range(depth):
            low[k * depth + z] = ref[z, 0:1]
            high[k * depth + z] = ref[z, width - 1 : width]
    gs, invs, first, last, _ = factors([tz[z] for z in range(depth)], [store[z] for z in range(depth)])
    for i, value in enumerate(gs + invs + first + last):
        kept[i] = value
    join(0, final, own, sib, first + last, cell, prod, *outs)


def join_kernel(level, final, own, sib, answers, cell, prod, *outs):
    join(level, final, own, sib, [answers[i] for i in range(answers.shape[0])], cell, prod, *outs)


def join(level, final, own, sib, answers, cell, prod, found, *outs):
    depth = len(answers) // 2
    width, long = answers[0].shape
    _, c, _, _, c_, _, g = pair(level, own, sib)
    first, both, last = join_coefs(level, own, sib)
    yf, yl = join_ends(level, own, sib, (own[3], own[4]), (sib[3], sib[4]))
    lower = choose(level, own[5], sib[5])[1]
    right, later = (is_right(level), is_right(level + 1))
    cg, cg_ = (c * g, c_ * g)
    tops, bottoms = ([], [])
    for z in range(depth):
        kf, kl = (answers[z], answers[depth + z])
        tops.append(jnp.where(right, cg * kf, kf - cg * kl))
        bottoms.append(jnp.where(right, kl - cg_ * kf, cg_ * kl))
    tables = [answers[:depth], answers[depth:]] if level else []
    if final:
        (face,) = outs
        face[0], face[1] = (jnp.where(later, first, last), jnp.where(later, yf, yl))
        face[2] = lower
        tables.append([jnp.where(later, tops[z], bottoms[z]) for z in range(depth)])
    else:
        out, more = outs
        for i, value in enumerate((first, both, last, yf, yl, lower)):
            out[i] = value
        for i, value in enumerate(tops + bottoms):
            more[i] = value
    if tables:
        where = cell[...]
        hot = onehot(lax.rem(where, long), long).astype(BF16)
        got = pick([jnp.concatenate(t, 0) for t in tables], lax.div(where, long), hot)
        found[...] = jnp.concatenate([prod[...] * value for value in got], 1)
    else:
        found[...] = jnp.zeros(found.shape, F32)


def groups_of(levels):
    layers = lax.axis_size("layer")
    l = lax.axis_index("layer")
    base = lax.axis_index("tile") * layers
    out = [[base + l]]
    for level in range(levels):
        out.append([base + (((l >> level) ^ 1) << level) + i for i in range(1 << level)])
    return out


def front_kernel(recv, found, inverse, send, held, sems):
    devices = recv.shape[0]
    count = recv.shape[2] // 3
    rows, length = inverse.shape
    lanes = 128
    chunks = sems.shape[0]
    wide = length // chunks
    found = found[...]
    copies = [
        pltpu.make_async_copy(inverse.at[:, pl.ds(i * wide, wide)], held.at[:, pl.ds(i * wide, wide)], sems.at[i])
        for i in range(chunks)
    ]
    for copy in copies:
        copy.start()
    terms, index = (recv[:, 0, :count], recv[:, 0, count : 2 * count])
    high = jnp.floor(index * (1.0 / lanes))
    low = index - high * lanes
    parts = [p.astype(F32) for p in split(terms)[:PARTS]]
    row_of = iota((length // lanes, count), 0).astype(F32)
    lane_of = iota((lanes, count), 0).astype(F32)
    flipped = jnp.zeros((lanes, PARTS * (length // lanes)), F32)
    for d in range(devices):
        hit = row_of == high[d : d + 1]
        left = jnp.concatenate([jnp.where(hit, p[d : d + 1], 0.0).astype(BF16) for p in parts], 0)
        right = jnp.where(lane_of == low[d : d + 1], 1.0, 0.0).astype(BF16)
        flipped = flipped + dot_nt(right, left)
    total = fold(jnp.transpose(flipped), PARTS)
    acc = jnp.zeros((rows, lanes), F32)
    for i in range(chunks):
        copies[i].wait()
        for r in range(i * wide // lanes, (i + 1) * wide // lanes):
            acc = acc + held[:, r * lanes : (r + 1) * lanes] * total[r : r + 1]
    out = jnp.transpose(jnp.broadcast_to(jnp.sum(acc, axis=1, keepdims=True), (rows, lanes)))
    pad = send.shape[2] - out.shape[1] - found.shape[1]
    pieces = [out[0:1], found] + ([jnp.zeros((1, pad), F32)] if pad else [])
    send[...] = jnp.broadcast_to(jnp.concatenate(pieces, 1)[:, None], send.shape)


def gathered(values, rows_hot, lanes_hot, start, size, ext, parts):
    hot = lanes_hot[:, start : start + size]
    pieces = [hot * p for v in values for p in split(v)[:parts]]
    got = dot_nt(rows_hot[:, start : start + size], jnp.concatenate(pieces, 0))
    planes = []
    lanes = hot.shape[0]
    for i in range(len(values)):
        plane = got[:, i * parts * lanes : (i * parts + 1) * lanes]
        for k in range(1, parts):
            j = i * parts + k
            plane = plane + got[:, j * lanes : (j + 1) * lanes]
        planes.append(jnp.concatenate([plane[r : r + ext] for r in range(0, plane.shape[0], ext)], 1))
    return planes


def beside(centre, tx, ty):
    width, long = centre.shape
    row, col = (iota(centre.shape, 0), iota(centre.shape, 1))
    total = tx * jnp.where(row == width - 1, 0.0, pltpu.roll(centre, width - 1, 0))
    total = total + jnp.where(row == 0, 0.0, pltpu.roll(tx * centre, 1, 0))
    total = total + ty * jnp.where(col == long - 1, 0.0, pltpu.roll(centre, long - 1, 1))
    return total + jnp.where(col == 0, 0.0, pltpu.roll(ty * centre, 1, 1))


def tile_rows(first, last, one, two):
    odd = is_right(0, "tile")
    one[...] = jnp.where(odd, first, last)
    two[...] = jnp.where(odd, last, first)


def table_kernel(lists, shape, terms, hots, only=None):
    _, width, long = shape
    rows_hot, lanes_hot, sol_hot, sol_row, layer = hots
    lanes = 128
    rows = sol_hot.shape[0]
    count = terms.shape[2] // 3
    at = 0
    for members in lists:
        for device in members:
            entry = terms[device]
            index = entry[:, count : 2 * count].astype(I32)
            cell = entry[:, 2 * count :].astype(I32)
            y, x = lax.rem(cell, long), lax.rem(lax.div(cell, long), width)
            if only is None:
                row = lax.div(y, lanes) * width + x
            else:
                row = jnp.where(x == only, lax.div(y, lanes), -1)
            here = pl.ds(at, count)
            rows_hot[:, here] = onehot(row, rows_hot.shape[0]).astype(BF16)
            lanes_hot[:, here] = onehot(lax.rem(y, lanes), lanes).astype(BF16)
            sol_hot[:, here] = onehot(lax.rem(index, rows), rows).astype(BF16)
            sol_row[:, here] = lax.div(index, rows)
            if at < layer.shape[1]:
                layer[:, here] = lax.div(cell, long * width)
            at += count


def column_solve(levels, recv, lists, hots, listing, planes_of, sib):
    rows_hot, lanes_hot, sol_hot, sol_row, layer = hots
    rows, count = (sol_hot.shape[0], layer.shape[1])
    table = jnp.concatenate(split(recv[...].reshape(recv.shape[0], recv.shape[2])[:, :rows]), 0)
    sol = fold(dot(table, sol_hot[...]))
    sol = jnp.sum(jnp.where(iota(sol.shape, 0) == sol_row[...], sol, 0.0), axis=0, keepdims=True)
    layer = layer[...]

    def listed(group, column):
        at = rows + column * count
        return jnp.concatenate([recv[device][:, at : at + count] for device in group], 1)

    mine_list, sib_list = listing
    tz, pres, (gs, invs, first, final, coefs) = planes_of()
    depth = len(tz)
    high = tz[0].shape[0]
    own = [coefs]
    start = layer.shape[1]
    value = mine_list * sol[:, :start]
    values = [jnp.where(layer == z, value, 0.0) for z in range(depth)]
    change = gathered(values, rows_hot, lanes_hot, 0, start, high, PARTS)
    y = local_solve([pres[z] - change[z] for z in range(depth)], gs, invs, tz)
    mine = (y[0], y[-1])
    steps = []
    for level in range(levels):
        size = len(lists[level + 1]) * count
        top = level == levels - 1
        if level:
            columns = [2 * level - 2] if top else [2 * level - 2, 2 * level - 1]
            values = [listed(lists[level + 1], c) for c in columns]
        else:
            values = [sib_list[:, i * count : (i + 1) * count] for i in range(2)]
        values = [value * sol[:, start : start + size] for value in values]
        change = gathered(values, rows_hot, lanes_hot, start, size, high, PARTS)
        start += size
        if top:
            other = sib[level][1] - change[0]
            steps.append((mine, (other, other)))
        else:
            other = (sib[level][3] - change[0], sib[level][4] - change[1])
            steps.append((mine, other))
            mine = join_ends(level, own[level], sib[level], mine, other)
            own.append(join_coefs(level, own[level], sib[level]))
    above = below = tzp = jnp.zeros(tz[0].shape, F32)
    place = lax.axis_index("layer")
    for level in range(levels - 1, -1, -1):
        mine, other = steps[level]
        yl, _ = choose(level, mine[1], other[1])
        _, yf_ = choose(level, mine[0], other[0])
        flux = yl - yf_
        if level == levels - 1:
            b, _ = choose(level, own[level][2], sib[level][0])
            _, af_ = choose(level, own[level][0], sib[level][0])
            g = 1.0 / (b + af_)
            before = sib[level][2]
        else:
            _, c, _, _, c_, _, g = pair(level, own[level], sib[level])
            flux = flux + c * above - c_ * below
            before = sib[level][5]
        tzp = jnp.where(place % (2 << level) == 1 << level, before, tzp)
        flux = g * flux
        right = is_right(level)
        above, below = (jnp.where(right, flux, above), jnp.where(right, below, -flux))
    return [y[z] + first[z] * above + final[z] * below for z in range(depth)], above, below, tzp


def pressure_kernel(levels, ready, recv, pres, *refs):
    hots, sib, (tz, kept, tx, prod, _, p, coupled_z, one) = (refs[:5], refs[5 : 5 + levels], refs[5 + levels :])
    depth, width, _ = pres.shape
    odd = is_right(0, "tile")
    lists = groups_of(levels)

    def planes_of():
        tzs, pressures = ([ref[z] for z in range(depth)] for ref in (tz, pres))
        gs, invs, first, final = ([kept[k * depth + z] for z in range(depth)] for k in range(4))
        return tzs, pressures, (gs, invs, first, final, block_ends(first, final, tzs))

    ready(0)
    listing = (prod[...], sib[0][6, 0:1])
    values, above, below, tzp = column_solve(levels, recv, lists, hots, listing, planes_of, sib)
    tzs = [tz[z] for z in range(depth)]
    is_last = lax.axis_index("layer") == (1 << levels) - 1
    for z in range(depth):
        p[z] = values[z]
        one[z] = jnp.where(odd, values[z][0:1], (tx[z] * values[z])[width - 1 :])
        total = above + tzp * values[z] if z == 0 else tzs[z - 1] * values[z - 1]
        if z == depth - 1:
            coupled_z[z] = total + jnp.where(is_last, 0.0, below + tzs[z] * values[z])
        else:
            coupled_z[z] = total + tzs[z] * values[z + 1]
    ready(1)


def edge_kernel(levels, shape, low, high, prod, terms, *refs):
    sib, two, hots = (refs[:levels], refs[levels], refs[levels + 1 :])
    table_kernel(groups_of(levels), shape, terms, hots)
    odd = is_right(0, "tile")
    n = low.shape[0]
    two[pl.ds(0, n)] = jnp.where(odd, high[...], low[...])
    at = n
    for block in sib:
        width = block.shape[1]
        for i in range(min(6, block.shape[0])):
            two[at] = jnp.where(odd, block[i, width - 1 : width], block[i, 0:1])
            at += 1
    two[at] = sib[0][6, 0:1]
    two[at + 1] = jnp.zeros((1, two.shape[2]), F32)
    two[at + 1, :, : prod.shape[1]] = prod[...]


def first_three(kernel, ready, one, two, three, _rhs, _diag, _ty, _binv, *rest):
    kernel(one, two, three, *rest)
    ready(0)


def beyond_kernel(levels, shapes, shape, recv, terms, two, row, *hots):
    depth, width, long = shape
    tiles, layers = (lax.axis_size("tile"), lax.axis_size("layer"))
    tile = lax.axis_index("tile")
    odd = is_right(0, "tile")
    count = 4 * depth + sum(shapes)
    planes = [two[i] for i in range(count)]
    step = jnp.where(odd, layers, -layers)
    lists = [[jnp.clip(device + step, 0, tiles * layers - 1) for device in members] for members in groups_of(levels)]
    table_kernel(lists, shape, terms, hots, jnp.where(odd, 0, width - 1))
    exists = jnp.where(odd, (tile < tiles - 1).astype(F32), (tile > 0).astype(F32)) + jnp.zeros((1, long), F32)
    blocks = []
    at = 4 * depth
    for size in shapes:
        blocks.append([planes[at + i] for i in range(size)])
        at += size

    def planes_of():
        kept = [planes[depth + z] for z in range(depth)]
        tzs = [planes[z] for z in range(depth)]
        found = factors(tzs, [jnp.where(value == 0.0, 1.0, value) for value in kept])
        return tzs, [planes[2 * depth + z] for z in range(depth)], found

    listing = (two[count + 1, :, : terms.shape[2] // 3], two[count])
    values, _, _, _ = column_solve(levels, recv, lists, hots, listing, planes_of, blocks)
    for z in range(depth):
        found = jnp.where(exists > 0.0, values[z], 0.0)
        row[z] = jnp.where(odd, found, found * two[3 * depth + z])


def search_kernel(p, coupled_z, two, one, tx, ty, tz, rhs, column, first_inv, later_inv, s, outer, row_two, row_one, inner):
    depth, width, _ = p.shape
    odd = is_right(0, "tile")
    right = is_right(0)
    row = iota(p.shape[1:], 0)
    for z in range(depth):
        centre = p[z]
        after = jnp.where(odd, two[z], one[z])
        before = jnp.where(odd, one[z], two[z])
        coupled = coupled_z[z] + beside(centre, tx[z], ty[z])
        coupled = coupled + jnp.where(row == 0, before, 0.0) + jnp.where(row == width - 1, tx[z] * after, 0.0)
        remain = [rhs[c, z] - column[c, z] * centre for c in range(3)]
        remain[0] = remain[0] + coupled
        for c in range(3):
            binv = [later_inv[c - 1, d, z] if c else first_inv[0, d, z] for d in range(3)]
            value = binv[0] * remain[0] + binv[1] * remain[1] + binv[2] * remain[2]
            if c == 0:
                value = centre + value
            s[c, z] = value
            tile_rows(value[0:1], (tx[z] * value)[width - 1 :], row_one.at[c, z], row_two.at[c, z])
    for c in range(3):
        top, bottom = (s[c, 0], tz[depth - 1] * s[c, depth - 1])
        inner[c] = jnp.where(right, top, bottom)
        outer[c] = jnp.where(right, bottom, top)


def inner_kernel(ready, s, diag, tz, tx, ty, image):
    depth = s.shape[1]
    for z in range(depth):
        for c in range(3):
            total = beside(s[c, z], tx[z], ty[z])
            if z:
                total = total + tz[z - 1] * s[c, z - 1]
            if z < depth - 1:
                total = total + tz[z] * s[c, z + 1]
            image[c, z] = total
    ready(0)
    for z in range(depth):
        for c in range(3):
            total = diag[c, 0, z] * s[0, z] + diag[c, 1, z] * s[1, z] + diag[c, 2, z] * s[2, z]
            image[c, z] = total - image[c, z]


def image_kernel(part, inner, outer, row_two, row_one, rhs, tz, tx, image, send):
    depth, width = part.shape[1:3]
    right, odd = (is_right(0), is_right(0, "tile"))
    row = iota(part.shape[2:], 0)
    along = power = start = 0.0
    for z in range(depth):
        for c in range(3):
            value = part[c, z]
            if z == 0:
                value = value - jnp.where(right, inner[c], outer[c])
            if z == depth - 1:
                value = value - tz[z] * jnp.where(right, outer[c], inner[c])
            after = jnp.where(odd, row_two[c, z], row_one[c, z])
            before = jnp.where(odd, row_one[c, z], row_two[c, z])
            value = value - jnp.where(row == 0, before, 0.0) - jnp.where(row == width - 1, tx[z] * after, 0.0)
            image[c, z] = value
            given = rhs[c, z]
            along = along + value * given
            power = power + value * value
            start = start + given * given
    along, power, start = (jnp.sum(along), jnp.sum(power), jnp.sum(start))
    omega = along / jnp.where(power > 0.0, power, 1.0)
    square = cross = 0.0
    for z in range(depth):
        for c in range(3):
            value = image[c, z]
            left = rhs[c, z] - omega * value
            square = square + left * left
            cross = cross + left * value
    lane = iota((1, send.shape[2]), 1)
    out = jnp.zeros((1, send.shape[2]), F32)
    for i, value in enumerate((along, power, start, jnp.sum(square), jnp.sum(cross), omega)):
        out = jnp.where(lane == i, value, out)
    send[...] = jnp.broadcast_to(out[:, None], send.shape)


def finish_kernel(recv, s, image, rhs, update, lin_res, ratio):
    sums = recv[...].reshape(recv.shape[0], recv.shape[2])
    whole = jnp.sum(sums, axis=0, keepdims=True)
    omega = whole[:, 0:1] / whole[:, 1:2]
    shift = sums[:, 5:6] - omega
    square = sums[:, 3:4] + 2.0 * shift * sums[:, 4:5] + shift * shift * sums[:, 1:2]
    ratio[...] = jnp.sqrt(jnp.sum(square, axis=0, keepdims=True) / whole[:, 2:3])
    for c in range(3):
        for z in range(s.shape[1]):
            update[c, z] = omega * s[c, z]
            lin_res[c, z] = rhs[c, z] - omega * image[c, z]


def flip(x, level, axis="layer"):
    return lax.ppermute(x, axis, [(i, i ^ (1 << level)) for i in range(lax.axis_size(axis))])


def neighbour(x, axis="layer"):
    pairs = [(i, i + 1) for i in range(1, lax.axis_size(axis) - 1, 2)]
    return lax.ppermute(x, axis, pairs + [(j, i) for i, j in pairs])


def everywhere(x):
    return lax.all_to_all(x, BOTH, split_axis=0, concat_axis=0, tiled=True)


def shards(rhs, weights, block_diag, block_inv, tx, ty, tz, store, cell, front, prod, inverse):
    layers = lax.axis_size("layer")
    devices = lax.axis_size("tile") * layers
    levels = layers.bit_length() - 1
    depth, width, long = tx.shape
    count = cell.shape[0]
    rows = inverse.shape[0]
    lists = layers * count
    cell, front, prod = (cell.reshape(1, -1), front.reshape(1, -1), prod.reshape(1, -1))
    field = vmem(tx.shape)

    def planes(n):
        return vmem((n, width, long))

    hbm_spec = pl.BlockSpec(memory_space=pltpu.HBM)
    given = (cell, front, prod, rhs, weights, tz, store)
    pres, send, ends = pl.pallas_call(
        pres_kernel,
        out_shape=(field, vmem((devices, 1, 3 * count)), planes(7)),
        in_specs=[hbm_spec] * len(given),
        out_specs=(VM,) * 3,
        scratch_shapes=[vmem(a.shape, a.dtype) for a in given] + [pltpu.SemaphoreType.DMA((len(given),))],
        compiler_params=pltpu.CompilerParams(vmem_limit_bytes=LIMIT),
    )(*[pltpu.with_memory_space_constraint(a, pltpu.HBM) for a in given])
    terms = everywhere(send)
    sib, found = ([], [])
    for level in range(levels - 1):
        sib.append(flip(ends, level))
        final = level == levels - 2
        many = (2 if level else 0) + (1 if final else 0)
        outs = (vmem((1, max(1, many) * count)), *((planes(3),) if final else (planes(6), planes(2 * depth))))
        if level == 0:
            rim = vmem((4 * depth, 1, long))
            kept, low, high, *got = call(
                functools.partial(first_join_kernel, final),
                (hbm((4 * depth, width, long)), rim, rim, *outs),
                (ends, sib[-1], pres, tz, store, tx, cell, prod),
                far=range(3, 8),
            )
        else:
            got = call(
                functools.partial(join_kernel, level, final), outs, (ends, sib[-1], answers, cell, prod), far=(3, 4)
            )
        if many:
            found.append(got[0])
        if final:
            face = got[1]
        else:
            ends, answers = got[1:]
    found = found[0] if len(found) == 1 else jnp.concatenate(found, 1)
    terms, face, found = lax.optimization_barrier((terms, face, found))
    sib.append(flip(face, levels - 1))
    chunks = 8
    send = pl.pallas_call(
        front_kernel,
        out_shape=vmem((devices, 1, max(rows + found.shape[1], 3 * count))),
        in_specs=[VM, VM, hbm_spec],
        out_specs=VM,
        scratch_shapes=[vmem(inverse.shape), pltpu.SemaphoreType.DMA((chunks,))],
        compiler_params=pltpu.CompilerParams(vmem_limit_bytes=LIMIT),
    )(terms, found, pltpu.with_memory_space_constraint(inverse, pltpu.HBM))
    sizes = [min(6, block.shape[0]) for block in sib]
    rim = vmem((4 * depth + sum(sizes) + 2, 1, long))
    send, low, high = lax.optimization_barrier((send, low, high))

    def hots(high):
        return (
            vmem((high * long // 128, lists), BF16),
            vmem((128, lists), BF16),
            vmem((rows, lists), BF16),
            vmem((1, lists), I32),
            vmem((1, count), I32),
        )

    two, *made = call(
        functools.partial(edge_kernel, levels, (depth, width, long)),
        (rim, *hots(width)),
        (low, high, prod, terms, *sib),
    )
    sol = everywhere(send)
    two = neighbour(two, "tile")
    at = 7 + levels
    row3 = vmem((depth, 1, long))
    p, coupled_z, one, tz, tx, later_inv = call(
        functools.partial(pressure_kernel, levels),
        (field, field, row3),
        (sol, pres, *made, *sib, tz, kept, tx, prod, block_inv),
        far=range(at, at + 5),
        keep=(at, at + 2, at + 4),
        cut={at + 4: (1, 3)},
        late=(range(at, at + 4), (at + 4,)),
    )
    sol, one, terms = lax.optimization_barrier((sol, one, terms))
    one = flip(one, 0, "tile")
    two, rhs, first_column, ty, first_inv = call(
        functools.partial(first_three, functools.partial(beyond_kernel, levels, sizes, (depth, width, long))),
        (row3,),
        (sol, terms, two, rhs, block_diag, ty, block_inv),
        far=(3, 4, 5, 6),
        keep=(3, 4, 5, 6),
        column=(4,),
        cut={6: (0, 1)},
        late=((3, 4, 5, 6),),
        scratch=hots(1),
    )
    row9 = vmem((3, depth, 1, long))
    plane3 = planes(3)
    s, outer, row_two, row_one, inner = call(
        search_kernel,
        (vmem(rhs.shape), plane3, row9, row9, plane3),
        (p, coupled_z, two, one, tx, ty, tz, rhs, first_column, first_inv, later_inv),
    )
    outer, row_two = (neighbour(outer), neighbour(row_two, "tile"))
    row_one, inner = (flip(row_one, 0, "tile"), flip(inner, 0))
    (part,) = call(inner_kernel, (vmem(rhs.shape),), (s, block_diag, tz, tx, ty), far=(1,), late=((1,),))
    image, send = call(
        image_kernel,
        (vmem(rhs.shape), vmem((devices, 1, 128))),
        (part, inner, outer, row_two, row_one, rhs, tz, tx),
    )
    sums = everywhere(send)
    update, lin_res, ratio = call(
        finish_kernel, (hbm(rhs.shape), hbm(rhs.shape), hbm((1, 1))), (sums, s, image, rhs)
    )
    return (update, lin_res, ratio.reshape(()))


def solution(mesh):
    return jax.shard_map(
        shards,
        mesh=mesh,
        in_specs=(
            P(None, "layer", "tile", None),
            P(None, "layer", "tile", None),
            P(None, None, "layer", "tile", None),
            P(None, None, "layer", "tile", None),
            P("layer", "tile", None),
            P("layer", "tile", None),
            P("layer", "tile", None),
            P("layer", "tile", None),
            P(("tile", "layer")),
            P(("tile", "layer")),
            P(("tile", "layer")),
            P(("tile", "layer"), None),
        ),
        out_specs=(P(None, "layer", "tile", None), P(None, "layer", "tile", None), P()),
        check_vma=False,
    )
```

```python
import functools
import jax
import jax.numpy as jnp
from jax import lax
from jax.experimental import pallas as pl
from jax.experimental.pallas import tpu as pltpu
from jax.sharding import PartitionSpec as P

F32 = jnp.float32
BF16 = jnp.bfloat16
I32 = jnp.int32
BOTH = ("tile", "layer")
VM = pl.BlockSpec(memory_space=pltpu.VMEM)
LIMIT = 16 << 20
PARTS = 2


def hbm(shape):
    return jax.ShapeDtypeStruct(shape, F32)


def vmem(shape, dtype=F32):
    return pltpu.VMEM(shape, dtype)


def staged(kernel, where, outs, kept, column, late, *refs):
    count, sems = (len(where), refs[-1])
    held = list(refs[count + outs + len(kept) : -1])
    target_count = sum(where) - len(kept)
    held, extra = (held[:target_count], held[target_count:])
    target = dict(zip(kept, refs[count + outs : count + outs + len(kept)]))
    operands, copies = ([], [])
    for i, far in enumerate(where):
        if far:
            to = target[i] if i in target else held.pop(0)
            part = refs[i].at[:, 0] if i in column else refs[i]
            copies.append(pltpu.make_async_copy(part, to, sems.at[len(copies)]))
            operands.append(to)
        else:
            operands.append(refs[i])
    places = [i for i, far in enumerate(where) if far]
    for copy in copies:
        copy.start()
    for i, copy in zip(places, copies):
        if not any(i in group for group in late):
            copy.wait()

    def ready(k):
        for i, copy in zip(places, copies):
            if i in late[k]:
                copy.wait()

    more = (ready,) if late else ()
    kernel(*more, *operands, *refs[count : count + outs], *extra)


def call(kernel, outs, args, far=(), keep=(), column=(), late=(), scratch=(), limit=LIMIT):
    where = [i in far for i in range(len(args))]
    spaces = [pltpu.HBM if w else pltpu.VMEM for w in where]
    shapes = [a.shape[:1] + a.shape[2:] if i in column else a.shape for i, a in enumerate(args)]
    every = (*outs, *(vmem(shapes[i], args[i].dtype) for i in keep))
    return pl.pallas_call(
        functools.partial(staged, kernel, where, len(outs), tuple(keep), tuple(column), tuple(late)),
        out_shape=every,
        in_specs=[pl.BlockSpec(memory_space=s) for s in spaces],
        out_specs=(VM,) * len(every),
        scratch_shapes=[vmem(shapes[i], a.dtype) for i, a in enumerate(args) if where[i] and i not in keep]
        + [*scratch, pltpu.SemaphoreType.DMA((max(1, sum(where)),))],
        compiler_params=pltpu.CompilerParams(vmem_limit_bytes=limit),
    )(*[pltpu.with_memory_space_constraint(a, s) for a, s in zip(args, spaces)])


def iota(shape, dim):
    return lax.broadcasted_iota(I32, shape, dim)


def split(x):
    one = x.astype(BF16)
    rest = x - one.astype(F32)
    two = rest.astype(BF16)
    three = (rest - two.astype(F32)).astype(BF16)
    return [one, two, three]


def fold(x, parts=3):
    n = x.shape[0] // parts
    total = x[(parts - 1) * n :]
    for i in range(parts - 2, -1, -1):
        total = x[i * n : (i + 1) * n] + total
    return total


def onehot(index, size):
    return jnp.where(iota((size, index.shape[1]), 0) == index, 1.0, 0.0)


def dot(a, b):
    return lax.dot_general(a, b, (((1,), (0,)), ((), ())), preferred_element_type=F32)


def dot_nt(a, b):
    return lax.dot_general(a, b, (((1,), (1,)), ((), ())), preferred_element_type=F32)


def pick(tables, hi, hot):
    rows = tables[0].shape[0]
    parts = jnp.concatenate([p for table in tables for p in split(table)[:PARTS]], 0)
    got = dot(parts, hot)
    mask = onehot(hi, rows)
    n = PARTS * rows
    return [jnp.sum(fold(got[i * n : (i + 1) * n], PARTS) * mask, axis=0, keepdims=True) for i in range(len(tables))]


def pres_kernel(cell_in, front_in, prod_in, rhs_in, wts_in, tz_in, store_in, pres, send, ends, *scratch):
    (cell, front, prod, rhs, wts, tz, store), sems = scratch[:-1], scratch[-1]
    pairs = ((cell_in, cell), (front_in, front), (prod_in, prod), (tz_in, tz), (store_in, store), (rhs_in, rhs), (wts_in, wts))
    copies = [pltpu.make_async_copy(a, b, sems.at[i]) for i, (a, b) in enumerate(pairs)]
    for copy in copies:
        copy.start()
    for copy in copies[:3]:
        copy.wait()
    depth, width, long = pres.shape
    where = cell[...]
    hot = onehot(lax.rem(where, long), long).astype(BF16)
    for copy in copies[3:5]:
        copy.wait()
    tzs = [tz[z] for z in range(depth)]
    gs, invs, first, final, coefs = factors(tzs, [store[z] for z in range(depth)])
    row = lax.div(where, long)
    kf, kl = pick([jnp.concatenate(first, 0), jnp.concatenate(final, 0)], row, hot)
    for copy in copies[5:]:
        copy.wait()
    for z in range(depth):
        pres[z] = wts[0, z] * rhs[0, z] + wts[1, z] * rhs[1, z] + wts[2, z] * rhs[2, z]
    (found,) = pick([pres[...].reshape(depth * width, long)], row, hot)
    both = jnp.concatenate([prod[...] * found, front[...].astype(F32), where.astype(F32)], 1)
    send[...] = jnp.broadcast_to(both[:, None], send.shape)
    y = local_solve([pres[z] for z in range(depth)], gs, invs, tzs)
    for i, value in enumerate((*coefs, y[0], y[-1], tzs[-1])):
        ends[i] = value
    ends[6] = jnp.zeros((width, long), F32)
    ends[6, 0:1, : 2 * where.shape[1]] = jnp.concatenate([prod[...] * kf, prod[...] * kl], 1)


def is_right(level, axis="layer"):
    return (lax.axis_index(axis) >> level) % 2 == 1


def choose(level, mine, other, axis="layer"):
    right = is_right(level, axis)
    return (jnp.where(right, other, mine), jnp.where(right, mine, other))


def local_solve(rhs, upper, inv, tz):
    depth = len(rhs)
    y = [rhs[0] * inv[0]]
    for z in range(1, depth):
        y.append((rhs[z] + tz[z - 1] * y[-1]) * inv[z])
    for z in range(depth - 2, -1, -1):
        y[z] = y[z] + upper[z] * y[z + 1]
    return y


def factors(tz, store):
    depth = len(tz)
    gs, invs = ([], [])
    own = None
    for z in range(depth):
        own = store[z] if z == 0 else store[z] + gs[-1] * own
        invs.append(1.0 / (own + tz[z] if z < depth - 1 else own))
        gs.append(tz[z] * invs[-1])
    first = [invs[0]]
    for z in range(1, depth):
        first.append(tz[z - 1] * first[-1] * invs[z])
    final = [None] * depth
    final[-1] = invs[-1]
    for z in range(depth - 2, -1, -1):
        first[z] = first[z] + gs[z] * first[z + 1]
        final[z] = gs[z] * final[z + 1]
    return gs, invs, first, final, block_ends(first, final, tz)


def block_ends(first, final, tz):
    return (first[0], first[-1], final[-1] + 1.0 / jnp.maximum(tz[-1], 1e-30))


def pair(level, own, sib):
    af, af_ = choose(level, own[0], sib[0])
    c, c_ = choose(level, own[1], sib[1])
    b, b_ = choose(level, own[2], sib[2])
    return af, c, b, af_, c_, b_, 1.0 / (b + af_)


def join_coefs(level, own, sib):
    af, c, _, _, c_, b_, g = pair(level, own, sib)
    return (af - c * c * g, c * c_ * g, b_ - c_ * c_ * g)


def join_ends(level, own, sib, mine, other):
    _, c, _, _, c_, _, g = pair(level, own, sib)
    yf, yf_ = choose(level, mine[0], other[0])
    yl, yl_ = choose(level, mine[1], other[1])
    flux = g * (yl - yf_)
    return (yf - c * flux, yl_ + c_ * flux)


def first_join_kernel(final, own, sib, pres, tz, store, tx, cell, prod, kept, low, high, *outs):
    depth, width, _ = tz.shape
    for k, ref in enumerate((tz, store, pres, tx)):
        for z in range(depth):
            low[k * depth + z] = ref[z, 0:1]
            high[k * depth + z] = ref[z, width - 1 : width]
    gs, invs, first, last, _ = factors([tz[z] for z in range(depth)], [store[z] for z in range(depth)])
    for i, value in enumerate(gs + invs + first + last):
        kept[i] = value
    join(0, final, own, sib, first + last, cell, prod, *outs)


def join_kernel(level, final, own, sib, answers, cell, prod, *outs):
    join(level, final, own, sib, [answers[i] for i in range(answers.shape[0])], cell, prod, *outs)


def join(level, final, own, sib, answers, cell, prod, found, *outs):
    depth = len(answers) // 2
    width, long = answers[0].shape
    _, c, _, _, c_, _, g = pair(level, own, sib)
    first, both, last = join_coefs(level, own, sib)
    yf, yl = join_ends(level, own, sib, (own[3], own[4]), (sib[3], sib[4]))
    lower = choose(level, own[5], sib[5])[1]
    right, later = (is_right(level), is_right(level + 1))
    cg, cg_ = (c * g, c_ * g)
    tops, bottoms = ([], [])
    for z in range(depth):
        kf, kl = (answers[z], answers[depth + z])
        tops.append(jnp.where(right, cg * kf, kf - cg * kl))
        bottoms.append(jnp.where(right, kl - cg_ * kf, cg_ * kl))
    tables = [answers[:depth], answers[depth:]] if level else []
    if final:
        (face,) = outs
        face[0], face[1] = (jnp.where(later, first, last), jnp.where(later, yf, yl))
        face[2] = lower
        tables.append([jnp.where(later, tops[z], bottoms[z]) for z in range(depth)])
    else:
        out, more = outs
        for i, value in enumerate((first, both, last, yf, yl, lower)):
            out[i] = value
        for i, value in enumerate(tops + bottoms):
            more[i] = value
    if tables:
        where = cell[...]
        hot = onehot(lax.rem(where, long), long).astype(BF16)
        got = pick([jnp.concatenate(t, 0) for t in tables], lax.div(where, long), hot)
        found[...] = jnp.concatenate([prod[...] * value for value in got], 1)
    else:
        found[...] = jnp.zeros(found.shape, F32)


def groups_of(levels):
    layers = lax.axis_size("layer")
    l = lax.axis_index("layer")
    base = lax.axis_index("tile") * layers
    out = [[base + l]]
    for level in range(levels):
        out.append([base + (((l >> level) ^ 1) << level) + i for i in range(1 << level)])
    return out


def front_kernel(recv, found, inverse, send, held, sems):
    devices = recv.shape[0]
    count = recv.shape[2] // 3
    rows, length = inverse.shape
    lanes = 128
    chunks = sems.shape[0]
    wide = length // chunks
    found = found[...]
    copies = [
        pltpu.make_async_copy(inverse.at[:, pl.ds(i * wide, wide)], held.at[:, pl.ds(i * wide, wide)], sems.at[i])
        for i in range(chunks)
    ]
    for copy in copies:
        copy.start()
    terms, index = (recv[:, 0, :count], recv[:, 0, count : 2 * count])
    high = jnp.floor(index * (1.0 / lanes))
    low = index - high * lanes
    parts = [p.astype(F32) for p in split(terms)[:PARTS]]
    row_of = iota((length // lanes, count), 0).astype(F32)
    lane_of = iota((lanes, count), 0).astype(F32)
    flipped = jnp.zeros((lanes, PARTS * (length // lanes)), F32)
    for d in range(devices):
        hit = row_of == high[d : d + 1]
        left = jnp.concatenate([jnp.where(hit, p[d : d + 1], 0.0).astype(BF16) for p in parts], 0)
        right = jnp.where(lane_of == low[d : d + 1], 1.0, 0.0).astype(BF16)
        flipped = flipped + dot_nt(right, left)
    total = fold(jnp.transpose(flipped), PARTS)
    acc = jnp.zeros((rows, lanes), F32)
    for i in range(chunks):
        copies[i].wait()
        for r in range(i * wide // lanes, (i + 1) * wide // lanes):
            acc = acc + held[:, r * lanes : (r + 1) * lanes] * total[r : r + 1]
    out = jnp.transpose(jnp.broadcast_to(jnp.sum(acc, axis=1, keepdims=True), (rows, lanes)))
    pad = send.shape[2] - out.shape[1] - found.shape[1]
    pieces = [out[0:1], found] + ([jnp.zeros((1, pad), F32)] if pad else [])
    send[...] = jnp.broadcast_to(jnp.concatenate(pieces, 1)[:, None], send.shape)


def gathered(values, rows_hot, lanes_hot, start, size, ext, parts):
    hot = lanes_hot[:, start : start + size]
    pieces = [hot * p for v in values for p in split(v)[:parts]]
    got = dot_nt(rows_hot[:, start : start + size], jnp.concatenate(pieces, 0))
    planes = []
    lanes = hot.shape[0]
    for i in range(len(values)):
        plane = got[:, i * parts * lanes : (i * parts + 1) * lanes]
        for k in range(1, parts):
            j = i * parts + k
            plane = plane + got[:, j * lanes : (j + 1) * lanes]
        planes.append(jnp.concatenate([plane[r : r + ext] for r in range(0, plane.shape[0], ext)], 1))
    return planes


def beside(centre, tx, ty):
    width, long = centre.shape
    row, col = (iota(centre.shape, 0), iota(centre.shape, 1))
    total = tx * jnp.where(row == width - 1, 0.0, pltpu.roll(centre, width - 1, 0))
    total = total + jnp.where(row == 0, 0.0, pltpu.roll(tx * centre, 1, 0))
    total = total + ty * jnp.where(col == long - 1, 0.0, pltpu.roll(centre, long - 1, 1))
    return total + jnp.where(col == 0, 0.0, pltpu.roll(ty * centre, 1, 1))


def tile_rows(first, last, one, two):
    odd = is_right(0, "tile")
    one[...] = jnp.where(odd, first, last)
    two[...] = jnp.where(odd, last, first)


def table_kernel(lists, shape, terms, hots, only=None):
    _, width, long = shape
    rows_hot, lanes_hot, sol_hot, sol_row, layer = hots
    lanes = 128
    rows = sol_hot.shape[0]
    count = terms.shape[2] // 3
    at = 0
    for members in lists:
        for device in members:
            entry = terms[device]
            index = entry[:, count : 2 * count].astype(I32)
            cell = entry[:, 2 * count :].astype(I32)
            y, x = lax.rem(cell, long), lax.rem(lax.div(cell, long), width)
            if only is None:
                row = lax.div(y, lanes) * width + x
            else:
                row = jnp.where(x == only, lax.div(y, lanes), -1)
            here = pl.ds(at, count)
            rows_hot[:, here] = onehot(row, rows_hot.shape[0]).astype(BF16)
            lanes_hot[:, here] = onehot(lax.rem(y, lanes), lanes).astype(BF16)
            sol_hot[:, here] = onehot(lax.rem(index, rows), rows).astype(BF16)
            sol_row[:, here] = lax.div(index, rows)
            if at < layer.shape[1]:
                layer[:, here] = lax.div(cell, long * width)
            at += count


def column_solve(levels, recv, lists, hots, listing, planes_of, sib):
    rows_hot, lanes_hot, sol_hot, sol_row, layer = hots
    rows, count = (sol_hot.shape[0], layer.shape[1])
    table = jnp.concatenate(split(recv[...].reshape(recv.shape[0], recv.shape[2])[:, :rows]), 0)
    sol = fold(dot(table, sol_hot[...]))
    sol = jnp.sum(jnp.where(iota(sol.shape, 0) == sol_row[...], sol, 0.0), axis=0, keepdims=True)
    layer = layer[...]

    def listed(group, column):
        at = rows + column * count
        return jnp.concatenate([recv[device][:, at : at + count] for device in group], 1)

    mine_list, sib_list = listing
    tz, pres, (gs, invs, first, final, coefs) = planes_of()
    depth = len(tz)
    high = tz[0].shape[0]
    own = [coefs]
    start = layer.shape[1]
    value = mine_list * sol[:, :start]
    values = [jnp.where(layer == z, value, 0.0) for z in range(depth)]
    change = gathered(values, rows_hot, lanes_hot, 0, start, high, PARTS)
    y = local_solve([pres[z] - change[z] for z in range(depth)], gs, invs, tz)
    mine = (y[0], y[-1])
    steps = []
    for level in range(levels):
        size = len(lists[level + 1]) * count
        top = level == levels - 1
        if level:
            columns = [2 * level - 2] if top else [2 * level - 2, 2 * level - 1]
            values = [listed(lists[level + 1], c) for c in columns]
        else:
            values = [sib_list[:, i * count : (i + 1) * count] for i in range(2)]
        values = [value * sol[:, start : start + size] for value in values]
        change = gathered(values, rows_hot, lanes_hot, start, size, high, PARTS)
        start += size
        if top:
            other = sib[level][1] - change[0]
            steps.append((mine, (other, other)))
        else:
            other = (sib[level][3] - change[0], sib[level][4] - change[1])
            steps.append((mine, other))
            mine = join_ends(level, own[level], sib[level], mine, other)
            own.append(join_coefs(level, own[level], sib[level]))
    above = below = tzp = jnp.zeros(tz[0].shape, F32)
    place = lax.axis_index("layer")
    for level in range(levels - 1, -1, -1):
        mine, other = steps[level]
        yl, _ = choose(level, mine[1], other[1])
        _, yf_ = choose(level, mine[0], other[0])
        flux = yl - yf_
        if level == levels - 1:
            b, _ = choose(level, own[level][2], sib[level][0])
            _, af_ = choose(level, own[level][0], sib[level][0])
            g = 1.0 / (b + af_)
            before = sib[level][2]
        else:
            _, c, _, _, c_, _, g = pair(level, own[level], sib[level])
            flux = flux + c * above - c_ * below
            before = sib[level][5]
        tzp = jnp.where(place % (2 << level) == 1 << level, before, tzp)
        flux = g * flux
        right = is_right(level)
        above, below = (jnp.where(right, flux, above), jnp.where(right, below, -flux))
    return [y[z] + first[z] * above + final[z] * below for z in range(depth)], above, below, tzp


def pressure_kernel(levels, ready, recv, terms, pres, *refs):
    sib, (tz, kept, tx, prod, _, p, coupled_z, one, *hots) = (refs[:levels], refs[levels:])
    depth, width, _ = pres.shape
    odd = is_right(0, "tile")
    lists = groups_of(levels)
    table_kernel(lists, pres.shape, terms, hots)

    def planes_of():
        tzs, pressures = ([ref[z] for z in range(depth)] for ref in (tz, pres))
        gs, invs, first, final = ([kept[k * depth + z] for z in range(depth)] for k in range(4))
        return tzs, pressures, (gs, invs, first, final, block_ends(first, final, tzs))

    ready(0)
    listing = (prod[...], sib[0][6, 0:1])
    values, above, below, tzp = column_solve(levels, recv, lists, hots, listing, planes_of, sib)
    tzs = [tz[z] for z in range(depth)]
    is_last = lax.axis_index("layer") == (1 << levels) - 1
    for z in range(depth):
        p[z] = values[z]
        one[z] = jnp.where(odd, values[z][0:1], (tx[z] * values[z])[width - 1 :])
        total = above + tzp * values[z] if z == 0 else tzs[z - 1] * values[z - 1]
        if z == depth - 1:
            coupled_z[z] = total + jnp.where(is_last, 0.0, below + tzs[z] * values[z])
        else:
            coupled_z[z] = total + tzs[z] * values[z + 1]
    ready(1)


def edge_kernel(levels, low, high, prod, *refs):
    sib, two = (refs[:levels], refs[levels])
    odd = is_right(0, "tile")
    n = low.shape[0]
    two[pl.ds(0, n)] = jnp.where(odd, high[...], low[...])
    at = n
    for block in sib:
        width = block.shape[1]
        for i in range(min(6, block.shape[0])):
            two[at] = jnp.where(odd, block[i, width - 1 : width], block[i, 0:1])
            at += 1
    two[at] = sib[0][6, 0:1]
    two[at + 1] = jnp.zeros((1, two.shape[2]), F32)
    two[at + 1, :, : prod.shape[1]] = prod[...]


def first_three(kernel, ready, one, two, three, _rhs, _diag, _ty, *rest):
    kernel(one, two, three, *rest)
    ready(0)


def beyond_kernel(levels, shapes, shape, recv, terms, two, row, *hots):
    depth, width, long = shape
    tiles, layers = (lax.axis_size("tile"), lax.axis_size("layer"))
    tile = lax.axis_index("tile")
    odd = is_right(0, "tile")
    count = 4 * depth + sum(shapes)
    planes = [two[i] for i in range(count)]
    step = jnp.where(odd, layers, -layers)
    lists = [[jnp.clip(device + step, 0, tiles * layers - 1) for device in members] for members in groups_of(levels)]
    table_kernel(lists, shape, terms, hots, jnp.where(odd, 0, width - 1))
    exists = jnp.where(odd, (tile < tiles - 1).astype(F32), (tile > 0).astype(F32)) + jnp.zeros((1, long), F32)
    blocks = []
    at = 4 * depth
    for size in shapes:
        blocks.append([planes[at + i] for i in range(size)])
        at += size

    def planes_of():
        kept = [planes[depth + z] for z in range(depth)]
        tzs = [planes[z] for z in range(depth)]
        found = factors(tzs, [jnp.where(value == 0.0, 1.0, value) for value in kept])
        return tzs, [planes[2 * depth + z] for z in range(depth)], found

    listing = (two[count + 1, :, : terms.shape[2] // 3], two[count])
    values, _, _, _ = column_solve(levels, recv, lists, hots, listing, planes_of, blocks)
    for z in range(depth):
        found = jnp.where(exists > 0.0, values[z], 0.0)
        row[z] = jnp.where(odd, found, found * two[3 * depth + z])


def search_kernel(p, coupled_z, two, one, tx, ty, tz, rhs, column, binv, s, outer, row_two, row_one, inner):
    depth, width, _ = p.shape
    odd = is_right(0, "tile")
    right = is_right(0)
    row = iota(p.shape[1:], 0)
    for z in range(depth):
        centre = p[z]
        after = jnp.where(odd, two[z], one[z])
        before = jnp.where(odd, one[z], two[z])
        coupled = coupled_z[z] + beside(centre, tx[z], ty[z])
        coupled = coupled + jnp.where(row == 0, before, 0.0) + jnp.where(row == width - 1, tx[z] * after, 0.0)
        remain = [rhs[c, z] - column[c, z] * centre for c in range(3)]
        remain[0] = remain[0] + coupled
        for c in range(3):
            value = binv[c, 0, z] * remain[0] + binv[c, 1, z] * remain[1] + binv[c, 2, z] * remain[2]
            if c == 0:
                value = centre + value
            s[c, z] = value
            tile_rows(value[0:1], (tx[z] * value)[width - 1 :], row_one.at[c, z], row_two.at[c, z])
    for c in range(3):
        top, bottom = (s[c, 0], tz[depth - 1] * s[c, depth - 1])
        inner[c] = jnp.where(right, top, bottom)
        outer[c] = jnp.where(right, bottom, top)


def inner_kernel(ready, s, diag, tz, tx, ty, image):
    depth = s.shape[1]
    for z in range(depth):
        for c in range(3):
            total = beside(s[c, z], tx[z], ty[z])
            if z:
                total = total + tz[z - 1] * s[c, z - 1]
            if z < depth - 1:
                total = total + tz[z] * s[c, z + 1]
            image[c, z] = total
    ready(0)
    for z in range(depth):
        for c in range(3):
            total = diag[c, 0, z] * s[0, z] + diag[c, 1, z] * s[1, z] + diag[c, 2, z] * s[2, z]
            image[c, z] = total - image[c, z]


def image_kernel(part, inner, outer, row_one, row_two, rhs, tz, tx, image, send):
    depth, width = part.shape[1:3]
    right, odd = (is_right(0), is_right(0, "tile"))
    row = iota(part.shape[2:], 0)
    along = power = start = 0.0
    for z in range(depth):
        for c in range(3):
            value = part[c, z]
            if z == 0:
                value = value - jnp.where(right, inner[c], outer[c])
            if z == depth - 1:
                value = value - tz[z] * jnp.where(right, outer[c], inner[c])
            after = jnp.where(odd, row_two[c, z], row_one[c, z])
            before = jnp.where(odd, row_one[c, z], row_two[c, z])
            value = value - jnp.where(row == 0, before, 0.0) - jnp.where(row == width - 1, tx[z] * after, 0.0)
            image[c, z] = value
            given = rhs[c, z]
            along = along + value * given
            power = power + value * value
            start = start + given * given
    along, power, start = (jnp.sum(along), jnp.sum(power), jnp.sum(start))
    omega = along / jnp.where(power > 0.0, power, 1.0)
    square = cross = 0.0
    for z in range(depth):
        for c in range(3):
            value = image[c, z]
            left = rhs[c, z] - omega * value
            square = square + left * left
            cross = cross + left * value
    lane = iota((1, send.shape[2]), 1)
    out = jnp.zeros((1, send.shape[2]), F32)
    for i, value in enumerate((along, power, start, jnp.sum(square), jnp.sum(cross), omega)):
        out = jnp.where(lane == i, value, out)
    send[...] = jnp.broadcast_to(out[:, None], send.shape)


def finish_kernel(recv, s, image, rhs, update, lin_res, ratio):
    sums = recv[...].reshape(recv.shape[0], recv.shape[2])
    whole = jnp.sum(sums, axis=0, keepdims=True)
    omega = whole[:, 0:1] / whole[:, 1:2]
    shift = sums[:, 5:6] - omega
    square = sums[:, 3:4] + 2.0 * shift * sums[:, 4:5] + shift * shift * sums[:, 1:2]
    ratio[...] = jnp.sqrt(jnp.sum(square, axis=0, keepdims=True) / whole[:, 2:3])
    for c in range(3):
        for z in range(s.shape[1]):
            update[c, z] = omega * s[c, z]
            lin_res[c, z] = rhs[c, z] - omega * image[c, z]


def flip(x, level, axis="layer"):
    return lax.ppermute(x, axis, [(i, i ^ (1 << level)) for i in range(lax.axis_size(axis))])


def neighbour(x, axis="layer"):
    pairs = [(i, i + 1) for i in range(1, lax.axis_size(axis) - 1, 2)]
    return lax.ppermute(x, axis, pairs + [(j, i) for i, j in pairs])


def everywhere(x):
    return lax.all_to_all(x, BOTH, split_axis=0, concat_axis=0, tiled=True)


def shards(rhs, weights, block_diag, block_inv, tx, ty, tz, store, cell, front, prod, inverse):
    layers = lax.axis_size("layer")
    devices = lax.axis_size("tile") * layers
    levels = layers.bit_length() - 1
    depth, width, long = tx.shape
    count = cell.shape[0]
    rows = inverse.shape[0]
    lists = layers * count
    cell, front, prod = (cell.reshape(1, -1), front.reshape(1, -1), prod.reshape(1, -1))
    field = vmem(tx.shape)

    def planes(n):
        return vmem((n, width, long))

    hbm_spec = pl.BlockSpec(memory_space=pltpu.HBM)
    given = (cell, front, prod, rhs, weights, tz, store)
    pres, send, ends = pl.pallas_call(
        pres_kernel,
        out_shape=(field, vmem((devices, 1, 3 * count)), planes(7)),
        in_specs=[hbm_spec] * len(given),
        out_specs=(VM,) * 3,
        scratch_shapes=[vmem(a.shape, a.dtype) for a in given] + [pltpu.SemaphoreType.DMA((len(given),))],
        compiler_params=pltpu.CompilerParams(vmem_limit_bytes=LIMIT),
    )(*[pltpu.with_memory_space_constraint(a, pltpu.HBM) for a in given])
    terms = everywhere(send)
    sib, found = ([], [])
    for level in range(levels - 1):
        sib.append(flip(ends, level))
        final = level == levels - 2
        many = (2 if level else 0) + (1 if final else 0)
        outs = (vmem((1, max(1, many) * count)), *((planes(3),) if final else (planes(6), planes(2 * depth))))
        if level == 0:
            rim = vmem((4 * depth, 1, long))
            kept, low, high, *got = call(
                functools.partial(first_join_kernel, final),
                (hbm((4 * depth, width, long)), rim, rim, *outs),
                (ends, sib[-1], pres, tz, store, tx, cell, prod),
                far=range(3, 8),
            )
        else:
            got = call(
                functools.partial(join_kernel, level, final), outs, (ends, sib[-1], answers, cell, prod), far=(3, 4)
            )
        if many:
            found.append(got[0])
        if final:
            face = got[1]
        else:
            ends, answers = got[1:]
    found = found[0] if len(found) == 1 else jnp.concatenate(found, 1)
    terms, face, found = lax.optimization_barrier((terms, face, found))
    sib.append(flip(face, levels - 1))
    chunks = 8
    send = pl.pallas_call(
        front_kernel,
        out_shape=vmem((devices, 1, max(rows + found.shape[1], 3 * count))),
        in_specs=[VM, VM, hbm_spec],
        out_specs=VM,
        scratch_shapes=[vmem(inverse.shape), pltpu.SemaphoreType.DMA((chunks,))],
        compiler_params=pltpu.CompilerParams(vmem_limit_bytes=LIMIT),
    )(terms, found, pltpu.with_memory_space_constraint(inverse, pltpu.HBM))
    sizes = [min(6, block.shape[0]) for block in sib]
    rim = vmem((4 * depth + sum(sizes) + 2, 1, long))
    send, low, high = lax.optimization_barrier((send, low, high))
    (two,) = call(functools.partial(edge_kernel, levels), (rim,), (low, high, prod, *sib))
    sol = everywhere(send)
    two = neighbour(two, "tile")

    def hots(high):
        return (
            vmem((high * long // 128, lists), BF16),
            vmem((128, lists), BF16),
            vmem((rows, lists), BF16),
            vmem((1, lists), I32),
            vmem((1, count), I32),
        )

    at = 3 + levels
    row3 = vmem((depth, 1, long))
    p, coupled_z, one, tz, tx, block_inv = call(
        functools.partial(pressure_kernel, levels),
        (field, field, row3),
        (sol, terms, pres, *sib, tz, kept, tx, prod, block_inv),
        far=range(at, at + 5),
        keep=(at, at + 2, at + 4),
        late=(range(at, at + 4), (at + 4,)),
        scratch=hots(width),
    )
    sol, one, terms = lax.optimization_barrier((sol, one, terms))
    one = flip(one, 0, "tile")
    two, rhs, first_column, ty = call(
        functools.partial(first_three, functools.partial(beyond_kernel, levels, sizes, (depth, width, long))),
        (row3,),
        (sol, terms, two, rhs, block_diag, ty),
        far=(3, 4, 5),
        keep=(3, 4, 5),
        column=(4,),
        late=((3, 4, 5),),
        scratch=hots(1),
    )
    row9 = vmem((3, depth, 1, long))
    plane3 = planes(3)
    s, outer, row_two, row_one, inner = call(
        search_kernel,
        (vmem(rhs.shape), plane3, row9, row9, plane3),
        (p, coupled_z, two, one, tx, ty, tz, rhs, first_column, block_inv),
    )
    outer, row_two = (neighbour(outer), neighbour(row_two, "tile"))
    row_one, inner = (flip(row_one, 0, "tile"), flip(inner, 0))
    (part,) = call(inner_kernel, (vmem(rhs.shape),), (s, block_diag, tz, tx, ty), far=(1,), late=((1,),))
    image, send = call(
        image_kernel,
        (vmem(rhs.shape), vmem((devices, 1, 128))),
        (part, inner, outer, row_one, row_two, rhs, tz, tx),
    )
    sums = everywhere(send)
    update, lin_res, ratio = call(
        finish_kernel, (hbm(rhs.shape), hbm(rhs.shape), hbm((1, 1))), (sums, s, image, rhs)
    )
    return (update, lin_res, ratio.reshape(()))


def solution(mesh):
    return jax.shard_map(
        shards,
        mesh=mesh,
        in_specs=(
            P(None, "layer", "tile", None),
            P(None, "layer", "tile", None),
            P(None, None, "layer", "tile", None),
            P(None, None, "layer", "tile", None),
            P("layer", "tile", None),
            P("layer", "tile", None),
            P("layer", "tile", None),
            P("layer", "tile", None),
            P(("tile", "layer")),
            P(("tile", "layer")),
            P(("tile", "layer")),
            P(("tile", "layer"), None),
        ),
        out_specs=(P(None, "layer", "tile", None), P(None, "layer", "tile", None), P()),
        check_vma=False,
    )
```

```python
import functools
import jax
import jax.numpy as jnp
from jax import lax
from jax.experimental import pallas as pl
from jax.experimental.pallas import tpu as pltpu
from jax.sharding import PartitionSpec as P

F32 = jnp.float32
BF16 = jnp.bfloat16
I32 = jnp.int32
BOTH = ("tile", "layer")
VM = pl.BlockSpec(memory_space=pltpu.VMEM)
LIMIT = 16 << 20
PARTS = 2


def hbm(shape):
    return jax.ShapeDtypeStruct(shape, F32)


def vmem(shape, dtype=F32):
    return pltpu.VMEM(shape, dtype)


def staged(kernel, where, outs, kept, column, late, *refs):
    count, sems = (len(where), refs[-1])
    held = list(refs[count + outs + len(kept) : -1])
    target_count = sum(where) - len(kept)
    held, extra = (held[:target_count], held[target_count:])
    target = dict(zip(kept, refs[count + outs : count + outs + len(kept)]))
    operands, copies = ([], [])
    for i, far in enumerate(where):
        if far:
            to = target[i] if i in target else held.pop(0)
            part = refs[i].at[:, 0] if i in column else refs[i]
            copies.append(pltpu.make_async_copy(part, to, sems.at[len(copies)]))
            operands.append(to)
        else:
            operands.append(refs[i])
    places = [i for i, far in enumerate(where) if far]
    for copy in copies:
        copy.start()
    for i, copy in zip(places, copies):
        if not any(i in group for group in late):
            copy.wait()

    def ready(k):
        for i, copy in zip(places, copies):
            if i in late[k]:
                copy.wait()

    more = (ready,) if late else ()
    kernel(*more, *operands, *refs[count : count + outs], *extra)


def call(kernel, outs, args, far=(), keep=(), column=(), late=(), scratch=(), limit=LIMIT):
    where = [i in far for i in range(len(args))]
    spaces = [pltpu.HBM if w else pltpu.VMEM for w in where]
    shapes = [a.shape[:1] + a.shape[2:] if i in column else a.shape for i, a in enumerate(args)]
    every = (*outs, *(vmem(shapes[i], args[i].dtype) for i in keep))
    return pl.pallas_call(
        functools.partial(staged, kernel, where, len(outs), tuple(keep), tuple(column), tuple(late)),
        out_shape=every,
        in_specs=[pl.BlockSpec(memory_space=s) for s in spaces],
        out_specs=(VM,) * len(every),
        scratch_shapes=[vmem(shapes[i], a.dtype) for i, a in enumerate(args) if where[i] and i not in keep]
        + [*scratch, pltpu.SemaphoreType.DMA((max(1, sum(where)),))],
        compiler_params=pltpu.CompilerParams(vmem_limit_bytes=limit),
    )(*[pltpu.with_memory_space_constraint(a, s) for a, s in zip(args, spaces)])


def iota(shape, dim):
    return lax.broadcasted_iota(I32, shape, dim)


def split(x):
    one = x.astype(BF16)
    rest = x - one.astype(F32)
    two = rest.astype(BF16)
    three = (rest - two.astype(F32)).astype(BF16)
    return [one, two, three]


def fold(x, parts=3):
    n = x.shape[0] // parts
    total = x[(parts - 1) * n :]
    for i in range(parts - 2, -1, -1):
        total = x[i * n : (i + 1) * n] + total
    return total


def onehot(index, size):
    return jnp.where(iota((size, index.shape[1]), 0) == index, 1.0, 0.0)


def dot(a, b):
    return lax.dot_general(a, b, (((1,), (0,)), ((), ())), preferred_element_type=F32)


def dot_nt(a, b):
    return lax.dot_general(a, b, (((1,), (1,)), ((), ())), preferred_element_type=F32)


def pick(tables, hi, hot):
    rows = tables[0].shape[0]
    parts = jnp.concatenate([p for table in tables for p in split(table)[:PARTS]], 0)
    got = dot(parts, hot)
    mask = onehot(hi, rows)
    n = PARTS * rows
    return [jnp.sum(fold(got[i * n : (i + 1) * n], PARTS) * mask, axis=0, keepdims=True) for i in range(len(tables))]


def pres_kernel(cell_in, front_in, prod_in, rhs_in, wts_in, tz_in, store_in, pres, send, ends, *scratch):
    (cell, front, prod, rhs, wts, tz, store), sems = scratch[:-1], scratch[-1]
    pairs = ((cell_in, cell), (front_in, front), (prod_in, prod), (tz_in, tz), (store_in, store), (rhs_in, rhs), (wts_in, wts))
    copies = [pltpu.make_async_copy(a, b, sems.at[i]) for i, (a, b) in enumerate(pairs)]
    for copy in copies:
        copy.start()
    for copy in copies[:3]:
        copy.wait()
    depth, width, long = pres.shape
    where = cell[...]
    hot = onehot(lax.rem(where, long), long).astype(BF16)
    for copy in copies[3:5]:
        copy.wait()
    tzs = [tz[z] for z in range(depth)]
    gs, invs, first, final, coefs = factors(tzs, [store[z] for z in range(depth)])
    row = lax.div(where, long)
    kf, kl = pick([jnp.concatenate(first, 0), jnp.concatenate(final, 0)], row, hot)
    for copy in copies[5:]:
        copy.wait()
    for z in range(depth):
        pres[z] = wts[0, z] * rhs[0, z] + wts[1, z] * rhs[1, z] + wts[2, z] * rhs[2, z]
    (found,) = pick([pres[...].reshape(depth * width, long)], row, hot)
    both = jnp.concatenate([prod[...] * found, front[...].astype(F32), where.astype(F32)], 1)
    send[...] = jnp.broadcast_to(both[:, None], send.shape)
    y = local_solve([pres[z] for z in range(depth)], gs, invs, tzs)
    for i, value in enumerate((*coefs, y[0], y[-1], tzs[-1])):
        ends[i] = value
    ends[6] = jnp.zeros((width, long), F32)
    ends[6, 0:1, : 2 * where.shape[1]] = jnp.concatenate([prod[...] * kf, prod[...] * kl], 1)


def is_right(level, axis="layer"):
    return (lax.axis_index(axis) >> level) % 2 == 1


def choose(level, mine, other, axis="layer"):
    right = is_right(level, axis)
    return (jnp.where(right, other, mine), jnp.where(right, mine, other))


def local_solve(rhs, upper, inv, tz):
    depth = len(rhs)
    y = [rhs[0] * inv[0]]
    for z in range(1, depth):
        y.append((rhs[z] + tz[z - 1] * y[-1]) * inv[z])
    for z in range(depth - 2, -1, -1):
        y[z] = y[z] + upper[z] * y[z + 1]
    return y


def factors(tz, store):
    depth = len(tz)
    gs, invs = ([], [])
    own = None
    for z in range(depth):
        own = store[z] if z == 0 else store[z] + gs[-1] * own
        invs.append(1.0 / (own + tz[z] if z < depth - 1 else own))
        gs.append(tz[z] * invs[-1])
    first = [invs[0]]
    for z in range(1, depth):
        first.append(tz[z - 1] * first[-1] * invs[z])
    final = [None] * depth
    final[-1] = invs[-1]
    for z in range(depth - 2, -1, -1):
        first[z] = first[z] + gs[z] * first[z + 1]
        final[z] = gs[z] * final[z + 1]
    return gs, invs, first, final, block_ends(first, final, tz)


def block_ends(first, final, tz):
    return (first[0], first[-1], final[-1] + 1.0 / jnp.maximum(tz[-1], 1e-30))


def pair(level, own, sib):
    af, af_ = choose(level, own[0], sib[0])
    c, c_ = choose(level, own[1], sib[1])
    b, b_ = choose(level, own[2], sib[2])
    return af, c, b, af_, c_, b_, 1.0 / (b + af_)


def join_coefs(level, own, sib):
    af, c, _, _, c_, b_, g = pair(level, own, sib)
    return (af - c * c * g, c * c_ * g, b_ - c_ * c_ * g)


def join_ends(level, own, sib, mine, other):
    _, c, _, _, c_, _, g = pair(level, own, sib)
    yf, yf_ = choose(level, mine[0], other[0])
    yl, yl_ = choose(level, mine[1], other[1])
    flux = g * (yl - yf_)
    return (yf - c * flux, yl_ + c_ * flux)


def first_join_kernel(final, own, sib, pres, tz, store, tx, cell, prod, kept, low, high, *outs):
    depth, width, _ = tz.shape
    for k, ref in enumerate((tz, store, pres, tx)):
        for z in range(depth):
            low[k * depth + z] = ref[z, 0:1]
            high[k * depth + z] = ref[z, width - 1 : width]
    gs, invs, first, last, _ = factors([tz[z] for z in range(depth)], [store[z] for z in range(depth)])
    for i, value in enumerate(gs + invs + first + last):
        kept[i] = value
    join(0, final, own, sib, first + last, cell, prod, *outs)


def join_kernel(level, final, own, sib, answers, cell, prod, *outs):
    join(level, final, own, sib, [answers[i] for i in range(answers.shape[0])], cell, prod, *outs)


def join(level, final, own, sib, answers, cell, prod, found, *outs):
    depth = len(answers) // 2
    width, long = answers[0].shape
    _, c, _, _, c_, _, g = pair(level, own, sib)
    first, both, last = join_coefs(level, own, sib)
    yf, yl = join_ends(level, own, sib, (own[3], own[4]), (sib[3], sib[4]))
    lower = choose(level, own[5], sib[5])[1]
    right, later = (is_right(level), is_right(level + 1))
    cg, cg_ = (c * g, c_ * g)
    tops, bottoms = ([], [])
    for z in range(depth):
        kf, kl = (answers[z], answers[depth + z])
        tops.append(jnp.where(right, cg * kf, kf - cg * kl))
        bottoms.append(jnp.where(right, kl - cg_ * kf, cg_ * kl))
    tables = [answers[:depth], answers[depth:]] if level else []
    if final:
        (face,) = outs
        face[0], face[1] = (jnp.where(later, first, last), jnp.where(later, yf, yl))
        face[2] = lower
        tables.append([jnp.where(later, tops[z], bottoms[z]) for z in range(depth)])
    else:
        out, more = outs
        for i, value in enumerate((first, both, last, yf, yl, lower)):
            out[i] = value
        for i, value in enumerate(tops + bottoms):
            more[i] = value
    if tables:
        where = cell[...]
        hot = onehot(lax.rem(where, long), long).astype(BF16)
        got = pick([jnp.concatenate(t, 0) for t in tables], lax.div(where, long), hot)
        found[...] = jnp.concatenate([prod[...] * value for value in got], 1)
    else:
        found[...] = jnp.zeros(found.shape, F32)


def groups_of(levels):
    layers = lax.axis_size("layer")
    l = lax.axis_index("layer")
    base = lax.axis_index("tile") * layers
    out = [[base + l]]
    for level in range(levels):
        out.append([base + (((l >> level) ^ 1) << level) + i for i in range(1 << level)])
    return out


def front_kernel(recv, found, inverse, send, held, sems):
    devices = recv.shape[0]
    count = recv.shape[2] // 3
    rows, length = inverse.shape
    lanes = 128
    chunks = sems.shape[0]
    wide = length // chunks
    found = found[...]
    copies = [
        pltpu.make_async_copy(inverse.at[:, pl.ds(i * wide, wide)], held.at[:, pl.ds(i * wide, wide)], sems.at[i])
        for i in range(chunks)
    ]
    for copy in copies:
        copy.start()
    terms, index = (recv[:, 0, :count], recv[:, 0, count : 2 * count])
    high = jnp.floor(index * (1.0 / lanes))
    low = index - high * lanes
    parts = [p.astype(F32) for p in split(terms)[:PARTS]]
    row_of = iota((length // lanes, count), 0).astype(F32)
    lane_of = iota((lanes, count), 0).astype(F32)
    flipped = jnp.zeros((lanes, PARTS * (length // lanes)), F32)
    for d in range(devices):
        hit = row_of == high[d : d + 1]
        left = jnp.concatenate([jnp.where(hit, p[d : d + 1], 0.0).astype(BF16) for p in parts], 0)
        right = jnp.where(lane_of == low[d : d + 1], 1.0, 0.0).astype(BF16)
        flipped = flipped + dot_nt(right, left)
    total = fold(jnp.transpose(flipped), PARTS)
    acc = jnp.zeros((rows, lanes), F32)
    for i in range(chunks):
        copies[i].wait()
        for r in range(i * wide // lanes, (i + 1) * wide // lanes):
            acc = acc + held[:, r * lanes : (r + 1) * lanes] * total[r : r + 1]
    out = jnp.transpose(jnp.broadcast_to(jnp.sum(acc, axis=1, keepdims=True), (rows, lanes)))
    pad = send.shape[2] - out.shape[1] - found.shape[1]
    pieces = [out[0:1], found] + ([jnp.zeros((1, pad), F32)] if pad else [])
    send[...] = jnp.broadcast_to(jnp.concatenate(pieces, 1)[:, None], send.shape)


def gathered(values, rows_hot, lanes_hot, start, size, ext, parts):
    hot = lanes_hot[:, start : start + size]
    pieces = [hot * p for v in values for p in split(v)[:parts]]
    got = dot_nt(rows_hot[:, start : start + size], jnp.concatenate(pieces, 0))
    planes = []
    lanes = hot.shape[0]
    for i in range(len(values)):
        plane = got[:, i * parts * lanes : (i * parts + 1) * lanes]
        for k in range(1, parts):
            j = i * parts + k
            plane = plane + got[:, j * lanes : (j + 1) * lanes]
        planes.append(jnp.concatenate([plane[r : r + ext] for r in range(0, plane.shape[0], ext)], 1))
    return planes


def beside(centre, tx, ty):
    width, long = centre.shape
    row, col = (iota(centre.shape, 0), iota(centre.shape, 1))
    total = tx * jnp.where(row == width - 1, 0.0, pltpu.roll(centre, width - 1, 0))
    total = total + jnp.where(row == 0, 0.0, pltpu.roll(tx * centre, 1, 0))
    total = total + ty * jnp.where(col == long - 1, 0.0, pltpu.roll(centre, long - 1, 1))
    return total + jnp.where(col == 0, 0.0, pltpu.roll(ty * centre, 1, 1))


def tile_rows(first, last, one, two):
    odd = is_right(0, "tile")
    one[...] = jnp.where(odd, first, last)
    two[...] = jnp.where(odd, last, first)


def table_kernel(lists, shape, terms, hots, only=None):
    _, width, long = shape
    rows_hot, lanes_hot, sol_hot, sol_row, layer = hots
    lanes = 128
    rows = sol_hot.shape[0]
    count = terms.shape[2] // 3
    at = 0
    for members in lists:
        for device in members:
            entry = terms[device]
            index = entry[:, count : 2 * count].astype(I32)
            cell = entry[:, 2 * count :].astype(I32)
            y, x = lax.rem(cell, long), lax.rem(lax.div(cell, long), width)
            if only is None:
                row = lax.div(y, lanes) * width + x
            else:
                row = jnp.where(x == only, lax.div(y, lanes), -1)
            here = pl.ds(at, count)
            rows_hot[:, here] = onehot(row, rows_hot.shape[0]).astype(BF16)
            lanes_hot[:, here] = onehot(lax.rem(y, lanes), lanes).astype(BF16)
            sol_hot[:, here] = onehot(lax.rem(index, rows), rows).astype(BF16)
            sol_row[:, here] = lax.div(index, rows)
            if at < layer.shape[1]:
                layer[:, here] = lax.div(cell, long * width)
            at += count


def column_solve(levels, recv, lists, hots, listing, planes_of, sib):
    rows_hot, lanes_hot, sol_hot, sol_row, layer = hots
    rows, count = (sol_hot.shape[0], layer.shape[1])
    table = jnp.concatenate(split(recv[...].reshape(recv.shape[0], recv.shape[2])[:, :rows]), 0)
    sol = fold(dot(table, sol_hot[...]))
    sol = jnp.sum(jnp.where(iota(sol.shape, 0) == sol_row[...], sol, 0.0), axis=0, keepdims=True)
    layer = layer[...]

    def listed(group, column):
        at = rows + column * count
        return jnp.concatenate([recv[device][:, at : at + count] for device in group], 1)

    mine_list, sib_list = listing
    tz, pres, (gs, invs, first, final, coefs) = planes_of()
    depth = len(tz)
    high = tz[0].shape[0]
    own = [coefs]
    start = layer.shape[1]
    value = mine_list * sol[:, :start]
    values = [jnp.where(layer == z, value, 0.0) for z in range(depth)]
    change = gathered(values, rows_hot, lanes_hot, 0, start, high, PARTS)
    y = local_solve([pres[z] - change[z] for z in range(depth)], gs, invs, tz)
    mine = (y[0], y[-1])
    steps = []
    for level in range(levels):
        size = len(lists[level + 1]) * count
        top = level == levels - 1
        if level:
            columns = [2 * level - 2] if top else [2 * level - 2, 2 * level - 1]
            values = [listed(lists[level + 1], c) for c in columns]
        else:
            values = [sib_list[:, i * count : (i + 1) * count] for i in range(2)]
        values = [value * sol[:, start : start + size] for value in values]
        change = gathered(values, rows_hot, lanes_hot, start, size, high, PARTS)
        start += size
        if top:
            other = sib[level][1] - change[0]
            steps.append((mine, (other, other)))
        else:
            other = (sib[level][3] - change[0], sib[level][4] - change[1])
            steps.append((mine, other))
            mine = join_ends(level, own[level], sib[level], mine, other)
            own.append(join_coefs(level, own[level], sib[level]))
    above = below = tzp = jnp.zeros(tz[0].shape, F32)
    place = lax.axis_index("layer")
    for level in range(levels - 1, -1, -1):
        mine, other = steps[level]
        yl, _ = choose(level, mine[1], other[1])
        _, yf_ = choose(level, mine[0], other[0])
        flux = yl - yf_
        if level == levels - 1:
            b, _ = choose(level, own[level][2], sib[level][0])
            _, af_ = choose(level, own[level][0], sib[level][0])
            g = 1.0 / (b + af_)
            before = sib[level][2]
        else:
            _, c, _, _, c_, _, g = pair(level, own[level], sib[level])
            flux = flux + c * above - c_ * below
            before = sib[level][5]
        tzp = jnp.where(place % (2 << level) == 1 << level, before, tzp)
        flux = g * flux
        right = is_right(level)
        above, below = (jnp.where(right, flux, above), jnp.where(right, below, -flux))
    return [y[z] + first[z] * above + final[z] * below for z in range(depth)], above, below, tzp


def pressure_kernel(levels, ready, recv, terms, pres, *refs):
    sib, (tz, kept, tx, prod, _, p, coupled_z, one, *hots) = (refs[:levels], refs[levels:])
    depth, width, _ = pres.shape
    odd = is_right(0, "tile")
    lists = groups_of(levels)
    table_kernel(lists, pres.shape, terms, hots)

    def planes_of():
        tzs, pressures = ([ref[z] for z in range(depth)] for ref in (tz, pres))
        gs, invs, first, final = ([kept[k * depth + z] for z in range(depth)] for k in range(4))
        return tzs, pressures, (gs, invs, first, final, block_ends(first, final, tzs))

    ready(0)
    listing = (prod[...], sib[0][6, 0:1])
    values, above, below, tzp = column_solve(levels, recv, lists, hots, listing, planes_of, sib)
    tzs = [tz[z] for z in range(depth)]
    is_last = lax.axis_index("layer") == (1 << levels) - 1
    for z in range(depth):
        p[z] = values[z]
        one[z] = jnp.where(odd, values[z][0:1], (tx[z] * values[z])[width - 1 :])
        total = above + tzp * values[z] if z == 0 else tzs[z - 1] * values[z - 1]
        if z == depth - 1:
            coupled_z[z] = total + jnp.where(is_last, 0.0, below + tzs[z] * values[z])
        else:
            coupled_z[z] = total + tzs[z] * values[z + 1]
    ready(1)


def edge_kernel(levels, low, high, prod, *refs):
    sib, two = (refs[:levels], refs[levels])
    odd = is_right(0, "tile")
    n = low.shape[0]
    two[pl.ds(0, n)] = jnp.where(odd, high[...], low[...])
    at = n
    for block in sib:
        width = block.shape[1]
        for i in range(min(6, block.shape[0])):
            two[at] = jnp.where(odd, block[i, width - 1 : width], block[i, 0:1])
            at += 1
    two[at] = sib[0][6, 0:1]
    two[at + 1] = jnp.zeros((1, two.shape[2]), F32)
    two[at + 1, :, : prod.shape[1]] = prod[...]


def first_three(kernel, ready, one, two, three, _rhs, _diag, _ty, *rest):
    kernel(one, two, three, *rest)
    ready(0)


def beyond_kernel(levels, shapes, shape, recv, terms, two, row, *hots):
    depth, width, long = shape
    tiles, layers = (lax.axis_size("tile"), lax.axis_size("layer"))
    tile = lax.axis_index("tile")
    odd = is_right(0, "tile")
    count = 4 * depth + sum(shapes)
    planes = [two[i] for i in range(count)]
    step = jnp.where(odd, layers, -layers)
    lists = [[jnp.clip(device + step, 0, tiles * layers - 1) for device in members] for members in groups_of(levels)]
    table_kernel(lists, shape, terms, hots, jnp.where(odd, 0, width - 1))
    exists = jnp.where(odd, (tile < tiles - 1).astype(F32), (tile > 0).astype(F32)) + jnp.zeros((1, long), F32)
    blocks = []
    at = 4 * depth
    for size in shapes:
        blocks.append([planes[at + i] for i in range(size)])
        at += size

    def planes_of():
        kept = [planes[depth + z] for z in range(depth)]
        tzs = [planes[z] for z in range(depth)]
        found = factors(tzs, [jnp.where(value == 0.0, 1.0, value) for value in kept])
        return tzs, [planes[2 * depth + z] for z in range(depth)], found

    listing = (two[count + 1, :, : terms.shape[2] // 3], two[count])
    values, _, _, _ = column_solve(levels, recv, lists, hots, listing, planes_of, blocks)
    for z in range(depth):
        found = jnp.where(exists > 0.0, values[z], 0.0)
        row[z] = jnp.where(odd, found, found * two[3 * depth + z])


def search_kernel(p, coupled_z, two, one, tx, ty, tz, rhs, column, binv, s, outer, row_two, row_one, inner):
    depth, width, _ = p.shape
    odd = is_right(0, "tile")
    right = is_right(0)
    row = iota(p.shape[1:], 0)
    for z in range(depth):
        centre = p[z]
        after = jnp.where(odd, two[z], one[z])
        before = jnp.where(odd, one[z], two[z])
        coupled = coupled_z[z] + beside(centre, tx[z], ty[z])
        coupled = coupled + jnp.where(row == 0, before, 0.0) + jnp.where(row == width - 1, tx[z] * after, 0.0)
        remain = [rhs[c, z] - column[c, z] * centre for c in range(3)]
        remain[0] = remain[0] + coupled
        for c in range(3):
            value = binv[c, 0, z] * remain[0] + binv[c, 1, z] * remain[1] + binv[c, 2, z] * remain[2]
            if c == 0:
                value = centre + value
            s[c, z] = value
            tile_rows(value[0:1], (tx[z] * value)[width - 1 :], row_one.at[c, z], row_two.at[c, z])
    for c in range(3):
        top, bottom = (s[c, 0], tz[depth - 1] * s[c, depth - 1])
        inner[c] = jnp.where(right, top, bottom)
        outer[c] = jnp.where(right, bottom, top)


def inner_kernel(ready, s, diag, tz, tx, ty, image):
    depth = s.shape[1]
    for z in range(depth):
        for c in range(3):
            total = beside(s[c, z], tx[z], ty[z])
            if z:
                total = total + tz[z - 1] * s[c, z - 1]
            if z < depth - 1:
                total = total + tz[z] * s[c, z + 1]
            image[c, z] = total
    ready(0)
    for z in range(depth):
        for c in range(3):
            total = diag[c, 0, z] * s[0, z] + diag[c, 1, z] * s[1, z] + diag[c, 2, z] * s[2, z]
            image[c, z] = total - image[c, z]


def image_kernel(part, inner, outer, row_two, row_one, rhs, tz, tx, image, send):
    depth, width = part.shape[1:3]
    right, odd = (is_right(0), is_right(0, "tile"))
    row = iota(part.shape[2:], 0)
    along = power = start = 0.0
    for z in range(depth):
        for c in range(3):
            value = part[c, z]
            if z == 0:
                value = value - jnp.where(right, inner[c], outer[c])
            if z == depth - 1:
                value = value - tz[z] * jnp.where(right, outer[c], inner[c])
            after = jnp.where(odd, row_two[c, z], row_one[c, z])
            before = jnp.where(odd, row_one[c, z], row_two[c, z])
            value = value - jnp.where(row == 0, before, 0.0) - jnp.where(row == width - 1, tx[z] * after, 0.0)
            image[c, z] = value
            given = rhs[c, z]
            along = along + value * given
            power = power + value * value
            start = start + given * given
    along, power, start = (jnp.sum(along), jnp.sum(power), jnp.sum(start))
    omega = along / jnp.where(power > 0.0, power, 1.0)
    square = cross = 0.0
    for z in range(depth):
        for c in range(3):
            value = image[c, z]
            left = rhs[c, z] - omega * value
            square = square + left * left
            cross = cross + left * value
    lane = iota((1, send.shape[2]), 1)
    out = jnp.zeros((1, send.shape[2]), F32)
    for i, value in enumerate((along, power, start, jnp.sum(square), jnp.sum(cross), omega)):
        out = jnp.where(lane == i, value, out)
    send[...] = jnp.broadcast_to(out[:, None], send.shape)


def finish_kernel(recv, s, image, rhs, update, lin_res, ratio):
    sums = recv[...].reshape(recv.shape[0], recv.shape[2])
    whole = jnp.sum(sums, axis=0, keepdims=True)
    omega = whole[:, 0:1] / whole[:, 1:2]
    shift = sums[:, 5:6] - omega
    square = sums[:, 3:4] + 2.0 * shift * sums[:, 4:5] + shift * shift * sums[:, 1:2]
    ratio[...] = jnp.sqrt(jnp.sum(square, axis=0, keepdims=True) / whole[:, 2:3])
    for c in range(3):
        for z in range(s.shape[1]):
            update[c, z] = omega * s[c, z]
            lin_res[c, z] = rhs[c, z] - omega * image[c, z]


def flip(x, level, axis="layer"):
    return lax.ppermute(x, axis, [(i, i ^ (1 << level)) for i in range(lax.axis_size(axis))])


def neighbour(x, axis="layer"):
    pairs = [(i, i + 1) for i in range(1, lax.axis_size(axis) - 1, 2)]
    return lax.ppermute(x, axis, pairs + [(j, i) for i, j in pairs])


def everywhere(x):
    return lax.all_to_all(x, BOTH, split_axis=0, concat_axis=0, tiled=True)


def shards(rhs, weights, block_diag, block_inv, tx, ty, tz, store, cell, front, prod, inverse):
    layers = lax.axis_size("layer")
    devices = lax.axis_size("tile") * layers
    levels = layers.bit_length() - 1
    depth, width, long = tx.shape
    count = cell.shape[0]
    rows = inverse.shape[0]
    lists = layers * count
    cell, front, prod = (cell.reshape(1, -1), front.reshape(1, -1), prod.reshape(1, -1))
    field = vmem(tx.shape)

    def planes(n):
        return vmem((n, width, long))

    hbm_spec = pl.BlockSpec(memory_space=pltpu.HBM)
    given = (cell, front, prod, rhs, weights, tz, store)
    pres, send, ends = pl.pallas_call(
        pres_kernel,
        out_shape=(field, vmem((devices, 1, 3 * count)), planes(7)),
        in_specs=[hbm_spec] * len(given),
        out_specs=(VM,) * 3,
        scratch_shapes=[vmem(a.shape, a.dtype) for a in given] + [pltpu.SemaphoreType.DMA((len(given),))],
        compiler_params=pltpu.CompilerParams(vmem_limit_bytes=LIMIT),
    )(*[pltpu.with_memory_space_constraint(a, pltpu.HBM) for a in given])
    terms = everywhere(send)
    sib, found = ([], [])
    for level in range(levels - 1):
        sib.append(flip(ends, level))
        final = level == levels - 2
        many = (2 if level else 0) + (1 if final else 0)
        outs = (vmem((1, max(1, many) * count)), *((planes(3),) if final else (planes(6), planes(2 * depth))))
        if level == 0:
            rim = vmem((4 * depth, 1, long))
            kept, low, high, *got = call(
                functools.partial(first_join_kernel, final),
                (hbm((4 * depth, width, long)), rim, rim, *outs),
                (ends, sib[-1], pres, tz, store, tx, cell, prod),
                far=range(3, 8),
            )
        else:
            got = call(
                functools.partial(join_kernel, level, final), outs, (ends, sib[-1], answers, cell, prod), far=(3, 4)
            )
        if many:
            found.append(got[0])
        if final:
            face = got[1]
        else:
            ends, answers = got[1:]
    found = found[0] if len(found) == 1 else jnp.concatenate(found, 1)
    terms, face, found = lax.optimization_barrier((terms, face, found))
    sib.append(flip(face, levels - 1))
    chunks = 8
    send = pl.pallas_call(
        front_kernel,
        out_shape=vmem((devices, 1, max(rows + found.shape[1], 3 * count))),
        in_specs=[VM, VM, hbm_spec],
        out_specs=VM,
        scratch_shapes=[vmem(inverse.shape), pltpu.SemaphoreType.DMA((chunks,))],
        compiler_params=pltpu.CompilerParams(vmem_limit_bytes=LIMIT),
    )(terms, found, pltpu.with_memory_space_constraint(inverse, pltpu.HBM))
    sizes = [min(6, block.shape[0]) for block in sib]
    rim = vmem((4 * depth + sum(sizes) + 2, 1, long))
    send, low, high = lax.optimization_barrier((send, low, high))
    (two,) = call(functools.partial(edge_kernel, levels), (rim,), (low, high, prod, *sib))
    sol = everywhere(send)
    two = neighbour(two, "tile")

    def hots(high):
        return (
            vmem((high * long // 128, lists), BF16),
            vmem((128, lists), BF16),
            vmem((rows, lists), BF16),
            vmem((1, lists), I32),
            vmem((1, count), I32),
        )

    at = 3 + levels
    row3 = vmem((depth, 1, long))
    p, coupled_z, one, tz, tx, block_inv = call(
        functools.partial(pressure_kernel, levels),
        (field, field, row3),
        (sol, terms, pres, *sib, tz, kept, tx, prod, block_inv),
        far=range(at, at + 5),
        keep=(at, at + 2, at + 4),
        late=(range(at, at + 4), (at + 4,)),
        scratch=hots(width),
    )
    sol, one, terms = lax.optimization_barrier((sol, one, terms))
    one = flip(one, 0, "tile")
    two, rhs, first_column, ty = call(
        functools.partial(first_three, functools.partial(beyond_kernel, levels, sizes, (depth, width, long))),
        (row3,),
        (sol, terms, two, rhs, block_diag, ty),
        far=(3, 4, 5),
        keep=(3, 4, 5),
        column=(4,),
        late=((3, 4, 5),),
        scratch=hots(1),
    )
    row9 = vmem((3, depth, 1, long))
    plane3 = planes(3)
    s, outer, row_two, row_one, inner = call(
        search_kernel,
        (vmem(rhs.shape), plane3, row9, row9, plane3),
        (p, coupled_z, two, one, tx, ty, tz, rhs, first_column, block_inv),
    )
    outer, row_two = (neighbour(outer), neighbour(row_two, "tile"))
    row_one, inner = (flip(row_one, 0, "tile"), flip(inner, 0))
    (part,) = call(inner_kernel, (vmem(rhs.shape),), (s, block_diag, tz, tx, ty), far=(1,), late=((1,),))
    image, send = call(
        image_kernel,
        (vmem(rhs.shape), vmem((devices, 1, 128))),
        (part, inner, outer, row_two, row_one, rhs, tz, tx),
    )
    sums = everywhere(send)
    update, lin_res, ratio = call(
        finish_kernel, (hbm(rhs.shape), hbm(rhs.shape), hbm((1, 1))), (sums, s, image, rhs)
    )
    return (update, lin_res, ratio.reshape(()))


def solution(mesh):
    return jax.shard_map(
        shards,
        mesh=mesh,
        in_specs=(
            P(None, "layer", "tile", None),
            P(None, "layer", "tile", None),
            P(None, None, "layer", "tile", None),
            P(None, None, "layer", "tile", None),
            P("layer", "tile", None),
            P("layer", "tile", None),
            P("layer", "tile", None),
            P("layer", "tile", None),
            P(("tile", "layer")),
            P(("tile", "layer")),
            P(("tile", "layer")),
            P(("tile", "layer"), None),
        ),
        out_specs=(P(None, "layer", "tile", None), P(None, "layer", "tile", None), P()),
        check_vma=False,
    )
```
